32 devices in a mesh: dp: 4 (over z), mp: 8 (over y, x, core).
Axes of the slice: x: 2, y: 2, z: 4, core: 2. Of those that a mesh axis runs over, the one named last changes fastest.
Arguments:
- inputs: bfloat16 [8192, 2048], P(('dp', 'mp')), may hold values from -6 to 6
- out_grad: bfloat16 [8192, 2048], P(('dp', 'mp')), may hold values from -6 to 6
- project_weight: float32 [2, 2048, 3, 2048], P(None, 'dp', None, 'mp'), may hold values from -0.125 to 0.125
- dense_weight: float32 [2, 2048, 2048], P(None, 'mp', 'dp'), may hold values from -0.5 to 0.5
- up_weight: float32 [2, 2048, 8192], P(None, 'dp', 'mp'), may hold values from -0.125 to 0.125
- down_weight: float32 [2, 8192, 2048], P(None, 'mp', 'dp'), may hold values from -0.09375 to 0.09375
- project_bias: float32 [2, 2, 2048], P(None, None, 'mp'), may hold values from -3 to 3
- up_bias: float32 [2, 8192], P(None, 'mp'), may hold values from -3 to 3
- norm_gain: float32 [2, 2, 2048], replicated, may hold values from 0.1 to 1.9
- norm_bias: float32 [2, 2, 2048], replicated, may hold values from -3 to 3
- output_bias: float32 [2, 2, 2048], replicated, may hold values from -3 to 3
Outputs:
- outputs: bfloat16 [8192, 2048], P(('dp', 'mp'))
- input_grad: float32 [8192, 2048], P(('dp', 'mp'))
- project_grad: float32 [2, 2048, 3, 2048], P(None, 'dp', None, 'mp')
- dense_grad: float32 [2, 2048, 2048], P(None, 'mp', 'dp')
- up_grad: float32 [2, 2048, 8192], P(None, 'dp', 'mp')
- down_grad: float32 [2, 8192, 2048], P(None, 'mp', 'dp')
- project_bias_grad: float32 [2, 2, 2048], P(None, None, 'mp')
- up_bias_grad: float32 [2, 8192], P(None, 'mp')
- gain_grad: float32 [2, 2, 2048], replicated
- norm_bias_grad: float32 [2, 2, 2048], replicated
- output_bias_grad: float32 [2, 2, 2048], replicated
The draws below stay inside these ranges and needn't reach their ends.
All inputs are finite; a program needn't handle non-finite values.
Results may differ from the reference program's by a relative error of at most 0.029.
Values may be sent and summed in bfloat16 or wider, within the bound.
A program may use at most 256 MiB of HBM per device.

```python
import jax
import jax.numpy as jnp
from jax import lax

D = 2048
N_HEADS = 16
FF = 8192
HEAD = 128
LAYERS = 2
BLOCK = 256
LEN = 2048
TOKENS = 8192


def steps_of(rng, extent, split, low, high):
    factor_of = 1.0
    for position, blocks in split:
        heights = jax.random.uniform(jax.random.fold_in(jax.random.fold_in(rng, 6), position), (blocks,), jnp.float32, low / len(split), high / len(split))
        factor_of = factor_of * jnp.repeat(jnp.exp(heights), extent[position] // blocks).reshape((-1,) + (1,) * (len(extent) - 1 - position))
    return factor_of


def scatter_about(key, extent, scale, bound, cuts=(), held_as=jnp.bfloat16):
    array = scale * jax.random.normal(key, extent, jnp.float32)
    if cuts:
        array = array * steps_of(key, extent, cuts, -0.22, 0.18)
    return jnp.clip(array, -bound, bound).astype(held_as)


def setup_inputs(seed: int = 0) -> dict:
    key_list = jax.random.split(jax.random.key(seed), 12)
    return {
        "inputs": scatter_about(key_list[0], (TOKENS, D), 1.0, 6.0, ((0, 32),)),
        "out_grad": scatter_about(key_list[1], (TOKENS, D), 1.0, 6.0, ((0, 32),)),
        "project_weight": scatter_about(key_list[2], (LAYERS, D, 3, D), D ** -0.5, 0.125, ((1, 4), (3, 8)), jnp.float32),
        "dense_weight": scatter_about(key_list[3], (LAYERS, D, D), (D // 16) ** -0.5, 0.5, ((1, 8), (2, 4)), jnp.float32),
        "up_weight": scatter_about(key_list[4], (LAYERS, D, FF), D ** -0.5, 0.125, ((1, 4), (2, 8)), jnp.float32),
        "down_weight": scatter_about(key_list[5], (LAYERS, FF, D), (FF // 2) ** -0.5, 0.09375, ((1, 8), (2, 4)), jnp.float32),
        "project_bias": scatter_about(key_list[6], (LAYERS, 2, D), 0.5, 3.0, ((2, 8),), jnp.float32),
        "up_bias": scatter_about(key_list[7], (LAYERS, FF), 0.5, 3.0, ((1, 8),), jnp.float32),
        "norm_gain": jnp.clip(1.0 + 0.18 * jax.random.normal(key_list[8], (LAYERS, 2, D), jnp.float32), 0.1, 1.9),
        "norm_bias": scatter_about(key_list[9], (LAYERS, 2, D), 0.5, 3.0, (), jnp.float32),
        "output_bias": scatter_about(key_list[10], (LAYERS, 2, D), 0.5, 3.0, (), jnp.float32),
    }


norm_eps = 1e-05

@jax.custom_vjp
def low(v):
    return lax.optimization_barrier(v.astype(jnp.bfloat16)).astype(jnp.float32)

@jax.custom_vjp
def low_back(v):
    return v

def low_keep(v):
    return (low(v), None)

def low_pass(kept, grad):
    return (grad,)

def back_keep(v):
    return (v, None)

def back_low(kept, grad):
    return (low(grad),)
low.defvjp(low_keep, low_pass)
low_back.defvjp(back_keep, back_low)

def layer_norm(values, scale_row, shift_row):
    centre = lax.optimization_barrier(jnp.mean(values, axis=-1, keepdims=True))
    centred = values - centre
    spread = lax.optimization_barrier(jnp.mean(centred * centred, axis=-1, keepdims=True))
    return centred * lax.rsqrt(spread + norm_eps) * scale_row + shift_row

def gelu_tanh(values):
    return 0.5 * values * (1.0 + jnp.tanh(0.7978845608028654 * (values + 0.044715 * values * values * values)))

def head_attend(operands):
    queries, keys, values, slope = operands
    positions = lax.iota(jnp.int32, LEN)
    distance = jnp.abs(positions[:, None] - positions[None, :]).astype(jnp.float32)
    allowed = positions[None, :] // BLOCK <= positions[:, None] // BLOCK
    scores = jnp.dot(queries, keys.T, precision=lax.Precision.HIGHEST) * HEAD ** (-0.5) - slope * distance
    scores = jnp.where(allowed, low_back(scores), -1e+30)
    highest = lax.optimization_barrier(jnp.max(scores, axis=-1, keepdims=True))
    weights = jnp.exp(scores - highest)
    weights = low(weights / lax.optimization_barrier(jnp.sum(weights, axis=-1, keepdims=True)))
    return jnp.dot(weights, values, precision=lax.Precision.HIGHEST)

def layers_forward(stream, params):
    project_weight, dense_weight, up_weight, down_weight, project_bias, up_bias, norm_gain, norm_bias, output_bias = params
    slopes = 2.0 ** (-8.0 * jnp.arange(1, N_HEADS + 1, dtype=jnp.float32) / N_HEADS)
    for layer_index in range(LAYERS):
        normed = low(layer_norm(stream, norm_gain[layer_index, 0], norm_bias[layer_index, 0]))
        weight_low = low(project_weight[layer_index]).reshape(D, 3 * D)
        project = jnp.dot(normed, weight_low, precision=lax.Precision.HIGHEST).reshape(LEN, 3, D)
        shifts = jnp.stack([project_bias[layer_index, 0], jnp.zeros((D,), project.dtype), project_bias[layer_index, 1]])
        project = low(low_back(project + shifts))
        head_major = jnp.transpose(project.reshape(LEN, 3, N_HEADS, HEAD), (1, 2, 0, 3))
        context = lax.map(jax.checkpoint(head_attend), (head_major[0], head_major[1], head_major[2], slopes))
        context = low(low_back(jnp.transpose(context, (1, 0, 2)).reshape(LEN, D)))
        branch = jnp.dot(context, low(dense_weight[layer_index]), precision=lax.Precision.HIGHEST)
        middle = stream + low_back(branch) + output_bias[layer_index, 0]
        normed = low(layer_norm(middle, norm_gain[layer_index, 1], norm_bias[layer_index, 1]))
        hidden = low_back(jnp.dot(normed, low(up_weight[layer_index]), precision=lax.Precision.HIGHEST) + up_bias[layer_index])
        active = low(gelu_tanh(hidden))
        branch = jnp.dot(active, low(down_weight[layer_index]), precision=lax.Precision.HIGHEST)
        stream = middle + low_back(branch) + output_bias[layer_index, 1]
    return stream

def reference(inputs, out_grad, project_weight, dense_weight, up_weight, down_weight, project_bias, up_bias, norm_gain, norm_bias, output_bias):
    params = (project_weight, dense_weight, up_weight, down_weight, project_bias, up_bias, norm_gain, norm_bias, output_bias)
    sequences = inputs.shape[0] // LEN
    streams = inputs.astype(jnp.float32).reshape(sequences, LEN, D)
    cotangents = out_grad.astype(jnp.float32).reshape(sequences, LEN, D)

    def one_sequence(totals, sequence_pair):
        stream, cotangent = sequence_pair
        result, backward = jax.vjp(layers_forward, stream, params)
        grad_stream, grad_params = backward(cotangent)
        totals = jax.tree.map(lambda left, right: left + right, totals, grad_params)
        return (totals, (result, grad_stream))
    initial = jax.tree.map(jnp.zeros_like, params)
    totals, (results, grad_streams) = lax.scan(one_sequence, initial, (streams, cotangents))
    return (results.reshape(-1, D).astype(jnp.bfloat16), grad_streams.reshape(-1, D), totals[0], totals[1], totals[2], totals[3], totals[4], totals[5], totals[6], totals[7], totals[8])
```

```python
import functools

import jax
import jax.numpy as jnp
from jax import lax
from jax.experimental import pallas as pl
from jax.experimental.pallas import tpu as pltpu
from jax.sharding import PartitionSpec as P

N_HEADS = 16
BLOCK = 256
LOG2E = 1.4426950408889634
MESH = pl.DeviceIdType.MESH
NT_DIMS = (((1,), (1,)), ((), ()))
norm_eps = 1e-05


def nt(a, b):
    return lax.dot_general(a, b, NT_DIMS, preferred_element_type=jnp.float32)


def nn(a, b):
    return jnp.dot(a, b, preferred_element_type=jnp.float32)


def bias_tile(slope, first_key, first_query, keys, queries):
    kp = first_key + lax.broadcasted_iota(jnp.int32, (keys, queries), 0)
    qp = first_query + lax.broadcasted_iota(jnp.int32, (keys, queries), 1)
    return (jnp.abs(qp - kp).astype(jnp.float32)) * (-slope * LOG2E)

def scores_t(q, k, slope, i, B):
    L = (i+1)*B
    factor = q.shape[1] ** (-0.5) * LOG2E
    st = nt(k, q) * factor
    key = lax.broadcasted_iota(jnp.int32, (L, 1), 0)
    if i > 0:
        m = i * B
        kp = lax.broadcasted_iota(jnp.int32, (m, 1), 0).astype(jnp.float32)
        qp = (m + lax.broadcasted_iota(jnp.int32, (1, B), 1)).astype(jnp.float32)
        head = st[:m] - (qp - kp) * (slope * LOG2E)
        tail = st[m:] + bias_tile(slope, 0, 0, B, B)
        return head, tail
    return None, st + bias_tile(slope, 0, 0, B, B)

def attend_fwd_kernel(slope_ref, q_ref, k_ref, v_ref, ctx_ref, lse_ref, vt_ref):
    B = BLOCK
    slope = slope_ref[pl.program_id(0)]
    T = q_ref.shape[0]
    vt_ref[...] = v_ref[...].T
    for i in range(T // B):
        L = (i+1)*B
        head, tail = scores_t(q_ref[i*B:L, :], k_ref[:L, :], slope, i, B)
        top = jnp.max(tail, axis=0, keepdims=True)
        if head is not None:
            top = jnp.maximum(top, jnp.max(head, axis=0, keepdims=True))
        pt = jnp.exp2(tail - top)
        den = jnp.sum(pt, axis=0, keepdims=True)
        ct = nn(vt_ref[:, i*B:L], pt.astype(jnp.bfloat16))
        if head is not None:
            ph = jnp.exp2(head - top)
            den = den + jnp.sum(ph, axis=0, keepdims=True)
            ct = ct + nn(vt_ref[:, :i*B], ph.astype(jnp.bfloat16))
        ctx_ref[i*B:L, :] = (ct / den).T.astype(ctx_ref.dtype)
        lse_ref[0, i:i+1, :] = top + jnp.log2(den)

def attend_bwd_kernel(slope_ref, q_ref, k_ref, v_ref, g_ref, c_ref, lse_ref, out_ref, sums_ref, kt_ref, dk_ref, dv_ref):
    B = BLOCK
    slope = slope_ref[pl.program_id(0)]
    T = q_ref.shape[0]
    W = q_ref.shape[1]
    factor = W ** (-0.5)
    kt_ref[...] = k_ref[...].T
    qsum = jnp.zeros((1, W), jnp.float32)
    n = T // B
    for i in reversed(range(n)):
        L = (i+1)*B
        q = q_ref[i*B:L, :]
        g = g_ref[i*B:L, :]
        head, tail = scores_t(q, k_ref[:L, :], slope, i, B)
        prod = g.astype(jnp.float32) * c_ref[i*B:L, :].astype(jnp.float32)
        inner = lax.dot_general(jnp.ones((8, W), jnp.float32), prod, NT_DIMS, preferred_element_type=jnp.float32, precision=lax.Precision.HIGHEST)[:1]
        lse = lse_ref[0, i:i+1, :]
        dpt = nt(v_ref[:L, :], g)
        dqt = None
        for part, lo, hi in ((head, 0, i*B), (tail, i*B, L)):
            if part is None:
                continue
            pt = jnp.exp2(part - lse)
            ds = (pt * (dpt[lo:hi] - inner)).astype(jnp.bfloat16)
            pt = pt.astype(jnp.bfloat16)
            dk = nn(ds, q)
            dv = nn(pt, g)
            if i == n - 1:
                dk_ref[lo:hi, :] = dk
                dv_ref[lo:hi, :] = dv
            else:
                dk_ref[lo:hi, :] += dk
                dv_ref[lo:hi, :] += dv
            t = nn(kt_ref[:, lo:hi], ds)
            dqt = t if dqt is None else dqt + t
        dq = (dqt * factor).T.astype(jnp.bfloat16)
        out_ref[0, i*B:L, :] = dq
        qsum += jnp.sum(dq.astype(jnp.float32), axis=0, keepdims=True)
    out_ref[1] = (dk_ref[...] * factor).astype(jnp.bfloat16)
    dv = dv_ref[...].astype(jnp.bfloat16)
    out_ref[2] = dv
    sums_ref[0:1, :] = qsum
    sums_ref[1:2, :] = jnp.sum(dv.astype(jnp.float32), axis=0, keepdims=True)

def attend_fwd(project, slopes):
    T, W = project.shape
    H = W // 384
    col = lambda part: pl.BlockSpec((T, 128), lambda h, part=part: (0, part * H + h))
    return pl.pallas_call(
        attend_fwd_kernel, grid=(H,),
        out_shape=(jax.ShapeDtypeStruct((T, H*128), jnp.bfloat16), jax.ShapeDtypeStruct((H, T//BLOCK, BLOCK), jnp.float32)),
        in_specs=[pl.BlockSpec(memory_space=pltpu.SMEM), col(0), col(1), col(2)],
        out_specs=(pl.BlockSpec((T,128), lambda h: (0,h)), pl.BlockSpec((1, T//BLOCK, BLOCK), lambda h: (h,0,0))),
        scratch_shapes=[pltpu.VMEM((128, T), jnp.bfloat16)],
        compiler_params=pltpu.CompilerParams(vmem_limit_bytes=48<<20),
        cost_estimate=pl.CostEstimate(flops=4*T*T*128*H//2, bytes_accessed=8*T*H*128, transcendentals=T*T*H//2),
        name="attend_fwd")(slopes, project, project, project)

def attend_bwd(project, grad_context, context, lse, slopes):
    T, W = project.shape
    H = W // 384
    col = lambda part: pl.BlockSpec((T, 128), lambda h, part=part: (0, part * H + h))
    return pl.pallas_call(
        attend_bwd_kernel, grid=(H,),
        out_shape=(jax.ShapeDtypeStruct((3, T, H*128), jnp.bfloat16), jax.ShapeDtypeStruct((2, H*128), jnp.float32)),
        in_specs=[pl.BlockSpec(memory_space=pltpu.SMEM), col(0), col(1), col(2), col(0), col(0), pl.BlockSpec((1, T//BLOCK, BLOCK), lambda h: (h,0,0))],
        out_specs=(pl.BlockSpec((3, T,128), lambda h: (0, 0,h)), pl.BlockSpec((2,128), lambda h: (0,h))),
        scratch_shapes=[pltpu.VMEM((128, T), jnp.bfloat16), pltpu.VMEM((T,128), jnp.float32), pltpu.VMEM((T,128), jnp.float32)],
        compiler_params=pltpu.CompilerParams(vmem_limit_bytes=56<<20),
        cost_estimate=pl.CostEstimate(flops=10*T*T*128*H//2, bytes_accessed=16*T*H*128, transcendentals=T*T*H//2),
        name="attend_bwd")(slopes, project, project, project, grad_context, context, lse)


def peers():
    me = lax.axis_index("mp")
    core = me % 2
    bx = (me // 2) % 2
    by = me // 4
    return me, core, bx, by, me + 1 - 2 * core, me + 2 - 4 * bx, me + 4 - 8 * by


def owner(rel, core, bx, by):
    c = core if rel % 2 == 0 else 1 - core
    x = bx if (rel // 2) % 2 == 0 else 1 - bx
    y = by if rel // 4 == 0 else 1 - by
    return y * 4 + x * 2 + c


def enter(partner, xn, yn):
    barrier = pltpu.get_barrier_semaphore()
    for n in (partner, xn, yn):
        pl.semaphore_signal(barrier, inc=1, device_id={"mp": n}, device_id_type=MESH)
    pl.semaphore_wait(barrier, 3)


def gather_kernel(C, n_in, n_out, body, *refs):
    x_ref, ins = refs[0], refs[1 : 1 + n_in]
    full_ref, outs = refs[1 + n_in], refs[2 + n_in : 2 + n_in + n_out]
    buf, send, recv, loc = refs[2 + n_in + n_out :]
    R, D = x_ref.shape
    rc = R // C
    me, core, bx, by, partner, xn, yn = peers()
    enter(partner, xn, yn)

    def copy(src, rel, k, target, sidx):
        rows = pl.ds(k * rc, rc)
        return pltpu.make_async_remote_copy(
            src_ref=src.at[rows, :],
            dst_ref=buf.at[rel, rows, :],
            send_sem=send.at[sidx, k],
            recv_sem=recv.at[rel, k],
            device_id={"mp": target},
            device_id_type=MESH,
        )

    def arrive(rel, k):
        copy(x_ref, rel, k, partner, 0).wait_recv()

    sent = []
    for k in range(C):
        for rel, target, s in ((2, xn, 1), (4, yn, 2), (1, partner, 0)):
            c = copy(x_ref, rel, k, target, s)
            c.start()
            sent.append(c)

    def block(rel):
        src = x_ref if rel == 0 else buf.at[rel]
        start = pl.multiple_of(owner(rel, core, bx, by) * R, R)
        rows = pl.ds(start, R)
        lc = pltpu.make_async_copy(src, full_ref.at[rows, :], loc.at[rel])
        lc.start()
        body(rel == 0, src, rows, ins, outs)
        return lc

    locs = [block(0)]
    dl = 4 - 2 * core
    fwd_target = jnp.where(core == 0, xn, yn)
    for k in range(C):
        arrive(2, k)
        arrive(4, k)
        for c in (
            copy(buf.at[dl], 6, k, fwd_target, 3),
            copy(buf.at[2], 3, k, partner, 4),
            copy(buf.at[4], 5, k, partner, 5),
        ):
            c.start()
            sent.append(c)
        if k == 0:
            for kk in range(C):
                arrive(1, kk)
            locs.append(block(1))
        if k >= 1:
            arrive(6, k - 1)
            c = copy(buf.at[6], 7, k - 1, partner, 6)
            c.start()
            sent.append(c)
    locs.append(block(2))
    locs.append(block(4))
    arrive(6, C - 1)
    c = copy(buf.at[6], 7, C - 1, partner, 6)
    c.start()
    sent.append(c)
    for k in range(C):
        arrive(3, k)
        arrive(5, k)
    locs.append(block(3))
    locs.append(block(5))
    locs.append(block(6))
    for k in range(C):
        arrive(7, k)
    locs.append(block(7))
    for c in sent:
        c.wait_send()
    for c in locs:
        c.wait()


def gather_call(name, cid, x, ins, outs, body, C=4):
    R, D = x.shape
    vmem = pl.BlockSpec(memory_space=pltpu.VMEM)
    flops = 2 * 8 * R * D * outs[0].shape[1]
    return pl.pallas_call(
        functools.partial(gather_kernel, C, len(ins), len(outs), body),
        out_shape=(jax.ShapeDtypeStruct((8 * R, D), x.dtype), *outs),
        in_specs=[vmem] * (1 + len(ins)),
        out_specs=(pl.BlockSpec(memory_space=pl.ANY),) + (vmem,) * len(outs),
        scratch_shapes=[
            pltpu.VMEM((8, R, D), x.dtype),
            pltpu.SemaphoreType.DMA((7, C)),
            pltpu.SemaphoreType.DMA((8, C)),
            pltpu.SemaphoreType.DMA((8,)),
        ],
        compiler_params=pltpu.CompilerParams(
            collective_id=cid, has_side_effects=True, vmem_limit_bytes=60 << 20
        ),
        cost_estimate=pl.CostEstimate(flops=flops, bytes_accessed=32 * R * D, transcendentals=0),
        name=name,
    )(x, *ins)


def tiles(n, step, f):
    step = min(step, n)

    @pl.loop(0, n // step)
    def _(j):
        f(pl.ds(pl.multiple_of(j * step, step), step))


def project_body(first, src, rows, ins, outs):
    w, shift = ins

    def f(cols):
        outs[0][rows, cols] = (nn(src[...], w[:, cols]) + shift[:, cols]).astype(jnp.bfloat16)

    tiles(w.shape[1], 256, f)


def up_body(first, src, rows, ins, outs):
    w, shift = ins

    def f(cols):
        v = nn(src[...], w[:, cols]) + shift[:, cols]
        t = jnp.tanh(0.7978845608028654 * (v + 0.044715 * v * v * v))
        outs[0][rows, cols] = (0.5 * v * (1.0 + t)).astype(jnp.bfloat16)
        d = 0.5 * (1.0 + t) + 0.5 * v * (1.0 - t * t) * (
            0.7978845608028654 * (1.0 + 3 * 0.044715 * v * v)
        )
        outs[1][rows, cols] = d.astype(jnp.bfloat16)

    tiles(w.shape[1], 256, f)


def wide_nt(src, w, cols):
    Z, _, d = w.shape
    total = None
    for z in range(Z):
        t = nt(src[:, z * d : (z + 1) * d], w[z, cols, :])
        total = t if total is None else total + t
    return total


def down_back_body(first, src, rows, ins, outs):
    w, slope = ins

    def f(cols):
        g = wide_nt(src, w, cols) * slope[rows, cols].astype(jnp.float32)
        g = g.astype(jnp.bfloat16)
        outs[0][rows, cols] = g
        sums = jnp.sum(g.astype(jnp.float32), axis=0, keepdims=True)
        if first:
            outs[1][:, cols] = sums
        else:
            outs[1][:, cols] += sums

    tiles(w.shape[1], 256, f)


def dense_back_body(first, src, rows, ins, outs):
    (w,) = ins

    def f(cols):
        outs[0][rows, cols] = wide_nt(src, w, cols).astype(jnp.bfloat16)

    tiles(w.shape[1], 256, f)


def scatter_kernel(C, n_in, body, *refs):
    ins, out_ref = refs[:n_in], refs[n_in]
    pbuf, rbuf, send, recv = refs[n_in + 1 :]
    R, D = out_ref.shape
    rc = R // C
    me, core, bx, by, partner, xn, yn = peers()
    enter(partner, xn, yn)
    dn = jnp.where(core == 0, yn, xn)
    fn = jnp.where(core == 0, xn, yn)

    def copy(src, slot, k, target):
        rows = pl.ds(k * rc, rc)
        return pltpu.make_async_remote_copy(
            src_ref=src.at[rows, :],
            dst_ref=rbuf.at[slot, rows, :],
            send_sem=send.at[slot, k],
            recv_sem=recv.at[slot, k],
            device_id={"mp": target},
            device_id_type=MESH,
        )

    sent = []

    def send_one(src, slot, target, k):
        c = copy(src, slot, k, target)
        c.start()
        sent.append(c)

    def arrive(slot, k):
        copy(pbuf.at[0], slot, k, partner).wait_recv()

    def dest_rank(which, c):
        if which == "diag":
            return (1 - by) * 4 + (1 - bx) * 2 + c
        if which == "me":
            return by * 4 + bx * 2 + c
        flip_y = (1 - c) if which == "direct" else c
        y = by + flip_y * (1 - 2 * by)
        x = bx + (1 - flip_y) * (1 - 2 * bx)
        return y * 4 + x * 2 + c

    def compute(which, c, slot):
        rows = pl.ds(pl.multiple_of(dest_rank(which, c) * R, R), R)
        body(rows, ins, pbuf.at[slot])

    def add(slot, rslot, k):
        @pl.loop(0, rc // 16)
        def _(i):
            rows = pl.ds(pl.multiple_of(k * rc + i * 16, 16), 16)
            pbuf[slot, rows, :] = (
                pbuf[slot, rows, :].astype(jnp.float32) + rbuf[rslot, rows, :].astype(jnp.float32)
            ).astype(pbuf.dtype)

    for i, which in enumerate(("diag", "direct", "onward", "me")):
        compute(which, 1 - core, i)
        for k in range(C):
            send_one(pbuf.at[i], i, partner, k)
        compute(which, core, 4 + i)
        for k in range(C):
            arrive(i, k)
            add(4 + i, i, k)
            if i == 0:
                send_one(pbuf.at[4], 4, dn, k)
            if i == 1:
                send_one(pbuf.at[5], 5, dn, k)
            if i == 2:
                arrive(4, k)
                add(6, 4, k)
                send_one(pbuf.at[6], 6, fn, k)
    for k in range(C):
        arrive(5, k)
        arrive(6, k)

        @pl.loop(0, rc // 16)
        def _(i):
            rows = pl.ds(pl.multiple_of(k * rc + i * 16, 16), 16)
            out_ref[rows, :] = (
                pbuf[7, rows, :].astype(jnp.float32)
                + rbuf[5, rows, :].astype(jnp.float32)
                + rbuf[6, rows, :].astype(jnp.float32)
            )
    for c in sent:
        c.wait_send()


def scatter_call(name, cid, T, D, ins, body, C=4):
    R = T // 8
    vmem = pl.BlockSpec(memory_space=pltpu.VMEM)
    return pl.pallas_call(
        functools.partial(scatter_kernel, C, len(ins), body),
        out_shape=jax.ShapeDtypeStruct((R, D), jnp.float32),
        in_specs=[vmem] * len(ins),
        out_specs=vmem,
        scratch_shapes=[
            pltpu.VMEM((8, R, D), jnp.bfloat16),
            pltpu.VMEM((7, R, D), jnp.bfloat16),
            pltpu.SemaphoreType.DMA((7, C)),
            pltpu.SemaphoreType.DMA((7, C)),
        ],
        compiler_params=pltpu.CompilerParams(
            collective_id=cid, has_side_effects=True, vmem_limit_bytes=60 << 20
        ),
        cost_estimate=pl.CostEstimate(flops=2 * T * D * 1024, bytes_accessed=32 * R * D, transcendentals=0),
        name=name,
    )(*ins)


def row_split_body(rows, ins, out):
    a, w = ins
    Z, _, d = w.shape
    for z in range(Z):
        out[:, z * d : (z + 1) * d] = nn(a[rows, :], w[z]).astype(out.dtype)


def up_back_body(rows, ins, out):
    a, w = ins

    def f(cols):
        out[:, cols] = nt(a[rows, :], w[cols, :]).astype(out.dtype)

    tiles(w.shape[0], 512, f)


def project_back_body(rows, ins, out):
    a, w = ins
    S, _, width = a.shape

    def f(cols):
        total = None
        for s in range(S):
            t = nt(a[s, rows, :], w[cols, s * width : (s + 1) * width])
            total = t if total is None else total + t
        out[:, cols] = total.astype(out.dtype)

    tiles(w.shape[0], 512, f)


def layer_norm(values, scale_row, shift_row):
    centre = jnp.mean(values, axis=-1, keepdims=True)
    centred = values - centre
    spread = jnp.mean(centred * centred, axis=-1, keepdims=True)
    return centred * lax.rsqrt(spread + norm_eps) * scale_row + shift_row


def gather_project(cid, normed, w, shift):
    if lax.axis_size("mp") == 8:
        out = jax.ShapeDtypeStruct((8 * normed.shape[0], w.shape[1]), jnp.bfloat16)
        return gather_call("gather_project", cid, normed, (w, shift[None]), (out,), project_body)
    full = lax.all_gather(normed, "mp", axis=0, tiled=True)
    return full, (nn(full, w) + shift).astype(jnp.bfloat16)


def gather_up(cid, normed, w, shift):
    if lax.axis_size("mp") == 8:
        out = jax.ShapeDtypeStruct((8 * normed.shape[0], w.shape[1]), jnp.bfloat16)
        return gather_call("gather_up", cid, normed, (w, shift[None]), (out, out), up_body)
    full = lax.all_gather(normed, "mp", axis=0, tiled=True)
    v = nn(full, w) + shift
    t = jnp.tanh(0.7978845608028654 * (v + 0.044715 * v * v * v))
    d = 0.5 * (1.0 + t) + 0.5 * v * (1.0 - t * t) * (
        0.7978845608028654 * (1.0 + 3 * 0.044715 * v * v)
    )
    return full, (0.5 * v * (1.0 + t)).astype(jnp.bfloat16), d.astype(jnp.bfloat16)


def gather_down_back(cid, grad, w, slope):
    if lax.axis_size("mp") == 8:
        outs = (
            jax.ShapeDtypeStruct(slope.shape, jnp.bfloat16),
            jax.ShapeDtypeStruct((1, slope.shape[1]), jnp.float32),
        )
        return gather_call("gather_down_back", cid, grad, (w, slope), outs, down_back_body)
    full = lax.all_gather(grad, "mp", axis=0, tiled=True)
    g = (wide_nt(full, w, slice(None)) * slope.astype(jnp.float32)).astype(jnp.bfloat16)
    return full, g, jnp.sum(g.astype(jnp.float32), axis=0, keepdims=True)


def gather_dense_back(cid, grad, w):
    if lax.axis_size("mp") == 8:
        out = jax.ShapeDtypeStruct((8 * grad.shape[0], w.shape[1]), jnp.bfloat16)
        return gather_call("gather_dense_back", cid, grad, (w,), (out,), dense_back_body)
    full = lax.all_gather(grad, "mp", axis=0, tiled=True)
    return full, wide_nt(full, w, slice(None)).astype(jnp.bfloat16)


def scatter(name, cid, T, D, ins, body):
    if lax.axis_size("mp") == 8:
        return scatter_call(name, cid, T, D, ins, body)
    a, w = ins
    if body is row_split_body:
        part = jnp.concatenate([nn(a, w[z]) for z in range(w.shape[0])], axis=1)
    elif body is up_back_body:
        part = nt(a, w)
    else:
        width = a.shape[2]
        part = sum(nt(a[s], w[:, s * width : (s + 1) * width]) for s in range(a.shape[0]))
    return lax.psum_scatter(
        part.astype(jnp.bfloat16), "mp", scatter_dimension=0, tiled=True
    ).astype(jnp.float32)


def shards(
    inputs,
    out_grad,
    project_weight,
    dense_weight,
    up_weight,
    down_weight,
    project_bias,
    up_bias,
    norm_gain,
    norm_bias,
    output_bias,
):
    tensor_size = lax.axis_size("mp")
    data_size = lax.axis_size("dp")
    tensor_rank = lax.axis_index("mp")
    row_count, model_width = inputs.shape
    total_rows = row_count * tensor_size
    inner_width = project_weight.shape[3]
    heads_here = N_HEADS // tensor_size
    layer_count = project_weight.shape[0]
    slopes = 2.0 ** (
        -8.0
        * (tensor_rank * heads_here + lax.iota(jnp.int32, heads_here) + 1).astype(jnp.float32)
        / N_HEADS
    )
    low = jnp.bfloat16
    gathered = []
    for l in range(layer_count):
        gathered.append(
            (
                lax.all_gather(
                    project_weight[l].reshape(-1, 3 * inner_width).astype(low),
                    "dp",
                    axis=0,
                    tiled=True,
                ),
                lax.all_gather(dense_weight[l].astype(low), "dp", axis=0),
                lax.all_gather(up_weight[l].astype(low), "dp", axis=0, tiled=True),
                lax.all_gather(down_weight[l].astype(low), "dp", axis=0),
            )
        )
    stream = inputs.astype(jnp.float32)
    stored = []
    for l in range(layer_count):
        w_project, w_dense, w_up, w_down = gathered[l]
        normed = layer_norm(stream, norm_gain[l, 0], norm_bias[l, 0]).astype(low)
        shift = jnp.concatenate(
            [project_bias[l, 0], jnp.zeros((inner_width,), jnp.float32), project_bias[l, 1]]
        )
        normed_all, project = gather_project(10 * l, normed, w_project, shift)
        context, log_norms = attend_fwd(project, slopes)
        attn_rows = scatter(
            "dense_scatter", 10 * l + 1, total_rows, model_width, (context, w_dense), row_split_body
        )
        middle = stream + attn_rows + output_bias[l, 0]
        normed2 = layer_norm(middle, norm_gain[l, 1], norm_bias[l, 1]).astype(low)
        normed2_all, active, slope = gather_up(10 * l + 2, normed2, w_up, up_bias[l])
        down_rows = scatter(
            "down_scatter", 10 * l + 3, total_rows, model_width, (active, w_down), row_split_body
        )
        stored.append(
            (stream, normed_all, project, log_norms, context, middle, normed2_all, active, slope)
        )
        stream = middle + down_rows + output_bias[l, 1]
    outputs = stream.astype(low)
    grad = out_grad.astype(jnp.float32)
    project_grads = [None] * layer_count
    dense_grads = [None] * layer_count
    up_grads = [None] * layer_count
    down_grads = [None] * layer_count
    copied = [None] * layer_count
    split = [None] * layer_count

    def reduce_dp(part):
        return lax.psum_scatter(part.astype(low), "dp", scatter_dimension=0, tiled=True).astype(
            jnp.float32
        )

    for l in reversed(range(layer_count)):
        w_project, w_dense, w_up, w_down = gathered[l]
        stream_in, normed_all, project, log_norms, context, middle, normed2_all, active, slope = (
            stored[l]
        )
        down_bias_grad = jnp.sum(grad, axis=0)
        grad_down, grad_hidden, up_bias_part = gather_down_back(
            10 * l + 4, grad.astype(low), w_down, slope
        )
        down_grads[l] = reduce_dp(
            jnp.einsum(
                "tf,tzd->zfd",
                active,
                grad_down.reshape(total_rows, data_size, -1),
                preferred_element_type=jnp.float32,
            )
        )[0]
        grad_normed2 = scatter(
            "up_back_scatter",
            10 * l + 5,
            total_rows,
            model_width,
            (grad_hidden, w_up),
            up_back_body,
        )
        up_grads[l] = reduce_dp(
            jnp.einsum("td,tf->df", normed2_all, grad_hidden, preferred_element_type=jnp.float32)
        )
        norm_back = jax.vjp(layer_norm, middle, norm_gain[l, 1], norm_bias[l, 1])[1]
        grad_from_norm, gain_second, shift_second = norm_back(grad_normed2)
        grad_middle = grad + grad_from_norm
        dense_bias_grad = jnp.sum(grad_middle, axis=0)
        grad_branch, grad_context = gather_dense_back(10 * l + 6, grad_middle.astype(low), w_dense)
        dense_grads[l] = reduce_dp(
            jnp.einsum(
                "ti,tzd->zid",
                context,
                grad_branch.reshape(total_rows, data_size, -1),
                preferred_element_type=jnp.float32,
            )
        )[0]
        grad_project, project_bias_part = attend_bwd(
            project, grad_context, context, log_norms, slopes
        )
        grad_normed = scatter(
            "project_back_scatter",
            10 * l + 7,
            total_rows,
            model_width,
            (grad_project, w_project),
            project_back_body,
        )
        project_grads[l] = reduce_dp(
            jnp.einsum(
                "td,sti->dsi", normed_all, grad_project, preferred_element_type=jnp.float32
            )
        )
        norm_back = jax.vjp(layer_norm, stream_in, norm_gain[l, 0], norm_bias[l, 0])[1]
        grad_from_norm, gain_first, shift_first = norm_back(grad_normed)
        grad = grad_middle + grad_from_norm
        copied[l] = lax.psum(
            jnp.stack(
                [gain_first, gain_second, shift_first, shift_second, dense_bias_grad, down_bias_grad]
            ),
            ("dp", "mp"),
        )
        split[l] = lax.psum(
            jnp.concatenate([project_bias_part.reshape(-1), up_bias_part.reshape(-1)]), "dp"
        )
    copied = jnp.stack(copied)
    split = jnp.stack(split)
    return (
        outputs,
        grad,
        jnp.stack(project_grads),
        jnp.stack(dense_grads),
        jnp.stack(up_grads),
        jnp.stack(down_grads),
        split[:, : 2 * inner_width].reshape(layer_count, 2, inner_width),
        split[:, 2 * inner_width :],
        copied[:, 0:2],
        copied[:, 2:4],
        copied[:, 4:6],
    )


def solution(mesh):
    rows = P(("dp", "mp"), None)
    specs = (P(None, "dp", None, "mp"), P(None, "mp", "dp"), P(None, "dp", "mp"), P(None, "mp", "dp"))
    biases = (P(None, None, "mp"), P(None, "mp"), P(), P(), P())
    return jax.shard_map(
        shards,
        mesh=mesh,
        in_specs=(rows, rows, *specs, *biases),
        out_specs=(rows, rows, *specs, *biases),
        check_vma=False,
    )
```

```python
import functools

import jax
import jax.numpy as jnp
from jax import lax
from jax.experimental import pallas as pl
from jax.experimental.pallas import tpu as pltpu
from jax.sharding import PartitionSpec as P

N_HEADS = 16
BLOCK = 256
LOG2E = 1.4426950408889634
MESH = pl.DeviceIdType.MESH
NT_DIMS = (((1,), (1,)), ((), ()))
norm_eps = 1e-05


def nt(a, b):
    return lax.dot_general(a, b, NT_DIMS, preferred_element_type=jnp.float32)


def nn(a, b):
    return jnp.dot(a, b, preferred_element_type=jnp.float32)


def bias_tile(slope, first_key, first_query, keys, queries):
    kp = first_key + lax.broadcasted_iota(jnp.int32, (keys, queries), 0)
    qp = first_query + lax.broadcasted_iota(jnp.int32, (keys, queries), 1)
    return (jnp.abs(qp - kp).astype(jnp.float32)) * (-slope * LOG2E)

def scores_t(q, k, slope, i, B):
    L = (i+1)*B
    factor = q.shape[1] ** (-0.5) * LOG2E
    st = nt(k, q) * factor
    key = lax.broadcasted_iota(jnp.int32, (L, 1), 0)
    if i > 0:
        m = i * B
        kp = lax.broadcasted_iota(jnp.int32, (m, 1), 0).astype(jnp.float32)
        qp = (m + lax.broadcasted_iota(jnp.int32, (1, B), 1)).astype(jnp.float32)
        head = st[:m] - (qp - kp) * (slope * LOG2E)
        tail = st[m:] + bias_tile(slope, 0, 0, B, B)
        return head, tail
    return None, st + bias_tile(slope, 0, 0, B, B)

def attend_fwd_kernel(slope_ref, q_ref, k_ref, v_ref, ctx_ref, lse_ref, vt_ref):
    B = BLOCK
    slope = slope_ref[pl.program_id(0)]
    T = q_ref.shape[0]
    vt_ref[...] = v_ref[...].T
    for i in range(T // B):
        L = (i+1)*B
        head, tail = scores_t(q_ref[i*B:L, :], k_ref[:L, :], slope, i, B)
        top = jnp.max(tail, axis=0, keepdims=True)
        if head is not None:
            top = jnp.maximum(top, jnp.max(head, axis=0, keepdims=True))
        pt = jnp.exp2(tail - top)
        den = jnp.sum(pt, axis=0, keepdims=True)
        ct = nn(vt_ref[:, i*B:L], pt.astype(jnp.bfloat16))
        if head is not None:
            ph = jnp.exp2(head - top)
            den = den + jnp.sum(ph, axis=0, keepdims=True)
            ct = ct + nn(vt_ref[:, :i*B], ph.astype(jnp.bfloat16))
        ctx_ref[i*B:L, :] = (ct / den).T.astype(ctx_ref.dtype)
        lse_ref[0, i:i+1, :] = top + jnp.log2(den)

def attend_bwd_kernel(slope_ref, q_ref, k_ref, v_ref, g_ref, c_ref, lse_ref, out_ref, sums_ref, kt_ref, dk_ref, dv_ref):
    B = BLOCK
    slope = slope_ref[pl.program_id(0)]
    T = q_ref.shape[0]
    W = q_ref.shape[1]
    factor = W ** (-0.5)
    kt_ref[...] = k_ref[...].T
    qsum = jnp.zeros((1, W), jnp.float32)
    n = T // B
    for i in reversed(range(n)):
        L = (i+1)*B
        q = q_ref[i*B:L, :]
        g = g_ref[i*B:L, :]
        head, tail = scores_t(q, k_ref[:L, :], slope, i, B)
        prod = g.astype(jnp.float32) * c_ref[i*B:L, :].astype(jnp.float32)
        inner = lax.dot_general(jnp.ones((8, W), jnp.float32), prod, NT_DIMS, preferred_element_type=jnp.float32, precision=lax.Precision.HIGHEST)[:1]
        lse = lse_ref[0, i:i+1, :]
        dpt = nt(v_ref[:L, :], g)
        dqt = None
        for part, lo, hi in ((head, 0, i*B), (tail, i*B, L)):
            if part is None:
                continue
            pt = jnp.exp2(part - lse)
            ds = (pt * (dpt[lo:hi] - inner)).astype(jnp.bfloat16)
            pt = pt.astype(jnp.bfloat16)
            dk = nn(ds, q)
            dv = nn(pt, g)
            if i == n - 1:
                dk_ref[lo:hi, :] = dk
                dv_ref[lo:hi, :] = dv
            else:
                dk_ref[lo:hi, :] += dk
                dv_ref[lo:hi, :] += dv
            t = nn(kt_ref[:, lo:hi], ds)
            dqt = t if dqt is None else dqt + t
        dq = (dqt * factor).T.astype(jnp.bfloat16)
        out_ref[0, i*B:L, :] = dq
        qsum += jnp.sum(dq.astype(jnp.float32), axis=0, keepdims=True)
    out_ref[1] = (dk_ref[...] * factor).astype(jnp.bfloat16)
    dv = dv_ref[...].astype(jnp.bfloat16)
    out_ref[2] = dv
    sums_ref[0:1, :] = qsum
    sums_ref[1:2, :] = jnp.sum(dv.astype(jnp.float32), axis=0, keepdims=True)

def attend_fwd(project, slopes):
    T, W = project.shape
    H = W // 384
    col = lambda part: pl.BlockSpec((T, 128), lambda h, part=part: (0, part * H + h))
    return pl.pallas_call(
        attend_fwd_kernel, grid=(H,),
        out_shape=(jax.ShapeDtypeStruct((T, H*128), jnp.bfloat16), jax.ShapeDtypeStruct((H, T//BLOCK, BLOCK), jnp.float32)),
        in_specs=[pl.BlockSpec(memory_space=pltpu.SMEM), col(0), col(1), col(2)],
        out_specs=(pl.BlockSpec((T,128), lambda h: (0,h)), pl.BlockSpec((1, T//BLOCK, BLOCK), lambda h: (h,0,0))),
        scratch_shapes=[pltpu.VMEM((128, T), jnp.bfloat16)],
        compiler_params=pltpu.CompilerParams(vmem_limit_bytes=48<<20),
        cost_estimate=cost(1 << 20),
        name="attend_fwd")(slopes, project, project, project)

def attend_bwd(project, grad_context, context, lse, slopes):
    T, W = project.shape
    H = W // 384
    col = lambda part: pl.BlockSpec((T, 128), lambda h, part=part: (0, part * H + h))
    return pl.pallas_call(
        attend_bwd_kernel, grid=(H,),
        out_shape=(jax.ShapeDtypeStruct((3, T, H*128), jnp.bfloat16), jax.ShapeDtypeStruct((2, H*128), jnp.float32)),
        in_specs=[pl.BlockSpec(memory_space=pltpu.SMEM), col(0), col(1), col(2), col(0), col(0), pl.BlockSpec((1, T//BLOCK, BLOCK), lambda h: (h,0,0))],
        out_specs=(pl.BlockSpec((3, T,128), lambda h: (0, 0,h)), pl.BlockSpec((2,128), lambda h: (0,h))),
        scratch_shapes=[pltpu.VMEM((128, T), jnp.bfloat16), pltpu.VMEM((T,128), jnp.float32), pltpu.VMEM((T,128), jnp.float32)],
        compiler_params=pltpu.CompilerParams(vmem_limit_bytes=56<<20),
        cost_estimate=cost(1 << 20),
        name="attend_bwd")(slopes, project, project, project, grad_context, context, lse)


def peers():
    me = lax.axis_index("mp")
    core = me % 2
    bx = (me // 2) % 2
    by = me // 4
    return me, core, bx, by, me + 1 - 2 * core, me + 2 - 4 * bx, me + 4 - 8 * by


def owner(rel, core, bx, by):
    c = core if rel % 2 == 0 else 1 - core
    x = bx if (rel // 2) % 2 == 0 else 1 - bx
    y = by if rel // 4 == 0 else 1 - by
    return y * 4 + x * 2 + c


def z_peers():
    z = lax.axis_index("dp")
    z1 = z + 1 - 2 * (z % 2)
    return z, z1, (z + 2) % 4, (z1 + 2) % 4


def enter(partner, xn, yn, z=False):
    barrier = pltpu.get_barrier_semaphore()
    for n in (partner, xn, yn):
        pl.semaphore_signal(barrier, inc=1, device_id={"mp": n}, device_id_type=MESH)
    if z:
        _, z1, z2, _ = z_peers()
        for n in (z1, z2):
            pl.semaphore_signal(barrier, inc=1, device_id={"dp": n}, device_id_type=MESH)
    pl.semaphore_wait(barrier, 5 if z else 3)


ZR = 128


def z_scratch(n, w):
    return (
        pltpu.VMEM((3, n, ZR, w), jnp.bfloat16),
        pltpu.VMEM((2, n, ZR, w), jnp.bfloat16),
        pltpu.SemaphoreType.DMA((3, n)),
        pltpu.SemaphoreType.DMA((3, n)),
        pltpu.SemaphoreType.DMA((2, n)),
    )


class ZSum:
    def __init__(self, plan, srcs, out, scratch):
        self.plan, self.srcs, self.out = plan, srcs, out
        self.recv, self.own, self.send_sem, self.recv_sem, self.loc = scratch
        self.z, self.z1, self.z2, self.z3 = z_peers()
        self.sent = []
        self.events = [functools.partial(self.event, c) for c in range(len(plan))]

    def block(self, c, z):
        i, row = self.plan[c]
        return self.srcs[i].at[z, pl.ds(row, ZR), :]

    def remote(self, src, kind, c, target):
        return pltpu.make_async_remote_copy(
            src_ref=src,
            dst_ref=self.recv.at[kind, c],
            send_sem=self.send_sem.at[kind, c],
            recv_sem=self.recv_sem.at[kind, c],
            device_id={"dp": target},
            device_id_type=MESH,
        )

    def push(self, *args):
        c = self.remote(*args)
        c.start()
        self.sent.append(c)

    def here(self, kind, c):
        return pltpu.make_async_copy(
            self.block(c, self.z2 if kind else self.z), self.own.at[kind, c], self.loc.at[kind, c]
        )

    def arrive(self, kind, c):
        self.remote(self.own.at[0, c], kind, c, self.z1).wait_recv()

    def start(self):
        for c in range(len(self.plan)):
            self.push(self.block(c, self.z3), 1, c, self.z1)
        for c in range(len(self.plan)):
            self.here(1, c).start()
            self.here(0, c).start()

    def event(self, c):
        self.arrive(1, c)
        self.here(1, c).wait()

        @pl.loop(0, ZR // 16)
        def _(i):
            rows = pl.ds(pl.multiple_of(i * 16, 16), 16)
            self.own[1, c, rows, :] = (
                self.own[1, c, rows, :].astype(jnp.float32)
                + self.recv[1, c, rows, :].astype(jnp.float32)
            ).astype(jnp.bfloat16)

        self.push(self.own.at[1, c], 2, c, self.z2)
        self.push(self.block(c, self.z1), 0, c, self.z1)

    def tick(self, n=1):
        for _ in range(min(n, len(self.events))):
            self.events.pop(0)()

    def finish(self):
        self.tick(len(self.events))
        for c in range(len(self.plan)):
            self.here(0, c).wait()
            self.arrive(0, c)
            self.arrive(2, c)

            @pl.loop(0, ZR // 16)
            def _(i):
                rows = pl.ds(pl.multiple_of(i * 16, 16), 16)
                to = pl.ds(pl.multiple_of(c * ZR + i * 16, 16), 16)
                self.out[to, :] = (
                    self.own[0, c, rows, :].astype(jnp.float32)
                    + self.recv[0, c, rows, :].astype(jnp.float32)
                    + self.recv[2, c, rows, :].astype(jnp.float32)
                )

        for c in self.sent:
            c.wait_send()


class NoZ:
    def start(self):
        pass

    def tick(self, n=1):
        pass

    def finish(self):
        pass


def z_task(plan, srcs, outs, scratch):
    return ZSum(plan, srcs, outs[0], scratch) if plan else NoZ()


def z_parts(z):
    if z is None or not z.plan:
        return (), (), ()
    w = z.arrays[0].shape[2]
    n = len(z.plan)
    return tuple(z.arrays), (jax.ShapeDtypeStruct((n * ZR, w), jnp.float32),), z_scratch(n, w)


def cost(flops):
    return pl.CostEstimate(flops=flops, bytes_accessed=1 << 16, transcendentals=0)


def gather_kernel(C, n_in, n_out, body, plan, n_src, *refs):
    x_ref, ins, refs = refs[0], refs[1 : 1 + n_in], refs[1 + n_in :]
    srcs, refs = refs[:n_src], refs[n_src:]
    full_ref, outs, refs = refs[0], refs[1 : 1 + n_out], refs[1 + n_out :]
    z_out, refs = (refs[:1], refs[1:]) if plan else ((), refs)
    buf, send, recv, loc = refs[:4]
    R, D = x_ref.shape
    rc = R // C
    me, core, bx, by, partner, xn, yn = peers()
    z = z_task(plan, srcs, z_out, refs[4:])
    enter(partner, xn, yn, bool(plan))
    z.start()
    sent = []

    def copy(src, rel, k, target, sidx):
        return pltpu.make_async_remote_copy(
            src_ref=src,
            dst_ref=buf.at[k, rel],
            send_sem=send.at[sidx, k],
            recv_sem=recv.at[rel, k],
            device_id={"mp": target},
            device_id_type=MESH,
        )

    def push(src, rel, k, target, sidx):
        c = copy(src, rel, k, target, sidx)
        c.start()
        sent.append(c)

    def arrive(rel, k):
        copy(buf.at[k, 0], rel, k, partner, 0).wait_recv()

    kept = []

    def keep(src, start, size, k, rel):
        c = pltpu.make_async_copy(src, full_ref.at[pl.ds(start, size), :], loc.at[k, rel])
        c.start()
        kept.append(c)

    def run(k, lo, hi):
        starts = []
        for rel in range(lo, hi):
            start = pl.multiple_of(owner(rel, core, bx, by) * R + k * rc, rc)
            keep(buf.at[k, rel], start, rc, k, rel)
            starts.append(start)
        body(
            False,
            lambda lo_=lo, hi_=hi: buf[k, lo_:hi_].reshape((hi_ - lo_) * rc, D),
            [pl.ds(s, rc) for s in starts],
            ins,
            outs,
        )

    for k in range(C):
        own = x_ref.at[pl.ds(k * rc, rc), :]
        push(own, 2, k, xn, 1)
        push(own, 4, k, yn, 2)
        push(own, 1, k, partner, 0)
    start = pl.multiple_of(me * R, R)
    keep(x_ref, start, R, 0, 0)
    body(True, lambda: x_ref[...], [pl.ds(start, R)], ins, outs)
    across = jnp.where(core == 0, xn, yn)
    for k in range(C + 2):
        if k < C:
            arrive(2, k)
            arrive(4, k)
            push(buf.at[k, 4 - 2 * core], 6, k, across, 3)
            push(buf.at[k, 2], 3, k, partner, 4)
            push(buf.at[k, 4], 5, k, partner, 5)
        if k == 0:
            starts = []
            other = owner(1, core, bx, by) * R
            for j in range(C):
                arrive(1, j)
                starts.append(pl.multiple_of(other + j * rc, rc))
                keep(buf.at[j, 1], starts[-1], rc, j, 1)
            body(
                False,
                lambda: buf[:, 1].reshape(R, D),
                [pl.ds(s, rc) for s in starts],
                ins,
                outs,
            )
        if 1 <= k <= C:
            arrive(3, k - 1)
            arrive(5, k - 1)
            run(k - 1, 2, 6)
            arrive(6, k - 1)
            push(buf.at[k - 1, 6], 7, k - 1, partner, 6)
        if k >= 2:
            arrive(7, k - 2)
            run(k - 2, 6, 8)
        if k >= 1:
            z.tick(-(-len(plan) // C))
    z.finish()
    for c in sent:
        c.wait_send()
    for c in kept:
        c.wait()


def gather_call(name, cid, x, ins, outs, body, z=None, C=4):
    R, D = x.shape
    vmem = pl.BlockSpec(memory_space=pltpu.VMEM)
    anywhere = pl.BlockSpec(memory_space=pl.ANY)
    srcs, z_out, more_scratch = z_parts(z)
    plan = tuple(z.plan) if z else ()
    out = pl.pallas_call(
        functools.partial(gather_kernel, C, len(ins), len(outs), body, plan, len(srcs)),
        out_shape=(jax.ShapeDtypeStruct((8 * R, D), x.dtype), *outs, *z_out),
        in_specs=[vmem] * (1 + len(ins)) + [anywhere] * len(srcs),
        out_specs=(anywhere,) + (vmem,) * (len(outs) + len(z_out)),
        scratch_shapes=[
            pltpu.VMEM((C, 8, R // C, D), x.dtype),
            pltpu.SemaphoreType.DMA((7, C)),
            pltpu.SemaphoreType.DMA((8, C)),
            pltpu.SemaphoreType.DMA((C, 8)),
            *more_scratch,
        ],
        compiler_params=pltpu.CompilerParams(
            collective_id=cid, has_side_effects=True, vmem_limit_bytes=60 << 20
        ),
        cost_estimate=cost(1 << 20),
        name=name,
    )(x, *ins, *srcs)
    if plan:
        z.done(out[-1])
        out = out[:-1]
    return out


def gather_only_kernel(C, n, *refs):
    xs, fulls = refs[:n], refs[n : 2 * n]
    send, recv, loc = refs[2 * n :]
    R, D = xs[0].shape
    rc = R // C
    me, core, bx, by, partner, xn, yn = peers()
    enter(partner, xn, yn)
    sent = []

    def copy(src, a, k, target, rel, sidx, whose):
        rows = pl.ds(pl.multiple_of(whose * R + k * rc, rc), rc)
        return pltpu.make_async_remote_copy(
            src_ref=fulls[a].at[rows, :] if src is None else src,
            dst_ref=fulls[a].at[rows, :],
            send_sem=send.at[a, sidx, k],
            recv_sem=recv.at[a, rel, k],
            device_id={"mp": target},
            device_id_type=MESH,
        )

    def push(*args):
        c = copy(*args)
        c.start()
        sent.append(c)

    def arrive(a, k, rel):
        copy(None, a, k, partner, rel, 0, owner(rel, core, bx, by)).wait_recv()

    kept = []
    for a in range(n):
        for k in range(C):
            own = xs[a].at[pl.ds(k * rc, rc), :]
            push(own, a, k, xn, 2, 1, me)
            push(own, a, k, yn, 4, 2, me)
            push(own, a, k, partner, 1, 0, me)
        c = pltpu.make_async_copy(
            xs[a], fulls[a].at[pl.ds(pl.multiple_of(me * R, R), R), :], loc.at[a]
        )
        c.start()
        kept.append(c)
    across = jnp.where(core == 0, xn, yn)
    x_core = owner(2, core, bx, by)
    y_core = owner(4, core, bx, by)
    through = jnp.where(core == 0, y_core, x_core)
    steps = [(a, k) for a in range(n) for k in range(C)]
    for i in range(len(steps) + 1):
        if i < len(steps):
            a, k = steps[i]
            arrive(a, k, 2)
            arrive(a, k, 4)
            push(None, a, k, across, 6, 3, through)
            push(None, a, k, partner, 3, 4, x_core)
            push(None, a, k, partner, 5, 5, y_core)
        if i >= 1:
            a, k = steps[i - 1]
            arrive(a, k, 6)
            push(None, a, k, partner, 7, 6, owner(6, core, bx, by))
    for a, k in steps:
        for rel in (1, 3, 5, 7):
            arrive(a, k, rel)
    for c in sent:
        c.wait_send()
    for c in kept:
        c.wait()


def gather_only(cid, *xs, C=4):
    R, D = xs[0].shape
    n = len(xs)
    anywhere = pl.BlockSpec(memory_space=pl.ANY)
    return pl.pallas_call(
        functools.partial(gather_only_kernel, C, n),
        out_shape=tuple(jax.ShapeDtypeStruct((8 * R, D), x.dtype) for x in xs),
        in_specs=[anywhere] * n,
        out_specs=(anywhere,) * n,
        scratch_shapes=[
            pltpu.SemaphoreType.DMA((n, 7, C)),
            pltpu.SemaphoreType.DMA((n, 8, C)),
            pltpu.SemaphoreType.DMA((n,)),
        ],
        compiler_params=pltpu.CompilerParams(collective_id=cid, has_side_effects=True),
        cost_estimate=cost(1 << 20),
        name="gather_rows",
    )(*xs)


def tiles(n, step, f):
    step = min(step, n)

    @pl.loop(0, n // step)
    def _(j):
        f(pl.ds(pl.multiple_of(j * step, step), step))


def put(ref, pieces, cols, value):
    at = 0
    for rows in pieces:
        ref[rows, cols] = value[at : at + rows.size]
        at += rows.size


def take(ref, pieces, cols):
    parts = [ref[rows, cols] for rows in pieces]
    return parts[0] if len(parts) == 1 else jnp.concatenate(parts, axis=0)


def project_body(first, lhs, pieces, ins, outs):
    w, shift = ins

    def f(cols):
        put(outs[0], pieces, cols, (nn(lhs(), w[:, cols]) + shift[:, cols]).astype(jnp.bfloat16))

    tiles(w.shape[1], 256, f)


def gelu_both(v):
    t = jnp.tanh(0.7978845608028654 * (v + 0.044715 * v * v * v))
    d = 0.5 * (1.0 + t) + 0.5 * v * (1.0 - t * t) * (
        0.7978845608028654 * (1.0 + 3 * 0.044715 * v * v)
    )
    return (0.5 * v * (1.0 + t)).astype(jnp.bfloat16), d.astype(jnp.bfloat16)


def up_body(first, lhs, pieces, ins, outs):
    w, shift = ins

    def f(cols):
        active, slope = gelu_both(nn(lhs(), w[:, cols]) + shift[:, cols])
        put(outs[0], pieces, cols, active)
        put(outs[1], pieces, cols, slope)

    tiles(w.shape[1], 256, f)


def wide_nt(src, w, cols):
    Z, _, d = w.shape
    total = None
    for z in range(Z):
        t = nt(src[:, z * d : (z + 1) * d], w[z, cols, :])
        total = t if total is None else total + t
    return total


def down_back_body(first, lhs, pieces, ins, outs):
    w, slope = ins

    def f(cols):
        g = wide_nt(lhs(), w, cols) * take(slope, pieces, cols).astype(jnp.float32)
        g = g.astype(jnp.bfloat16)
        put(outs[0], pieces, cols, g)
        sums = jnp.sum(g.astype(jnp.float32), axis=0, keepdims=True)
        if first:
            outs[1][:, cols] = sums
        else:
            outs[1][:, cols] += sums

    tiles(w.shape[1], 256, f)


def down_back_kernel(g_ref, w_ref, slope_ref, out_ref, sum_ref):
    def f(cols):
        g = wide_nt(g_ref[...], w_ref, cols) * slope_ref[:, cols].astype(jnp.float32)
        g = g.astype(jnp.bfloat16)
        out_ref[:, cols] = g
        sums = jnp.sum(g.astype(jnp.float32), axis=0, keepdims=True)

        @pl.when(pl.program_id(0) == 0)
        def _():
            sum_ref[:, cols] = sums

        @pl.when(pl.program_id(0) > 0)
        def _():
            sum_ref[:, cols] += sums

    tiles(w_ref.shape[1], 256, f)


def down_back_here(grad, w, slope):
    T, F = slope.shape
    D = grad.shape[1]
    return pl.pallas_call(
        down_back_kernel,
        grid=(T // BLOCK,),
        out_shape=(
            jax.ShapeDtypeStruct((T, F), jnp.bfloat16),
            jax.ShapeDtypeStruct((1, F), jnp.float32),
        ),
        in_specs=[
            pl.BlockSpec((BLOCK, D), lambda i: (i, 0)),
            pl.BlockSpec(w.shape, lambda i: (0, 0, 0)),
            pl.BlockSpec((BLOCK, F), lambda i: (i, 0)),
        ],
        out_specs=(pl.BlockSpec((BLOCK, F), lambda i: (i, 0)), pl.BlockSpec((1, F), lambda i: (0, 0))),
        compiler_params=pltpu.CompilerParams(vmem_limit_bytes=40 << 20),
        cost_estimate=cost(1 << 20),
        name="down_back",
    )(grad, w, slope)


def dense_back_body(first, lhs, pieces, ins, outs):
    (w,) = ins

    def f(cols):
        put(outs[0], pieces, cols, wide_nt(lhs(), w, cols).astype(jnp.bfloat16))

    tiles(w.shape[1], 256, f)


def scatter_kernel(C, n_in, n_more, n_more_out, body, filler, plan, n_src, n_scratch, *refs):
    ins, more = refs[:n_in], refs[n_in : n_in + n_more]
    srcs, rest = refs[n_in + n_more :][:n_src], refs[n_in + n_more + n_src :]
    out_ref, more_out, rest = rest[0], rest[1 : 1 + n_more_out], rest[1 + n_more_out :]
    z_out, rest = (rest[:1], rest[1:]) if plan else ((), rest)
    pbuf, rbuf, send, recv = rest[:4]
    scratch = rest[4 : 4 + n_scratch]
    z = z_task(plan, srcs, z_out, rest[4 + n_scratch :])
    R, D = out_ref.shape
    rc = R // C
    me, core, bx, by, partner, xn, yn = peers()
    steps = filler(ins, more, more_out, scratch) if filler else []
    enter(partner, xn, yn, bool(plan))
    z.start()
    dn = jnp.where(core == 0, yn, xn)
    fn = jnp.where(core == 0, xn, yn)
    sent = []

    def fill(n):
        for _ in range(min(n, len(steps))):
            steps.pop(0)()
            z.tick()

    def copy(src, slot, k, target):
        rows = pl.ds(k * rc, rc)
        return pltpu.make_async_remote_copy(
            src_ref=src.at[rows, :],
            dst_ref=rbuf.at[slot, rows, :],
            send_sem=send.at[slot, k],
            recv_sem=recv.at[slot, k],
            device_id={"mp": target},
            device_id_type=MESH,
        )

    def push(slot, to, target, k):
        c = copy(pbuf.at[slot], to, k, target)
        c.start()
        sent.append(c)

    def arrive(slot, k):
        copy(pbuf.at[0], slot, k, partner).wait_recv()

    def dest_rank(which, c):
        if which == 0:
            return (1 - by) * 4 + (1 - bx) * 2 + c
        if which == 3:
            return by * 4 + bx * 2 + c
        flip_y = (1 - c) if which == 1 else c
        y = by + flip_y * (1 - 2 * by)
        x = bx + (1 - flip_y) * (1 - 2 * bx)
        return y * 4 + x * 2 + c

    def compute(which, c, slot):
        rows = pl.ds(pl.multiple_of(dest_rank(which, c) * R, R), R)
        body(rows, ins, pbuf.at[slot])

    def theirs(which):
        compute(which, 1 - core, which)
        for k in range(C):
            push(which, which, partner, k)

    def add(slot, rslot, k):
        @pl.loop(0, rc // 16)
        def _(i):
            rows = pl.ds(pl.multiple_of(k * rc + i * 16, 16), 16)
            pbuf[slot, rows, :] = (
                pbuf[slot, rows, :].astype(jnp.float32) + rbuf[rslot, rows, :].astype(jnp.float32)
            ).astype(pbuf.dtype)

    def join(which):
        for k in range(C):
            arrive(which, k)
            add(4 + which, which, k)
            if which < 2:
                push(4 + which, 4 + which, dn, k)

    theirs(0)
    compute(0, core, 4)
    theirs(1)
    join(0)
    compute(1, core, 5)
    theirs(2)
    join(1)
    z.tick()
    compute(2, core, 6)
    theirs(3)
    join(2)
    z.tick()
    compute(3, core, 7)
    join(3)
    z.tick()
    fill(2)
    for k in range(C):
        arrive(4, k)
        add(6, 4, k)
        push(6, 6, fn, k)
        z.tick()
        fill(2)
    fill(len(steps))
    for k in range(C):
        arrive(5, k)
        arrive(6, k)

        @pl.loop(0, rc // 16)
        def _(i):
            rows = pl.ds(pl.multiple_of(k * rc + i * 16, 16), 16)
            out_ref[rows, :] = (
                pbuf[7, rows, :].astype(jnp.float32)
                + rbuf[5, rows, :].astype(jnp.float32)
                + rbuf[6, rows, :].astype(jnp.float32)
            )
    z.finish()
    for c in sent:
        c.wait_send()


def scatter_call(
    name, cid, T, D, ins, body, more=(), more_out=(), scratch=(), filler=None, z=None, C=4
):
    R = T // 8
    vmem = pl.BlockSpec(memory_space=pltpu.VMEM)
    anywhere = pl.BlockSpec(memory_space=pl.ANY)
    srcs, z_out, more_scratch = z_parts(z)
    plan = tuple(z.plan) if z else ()
    out = pl.pallas_call(
        functools.partial(
            scatter_kernel,
            C,
            len(ins),
            len(more),
            len(more_out),
            body,
            filler,
            plan,
            len(srcs),
            len(scratch),
        ),
        out_shape=(jax.ShapeDtypeStruct((R, D), jnp.float32), *more_out, *z_out),
        in_specs=[vmem] * len(ins) + [anywhere] * (len(more) + len(srcs)),
        out_specs=(vmem,) + (anywhere,) * len(more_out) + (vmem,) * len(z_out),
        scratch_shapes=[
            pltpu.VMEM((8, R, D), jnp.bfloat16),
            pltpu.VMEM((7, R, D), jnp.bfloat16),
            pltpu.SemaphoreType.DMA((7, C)),
            pltpu.SemaphoreType.DMA((7, C)),
            *scratch,
            *more_scratch,
        ],
        compiler_params=pltpu.CompilerParams(
            collective_id=cid, has_side_effects=True, vmem_limit_bytes=60 << 20
        ),
        cost_estimate=cost(1 << 20),
        name=name,
    )(*ins, *more, *srcs)
    if plan:
        z.done(out[-1])
        out = out[:-1]
    return out if more_out else out[0]


def row_split_body(rows, ins, out):
    a, w = ins
    Z, _, d = w.shape
    for z in range(Z):
        out[:, z * d : (z + 1) * d] = nn(a[rows, :], w[z]).astype(out.dtype)


def up_back_body(rows, ins, out):
    a, w = ins

    def f(cols):
        out[:, cols] = nt(a[rows, :], w[cols, :]).astype(out.dtype)

    tiles(w.shape[0], 512, f)


def project_back_body(rows, ins, out):
    a, w = ins
    S, _, width = a.shape

    def f(cols):
        total = None
        for s in range(S):
            t = nt(a[s, rows, :], w[cols, s * width : (s + 1) * width])
            total = t if total is None else total + t
        out[:, cols] = total.astype(out.dtype)

    tiles(w.shape[0], 512, f)


class Stream:
    def __init__(self, chunks, buf, sems, stage, out_sems):
        self.chunks, self.buf, self.sems = chunks, buf, sems
        self.stage, self.out_sems = stage, out_sems
        self.turn, self.flying = 0, [[], []]

    def fetch(self, i):
        src, j = self.chunks[i]
        w = self.buf.shape[2]
        return pltpu.make_async_copy(
            src.at[:, pl.ds(j * w, w)], self.buf.at[i % 2], self.sems.at[i % 2]
        )

    def get(self, i):
        self.fetch(i).wait()
        if i + 1 < len(self.chunks):
            self.fetch(i + 1).start()
        return self.buf.at[i % 2]

    def result(self, make, targets):
        slot = self.turn % 2
        self.turn += 1
        for c in self.flying[slot]:
            c.wait()
        make(self.stage.at[slot])
        self.flying[slot] = []
        for n, (lo, width, dest) in enumerate(targets):
            c = pltpu.make_async_copy(
                self.stage.at[slot, :, pl.ds(lo, width)], dest, self.out_sems.at[slot, n]
            )
            c.start()
            self.flying[slot].append(c)

    def drain(self):
        for slot in range(2):
            for c in self.flying[slot]:
                c.wait()


STREAM_SCRATCH = (
    pltpu.VMEM((2, 2048, 256), jnp.bfloat16),
    pltpu.SemaphoreType.DMA((2,)),
    pltpu.VMEM((2, 256, 1024), jnp.bfloat16),
    pltpu.SemaphoreType.DMA((2, 4)),
    pltpu.VMEM((256, 2048), jnp.bfloat16),
)


def ffn_filler(ins, more, more_out, scratch):
    hidden = ins[0]
    active, normed, grad = more
    (out,) = more_out
    buf, sems, stage, out_sems, turned, held, held_sem = scratch
    T, F = hidden.shape
    D = grad.shape[1]
    Z, _, d = out.shape
    w = buf.shape[2]
    half = stage.shape[2]
    stream = Stream(
        [(active, j) for j in range(F // w)] + [(normed, j) for j in range(D // w)],
        buf,
        sems,
        stage,
        out_sems,
    )
    held_copy = pltpu.make_async_copy(grad, held, held_sem)
    stream.fetch(0).start()
    held_copy.start()

    def product(right, lo):
        def make(tile):
            def f(cols):
                at = pl.ds(pl.multiple_of(lo + cols.start, 256), cols.size)
                tile[:, cols] = nn(turned[...], right[:, at]).astype(tile.dtype)

            tiles(half, 256, f)

        return make

    steps = []

    def down(j, h):
        def step():
            if h == 0:
                turned[...] = stream.get(j)[...].T
            if j == 0 and h == 0:
                held_copy.wait()
            targets = [
                (b * d, d, out.at[h * (half // d) + b, pl.ds(j * w, w), :]) for b in range(half // d)
            ]
            stream.result(product(held, h * half), targets)

        return step

    def up(j):
        def step():
            turned[...] = stream.get(F // w + j)[...].T
            z, r = (j * w) // d, (j * w) % d
            targets = [(b * d, d, out.at[z, pl.ds(F + b * d + r, w), :]) for b in range(F // d)]
            stream.result(product(hidden, 0), targets)

        return step

    for j in range(F // w):
        for h in range(D // half):
            steps.append(down(j, h))
    for j in range(D // w):
        steps.append(up(j))
    steps.append(stream.drain)
    return steps


def attn_filler(ins, more, more_out, scratch):
    parts = ins[0]
    context, grad, normed = more
    (out,) = more_out
    buf, sems, stage, out_sems, turned, ctx_t = scratch
    S, T, width = parts.shape
    D = grad.shape[1]
    Z = out.shape[0]
    d = D // Z
    w = buf.shape[2]
    n = D // w
    stream = Stream(
        [(context, 0)] + [(grad, j) for j in range(n)] + [(normed, j) for j in range(n)],
        buf,
        sems,
        stage,
        out_sems,
    )
    stream.fetch(0).start()
    steps = []

    def dense(j):
        def step():
            if j == 0:
                ctx_t[...] = stream.get(0)[...].T
            right = stream.get(1 + j)

            def make(tile):
                tile[:, :w] = nn(ctx_t[...], right[...]).astype(tile.dtype)

            z, r = (j * w) // d, (j * w) % d
            stream.result(make, [(0, w, out.at[z, pl.ds(0, width), pl.ds(r, w)])])

        return step

    def project(j):
        def step():
            turned[...] = stream.get(1 + n + j)[...].T

            def make(tile):
                for s in range(S):
                    tile[:, s * width : (s + 1) * width] = nn(turned[...], parts[s]).astype(
                        tile.dtype
                    )

            z, r = (j * w) // d, (j * w) % d
            side = pl.ds(r // w * width, width)
            stream.result(
                make,
                [(s * width, width, out.at[z, pl.ds(width + s * w, w), side]) for s in range(S)],
            )

        return step

    for j in range(n):
        steps.append(dense(j))
    for j in range(n):
        steps.append(project(j))
    steps.append(stream.drain)
    return steps


def finish_kernel(plan, n_src, v_ref, u_ref, *refs):
    srcs, refs = refs[:n_src], refs[n_src:]
    v_out, u_out, refs = refs[0], refs[1], refs[2:]
    z_out, refs = (refs[:1], refs[1:]) if plan else ((), refs)
    vs, us, v_in, u_in, send, recv = refs[:6]
    me, core, bx, by, partner, xn, yn = peers()
    z = z_task(plan, srcs, z_out, refs[6:])
    _, z1, z2, _ = z_peers()
    enter(partner, xn, yn, True)
    z.start()
    hops = (({"mp": partner}, False), ({"mp": xn}, False), ({"mp": yn}, False))
    hops += (({"dp": z1}, True), ({"dp": z2}, True))
    vs[0] = v_ref[...]
    us[3] = u_ref[...]
    z.tick()
    for i, (target, both) in enumerate(hops):
        copies = []
        for n, (src, dst) in enumerate(((vs, v_in), (us, u_in))[: 2 if both else 1]):
            c = pltpu.make_async_remote_copy(
                src_ref=src.at[i],
                dst_ref=dst.at[i],
                send_sem=send.at[n, i],
                recv_sem=recv.at[n, i],
                device_id=target,
                device_id_type=MESH,
            )
            c.start()
            copies.append(c)
        z.tick()
        for c in copies:
            c.wait()
        vs[i + 1] = vs[i] + v_in[i]
        if both:
            us[i + 1] = us[i] + u_in[i]
    v_out[...] = vs[5]
    u_out[...] = us[5]
    z.finish()


def finish_call(cid, v, u, z):
    vmem = pl.BlockSpec(memory_space=pltpu.VMEM)
    anywhere = pl.BlockSpec(memory_space=pl.ANY)
    srcs, z_out, more_scratch = z_parts(z)
    plan = tuple(z.plan)
    out = pl.pallas_call(
        functools.partial(finish_kernel, plan, len(srcs)),
        out_shape=(
            jax.ShapeDtypeStruct(v.shape, v.dtype),
            jax.ShapeDtypeStruct(u.shape, u.dtype),
            *z_out,
        ),
        in_specs=[vmem, vmem] + [anywhere] * len(srcs),
        out_specs=(vmem, vmem) + (vmem,) * len(z_out),
        scratch_shapes=[
            pltpu.VMEM((6, *v.shape), v.dtype),
            pltpu.VMEM((6, *u.shape), u.dtype),
            pltpu.VMEM((5, *v.shape), v.dtype),
            pltpu.VMEM((5, *u.shape), u.dtype),
            pltpu.SemaphoreType.DMA((2, 5)),
            pltpu.SemaphoreType.DMA((2, 5)),
            *more_scratch,
        ],
        compiler_params=pltpu.CompilerParams(
            collective_id=cid, has_side_effects=True, vmem_limit_bytes=60 << 20
        ),
        cost_estimate=cost(1 << 20),
        name="finish",
    )(v, u, *srcs)
    if plan:
        z.done(out[2])
    return out[0], out[1]


def layer_norm(values, scale_row, shift_row):
    centre = jnp.mean(values, axis=-1, keepdims=True)
    centred = values - centre
    spread = jnp.mean(centred * centred, axis=-1, keepdims=True)
    return centred * lax.rsqrt(spread + norm_eps) * scale_row + shift_row


def gather_sum(part):
    return lax.psum_scatter(
        part.astype(jnp.bfloat16), "mp", scatter_dimension=0, tiled=True
    ).astype(jnp.float32)


def gather_all(x):
    return lax.all_gather(x, "mp", axis=0, tiled=True)


def side_by_side(w):
    return jnp.concatenate([w[z] for z in range(w.shape[0])], axis=1)


def reduce_dp(part):
    return lax.psum_scatter(part.astype(jnp.bfloat16), "dp", scatter_dimension=0)


class Work:
    def __init__(self, backlog, limit):
        self.plan, self.arrays, self.pieces = [], [], []
        while limit and backlog.queue:
            entry = backlog.queue[0]
            key, array, row = entry
            if not any(a is array for a in self.arrays):
                self.arrays.append(array)
            i = [a is array for a in self.arrays].index(True)
            self.pieces.append((key, len(self.plan)))
            self.plan.append((i, row))
            limit -= 1
            entry[2] += ZR
            if entry[2] == array.shape[1]:
                backlog.queue.pop(0)
        self.backlog = backlog

    def done(self, result):
        for key, n in self.pieces:
            self.backlog.sums.setdefault(key, []).append(result[n * ZR : (n + 1) * ZR])


class Backlog:
    def __init__(self):
        self.queue, self.sums = [], {}

    def add(self, key, array):
        self.queue.append([key, array, 0])

    def take(self, limit):
        return Work(self, limit)

    def total(self, key):
        return jnp.concatenate(self.sums[key], axis=0)


class Fast:
    def __init__(self, T, D):
        self.T, self.D = T, D
        self.backlog = Backlog()

    def project(self, l, normed, w, shift, out_grad):
        T = self.T
        out = jax.ShapeDtypeStruct((T, w.shape[1]), jnp.bfloat16)
        if l == 0:
            full, self.last_grad = gather_only(0, normed, out_grad)
            return full, (nn(full, w) + shift).astype(jnp.bfloat16)
        return gather_call("gather_project", 10 * l, normed, (w, shift[None]), (out,), project_body)

    def dense(self, l, context, w):
        return scatter_call("dense_scatter", 10 * l + 1, self.T, self.D, (context, w), row_split_body)

    def up(self, l, normed, w, shift):
        out = jax.ShapeDtypeStruct((self.T, w.shape[1]), jnp.bfloat16)
        return gather_call("gather_up", 10 * l + 2, normed, (w, shift[None]), (out, out), up_body)

    def down(self, l, last, active, w):
        z = self.backlog.take(5) if last else None
        return scatter_call(
            "down_scatter", 10 * l + 3, self.T, self.D, (active, w), row_split_body, z=z
        )

    def down_back(self, l, last, grad, w, slope):
        if last:
            return self.last_grad, *down_back_here(self.last_grad, w, slope)
        F = slope.shape[1]
        outs = (
            jax.ShapeDtypeStruct((self.T, F), jnp.bfloat16),
            jax.ShapeDtypeStruct((1, F), jnp.float32),
        )
        z = self.backlog.take(5)
        return gather_call("gather_down_back", 10 * l + 4, grad, (w, slope), outs, down_back_body, z)

    def up_back(self, l, grad_hidden, w, active, normed, grad_down):
        T, F = grad_hidden.shape
        Z = lax.axis_size("dp")
        packed = jax.ShapeDtypeStruct((Z, 2 * F, self.D // Z), jnp.bfloat16)
        z = None if l else self.backlog.take(6)
        grad, packed = scatter_call(
            "up_back_scatter",
            10 * l + 5,
            T,
            self.D,
            (grad_hidden, w),
            up_back_body,
            more=(active, normed, grad_down),
            more_out=(packed,),
            scratch=STREAM_SCRATCH
            + (pltpu.VMEM((T, self.D), jnp.bfloat16), pltpu.SemaphoreType.DMA),
            filler=ffn_filler,
            z=z,
        )
        self.backlog.add(("ffn", l), packed)
        return grad

    def ffn_grads(self, l):
        summed = self.backlog.total(("ffn", l))
        d = summed.shape[1]
        F = summed.shape[0] // 2
        up = jnp.concatenate([summed[F + b * d : F + (b + 1) * d] for b in range(F // d)], axis=1)
        return up, summed[:F]

    def dense_back(self, l, grad, w):
        out = jax.ShapeDtypeStruct((self.T, w.shape[1]), jnp.bfloat16)
        z = self.backlog.take(4)
        return gather_call("gather_dense_back", 10 * l + 6, grad, (w,), (out,), dense_back_body, z)

    def project_back(self, l, grad_project, w, context, grad_branch, normed):
        S, T, width = grad_project.shape
        Z = lax.axis_size("dp")
        packed = jax.ShapeDtypeStruct((Z, (S + 1) * width, self.D // Z), jnp.bfloat16)
        grad, packed = scatter_call(
            "project_back_scatter",
            10 * l + 7,
            T,
            self.D,
            (grad_project, w),
            project_back_body,
            more=(context, grad_branch, normed),
            more_out=(packed,),
            scratch=STREAM_SCRATCH + (pltpu.VMEM((width, T), jnp.bfloat16),),
            filler=attn_filler,
            z=self.backlog.take(5),
        )
        self.backlog.add(("attn", l), packed)
        return grad

    def attn_grads(self, l):
        summed = self.backlog.total(("attn", l))
        w = summed.shape[1] // 2
        parts = [summed[(1 + s) * w : (2 + s) * w] for s in range(3)]
        parts = [jnp.concatenate([p[:, :w], p[:, w:]], axis=0) for p in parts]
        return jnp.stack(parts, axis=1), summed[:w]

    def finish(self, copied, split):
        rows = copied.shape[0] * copied.shape[1]
        v = jnp.concatenate([copied.reshape(rows, -1), jnp.zeros((-rows % 8, self.D), jnp.float32)])
        v, u = finish_call(9, v, split.reshape(8, -1), self.backlog.take(1000))
        return v[:rows].reshape(copied.shape), u.reshape(split.shape)


class Plain:
    def __init__(self, T, D):
        self.T, self.D = T, D
        self.ffn, self.attn = {}, {}

    def project(self, l, normed, w, shift, out_grad):
        full = gather_all(normed)
        return full, (nn(full, w) + shift).astype(jnp.bfloat16)

    def dense(self, l, context, w):
        return gather_sum(nn(context, side_by_side(w)))

    def up(self, l, normed, w, shift):
        full = gather_all(normed)
        return full, *gelu_both(nn(full, w) + shift)

    def down(self, l, last, active, w):
        return self.dense(l, active, w)

    def down_back(self, l, last, grad, w, slope):
        full = gather_all(grad)
        g = (nt(full, side_by_side(w)) * slope.astype(jnp.float32)).astype(jnp.bfloat16)
        return full, g, jnp.sum(g.astype(jnp.float32), axis=0, keepdims=True)

    def up_back(self, l, grad_hidden, w, active, normed, grad_down):
        Z = lax.axis_size("dp")
        F = grad_hidden.shape[1]
        d = self.D // Z
        up = jnp.einsum("td,tf->df", normed, grad_hidden, preferred_element_type=jnp.float32)
        down = jnp.einsum(
            "tf,tzd->zfd", active, grad_down.reshape(-1, Z, d), preferred_element_type=jnp.float32
        )
        packed = jnp.concatenate([down, up.reshape(Z, d * F // d, d)], axis=1)
        self.ffn[l] = reduce_dp(packed).astype(jnp.float32)
        return gather_sum(nt(grad_hidden, w))

    def ffn_grads(self, l):
        summed = self.ffn[l]
        d = summed.shape[1]
        F = summed.shape[0] // 2
        return summed[F:].reshape(d, F), summed[:F]

    def dense_back(self, l, grad, w):
        full = gather_all(grad)
        return full, nt(full, side_by_side(w)).astype(jnp.bfloat16)

    def project_back(self, l, grad_project, w, context, grad_branch, normed):
        S, T, width = grad_project.shape
        Z = lax.axis_size("dp")
        d = self.D // Z
        dense = jnp.einsum(
            "ti,tzd->zid", context, grad_branch.reshape(T, Z, d), preferred_element_type=jnp.float32
        )
        project = jnp.einsum(
            "td,sti->dsi", normed, grad_project, preferred_element_type=jnp.float32
        )
        packed = jnp.concatenate(
            [dense.reshape(Z, -1), project.reshape(Z, -1)], axis=1
        ).reshape(Z, -1, width)
        part = sum(nt(grad_project[s], w[:, s * width : (s + 1) * width]) for s in range(S))
        self.attn[l] = reduce_dp(packed).astype(jnp.float32)
        return gather_sum(part)

    def attn_grads(self, l):
        d = self.D // lax.axis_size("dp")
        rows, width = self.attn[l].shape
        flat = self.attn[l].reshape(-1)
        return flat[width * d :].reshape(d, 3, width), flat[: width * d].reshape(width, d)

    def finish(self, copied, split):
        return lax.psum(copied, ("dp", "mp")), lax.psum(split, "dp")


def shards(
    inputs,
    out_grad,
    project_weight,
    dense_weight,
    up_weight,
    down_weight,
    project_bias,
    up_bias,
    norm_gain,
    norm_bias,
    output_bias,
):
    tensor_size = lax.axis_size("mp")
    tensor_rank = lax.axis_index("mp")
    row_count, model_width = inputs.shape
    total_rows = row_count * tensor_size
    inner_width = project_weight.shape[3]
    heads_here = N_HEADS // tensor_size
    layer_count = project_weight.shape[0]
    slopes = 2.0 ** (
        -8.0
        * (tensor_rank * heads_here + lax.iota(jnp.int32, heads_here) + 1).astype(jnp.float32)
        / N_HEADS
    )
    low = jnp.bfloat16
    fast = tensor_size == 8 and lax.axis_size("dp") == 4 and row_count == 256
    ops = (Fast if fast else Plain)(total_rows, model_width)
    gathered = []
    for l in range(layer_count):
        gathered.append(
            (
                lax.all_gather(
                    project_weight[l].reshape(-1, 3 * inner_width).astype(low),
                    "dp",
                    axis=0,
                    tiled=True,
                ),
                lax.all_gather(dense_weight[l].astype(low), "dp", axis=0),
                lax.all_gather(up_weight[l].astype(low), "dp", axis=0, tiled=True),
                lax.all_gather(down_weight[l].astype(low), "dp", axis=0),
            )
        )
    stream = inputs.astype(jnp.float32)
    stored = []
    for l in range(layer_count):
        w_project, w_dense, w_up, w_down = gathered[l]
        normed = layer_norm(stream, norm_gain[l, 0], norm_bias[l, 0]).astype(low)
        shift = jnp.concatenate(
            [project_bias[l, 0], jnp.zeros((inner_width,), jnp.float32), project_bias[l, 1]]
        )
        normed_all, project = ops.project(l, normed, w_project, shift, out_grad)
        context, log_norms = attend_fwd(project, slopes)
        middle = stream + ops.dense(l, context, w_dense) + output_bias[l, 0]
        normed2 = layer_norm(middle, norm_gain[l, 1], norm_bias[l, 1]).astype(low)
        normed2_all, active, slope = ops.up(l, normed2, w_up, up_bias[l])
        stored.append(
            (stream, normed_all, project, log_norms, context, middle, normed2_all, active, slope)
        )
        if l < layer_count - 1:
            stream = middle + ops.down(l, False, active, w_down) + output_bias[l, 1]
    grad = out_grad.astype(jnp.float32)
    copied = [None] * layer_count
    split = [None] * layer_count
    for l in reversed(range(layer_count)):
        last = l == layer_count - 1
        w_project, w_dense, w_up, w_down = gathered[l]
        stream_in, normed_all, project, log_norms, context, middle, normed2_all, active, slope = (
            stored[l]
        )
        down_bias_grad = jnp.sum(grad, axis=0)
        grad_down, grad_hidden, up_bias_part = ops.down_back(l, last, grad.astype(low), w_down, slope)
        grad_normed2 = ops.up_back(l, grad_hidden, w_up, active, normed2_all, grad_down)
        if last:
            rows_out = middle + ops.down(l, True, active, w_down) + output_bias[l, 1]
            outputs = rows_out.astype(low)
        norm_back = jax.vjp(layer_norm, middle, norm_gain[l, 1], norm_bias[l, 1])[1]
        grad_from_norm, gain_second, shift_second = norm_back(grad_normed2)
        grad_middle = grad + grad_from_norm
        dense_bias_grad = jnp.sum(grad_middle, axis=0)
        grad_branch, grad_context = ops.dense_back(l, grad_middle.astype(low), w_dense)
        grad_project, project_bias_part = attend_bwd(
            project, grad_context, context, log_norms, slopes
        )
        grad_normed = ops.project_back(
            l, grad_project, w_project, context, grad_branch, normed_all
        )
        norm_back = jax.vjp(layer_norm, stream_in, norm_gain[l, 0], norm_bias[l, 0])[1]
        grad_from_norm, gain_first, shift_first = norm_back(grad_normed)
        grad = grad_middle + grad_from_norm
        copied[l] = jnp.stack(
            [gain_first, gain_second, shift_first, shift_second, dense_bias_grad, down_bias_grad]
        )
        split[l] = jnp.concatenate([project_bias_part.reshape(-1), up_bias_part.reshape(-1)])
    copied, split = ops.finish(jnp.stack(copied), jnp.stack(split))
    matrix_grads = [(*ops.attn_grads(l), *ops.ffn_grads(l)) for l in range(layer_count)]
    return (
        outputs,
        grad,
        *(jnp.stack(parts) for parts in zip(*matrix_grads)),
        split[:, : 2 * inner_width].reshape(layer_count, 2, inner_width),
        split[:, 2 * inner_width :],
        copied[:, 0:2],
        copied[:, 2:4],
        copied[:, 4:6],
    )


def solution(mesh):
    rows = P(("dp", "mp"), None)
    specs = (P(None, "dp", None, "mp"), P(None, "mp", "dp"), P(None, "dp", "mp"), P(None, "mp", "dp"))
    biases = (P(None, None, "mp"), P(None, "mp"), P(), P(), P())
    return jax.shard_map(
        shards,
        mesh=mesh,
        in_specs=(rows, rows, *specs, *biases),
        out_specs=(rows, rows, *specs, *biases),
        check_vma=False,
    )
```

```python
import functools

import jax
import jax.numpy as jnp
from jax import lax
from jax.experimental import pallas as pl
from jax.experimental.pallas import tpu as pltpu
from jax.sharding import PartitionSpec as P

N_HEADS = 16
BLOCK = 256
HEAD = 128
LOG2E = 1.4426950408889634
MESH = pl.DeviceIdType.MESH
NT_DIMS = (((1,), (1,)), ((), ()))
norm_eps = 1e-05


def nt(a, b):
    return lax.dot_general(a, b, NT_DIMS, preferred_element_type=jnp.float32)


def nn(a, b):
    return jnp.dot(a, b, preferred_element_type=jnp.float32)


def layer_norm(values, scale_row, shift_row):
    centre = jnp.mean(values, axis=-1, keepdims=True)
    centred = values - centre
    spread = jnp.mean(centred * centred, axis=-1, keepdims=True)
    return centred * lax.rsqrt(spread + norm_eps) * scale_row + shift_row


def peers():
    me = lax.axis_index("mp")
    core = me % 2
    bx = (me // 2) % 2
    by = me // 4
    return me, core, bx, by, me + 1 - 2 * core, me + 2 - 4 * bx, me + 4 - 8 * by


def owner(rel, core, bx, by):
    c = core if rel % 2 == 0 else 1 - core
    x = bx if (rel // 2) % 2 == 0 else 1 - bx
    y = by if rel // 4 == 0 else 1 - by
    return y * 4 + x * 2 + c


def z_peers():
    z = lax.axis_index("dp")
    z1 = z + 1 - 2 * (z % 2)
    return z, z1, (z + 2) % 4, (z1 + 2) % 4


def enter(partner, xn, yn, z=False):
    barrier = pltpu.get_barrier_semaphore()
    for n in (partner, xn, yn):
        pl.semaphore_signal(barrier, inc=1, device_id={"mp": n}, device_id_type=MESH)
    if z:
        _, z1, z2, _ = z_peers()
        for n in (z1, z2):
            pl.semaphore_signal(barrier, inc=1, device_id={"dp": n}, device_id_type=MESH)
    pl.semaphore_wait(barrier, 5 if z else 3)


ZR = 128


class ZSum:
    ahead = 3

    def __init__(self, plan, srcs, out, scratch):
        self.plan, self.srcs, self.out = plan, srcs, out[0]
        self.recv, self.own, self.send_sem, self.recv_sem, self.loc = scratch
        self.z, self.z1, self.z2, self.z3 = z_peers()
        self.sent = []
        self.events = [functools.partial(self.event, c) for c in range(len(plan))]

    def block(self, c, z):
        i, row = self.plan[c]
        return self.srcs[i].at[z, pl.ds(row, ZR), :]

    def remote(self, src, kind, c, target):
        return pltpu.make_async_remote_copy(
            src_ref=src,
            dst_ref=self.recv.at[kind, c],
            send_sem=self.send_sem.at[kind, c],
            recv_sem=self.recv_sem.at[kind, c],
            device_id={"dp": target},
            device_id_type=MESH,
        )

    def push(self, *args):
        c = self.remote(*args)
        c.start()
        self.sent.append(c)

    def here(self, kind, c):
        return pltpu.make_async_copy(
            self.block(c, self.z2 if kind else self.z), self.own.at[kind, c], self.loc.at[kind, c]
        )

    def arrive(self, kind, c):
        self.remote(self.own.at[0, c], kind, c, self.z1).wait_recv()

    def start(self):
        for c in range(min(self.ahead, len(self.plan))):
            self.push(self.block(c, self.z3), 1, c, self.z1)
        for c in range(len(self.plan)):
            self.here(1, c).start()
            self.here(0, c).start()

    def event(self, c):
        if c + self.ahead < len(self.plan):
            n = c + self.ahead
            self.push(self.block(n, self.z3), 1, n, self.z1)
        self.arrive(1, c)
        self.here(1, c).wait()

        @pl.loop(0, ZR // 16)
        def _(i):
            rows = pl.ds(pl.multiple_of(i * 16, 16), 16)
            self.own[1, c, rows, :] = (
                self.own[1, c, rows, :].astype(jnp.float32)
                + self.recv[1, c, rows, :].astype(jnp.float32)
            ).astype(jnp.bfloat16)

        self.push(self.own.at[1, c], 2, c, self.z2)
        self.push(self.block(c, self.z1), 0, c, self.z1)

    def tick(self, n=1):
        for _ in range(min(n, len(self.events))):
            self.events.pop(0)()

    def finish(self):
        self.tick(len(self.events))
        for c in range(len(self.plan)):
            self.here(0, c).wait()
            self.arrive(0, c)
            self.arrive(2, c)

            @pl.loop(0, ZR // 16)
            def _(i):
                rows = pl.ds(pl.multiple_of(i * 16, 16), 16)
                to = pl.ds(pl.multiple_of(c * ZR + i * 16, 16), 16)
                self.out[to, :] = (
                    self.own[0, c, rows, :].astype(jnp.float32)
                    + self.recv[0, c, rows, :].astype(jnp.float32)
                    + self.recv[2, c, rows, :].astype(jnp.float32)
                ).astype(jnp.bfloat16)

        for c in self.sent:
            c.wait_send()


class ZGather:
    ahead = 4

    def __init__(self, plan, srcs, outs, scratch):
        self.plan, self.srcs, self.outs = plan, srcs, outs
        self.send_sem, self.recv_sem, self.loc = scratch
        self.z, self.z1, self.z2, self.z3 = z_peers()
        self.sent = []
        self.passed, self.settled = 0, 0

    def place(self, c, z):
        i, row, size, _ = self.plan[c]
        return self.outs[i].at[z, pl.ds(row, size), :]

    def own(self, c):
        i, row, size, layer = self.plan[c]
        return self.srcs[i].at[layer, pl.ds(row, size), :]

    def remote(self, src, z, kind, c, target):
        return pltpu.make_async_remote_copy(
            src_ref=src,
            dst_ref=self.place(c, z),
            send_sem=self.send_sem.at[kind, c],
            recv_sem=self.recv_sem.at[kind, c],
            device_id={"dp": target},
            device_id_type=MESH,
        )

    def push(self, *args):
        c = self.remote(*args)
        c.start()
        self.sent.append(c)

    def here(self, c):
        return pltpu.make_async_copy(self.own(c), self.place(c, self.z), self.loc.at[c])

    def start(self):
        for c in range(len(self.plan)):
            if c < self.ahead:
                self.send_own(c)
            self.here(c).start()

    def send_own(self, c):
        self.push(self.own(c), self.z, 0, c, self.z2)
        self.push(self.own(c), self.z, 1, c, self.z1)

    def event(self, c):
        if c + self.ahead < len(self.plan):
            self.send_own(c + self.ahead)
        self.remote(self.own(c), self.z2, 0, c, self.z2).wait_recv()
        self.push(self.place(c, self.z2), self.z2, 2, c, self.z1)

    def tick(self, n=1):
        for _ in range(min(n, len(self.plan) - self.passed)):
            self.event(self.passed)
            self.passed += 1

    def settle(self, n):
        self.tick(n - self.passed)
        for c in range(self.settled, n):
            self.remote(self.own(c), self.z1, 1, c, self.z1).wait_recv()
            self.remote(self.own(c), self.z3, 2, c, self.z1).wait_recv()
            self.here(c).wait()
        self.settled = n

    def finish(self):
        self.settle(len(self.plan))
        for c in self.sent:
            c.wait_send()


class NoZ:
    ahead = 0

    def start(self):
        pass

    def tick(self, n=1):
        pass

    def finish(self):
        pass


class ZCall:
    plan, arrays, out_shapes, out_space, scratch = (), (), (), pltpu.VMEM, ()

    def make(self, refs):
        return NoZ()

    def done(self, results):
        pass

    def aliases(self, first_in, first_out):
        return {}

    def counts(self):
        return len(self.arrays), len(self.out_shapes), len(self.scratch)

    def in_specs(self):
        return [pl.BlockSpec(memory_space=pl.ANY)] * len(self.arrays)

    def out_specs(self):
        return (pl.BlockSpec(memory_space=self.out_space),) * len(self.out_shapes)


def sum_scratch(n, w):
    return (
        pltpu.VMEM((3, n, ZR, w), jnp.bfloat16),
        pltpu.VMEM((2, n, ZR, w), jnp.bfloat16),
        pltpu.SemaphoreType.DMA((3, n)),
        pltpu.SemaphoreType.DMA((3, n)),
        pltpu.SemaphoreType.DMA((2, n)),
    )


class SumCall(ZCall):
    def __init__(self, backlog, limit):
        self.plan, self.arrays, self.pieces = [], [], []
        while limit and backlog.queue:
            entry = backlog.queue[0]
            key, array, row = entry
            if not any(a is array for a in self.arrays):
                self.arrays.append(array)
            i = [a is array for a in self.arrays].index(True)
            self.pieces.append((key, row))
            self.plan.append((i, row))
            limit -= 1
            entry[2] += ZR
            if entry[2] == array.shape[1]:
                backlog.queue.pop(0)
        self.backlog = backlog
        n = len(self.plan)
        if n:
            w = self.arrays[0].shape[2]
            self.out_shapes = (jax.ShapeDtypeStruct((n * ZR, w), jnp.bfloat16),)
            self.scratch = sum_scratch(n, w)

    def make(self, refs):
        i, o, _ = self.counts()
        return ZSum(self.plan, refs[:i], refs[i : i + o], refs[i + o :]) if self.plan else NoZ()

    def done(self, results):
        for n, (key, row) in enumerate(self.pieces):
            self.backlog.sums.append((key, row, results[0], n * ZR))


class Backlog:
    def __init__(self):
        self.queue, self.sums = [], []

    def add(self, key, array, summed=None):
        done = 0 if summed is None else summed.shape[0]
        self.sums += [(key, row, summed, row) for row in range(0, done, ZR)]
        self.queue.append([key, array, done])

    def take(self, limit):
        return SumCall(self, limit)


class GatherCall(ZCall):
    out_space = pl.ANY

    def __init__(self, queue, limit):
        self.queue, self.keys, self.plan = queue, [], []
        shards, begun, shapes = [], [], []
        while limit and queue.entries:
            entry = queue.entries[0]
            key, shard, row, size, layer = entry
            if key not in self.keys:
                self.keys.append(key)
                shards.append(shard)
                shapes.append(jax.ShapeDtypeStruct((4, *shard.shape[1:]), shard.dtype))
                if key in queue.arrays:
                    begun.append((len(self.keys) - 1, queue.arrays[key]))
            self.plan.append((self.keys.index(key), row, size, layer))
            limit -= 1
            entry[2] += size
            if entry[2] == shard.shape[1]:
                queue.entries.pop(0)
        self.arrays = shards + [x for _, x in begun]
        self.begun = [i for i, _ in begun]
        self.out_shapes = tuple(shapes)
        n = len(self.plan)
        self.scratch = (
            pltpu.SemaphoreType.DMA((3, n)),
            pltpu.SemaphoreType.DMA((3, n)),
            pltpu.SemaphoreType.DMA((n,)),
        )

    def aliases(self, first_in, first_out):
        n = len(self.keys)
        return {first_in + n + j: first_out + i for j, i in enumerate(self.begun)}

    def make(self, refs):
        i, o, _ = self.counts()
        return ZGather(self.plan, refs[:i], refs[i : i + o], refs[i + o :])

    def done(self, results):
        for key, array in zip(self.keys, results):
            self.queue.arrays[key] = array


class GatherQueue:
    def __init__(self):
        self.entries, self.arrays = [], {}

    def add(self, key, shard, layer, size):
        self.entries.append([key, shard, 0, size, layer])

    def take(self, limit):
        return GatherCall(self, limit) if limit and self.entries else NO_Z


NO_Z = ZCall()


def cost(flops):
    return pl.CostEstimate(flops=flops, bytes_accessed=1 << 16, transcendentals=0)


def split_refs(refs, *counts):
    parts = []
    for n in counts:
        parts.append(refs[:n])
        refs = refs[n:]
    return parts


def bias_tile(slope, first_key, first_query, keys, queries):
    kp = first_key + lax.broadcasted_iota(jnp.int32, (keys, queries), 0)
    qp = first_query + lax.broadcasted_iota(jnp.int32, (keys, queries), 1)
    return (jnp.abs(qp - kp).astype(jnp.float32)) * (-slope * LOG2E)

def scores_t(q, k, slope, i, B):
    L = (i+1)*B
    factor = q.shape[1] ** (-0.5) * LOG2E
    st = nt(k, q) * factor
    key = lax.broadcasted_iota(jnp.int32, (L, 1), 0)
    if i > 0:
        m = i * B
        kp = lax.broadcasted_iota(jnp.int32, (m, 1), 0).astype(jnp.float32)
        qp = (m + lax.broadcasted_iota(jnp.int32, (1, B), 1)).astype(jnp.float32)
        head = st[:m] - (qp - kp) * (slope * LOG2E)
        tail = st[m:] + bias_tile(slope, 0, 0, B, B)
        return head, tail
    return None, st + bias_tile(slope, 0, 0, B, B)

def enter_z(zc):
    if zc.plan:
        _, z1, z2, _ = z_peers()
        barrier = pltpu.get_barrier_semaphore()
        for n in (z1, z2):
            pl.semaphore_signal(barrier, inc=1, device_id={"dp": n}, device_id_type=MESH)
        pl.semaphore_wait(barrier, 2)


def attend_fwd_kernel(zc, slope_ref, p_ref, *refs):
    zi, zo, zs = zc.counts()
    z_in, (ctx_ref, lse_ref), z_out, (vt_ref,), z_scratch = split_refs(refs, zi, 2, zo, 1, zs)
    z = zc.make(z_in + z_out + z_scratch)
    enter_z(zc)
    z.start()
    B = BLOCK
    T, W = p_ref.shape
    H = W // (3 * HEAD)
    for h in range(H):
        q, k, v = (pl.ds((part * H + h) * HEAD, HEAD) for part in range(3))
        slope = slope_ref[h]
        vt_ref[...] = p_ref[:, v].T
        for i in range(T // B):
            L = (i + 1) * B
            head, tail = scores_t(p_ref[i * B : L, q], p_ref[:L, k], slope, i, B)
            top = jnp.max(tail, axis=0, keepdims=True)
            if head is not None:
                top = jnp.maximum(top, jnp.max(head, axis=0, keepdims=True))
            pt = jnp.exp2(tail - top)
            den = jnp.sum(pt, axis=0, keepdims=True)
            ct = nn(vt_ref[:, i * B : L], pt.astype(jnp.bfloat16))
            if head is not None:
                ph = jnp.exp2(head - top)
                den = den + jnp.sum(ph, axis=0, keepdims=True)
                ct = ct + nn(vt_ref[:, : i * B], ph.astype(jnp.bfloat16))
            ctx_ref[i * B : L, pl.ds(h * HEAD, HEAD)] = (ct / den).T.astype(ctx_ref.dtype)
            lse_ref[h, i : i + 1, :] = top + jnp.log2(den)
            if i % 4 == 3:
                z.tick()
    z.finish()


def attend_bwd_kernel(zc, slope_ref, p_ref, g_ref, c_ref, lse_ref, *refs):
    zi, zo, zs = zc.counts()
    z_in, (out_ref, sums_ref), z_out, (kt_ref, dk_ref, dv_ref), z_scratch = split_refs(
        refs, zi, 2, zo, 3, zs
    )
    z = zc.make(z_in + z_out + z_scratch)
    enter_z(zc)
    z.start()
    B = BLOCK
    T, W = p_ref.shape
    H = W // (3 * HEAD)
    n = T // B
    factor = HEAD ** (-0.5)
    ones = jnp.ones((8, HEAD), jnp.float32)
    for h in range(H):
        qc, kc, vc = (pl.ds((part * H + h) * HEAD, HEAD) for part in range(3))
        cols = pl.ds(h * HEAD, HEAD)
        slope = slope_ref[h]
        kt_ref[...] = p_ref[:, kc].T
        qsum = jnp.zeros((1, HEAD), jnp.float32)
        for i in reversed(range(n)):
            L = (i + 1) * B
            q = p_ref[i * B : L, qc]
            g = g_ref[i * B : L, cols]
            head, tail = scores_t(q, p_ref[:L, kc], slope, i, B)
            prod = g.astype(jnp.float32) * c_ref[i * B : L, cols].astype(jnp.float32)
            inner = lax.dot_general(
                ones,
                prod,
                NT_DIMS,
                preferred_element_type=jnp.float32,
                precision=lax.Precision.HIGHEST,
            )[:1]
            lse = lse_ref[h, i : i + 1, :]
            dpt = nt(p_ref[:L, vc], g)
            dqt = None
            for part, lo, hi in ((head, 0, i * B), (tail, i * B, L)):
                if part is None:
                    continue
                pt = jnp.exp2(part - lse)
                ds = (pt * (dpt[lo:hi] - inner)).astype(jnp.bfloat16)
                pt = pt.astype(jnp.bfloat16)
                dk = nn(ds, q)
                dv = nn(pt, g)
                if i == n - 1:
                    dk_ref[lo:hi, :] = dk
                    dv_ref[lo:hi, :] = dv
                else:
                    dk_ref[lo:hi, :] += dk
                    dv_ref[lo:hi, :] += dv
                t = nn(kt_ref[:, lo:hi], ds)
                dqt = t if dqt is None else dqt + t
            dq = (dqt * factor).T.astype(jnp.bfloat16)
            out_ref[0, i * B : L, cols] = dq
            qsum += jnp.sum(dq.astype(jnp.float32), axis=0, keepdims=True)
            if i % 4 == 3:
                z.tick()
        out_ref[1, :, cols] = (dk_ref[...] * factor).astype(jnp.bfloat16)
        dv = dv_ref[...].astype(jnp.bfloat16)
        out_ref[2, :, cols] = dv
        sums_ref[0:1, cols] = qsum
        sums_ref[1:2, cols] = jnp.sum(dv.astype(jnp.float32), axis=0, keepdims=True)
    z.finish()


def attend_call(kernel, cid, name, slopes, arrays, outs, scratch, z):
    vmem = pl.BlockSpec(memory_space=pltpu.VMEM)
    out = pl.pallas_call(
        functools.partial(kernel, z),
        out_shape=(*outs, *z.out_shapes),
        in_specs=[pl.BlockSpec(memory_space=pltpu.SMEM)] + [vmem] * len(arrays) + z.in_specs(),
        out_specs=(vmem,) * len(outs) + z.out_specs(),
        scratch_shapes=[*scratch, *z.scratch],
        compiler_params=pltpu.CompilerParams(
            collective_id=cid if z.plan else None,
            has_side_effects=bool(z.plan),
            vmem_limit_bytes=60 << 20,
        ),
        input_output_aliases=z.aliases(1 + len(arrays), len(outs)),
        cost_estimate=cost(1 << 20),
        name=name,
    )(slopes, *arrays, *z.arrays)
    z.done(out[len(outs) :])
    return out[: len(outs)]


def attend_fwd(cid, project, slopes, z):
    T, W = project.shape
    H = W // (3 * HEAD)
    outs = (
        jax.ShapeDtypeStruct((T, H * HEAD), jnp.bfloat16),
        jax.ShapeDtypeStruct((H, T // BLOCK, BLOCK), jnp.float32),
    )
    scratch = (pltpu.VMEM((HEAD, T), jnp.bfloat16),)
    return attend_call(attend_fwd_kernel, cid, "attend_fwd", slopes, (project,), outs, scratch, z)


def attend_bwd(cid, project, grad_context, context, lse, slopes, z):
    T, W = project.shape
    H = W // (3 * HEAD)
    outs = (
        jax.ShapeDtypeStruct((3, T, H * HEAD), jnp.bfloat16),
        jax.ShapeDtypeStruct((2, H * HEAD), jnp.float32),
    )
    scratch = (
        pltpu.VMEM((HEAD, T), jnp.bfloat16),
        pltpu.VMEM((T, HEAD), jnp.float32),
        pltpu.VMEM((T, HEAD), jnp.float32),
    )
    arrays = (project, grad_context, context, lse)
    return attend_call(attend_bwd_kernel, cid, "attend_bwd", slopes, arrays, outs, scratch, z)


def gather_kernel(C, n_in, n_more, n_out, n_more_out, body, filler, zc, n_scratch, *refs):
    zi, zo, zs = zc.counts()
    (x_ref,), ins, more, z_in, (full_ref,), outs, more_out, z_out, own_scratch, scratch, z_scratch = (
        split_refs(refs, 1, n_in, n_more, zi, 1, n_out, n_more_out, zo, 4, n_scratch, zs)
    )
    steps = filler(ins, more, more_out, scratch) if filler else []

    def fill(n):
        for _ in range(min(n, len(steps))):
            steps.pop(0)()

    buf, send, recv, loc = own_scratch
    R, D = x_ref.shape
    rc = R // C
    me, core, bx, by, partner, xn, yn = peers()
    z = zc.make(z_in + z_out + z_scratch)
    enter(partner, xn, yn, bool(zc.plan))
    z.start()
    sent = []

    def copy(src, rel, k, target, sidx):
        return pltpu.make_async_remote_copy(
            src_ref=src,
            dst_ref=buf.at[k, rel],
            send_sem=send.at[sidx, k],
            recv_sem=recv.at[rel, k],
            device_id={"mp": target},
            device_id_type=MESH,
        )

    def push(src, rel, k, target, sidx):
        c = copy(src, rel, k, target, sidx)
        c.start()
        sent.append(c)

    def arrive(rel, k):
        copy(buf.at[k, 0], rel, k, partner, 0).wait_recv()

    kept = []

    def keep(src, start, size, k, rel):
        c = pltpu.make_async_copy(src, full_ref.at[pl.ds(start, size), :], loc.at[k, rel])
        c.start()
        kept.append(c)

    def run(k, lo, hi):
        starts = []
        for rel in range(lo, hi):
            start = pl.multiple_of(owner(rel, core, bx, by) * R + k * rc, rc)
            keep(buf.at[k, rel], start, rc, k, rel)
            starts.append(start)
        body(
            False,
            lambda lo_=lo, hi_=hi: buf[k, lo_:hi_].reshape((hi_ - lo_) * rc, D),
            [pl.ds(s, rc) for s in starts],
            ins,
            outs,
        )

    for k in range(C):
        own = x_ref.at[pl.ds(k * rc, rc), :]
        push(own, 2, k, xn, 1)
        push(own, 4, k, yn, 2)
        push(own, 1, k, partner, 0)
    start = pl.multiple_of(me * R, R)
    keep(x_ref, start, R, 0, 0)
    body(True, lambda: x_ref[...], [pl.ds(start, R)], ins, outs)
    z.tick()
    fill(2)
    across = jnp.where(core == 0, xn, yn)
    for k in range(C + 2):
        if k < C:
            arrive(2, k)
            arrive(4, k)
            push(buf.at[k, 4 - 2 * core], 6, k, across, 3)
            push(buf.at[k, 2], 3, k, partner, 4)
            push(buf.at[k, 4], 5, k, partner, 5)
        if k == 0:
            starts = []
            other = owner(1, core, bx, by) * R
            for j in range(C):
                arrive(1, j)
                starts.append(pl.multiple_of(other + j * rc, rc))
                keep(buf.at[j, 1], starts[-1], rc, j, 1)
            body(
                False,
                lambda: buf[:, 1].reshape(R, D),
                [pl.ds(s, rc) for s in starts],
                ins,
                outs,
            )
        if 1 <= k <= C:
            arrive(3, k - 1)
            arrive(5, k - 1)
            run(k - 1, 2, 6)
            arrive(6, k - 1)
            push(buf.at[k - 1, 6], 7, k - 1, partner, 6)
        if k >= 2:
            arrive(7, k - 2)
            run(k - 2, 6, 8)
        z.tick(-(-(len(zc.plan) - 1) // (C + 1)))
        fill(1)
    fill(len(steps))
    z.finish()
    for c in sent:
        c.wait_send()
    for c in kept:
        c.wait()


def gather_call(
    name, cid, x, ins, outs, body, z=NO_Z, more=(), more_out=(), scratch=(), filler=None, C=4
):
    R, D = x.shape
    vmem = pl.BlockSpec(memory_space=pltpu.VMEM)
    anywhere = pl.BlockSpec(memory_space=pl.ANY)
    spec = lambda inside: vmem if inside else anywhere
    counts = (len(ins), len(more), len(outs), len(more_out))
    out = pl.pallas_call(
        functools.partial(gather_kernel, C, *counts, body, filler, z, len(scratch)),
        out_shape=(
            jax.ShapeDtypeStruct((8 * R, D), x.dtype),
            *outs,
            *(shape for shape, _ in more_out),
            *z.out_shapes,
        ),
        in_specs=[vmem] * (1 + len(ins)) + [spec(i) for _, i in more] + z.in_specs(),
        out_specs=(anywhere,)
        + (vmem,) * len(outs)
        + tuple(spec(i) for _, i in more_out)
        + z.out_specs(),
        scratch_shapes=[
            pltpu.VMEM((C, 8, R // C, D), x.dtype),
            pltpu.SemaphoreType.DMA((7, C)),
            pltpu.SemaphoreType.DMA((8, C)),
            pltpu.SemaphoreType.DMA((C, 8)),
            *scratch,
            *z.scratch,
        ],
        compiler_params=pltpu.CompilerParams(
            collective_id=cid, has_side_effects=True, vmem_limit_bytes=60 << 20
        ),
        input_output_aliases=z.aliases(
            1 + len(ins) + len(more), 1 + len(outs) + len(more_out)
        ),
        cost_estimate=cost(1 << 20),
        name=name,
    )(x, *ins, *(x for x, _ in more), *z.arrays)
    n = 1 + len(outs) + len(more_out)
    z.done(out[n:])
    return out[:n]


def gather_only_kernel(C, n, n_after, zc, *refs):
    zi, zo, zs = zc.counts()
    xs, _, z_in, fulls, z_out, (send, recv, loc), z_scratch = split_refs(
        refs, n, n_after, zi, n, zo, 3, zs
    )
    R, D = xs[0].shape
    rc = R // C
    me, core, bx, by, partner, xn, yn = peers()
    z = zc.make(z_in + z_out + z_scratch)
    enter(partner, xn, yn, bool(zc.plan))
    sent = []

    def copy(src, a, k, target, rel, sidx, whose):
        rows = pl.ds(pl.multiple_of(whose * R + k * rc, rc), rc)
        return pltpu.make_async_remote_copy(
            src_ref=fulls[a].at[rows, :] if src is None else src,
            dst_ref=fulls[a].at[rows, :],
            send_sem=send.at[a, sidx, k],
            recv_sem=recv.at[a, rel, k],
            device_id={"mp": target},
            device_id_type=MESH,
        )

    def push(*args):
        c = copy(*args)
        c.start()
        sent.append(c)

    def arrive(a, k, rel):
        copy(None, a, k, partner, rel, 0, owner(rel, core, bx, by)).wait_recv()

    kept = []
    for a in range(n):
        for k in range(C):
            own = xs[a].at[pl.ds(k * rc, rc), :]
            push(own, a, k, xn, 2, 1, me)
            push(own, a, k, yn, 4, 2, me)
            push(own, a, k, partner, 1, 0, me)
        c = pltpu.make_async_copy(
            xs[a], fulls[a].at[pl.ds(pl.multiple_of(me * R, R), R), :], loc.at[a]
        )
        c.start()
        kept.append(c)
    z.start()
    across = jnp.where(core == 0, xn, yn)
    x_core = owner(2, core, bx, by)
    y_core = owner(4, core, bx, by)
    through = jnp.where(core == 0, y_core, x_core)
    steps = [(a, k) for a in range(n) for k in range(C)]
    for i in range(len(steps) + 1):
        if i < len(steps):
            a, k = steps[i]
            arrive(a, k, 2)
            arrive(a, k, 4)
            push(None, a, k, across, 6, 3, through)
            push(None, a, k, partner, 3, 4, x_core)
            push(None, a, k, partner, 5, 5, y_core)
        if i >= 1:
            a, k = steps[i - 1]
            arrive(a, k, 6)
            push(None, a, k, partner, 7, 6, owner(6, core, bx, by))
        z.tick(-(-len(zc.plan) // (len(steps) + 1)))
    for a, k in steps:
        for rel in (1, 3, 5, 7):
            arrive(a, k, rel)
    z.finish()
    for c in sent:
        c.wait_send()
    for c in kept:
        c.wait()


def gather_only(cid, xs, after=(), z=NO_Z, C=4):
    R, D = xs[0].shape
    n = len(xs)
    anywhere = pl.BlockSpec(memory_space=pl.ANY)
    out = pl.pallas_call(
        functools.partial(gather_only_kernel, C, n, len(after), z),
        out_shape=tuple(jax.ShapeDtypeStruct((8 * R, D), x.dtype) for x in xs) + tuple(z.out_shapes),
        in_specs=[anywhere] * (n + len(after)) + z.in_specs(),
        out_specs=(anywhere,) * n + z.out_specs(),
        scratch_shapes=[
            pltpu.SemaphoreType.DMA((n, 7, C)),
            pltpu.SemaphoreType.DMA((n, 8, C)),
            pltpu.SemaphoreType.DMA((n,)),
            *z.scratch,
        ],
        compiler_params=pltpu.CompilerParams(collective_id=cid, has_side_effects=True),
        input_output_aliases=z.aliases(n + len(after), n),
        cost_estimate=cost(1 << 20),
        name="gather_rows",
    )(*xs, *after, *z.arrays)
    z.done(out[n:])
    return out[:n]


def tiles(n, step, f):
    step = min(step, n)

    @pl.loop(0, n // step)
    def _(j):
        f(pl.ds(pl.multiple_of(j * step, step), step))


def put(ref, pieces, cols, value):
    at = 0
    for rows in pieces:
        ref[rows, cols] = value[at : at + rows.size]
        at += rows.size


def take(ref, pieces, cols):
    parts = [ref[rows, cols] for rows in pieces]
    return parts[0] if len(parts) == 1 else jnp.concatenate(parts, axis=0)


def project_body(first, lhs, pieces, ins, outs):
    w, shift = ins

    def f(cols):
        put(outs[0], pieces, cols, (nn(lhs(), w[:, cols]) + shift[:, cols]).astype(jnp.bfloat16))

    tiles(w.shape[1], 256, f)


def gelu_both(v):
    t = jnp.tanh(0.7978845608028654 * (v + 0.044715 * v * v * v))
    d = 0.5 * (1.0 + t) + 0.5 * v * (1.0 - t * t) * (
        0.7978845608028654 * (1.0 + 3 * 0.044715 * v * v)
    )
    return (0.5 * v * (1.0 + t)).astype(jnp.bfloat16), d.astype(jnp.bfloat16)


def up_body(first, lhs, pieces, ins, outs):
    w, shift = ins

    def f(cols):
        active, slope = gelu_both(nn(lhs(), w[:, cols]) + shift[:, cols])
        put(outs[0], pieces, cols, active)
        put(outs[1], pieces, cols, slope)

    tiles(w.shape[1], 256, f)


def wide_nt(src, w, cols):
    Z, _, d = w.shape
    total = None
    for z in range(Z):
        t = nt(src[:, z * d : (z + 1) * d], w[z, cols, :])
        total = t if total is None else total + t
    return total


def down_back_body(first, lhs, pieces, ins, outs):
    w, slope = ins

    def f(cols):
        g = wide_nt(lhs(), w, cols) * take(slope, pieces, cols).astype(jnp.float32)
        g = g.astype(jnp.bfloat16)
        put(outs[0], pieces, cols, g)
        sums = jnp.sum(g.astype(jnp.float32), axis=0, keepdims=True)
        if first:
            outs[1][:, cols] = sums
        else:
            outs[1][:, cols] += sums

    tiles(w.shape[1], 256, f)


def dense_back_body(first, lhs, pieces, ins, outs):
    (w,) = ins

    def f(cols):
        put(outs[0], pieces, cols, wide_nt(lhs(), w, cols).astype(jnp.bfloat16))

    tiles(w.shape[1], 256, f)


def scatter_kernel(C, n_in, n_more, n_more_out, body, filler, zc, n_scratch, late_n, *refs):
    zi, zo, zs = zc.counts()
    ins, more, z_in, (out_ref,), more_out, z_out, own_scratch, scratch, z_scratch = split_refs(
        refs, n_in, n_more, zi, 1, n_more_out, zo, 4, n_scratch, zs
    )
    pbuf, rbuf, send, recv = own_scratch
    z = zc.make(z_in + z_out + z_scratch)
    z.ahead = max(z.ahead, 6)
    R, D = out_ref.shape
    rc = R // C
    me, core, bx, by, partner, xn, yn = peers()
    steps, late = [], NoZ()
    if late_n:
        scratch, late_out, late_scratch = scratch[:-5], more_out[-1:], scratch[-5:]
        more_out = more_out[:-1]
        plan = [(0, ZR * c) for c in range(late_n)]
        late = ZSum(plan, more_out[:1], late_out, late_scratch)
        steps = filler(ins, more, more_out, scratch, late)
    elif filler:
        steps = filler(ins, more, more_out, scratch)
    enter(partner, xn, yn, bool(zc.plan or late_n))
    z.start()
    dn = jnp.where(core == 0, yn, xn)
    fn = jnp.where(core == 0, xn, yn)
    sent = []

    def fill(n):
        for _ in range(min(n, len(steps))):
            steps.pop(0)()

    def copy(src, slot, k, target):
        rows = pl.ds(k * rc, rc)
        return pltpu.make_async_remote_copy(
            src_ref=src.at[rows, :],
            dst_ref=rbuf.at[slot, rows, :],
            send_sem=send.at[slot, k],
            recv_sem=recv.at[slot, k],
            device_id={"mp": target},
            device_id_type=MESH,
        )

    def push(slot, to, target, k):
        c = copy(pbuf.at[slot], to, k, target)
        c.start()
        sent.append(c)

    def arrive(slot, k):
        copy(pbuf.at[0], slot, k, partner).wait_recv()

    def dest_rank(which, c):
        if which == 0:
            return (1 - by) * 4 + (1 - bx) * 2 + c
        if which == 3:
            return by * 4 + bx * 2 + c
        flip_y = (1 - c) if which == 1 else c
        y = by + flip_y * (1 - 2 * by)
        x = bx + (1 - flip_y) * (1 - 2 * bx)
        return y * 4 + x * 2 + c

    def compute(which, c, slot):
        rows = pl.ds(pl.multiple_of(dest_rank(which, c) * R, R), R)
        body(rows, ins, pbuf.at[slot])

    def theirs(which):
        compute(which, 1 - core, which)
        for k in range(C):
            push(which, which, partner, k)

    def add(slot, rslot, k):
        @pl.loop(0, rc // 16)
        def _(i):
            rows = pl.ds(pl.multiple_of(k * rc + i * 16, 16), 16)
            pbuf[slot, rows, :] = (
                pbuf[slot, rows, :].astype(jnp.float32) + rbuf[rslot, rows, :].astype(jnp.float32)
            ).astype(pbuf.dtype)

    def join(which):
        for k in range(C):
            arrive(which, k)
            add(4 + which, which, k)
            if which < 2:
                push(4 + which, 4 + which, dn, k)

    theirs(0)
    compute(0, core, 4)
    theirs(1)
    join(0)
    compute(1, core, 5)
    theirs(2)
    join(1)
    compute(2, core, 6)
    theirs(3)
    join(2)
    compute(3, core, 7)
    join(3)
    z.tick(3)
    for k in range(C):
        arrive(4, k)
        add(6, 4, k)
        push(6, 6, fn, k)
        z.tick(2)
        fill(2)
    fill(len(steps))
    for k in range(C):
        arrive(5, k)
        arrive(6, k)

        @pl.loop(0, rc // 16)
        def _(i):
            rows = pl.ds(pl.multiple_of(k * rc + i * 16, 16), 16)
            out_ref[rows, :] = (
                pbuf[7, rows, :].astype(jnp.float32)
                + rbuf[5, rows, :].astype(jnp.float32)
                + rbuf[6, rows, :].astype(jnp.float32)
            )
    z.finish()
    late.finish()
    for c in sent:
        c.wait_send()


def scatter_call(
    name, cid, T, D, ins, body, more=(), more_out=(), scratch=(), filler=None, z=NO_Z, late=0, C=4
):
    if late:
        w = more_out[0][0].shape[2]
        more_out = [*more_out, (jax.ShapeDtypeStruct((late * ZR, w), jnp.bfloat16), True)]
        scratch = [*scratch, *sum_scratch(late, w)]
    R = T // 8
    vmem = pl.BlockSpec(memory_space=pltpu.VMEM)
    anywhere = pl.BlockSpec(memory_space=pl.ANY)
    spec = lambda inside: vmem if inside else anywhere
    out = pl.pallas_call(
        functools.partial(
            scatter_kernel, C, len(ins), len(more), len(more_out), body, filler, z, len(scratch), late
        ),
        out_shape=(
            jax.ShapeDtypeStruct((R, D), jnp.float32),
            *(shape for shape, _ in more_out),
            *z.out_shapes,
        ),
        in_specs=[vmem] * len(ins) + [spec(i) for _, i in more] + z.in_specs(),
        out_specs=(vmem,) + tuple(spec(i) for _, i in more_out) + z.out_specs(),
        scratch_shapes=[
            pltpu.VMEM((8, R, D), jnp.bfloat16),
            pltpu.VMEM((7, R, D), jnp.bfloat16),
            pltpu.SemaphoreType.DMA((7, C)),
            pltpu.SemaphoreType.DMA((7, C)),
            *scratch,
            *z.scratch,
        ],
        compiler_params=pltpu.CompilerParams(
            collective_id=cid, has_side_effects=True, vmem_limit_bytes=60 << 20
        ),
        input_output_aliases=z.aliases(len(ins) + len(more), 1 + len(more_out)),
        cost_estimate=cost(1 << 20),
        name=name,
    )(*ins, *(x for x, _ in more), *z.arrays)
    z.done(out[1 + len(more_out) :])
    return out[: 1 + len(more_out)] if more_out else out[0]


def row_split_body(rows, ins, out):
    a, w = ins
    Z, _, d = w.shape
    for z in range(Z):
        out[:, z * d : (z + 1) * d] = nn(a[rows, :], w[z]).astype(out.dtype)


def up_back_body(rows, ins, out):
    a, w = ins

    def f(cols):
        out[:, cols] = nt(a[rows, :], w[cols, :]).astype(out.dtype)

    tiles(w.shape[0], 512, f)


def project_back_body(rows, ins, out):
    a, w = ins
    S, _, width = a.shape

    def f(cols):
        total = None
        for s in range(S):
            t = nt(a[s, rows, :], w[cols, s * width : (s + 1) * width])
            total = t if total is None else total + t
        out[:, cols] = total.astype(out.dtype)

    tiles(w.shape[0], 512, f)


class Stream:
    def __init__(self, chunks, buf, sems, stage, out_sems):
        self.chunks, self.buf, self.sems = chunks, buf, sems
        self.stage, self.out_sems = stage, out_sems
        self.turn, self.flying = 0, [[], []]

    def fetch(self, i):
        src, j = self.chunks[i]
        w = self.buf.shape[2]
        return pltpu.make_async_copy(
            src.at[:, pl.ds(j * w, w)], self.buf.at[i % 2], self.sems.at[i % 2]
        )

    def get(self, i):
        self.fetch(i).wait()
        if i + 1 < len(self.chunks):
            self.fetch(i + 1).start()
        return self.buf.at[i % 2]

    def result(self, make, targets):
        slot = self.turn % 2
        self.turn += 1
        for c in self.flying[slot]:
            c.wait()
        make(self.stage.at[slot])
        self.flying[slot] = []
        for n, (lo, width, dest) in enumerate(targets):
            c = pltpu.make_async_copy(
                self.stage.at[slot, :, pl.ds(lo, width)], dest, self.out_sems.at[slot, n]
            )
            c.start()
            self.flying[slot].append(c)

    def drain(self):
        for slot in range(2):
            for c in self.flying[slot]:
                c.wait()
            self.flying[slot] = []


STREAM_SCRATCH = (
    pltpu.VMEM((2, 2048, 256), jnp.bfloat16),
    pltpu.SemaphoreType.DMA((2,)),
    pltpu.VMEM((2, 256, 1024), jnp.bfloat16),
    pltpu.SemaphoreType.DMA((2, 4)),
    pltpu.VMEM((256, 2048), jnp.bfloat16),
)


def tile_product(turned, right, lo, half):
    def make(tile):
        def f(cols):
            at = pl.ds(pl.multiple_of(lo + cols.start, 256), cols.size)
            tile[:, cols] = nn(turned[...], right[:, at]).astype(tile.dtype)

        tiles(half, 256, f)

    return make


def down_steps(stream, out, turned, held, held_copy, chunk, n, w):
    half = stream.stage.shape[2]
    D = held.shape[1]
    d = out.shape[2]
    steps = []

    def step(j, h):
        if h == 0:
            turned[...] = chunk(j).T
        if j == 0 and h == 0 and held_copy is not None:
            held_copy.wait()
        targets = [
            (b * d, d, out.at[h * (half // d) + b, pl.ds(j * w, w), :]) for b in range(half // d)
        ]
        stream.result(tile_product(turned, held, h * half, half), targets)

    for j in range(n):
        for h in range(D // half):
            steps.append(functools.partial(step, j, h))
    return steps


def up_steps(stream, out, turned, hidden, first, D, w):
    F = hidden.shape[1]
    d = out.shape[2]

    def step(j):
        turned[...] = stream.get(first + j)[...].T
        z, r = (j * w) // d, (j * w) % d
        targets = [(b * d, d, out.at[z, pl.ds(b * d + r, w), :]) for b in range(F // d)]
        stream.result(tile_product(turned, hidden, 0, F), targets)

    return [functools.partial(step, j) for j in range(D // w)]


def down_filler(ins, more, more_out, scratch, late):
    active, grad = more
    (down_out,) = more_out
    buf, sems, stage, out_sems, turned, held, held_sem = scratch
    T, F = active.shape
    D = grad.shape[1]
    w = buf.shape[2]
    n = F // w
    stream = Stream([(active, j) for j in range(n)], buf, sems, stage, out_sems)
    held_copy = pltpu.make_async_copy(grad, held, held_sem)
    stream.fetch(0).start()
    held_copy.start()
    steps = down_steps(
        stream, down_out, turned, held, held_copy, lambda j: stream.get(j)[...], n, w
    )

    def early():
        stream.drain()
        late.start()

    first = len(late.plan) * ZR // w * (D // stage.shape[2])
    steps.insert(first, early)
    for i in range(len(late.plan)):
        steps.insert(first + 2 + 2 * i, late.tick)
    return steps + [stream.drain]


def up_filler(ins, more, more_out, scratch):
    hidden, normed = more
    buf, sems, stage, out_sems, turned = scratch
    D = normed.shape[1]
    w = buf.shape[2]
    stream = Stream([(normed, j) for j in range(D // w)], buf, sems, stage, out_sems)
    stream.fetch(0).start()
    return up_steps(stream, more_out[0], turned, hidden, 0, D, w) + [stream.drain]


def last_filler(ins, more, more_out, scratch):
    active, w_down = ins
    slope, grad = more
    hidden_out, sum_out, down_out = more_out
    stage, out_sems, turned, held, held_sem = scratch
    T, F = active.shape
    w = turned.shape[0]
    stream = Stream([], None, None, stage, out_sems)
    held_copy = pltpu.make_async_copy(grad, held, held_sem)
    held_copy.start()

    def back(i):
        if i == 0:
            held_copy.wait()
        rows = pl.ds(i * BLOCK, BLOCK)
        down_back_body(
            i == 0, lambda: held[rows, :], [rows], (w_down, slope), (hidden_out, sum_out)
        )

    steps = [functools.partial(back, i) for i in range(T // BLOCK)]
    steps += down_steps(
        stream, down_out, turned, held, None, lambda j: active[:, j * w : (j + 1) * w], F // w, w
    )
    return steps + [stream.drain]


def attn_filler(ins, more, more_out, scratch):
    parts = ins[0]
    context, grad, normed = more
    (out,) = more_out
    buf, sems, stage, out_sems, turned, ctx_t = scratch
    S, T, width = parts.shape
    D = grad.shape[1]
    Z = out.shape[0]
    d = D // Z
    w = buf.shape[2]
    n = D // w
    stream = Stream(
        [(context, 0)] + [(grad, j) for j in range(n)] + [(normed, j) for j in range(n)],
        buf,
        sems,
        stage,
        out_sems,
    )
    stream.fetch(0).start()
    steps = []

    def dense(j):
        def step():
            if j == 0:
                ctx_t[...] = stream.get(0)[...].T
            right = stream.get(1 + j)

            def make(tile):
                tile[:, :w] = nn(ctx_t[...], right[...]).astype(tile.dtype)

            z, r = (j * w) // d, (j * w) % d
            stream.result(make, [(0, w, out.at[z, pl.ds(0, width), pl.ds(r, w)])])

        return step

    def project(j):
        def step():
            turned[...] = stream.get(1 + n + j)[...].T

            def make(tile):
                for s in range(S):
                    tile[:, s * width : (s + 1) * width] = nn(turned[...], parts[s]).astype(
                        tile.dtype
                    )

            z, r = (j * w) // d, (j * w) % d
            side = pl.ds(r // w * width, width)
            stream.result(
                make,
                [(s * width, width, out.at[z, pl.ds(width + s * w, w), side]) for s in range(S)],
            )

        return step

    for j in range(n):
        steps.append(dense(j))
    for j in range(n):
        steps.append(project(j))
    steps.append(stream.drain)
    return steps


def finish_kernel(zc, *refs):
    zi, zo, zs = zc.counts()
    (v_ref, u_ref), z_in, (v_out, u_out), z_out, own_scratch, z_scratch = split_refs(
        refs, 2, zi, 2, zo, 6, zs
    )
    vs, us, v_in, u_in, send, recv = own_scratch
    me, core, bx, by, partner, xn, yn = peers()
    z = zc.make(z_in + z_out + z_scratch)
    _, z1, z2, _ = z_peers()
    enter(partner, xn, yn, True)
    z.start()
    hops = (({"mp": partner}, False), ({"mp": xn}, False), ({"mp": yn}, False))
    hops += (({"dp": z1}, True), ({"dp": z2}, True))
    vs[0] = v_ref[...]
    us[3] = u_ref[...]
    for i, (target, both) in enumerate(hops):
        copies = []
        for n, (src, dst) in enumerate(((vs, v_in), (us, u_in))[: 2 if both else 1]):
            c = pltpu.make_async_remote_copy(
                src_ref=src.at[i],
                dst_ref=dst.at[i],
                send_sem=send.at[n, i],
                recv_sem=recv.at[n, i],
                device_id=target,
                device_id_type=MESH,
            )
            c.start()
            copies.append(c)
        z.tick(2)
        for c in copies:
            c.wait()
        vs[i + 1] = vs[i] + v_in[i]
        if both:
            us[i + 1] = us[i] + u_in[i]
    v_out[...] = vs[5]
    u_out[...] = us[5]
    z.finish()


def finish_call(cid, v, u, z):
    vmem = pl.BlockSpec(memory_space=pltpu.VMEM)
    out = pl.pallas_call(
        functools.partial(finish_kernel, z),
        out_shape=(
            jax.ShapeDtypeStruct(v.shape, v.dtype),
            jax.ShapeDtypeStruct(u.shape, u.dtype),
            *z.out_shapes,
        ),
        in_specs=[vmem, vmem] + z.in_specs(),
        out_specs=(vmem, vmem) + z.out_specs(),
        scratch_shapes=[
            pltpu.VMEM((6, *v.shape), v.dtype),
            pltpu.VMEM((6, *u.shape), u.dtype),
            pltpu.VMEM((5, *v.shape), v.dtype),
            pltpu.VMEM((5, *u.shape), u.dtype),
            pltpu.SemaphoreType.DMA((2, 5)),
            pltpu.SemaphoreType.DMA((2, 5)),
            *z.scratch,
        ],
        compiler_params=pltpu.CompilerParams(
            collective_id=cid, has_side_effects=True, vmem_limit_bytes=60 << 20
        ),
        cost_estimate=cost(1 << 20),
        name="finish",
    )(v, u, *z.arrays)
    z.done(out[2:])
    return out[0], out[1]


def place_kernel(moves, n_src, *refs):
    srcs, outs, (low, wide, in_sem, out_sem) = split_refs(refs, n_src, 4, 4)
    depth = low.shape[0]

    def fetch(i):
        s, row, _ = moves[i]
        return pltpu.make_async_copy(
            srcs[s].at[pl.ds(row, ZR), :], low.at[i % depth], in_sem.at[i % depth]
        )

    def store(i):
        _, _, targets = moves[i]
        copies = []
        for n, (o, index, lo, width) in enumerate(targets):
            copies.append(
                pltpu.make_async_copy(
                    wide.at[i % depth, :, pl.ds(lo, width)],
                    outs[o].at[index],
                    out_sem.at[i % depth, n],
                )
            )
        return copies

    for i in range(min(depth, len(moves))):
        fetch(i).start()
    for i in range(len(moves)):
        fetch(i).wait()
        if i >= depth:
            for c in store(i - depth):
                c.wait()
        wide[i % depth] = low[i % depth].astype(jnp.float32)
        for c in store(i):
            c.start()
        if i + depth < len(moves):
            fetch(i + depth).start()
    for i in range(max(0, len(moves) - depth), len(moves)):
        for c in store(i):
            c.wait()


def place_call(sums, out_shapes, targets_of):
    arrays, moves = [], []
    for key, row, array, at in sums:
        if not any(a is array for a in arrays):
            arrays.append(array)
        i = [a is array for a in arrays].index(True)
        moves.append((i, at, targets_of(key, row)))
    w = arrays[0].shape[1]
    depth = 6
    anywhere = pl.BlockSpec(memory_space=pl.ANY)
    return pl.pallas_call(
        functools.partial(place_kernel, moves, len(arrays)),
        out_shape=tuple(out_shapes),
        in_specs=[anywhere] * len(arrays),
        out_specs=(anywhere,) * len(out_shapes),
        scratch_shapes=[
            pltpu.VMEM((depth, ZR, w), jnp.bfloat16),
            pltpu.VMEM((depth, ZR, w), jnp.float32),
            pltpu.SemaphoreType.DMA((depth,)),
            pltpu.SemaphoreType.DMA((depth, 2)),
        ],
        compiler_params=pltpu.CompilerParams(vmem_limit_bytes=40 << 20),
        cost_estimate=cost(1 << 20),
        name="place",
    )(*arrays)


def first_kernel(C, zc, n_project, *refs):
    zi, zo, zs = zc.counts()
    ins, z_in, outs, z_out, scratch, z_scratch = split_refs(refs, 6, zi, 6, zo, 13, zs)
    x_ref, gain_ref, bias_ref, shift_ref, up_ref, down_ref = ins
    full_ref, project_ref, up_out, down_out = *outs[:2], outs[2:4], outs[4:6]
    x_low, w_here, w_sem, wide, low, wide_sem, low_sem, *mine = scratch
    buf, send, recv, loc, wide2, low2 = mine
    R, D = x_ref.shape
    rc = R // C
    me, core, bx, by, partner, xn, yn = peers()
    z = zc.make(z_in + z_out + z_scratch)

    pieces = []
    both = ((up_ref, up_out, wide, low, 0), (down_ref, down_out, wide2, low2, 1))
    for l in range(2):
        for ref, out, w, n, stage in both:
            size = w.shape[1]
            pieces += [
                (ref.at[l, pl.ds(r, size), :], out[l].at[pl.ds(r, size), :], w, n, stage)
                for r in range(0, ref.shape[1], size)
            ]

    def read(i):
        src, _, w, _, stage = pieces[i]
        return pltpu.make_async_copy(src, w.at[i % 2], wide_sem.at[stage, i % 2])

    def write(i):
        _, dst, _, n, stage = pieces[i]
        return pltpu.make_async_copy(n.at[i % 2], dst, low_sem.at[stage, i % 2])

    def cast(i):
        _, _, w, n, _ = pieces[i]
        read(i).wait()
        if i >= 2:
            write(i - 2).wait()
        n[i % 2] = w[i % 2].astype(n.dtype)
        write(i).start()
        if i + 2 < len(pieces):
            read(i + 2).start()

    for i in range(2):
        read(i).start()
    enter(partner, xn, yn, True)
    z.start()

    @pl.loop(0, R // 16)
    def _(i):
        rows = pl.ds(pl.multiple_of(i * 16, 16), 16)
        v = x_ref[rows, :].astype(jnp.float32)
        x_low[rows, :] = layer_norm(v, gain_ref[...], bias_ref[...]).astype(x_low.dtype)

    sent = []

    def copy(src, rel, k, target, sidx):
        return pltpu.make_async_remote_copy(
            src_ref=src,
            dst_ref=buf.at[k, rel],
            send_sem=send.at[sidx, k],
            recv_sem=recv.at[rel, k],
            device_id={"mp": target},
            device_id_type=MESH,
        )

    def push(src, rel, k, target, sidx):
        c = copy(src, rel, k, target, sidx)
        c.start()
        sent.append(c)

    def arrive(rel, k):
        copy(buf.at[k, 0], rel, k, partner, 0).wait_recv()

    for k in range(C):
        own = x_low.at[pl.ds(k * rc, rc), :]
        push(own, 2, k, xn, 1)
        push(own, 4, k, yn, 2)
        push(own, 1, k, partner, 0)
    kept = [
        pltpu.make_async_copy(
            x_low, full_ref.at[pl.ds(pl.multiple_of(me * R, R), R), :], loc.at[0, 0]
        )
    ]
    kept[0].start()
    starts = [pl.multiple_of(owner(rel, core, bx, by) * R, R) for rel in range(8)]
    across = jnp.where(core == 0, xn, yn)
    z.tick()
    for k in range(C + 1):
        if k < C:
            arrive(2, k)
            arrive(4, k)
            push(buf.at[k, 4 - 2 * core], 6, k, across, 3)
            push(buf.at[k, 2], 3, k, partner, 4)
            push(buf.at[k, 4], 5, k, partner, 5)
        if k >= 1:
            arrive(6, k - 1)
            push(buf.at[k - 1, 6], 7, k - 1, partner, 6)
        z.tick()
        for i in range(2 * k, min(2 * k + 2, len(pieces))):
            cast(i)
        z.tick()
    for k in range(C):
        for rel in range(1, 8):
            if rel in (1, 3, 5, 7):
                arrive(rel, k)
            start = pl.multiple_of(starts[rel] + k * rc, rc)
            c = pltpu.make_async_copy(
                buf.at[k, rel], full_ref.at[pl.ds(start, rc), :], loc.at[k, rel]
            )
            c.start()
            kept.append(c)
    for i in range(2 * C + 2, len(pieces)):
        cast(i)
    for i in range(len(pieces) - 2, len(pieces)):
        write(i).wait()
    z.settle(n_project)
    weights = pltpu.make_async_copy(z_out[0], w_here, w_sem)
    weights.start()
    weights.wait()
    for rel in range(8):
        rows = pl.ds(starts[rel], R)

        def f(cols, rel=rel, rows=rows):
            lhs = x_low[...] if rel == 0 else buf[:, rel].reshape(R, D)
            w = w_here[:, :, cols].reshape(D, cols.size)
            project_ref[rows, cols] = (nn(lhs, w) + shift_ref[:, cols]).astype(jnp.bfloat16)

        tiles(project_ref.shape[1], 256, f)
        z.tick()
    z.finish()
    for c in sent:
        c.wait_send()
    for c in kept:
        c.wait()


def first_call(cid, x, gain, bias, shift, up, down, z, n_project, C=4):
    R, D = x.shape
    N = shift.shape[0]
    w = z.arrays[0]
    vmem = pl.BlockSpec(memory_space=pltpu.VMEM)
    anywhere = pl.BlockSpec(memory_space=pl.ANY)
    low = jnp.bfloat16
    out = pl.pallas_call(
        functools.partial(first_kernel, C, z, n_project),
        out_shape=(
            jax.ShapeDtypeStruct((8 * R, D), low),
            jax.ShapeDtypeStruct((8 * R, N), low),
            *[jax.ShapeDtypeStruct(up.shape[1:], low)] * 2,
            *[jax.ShapeDtypeStruct(down.shape[1:], low)] * 2,
            *z.out_shapes,
        ),
        in_specs=[vmem] * 4 + [anywhere] * 2 + z.in_specs(),
        out_specs=(anywhere, vmem) + (anywhere,) * 4 + z.out_specs(),
        scratch_shapes=[
            pltpu.VMEM((R, D), low),
            pltpu.VMEM((4, *w.shape[1:]), low),
            pltpu.SemaphoreType.DMA,
            pltpu.VMEM((2, 256, up.shape[2]), jnp.float32),
            pltpu.VMEM((2, 256, up.shape[2]), low),
            pltpu.SemaphoreType.DMA((2, 2)),
            pltpu.SemaphoreType.DMA((2, 2)),
            pltpu.VMEM((C, 8, R // C, D), low),
            pltpu.SemaphoreType.DMA((7, C)),
            pltpu.SemaphoreType.DMA((8, C)),
            pltpu.SemaphoreType.DMA((C, 8)),
            pltpu.VMEM((2, 512, down.shape[2]), jnp.float32),
            pltpu.VMEM((2, 512, down.shape[2]), low),
            *z.scratch,
        ],
        compiler_params=pltpu.CompilerParams(
            collective_id=cid, has_side_effects=True, vmem_limit_bytes=60 << 20
        ),
        cost_estimate=cost(1 << 20),
        name="first",
    )(x, gain[None], bias[None], shift[None], up, down, *z.arrays)
    z.done(out[6:])
    return out[:6]


def gather_sum(part):
    return lax.psum_scatter(
        part.astype(jnp.bfloat16), "mp", scatter_dimension=0, tiled=True
    ).astype(jnp.float32)


def gather_all(x):
    return lax.all_gather(x, "mp", axis=0, tiled=True)


def side_by_side(w):
    return jnp.concatenate([w[z] for z in range(w.shape[0])], axis=1)


def reduce_dp(part):
    return lax.psum_scatter(part.astype(jnp.bfloat16), "dp", scatter_dimension=0)


class Fast:
    def __init__(self, T, D):
        self.T, self.D = T, D
        self.backlog = Backlog()
        self.grads = None

    def start(self, x, gain, bias, shift, out_grad, weights):
        project, dense, up, down = weights
        low = jnp.bfloat16
        project = project.reshape(*project.shape[:2], -1).astype(low)
        dense = dense.astype(low)
        self.weights = queue = GatherQueue()
        queue.add(("project", 0), project, 0, 64)
        n_project = project.shape[1] // 64
        rows, out, up0, up1, down0, down1 = first_call(
            0, x, gain, bias, shift, up, down, queue.take(n_project), n_project
        )
        self.first = rows, out
        for key, shard in (
            (("up", 0), up0),
            (("down", 0), down0),
            (("project", 1), project[1]),
            (("up", 1), up1),
        ):
            queue.arrays[key] = lax.all_gather(shard, "dp", axis=0)
        queue.add(("dense", 0), dense, 0, 128)
        (self.grad_rows,) = gather_only(8, (out_grad,), z=queue.take(2))
        queue.add(("dense", 1), dense, 1, 128)
        queue.add(("down", 1), down1[None], 0, 128)

    def weight(self, name, l):
        w = self.weights.arrays[name, l]
        return w.reshape(-1, w.shape[2]) if name in ("project", "up") else w

    def project(self, l, normed, shift):
        if l == 0:
            return self.first
        w = self.weight("project", l)
        out = jax.ShapeDtypeStruct((self.T, w.shape[1]), jnp.bfloat16)
        return gather_call(
            "gather_project",
            10 * l,
            normed,
            (w, shift[None]),
            (out,),
            project_body,
            self.weights.take(2),
        )

    def attend(self, l, project, slopes):
        return attend_fwd(20 + l, project, slopes, NO_Z)

    def dense(self, l, context):
        return scatter_call(
            "dense_scatter",
            10 * l + 1,
            self.T,
            self.D,
            (context, self.weight("dense", l)),
            row_split_body,
            z=self.weights.take(3 * l),
        )

    def up(self, l, normed, shift):
        w = self.weight("up", l)
        out = jax.ShapeDtypeStruct((self.T, w.shape[1]), jnp.bfloat16)
        return gather_call(
            "gather_up",
            10 * l + 2,
            normed,
            (w, shift[None]),
            (out, out),
            up_body,
            self.weights.take(5 * l),
        )

    def down(self, l, active):
        return scatter_call(
            "down_scatter",
            10 * l + 3,
            self.T,
            self.D,
            (active, self.weight("down", l)),
            row_split_body,
            more=((self.grad_rows, False),),
        )

    def last_down(self, l, active, slope):
        T, F = active.shape
        Z = lax.axis_size("dp")
        grad = self.grad_rows
        rows, grad_hidden, sums, packed = scatter_call(
            "last_scatter",
            10 * l + 3,
            T,
            self.D,
            (active, self.weight("down", l)),
            row_split_body,
            more=((slope, True), (grad, False)),
            more_out=(
                (jax.ShapeDtypeStruct((T, F), jnp.bfloat16), True),
                (jax.ShapeDtypeStruct((1, F), jnp.float32), True),
                (jax.ShapeDtypeStruct((Z, F, self.D // Z), jnp.bfloat16), False),
            ),
            scratch=(*STREAM_SCRATCH[2:], pltpu.VMEM((T, self.D), jnp.bfloat16), pltpu.SemaphoreType.DMA),
            filler=last_filler,
        )
        self.backlog.add(("down", l), packed)
        return rows, grad, grad_hidden, sums

    def down_back(self, l, grad, slope):
        w = self.weight("down", l)
        F = slope.shape[1]
        outs = (
            jax.ShapeDtypeStruct((self.T, F), jnp.bfloat16),
            jax.ShapeDtypeStruct((1, F), jnp.float32),
        )
        z = self.backlog.take(5)
        return gather_call("gather_down_back", 10 * l + 4, grad, (w, slope), outs, down_back_body, z)

    def up_back(self, l, grad_hidden, active, normed, grad_down):
        T, F = grad_hidden.shape
        packed = jax.ShapeDtypeStruct((4, F, self.D // 4), jnp.bfloat16)
        self.for_up = grad_hidden, normed, packed
        args = (
            "up_back_scatter",
            10 * l + 5,
            T,
            self.D,
            (grad_hidden, self.weight("up", l)),
            up_back_body,
        )
        if l:
            return scatter_call(*args, z=self.backlog.take(5))
        out = scatter_call(
            *args,
            more=((active, False), (grad_down, False)),
            more_out=((packed, False),),
            scratch=STREAM_SCRATCH
            + (pltpu.VMEM((T, self.D), jnp.bfloat16), pltpu.SemaphoreType.DMA),
            filler=down_filler,
            z=self.backlog.take(4),
            late=2,
        )
        self.backlog.add(("down", l), out[1], out[2])
        return out[0]

    def dense_back(self, l, grad):
        w = self.weight("dense", l)
        out = jax.ShapeDtypeStruct((self.T, w.shape[1]), jnp.bfloat16)
        hidden, normed, packed = self.for_up
        full, out, up = gather_call(
            "gather_dense_back",
            10 * l + 6,
            grad,
            (w,),
            (out,),
            dense_back_body,
            self.backlog.take(4),
            more=((hidden, True), (normed, False)),
            more_out=((packed, False),),
            scratch=STREAM_SCRATCH,
            filler=up_filler,
        )
        self.backlog.add(("up", l), up)
        return full, out

    def attend_back(self, l, project, grad_context, context, log_norms, slopes):
        return attend_bwd(
            22 + l, project, grad_context, context, log_norms, slopes, self.backlog.take(2)
        )

    def project_back(self, l, grad_project, context, grad_branch, normed):
        S, T, width = grad_project.shape
        Z = lax.axis_size("dp")
        packed = jax.ShapeDtypeStruct((Z, (S + 1) * width, self.D // Z), jnp.bfloat16)
        grad, packed = scatter_call(
            "project_back_scatter",
            10 * l + 7,
            T,
            self.D,
            (grad_project, self.weight("project", l)),
            project_back_body,
            more=((context, False), (grad_branch, False), (normed, False)),
            more_out=((packed, False),),
            scratch=STREAM_SCRATCH + (pltpu.VMEM((width, T), jnp.bfloat16),),
            filler=attn_filler,
            z=self.backlog.take(5),
        )
        self.backlog.add(("attn", l), packed)
        return grad

    def matrix_grads(self, shapes):
        layers, d, parts, width = shapes[0]
        group = self.D // lax.axis_size("dp")

        def targets(key, row):
            kind, l = key
            if kind == "down":
                return [(3, (l, pl.ds(row, ZR)), 0, group)]
            if kind == "up":
                b, r = divmod(row, group)
                return [(2, (l, pl.ds(r, ZR), pl.ds(b * group, group)), 0, group)]
            if row < width:
                return [(1, (l, pl.ds(row, ZR)), 0, group)]
            s, r = divmod(row - width, width)
            return [(0, (l, s, pl.ds(h * width + r, ZR)), h * width, width) for h in range(2)]

        shapes = [(layers, parts, d, width), *shapes[1:]]
        out = place_call(
            self.backlog.sums, [jax.ShapeDtypeStruct(x, jnp.float32) for x in shapes], targets
        )
        return (out[0].transpose(0, 2, 1, 3), *out[1:])

    def finish(self, copied, split):
        rows = copied.shape[0] * copied.shape[1]
        v = jnp.concatenate([copied.reshape(rows, -1), jnp.zeros((-rows % 8, self.D), jnp.float32)])
        v, u = finish_call(9, v, split.reshape(8, -1), self.backlog.take(1000))
        return v[:rows].reshape(copied.shape), u.reshape(split.shape)


class Plain:
    def __init__(self, T, D):
        self.T, self.D = T, D
        self.ffn, self.attn = {}, {}

    def start(self, x, gain, bias, shift, out_grad, weights):
        self.first = layer_norm(x.astype(jnp.float32), gain, bias).astype(jnp.bfloat16)
        self.out_grad = out_grad
        low = jnp.bfloat16
        gathered = []
        for l in range(weights[0].shape[0]):
            project, dense, up, down = (x[l].astype(low) for x in weights)
            project = project.reshape(project.shape[0], -1)
            gathered.append(
                (
                    lax.all_gather(project, "dp", axis=0, tiled=True),
                    lax.all_gather(dense, "dp", axis=0),
                    lax.all_gather(up, "dp", axis=0, tiled=True),
                    lax.all_gather(down, "dp", axis=0),
                )
            )
        self.weights = gathered

    def project(self, l, normed, shift):
        w = self.weights[l][0]
        full = gather_all(normed if l else self.first)
        return full, (nn(full, w) + shift).astype(jnp.bfloat16)

    def attend(self, l, project, slopes):
        return attend_fwd(0, project, slopes, NO_Z)

    def dense(self, l, context):
        return gather_sum(nn(context, side_by_side(self.weights[l][1])))

    def up(self, l, normed, shift):
        w = self.weights[l][2]
        full = gather_all(normed)
        return full, *gelu_both(nn(full, w) + shift)

    def down(self, l, active):
        return gather_sum(nn(active, side_by_side(self.weights[l][3])))

    def last_down(self, l, active, slope):
        return self.down(l, active), *self.down_back(l, self.out_grad, slope)

    def down_back(self, l, grad, slope):
        full = gather_all(grad)
        g = (nt(full, side_by_side(self.weights[l][3])) * slope.astype(jnp.float32)).astype(jnp.bfloat16)
        return full, g, jnp.sum(g.astype(jnp.float32), axis=0, keepdims=True)

    def up_back(self, l, grad_hidden, active, normed, grad_down):
        Z = lax.axis_size("dp")
        F = grad_hidden.shape[1]
        d = self.D // Z
        up = jnp.einsum("td,tf->df", normed, grad_hidden, preferred_element_type=jnp.float32)
        down = jnp.einsum(
            "tf,tzd->zfd", active, grad_down.reshape(-1, Z, d), preferred_element_type=jnp.float32
        )
        packed = jnp.concatenate([down, up.reshape(Z, d * F // d, d)], axis=1)
        self.ffn[l] = reduce_dp(packed).astype(jnp.float32)
        return gather_sum(nt(grad_hidden, self.weights[l][2]))

    def ffn_grads(self, l):
        summed = self.ffn[l]
        d = summed.shape[1]
        F = summed.shape[0] // 2
        return summed[F:].reshape(d, F), summed[:F]

    def dense_back(self, l, grad):
        full = gather_all(grad)
        return full, nt(full, side_by_side(self.weights[l][1])).astype(jnp.bfloat16)

    def attend_back(self, l, project, grad_context, context, log_norms, slopes):
        return attend_bwd(0, project, grad_context, context, log_norms, slopes, NO_Z)

    def project_back(self, l, grad_project, context, grad_branch, normed):
        w = self.weights[l][0]
        S, T, width = grad_project.shape
        Z = lax.axis_size("dp")
        d = self.D // Z
        dense = jnp.einsum(
            "ti,tzd->zid", context, grad_branch.reshape(T, Z, d), preferred_element_type=jnp.float32
        )
        project = jnp.einsum(
            "td,sti->dsi", normed, grad_project, preferred_element_type=jnp.float32
        )
        packed = jnp.concatenate(
            [dense.reshape(Z, -1), project.reshape(Z, -1)], axis=1
        ).reshape(Z, -1, width)
        part = sum(nt(grad_project[s], w[:, s * width : (s + 1) * width]) for s in range(S))
        self.attn[l] = reduce_dp(packed).astype(jnp.float32)
        return gather_sum(part)

    def attn_grads(self, l):
        d = self.D // lax.axis_size("dp")
        rows, width = self.attn[l].shape
        flat = self.attn[l].reshape(-1)
        return flat[width * d :].reshape(d, 3, width), flat[: width * d].reshape(width, d)

    def matrix_grads(self, shapes):
        grads = [(*self.attn_grads(l), *self.ffn_grads(l)) for l in range(shapes[0][0])]
        return tuple(jnp.stack(parts) for parts in zip(*grads))

    def finish(self, copied, split):
        return lax.psum(copied, ("dp", "mp")), lax.psum(split, "dp")


def shards(
    inputs,
    out_grad,
    project_weight,
    dense_weight,
    up_weight,
    down_weight,
    project_bias,
    up_bias,
    norm_gain,
    norm_bias,
    output_bias,
):
    tensor_size = lax.axis_size("mp")
    tensor_rank = lax.axis_index("mp")
    row_count, model_width = inputs.shape
    total_rows = row_count * tensor_size
    inner_width = project_weight.shape[3]
    heads_here = N_HEADS // tensor_size
    layer_count = project_weight.shape[0]
    slopes = 2.0 ** (
        -8.0
        * (tensor_rank * heads_here + lax.iota(jnp.int32, heads_here) + 1).astype(jnp.float32)
        / N_HEADS
    )
    low = jnp.bfloat16
    fast = tensor_size == 8 and lax.axis_size("dp") == 4 and row_count == 256
    ops = (Fast if fast else Plain)(total_rows, model_width)
    stream = inputs.astype(jnp.float32)
    none = jnp.zeros((inner_width,), jnp.float32)
    shifts = [
        jnp.concatenate([project_bias[l, 0], none, project_bias[l, 1]]) for l in range(layer_count)
    ]
    weights = (project_weight, dense_weight, up_weight, down_weight)
    ops.start(inputs, norm_gain[0, 0], norm_bias[0, 0], shifts[0], out_grad, weights)
    normed = None
    stored = []
    for l in range(layer_count):
        if l:
            normed = layer_norm(stream, norm_gain[l, 0], norm_bias[l, 0]).astype(low)
        normed_all, project = ops.project(l, normed, shifts[l])
        context, log_norms = ops.attend(l, project, slopes)
        middle = stream + ops.dense(l, context) + output_bias[l, 0]
        normed2 = layer_norm(middle, norm_gain[l, 1], norm_bias[l, 1]).astype(low)
        normed2_all, active, slope = ops.up(l, normed2, up_bias[l])
        stored.append(
            (stream, normed_all, project, log_norms, context, middle, normed2_all, active, slope)
        )
        if l < layer_count - 1:
            stream = middle + ops.down(l, active) + output_bias[l, 1]
    grad = out_grad.astype(jnp.float32)
    copied = [None] * layer_count
    split = [None] * layer_count
    for l in reversed(range(layer_count)):
        last = l == layer_count - 1
        stream_in, normed_all, project, log_norms, context, middle, normed2_all, active, slope = (
            stored[l]
        )
        down_bias_grad = jnp.sum(grad, axis=0)
        if last:
            rows_out, grad_down, grad_hidden, up_bias_part = ops.last_down(l, active, slope)
            outputs = (middle + rows_out + output_bias[l, 1]).astype(low)
        else:
            grad_down, grad_hidden, up_bias_part = ops.down_back(l, grad.astype(low), slope)
        grad_normed2 = ops.up_back(l, grad_hidden, active, normed2_all, grad_down)
        norm_back = jax.vjp(layer_norm, middle, norm_gain[l, 1], norm_bias[l, 1])[1]
        grad_from_norm, gain_second, shift_second = norm_back(grad_normed2)
        grad_middle = grad + grad_from_norm
        dense_bias_grad = jnp.sum(grad_middle, axis=0)
        grad_branch, grad_context = ops.dense_back(l, grad_middle.astype(low))
        grad_project, project_bias_part = ops.attend_back(
            l, project, grad_context, context, log_norms, slopes
        )
        grad_normed = ops.project_back(l, grad_project, context, grad_branch, normed_all)
        norm_back = jax.vjp(layer_norm, stream_in, norm_gain[l, 0], norm_bias[l, 0])[1]
        grad_from_norm, gain_first, shift_first = norm_back(grad_normed)
        grad = grad_middle + grad_from_norm
        copied[l] = jnp.stack(
            [gain_first, gain_second, shift_first, shift_second, dense_bias_grad, down_bias_grad]
        )
        split[l] = jnp.concatenate([project_bias_part.reshape(-1), up_bias_part.reshape(-1)])
    copied, split = ops.finish(jnp.stack(copied), jnp.stack(split))
    matrix_grads = ops.matrix_grads([x.shape for x in weights])
    return (
        outputs,
        grad,
        *matrix_grads,
        split[:, : 2 * inner_width].reshape(layer_count, 2, inner_width),
        split[:, 2 * inner_width :],
        copied[:, 0:2],
        copied[:, 2:4],
        copied[:, 4:6],
    )


def solution(mesh):
    rows = P(("dp", "mp"), None)
    specs = (P(None, "dp", None, "mp"), P(None, "mp", "dp"), P(None, "dp", "mp"), P(None, "mp", "dp"))
    biases = (P(None, None, "mp"), P(None, "mp"), P(), P(), P())
    return jax.shard_map(
        shards,
        mesh=mesh,
        in_specs=(rows, rows, *specs, *biases),
        out_specs=(rows, rows, *specs, *biases),
        check_vma=False,
    )
```

```python
import functools

import jax
import jax.numpy as jnp
from jax import lax
from jax.experimental import pallas as pl
from jax.experimental.pallas import tpu as pltpu
from jax.sharding import PartitionSpec as P

N_HEADS = 16
BLOCK = 256
HEAD = 128
LOG2E = 1.4426950408889634
MESH = pl.DeviceIdType.MESH
NT_DIMS = (((1,), (1,)), ((), ()))
norm_eps = 1e-05


def nt(a, b):
    return lax.dot_general(a, b, NT_DIMS, preferred_element_type=jnp.float32)


def nn(a, b):
    return jnp.dot(a, b, preferred_element_type=jnp.float32)


def layer_norm(values, scale_row, shift_row):
    centre = jnp.mean(values, axis=-1, keepdims=True)
    centred = values - centre
    spread = jnp.mean(centred * centred, axis=-1, keepdims=True)
    return centred * lax.rsqrt(spread + norm_eps) * scale_row + shift_row


def peers():
    me = lax.axis_index("mp")
    core = me % 2
    bx = (me // 2) % 2
    by = me // 4
    return me, core, bx, by, me + 1 - 2 * core, me + 2 - 4 * bx, me + 4 - 8 * by


def owner(rel, core, bx, by):
    c = core if rel % 2 == 0 else 1 - core
    x = bx if (rel // 2) % 2 == 0 else 1 - bx
    y = by if rel // 4 == 0 else 1 - by
    return y * 4 + x * 2 + c


def z_peers():
    z = lax.axis_index("dp")
    z1 = z + 1 - 2 * (z % 2)
    return z, z1, (z + 2) % 4, (z1 + 2) % 4


def enter(partner, xn, yn, z=False):
    barrier = pltpu.get_barrier_semaphore()
    for n in (partner, xn, yn):
        pl.semaphore_signal(barrier, inc=1, device_id={"mp": n}, device_id_type=MESH)
    if z:
        _, z1, z2, _ = z_peers()
        for n in (z1, z2):
            pl.semaphore_signal(barrier, inc=1, device_id={"dp": n}, device_id_type=MESH)
    pl.semaphore_wait(barrier, 5 if z else 3)


ZR = 128


class ZSum:
    ahead = 3

    def __init__(self, plan, srcs, out, scratch):
        self.plan, self.srcs, self.out = plan, srcs, out[0]
        self.recv, self.own, self.send_sem, self.recv_sem, self.loc = scratch
        self.z, self.z1, self.z2, self.z3 = z_peers()
        self.sent, self.begun = [], False
        self.events = [functools.partial(self.event, c) for c in range(len(plan))]

    def block(self, c, z):
        i, row = self.plan[c]
        return self.srcs[i].at[z, pl.ds(row, ZR), :]

    def remote(self, src, kind, c, target):
        return pltpu.make_async_remote_copy(
            src_ref=src,
            dst_ref=self.recv.at[kind, c],
            send_sem=self.send_sem.at[kind, c],
            recv_sem=self.recv_sem.at[kind, c],
            device_id={"dp": target},
            device_id_type=MESH,
        )

    def push(self, *args):
        c = self.remote(*args)
        c.start()
        self.sent.append(c)

    def here(self, kind, c):
        return pltpu.make_async_copy(
            self.block(c, self.z2 if kind else self.z), self.own.at[kind, c], self.loc.at[kind, c]
        )

    def arrive(self, kind, c):
        self.remote(self.own.at[0, c], kind, c, self.z1).wait_recv()

    def start(self):
        self.begun = True
        for c in range(min(self.ahead, len(self.plan))):
            self.push(self.block(c, self.z3), 1, c, self.z1)
        for c in range(len(self.plan)):
            self.here(1, c).start()
            self.here(0, c).start()

    def event(self, c):
        if c + self.ahead < len(self.plan):
            n = c + self.ahead
            self.push(self.block(n, self.z3), 1, n, self.z1)
        self.arrive(1, c)
        self.here(1, c).wait()

        @pl.loop(0, ZR // 16)
        def _(i):
            rows = pl.ds(pl.multiple_of(i * 16, 16), 16)
            self.own[1, c, rows, :] = (
                self.own[1, c, rows, :].astype(jnp.float32)
                + self.recv[1, c, rows, :].astype(jnp.float32)
            ).astype(jnp.bfloat16)

        self.push(self.own.at[1, c], 2, c, self.z2)
        self.push(self.block(c, self.z1), 0, c, self.z1)

    def tick(self, n=1):
        n = min(n, len(self.events)) if self.begun else 0
        for _ in range(n):
            self.events.pop(0)()
        return n > 0

    def finish(self):
        self.tick(len(self.events))
        for c in range(len(self.plan)):
            self.here(0, c).wait()
            self.arrive(0, c)
            self.arrive(2, c)

            @pl.loop(0, ZR // 16)
            def _(i):
                rows = pl.ds(pl.multiple_of(i * 16, 16), 16)
                to = pl.ds(pl.multiple_of(c * ZR + i * 16, 16), 16)
                self.out[to, :] = (
                    self.own[0, c, rows, :].astype(jnp.float32)
                    + self.recv[0, c, rows, :].astype(jnp.float32)
                    + self.recv[2, c, rows, :].astype(jnp.float32)
                ).astype(jnp.bfloat16)

        for c in self.sent:
            c.wait_send()


class ZGather:
    ahead = 4

    def __init__(self, plan, srcs, outs, scratch):
        self.plan, self.srcs, self.outs = plan, srcs, outs
        self.send_sem, self.recv_sem, self.loc = scratch
        self.z, self.z1, self.z2, self.z3 = z_peers()
        self.sent = []
        self.passed, self.settled = 0, 0

    def place(self, c, z):
        i, row, size, _ = self.plan[c]
        return self.outs[i].at[z, pl.ds(row, size), :]

    def own(self, c):
        i, row, size, layer = self.plan[c]
        return self.srcs[i].at[layer, pl.ds(row, size), :]

    def remote(self, src, z, kind, c, target):
        return pltpu.make_async_remote_copy(
            src_ref=src,
            dst_ref=self.place(c, z),
            send_sem=self.send_sem.at[kind, c],
            recv_sem=self.recv_sem.at[kind, c],
            device_id={"dp": target},
            device_id_type=MESH,
        )

    def push(self, *args):
        c = self.remote(*args)
        c.start()
        self.sent.append(c)

    def here(self, c):
        return pltpu.make_async_copy(self.own(c), self.place(c, self.z), self.loc.at[c])

    def start(self):
        for c in range(len(self.plan)):
            if c < self.ahead:
                self.send_own(c)
            self.here(c).start()

    def send_own(self, c):
        self.push(self.own(c), self.z, 0, c, self.z2)
        self.push(self.own(c), self.z, 1, c, self.z1)

    def event(self, c):
        if c + self.ahead < len(self.plan):
            self.send_own(c + self.ahead)
        self.remote(self.own(c), self.z2, 0, c, self.z2).wait_recv()
        self.push(self.place(c, self.z2), self.z2, 2, c, self.z1)

    def tick(self, n=1):
        n = min(n, len(self.plan) - self.passed)
        for _ in range(n):
            self.event(self.passed)
            self.passed += 1
        return n > 0

    def settle(self, n):
        self.tick(n - self.passed)
        for c in range(self.settled, n):
            self.remote(self.own(c), self.z1, 1, c, self.z1).wait_recv()
            self.remote(self.own(c), self.z3, 2, c, self.z1).wait_recv()
            self.here(c).wait()
        self.settled = n

    def finish(self):
        self.settle(len(self.plan))
        for c in self.sent:
            c.wait_send()


class NoZ:
    ahead = 0

    def start(self):
        pass

    def tick(self, n=1):
        return False

    def finish(self):
        pass


class ZCall:
    plan, arrays, out_shapes, out_space, scratch = (), (), (), pltpu.VMEM, ()

    def make(self, refs):
        return NoZ()

    def done(self, results):
        pass

    def aliases(self, first_in, first_out):
        return {}

    def counts(self):
        return len(self.arrays), len(self.out_shapes), len(self.scratch)

    def in_specs(self):
        return [pl.BlockSpec(memory_space=pl.ANY)] * len(self.arrays)

    def out_specs(self):
        return (pl.BlockSpec(memory_space=self.out_space),) * len(self.out_shapes)


def sum_scratch(n, w):
    return (
        pltpu.VMEM((3, n, ZR, w), jnp.bfloat16),
        pltpu.VMEM((2, n, ZR, w), jnp.bfloat16),
        pltpu.SemaphoreType.DMA((3, n)),
        pltpu.SemaphoreType.DMA((3, n)),
        pltpu.SemaphoreType.DMA((2, n)),
    )


class SumCall(ZCall):
    def __init__(self, backlog, limit):
        self.plan, self.arrays, self.pieces = [], [], []
        while limit and backlog.queue:
            entry = backlog.queue[0]
            key, array, row = entry
            if not any(a is array for a in self.arrays):
                self.arrays.append(array)
            i = [a is array for a in self.arrays].index(True)
            self.pieces.append((key, row))
            self.plan.append((i, row))
            limit -= 1
            entry[2] += ZR
            if entry[2] == array.shape[1]:
                backlog.queue.pop(0)
        self.backlog = backlog
        n = len(self.plan)
        if n:
            w = self.arrays[0].shape[2]
            self.out_shapes = (jax.ShapeDtypeStruct((n * ZR, w), jnp.bfloat16),)
            self.scratch = sum_scratch(n, w)

    def make(self, refs):
        i, o, _ = self.counts()
        return ZSum(self.plan, refs[:i], refs[i : i + o], refs[i + o :]) if self.plan else NoZ()

    def done(self, results):
        for n, (key, row) in enumerate(self.pieces):
            self.backlog.sums.append((key, row, results[0], n * ZR))


class Backlog:
    def __init__(self):
        self.queue, self.sums = [], []

    def add(self, key, array, summed=None):
        done = 0 if summed is None else summed.shape[0]
        self.sums += [(key, row, summed, row) for row in range(0, done, ZR)]
        self.queue.append([key, array, done])

    def take(self, limit):
        return SumCall(self, limit)


class GatherCall(ZCall):
    out_space = pl.ANY

    def __init__(self, queue, limit):
        self.queue, self.keys, self.plan = queue, [], []
        shards, begun, shapes = [], [], []
        while limit and queue.entries:
            entry = queue.entries[0]
            key, shard, row, size, layer = entry
            if key not in self.keys:
                self.keys.append(key)
                shards.append(shard)
                shapes.append(jax.ShapeDtypeStruct((4, *shard.shape[1:]), shard.dtype))
                if key in queue.arrays:
                    begun.append((len(self.keys) - 1, queue.arrays[key]))
            self.plan.append((self.keys.index(key), row, size, layer))
            limit -= 1
            entry[2] += size
            if entry[2] == shard.shape[1]:
                queue.entries.pop(0)
        self.arrays = shards + [x for _, x in begun]
        self.begun = [i for i, _ in begun]
        self.out_shapes = tuple(shapes)
        n = len(self.plan)
        self.scratch = (
            pltpu.SemaphoreType.DMA((3, n)),
            pltpu.SemaphoreType.DMA((3, n)),
            pltpu.SemaphoreType.DMA((n,)),
        )

    def aliases(self, first_in, first_out):
        n = len(self.keys)
        return {first_in + n + j: first_out + i for j, i in enumerate(self.begun)}

    def make(self, refs):
        i, o, _ = self.counts()
        return ZGather(self.plan, refs[:i], refs[i : i + o], refs[i + o :])

    def done(self, results):
        for key, array in zip(self.keys, results):
            self.queue.arrays[key] = array


class GatherQueue:
    def __init__(self):
        self.entries, self.arrays = [], {}

    def add(self, key, shard, layer, size):
        self.entries.append([key, shard, 0, size, layer])

    def take(self, limit):
        return GatherCall(self, limit) if limit and self.entries else NO_Z


NO_Z = ZCall()


def cost(flops):
    return pl.CostEstimate(flops=flops, bytes_accessed=1 << 16, transcendentals=0)


def split_refs(refs, *counts):
    parts = []
    for n in counts:
        parts.append(refs[:n])
        refs = refs[n:]
    return parts


def bias_tile(slope, first_key, first_query, keys, queries):
    kp = first_key + lax.broadcasted_iota(jnp.int32, (keys, queries), 0)
    qp = first_query + lax.broadcasted_iota(jnp.int32, (keys, queries), 1)
    return (jnp.abs(qp - kp).astype(jnp.float32)) * (-slope * LOG2E)

def scores_t(q, k, slope, i, B):
    L = (i+1)*B
    factor = q.shape[1] ** (-0.5) * LOG2E
    st = nt(k, q) * factor
    key = lax.broadcasted_iota(jnp.int32, (L, 1), 0)
    if i > 0:
        m = i * B
        kp = lax.broadcasted_iota(jnp.int32, (m, 1), 0).astype(jnp.float32)
        qp = (m + lax.broadcasted_iota(jnp.int32, (1, B), 1)).astype(jnp.float32)
        head = st[:m] - (qp - kp) * (slope * LOG2E)
        tail = st[m:] + bias_tile(slope, 0, 0, B, B)
        return head, tail
    return None, st + bias_tile(slope, 0, 0, B, B)

def enter_z(zc):
    if zc.plan:
        _, z1, z2, _ = z_peers()
        barrier = pltpu.get_barrier_semaphore()
        for n in (z1, z2):
            pl.semaphore_signal(barrier, inc=1, device_id={"dp": n}, device_id_type=MESH)
        pl.semaphore_wait(barrier, 2)


def attend_fwd_kernel(zc, slope_ref, p_ref, *refs):
    zi, zo, zs = zc.counts()
    z_in, (ctx_ref, lse_ref), z_out, (vt_ref,), z_scratch = split_refs(refs, zi, 2, zo, 1, zs)
    z = zc.make(z_in + z_out + z_scratch)
    enter_z(zc)
    z.start()
    B = BLOCK
    T, W = p_ref.shape
    H = W // (3 * HEAD)
    for h in range(H):
        q, k, v = (pl.ds((part * H + h) * HEAD, HEAD) for part in range(3))
        slope = slope_ref[h]
        vt_ref[...] = p_ref[:, v].T
        for i in range(T // B):
            L = (i + 1) * B
            head, tail = scores_t(p_ref[i * B : L, q], p_ref[:L, k], slope, i, B)
            top = jnp.max(tail, axis=0, keepdims=True)
            if head is not None:
                top = jnp.maximum(top, jnp.max(head, axis=0, keepdims=True))
            pt = jnp.exp2(tail - top)
            den = jnp.sum(pt, axis=0, keepdims=True)
            ct = nn(vt_ref[:, i * B : L], pt.astype(jnp.bfloat16))
            if head is not None:
                ph = jnp.exp2(head - top)
                den = den + jnp.sum(ph, axis=0, keepdims=True)
                ct = ct + nn(vt_ref[:, : i * B], ph.astype(jnp.bfloat16))
            ctx_ref[i * B : L, pl.ds(h * HEAD, HEAD)] = (ct / den).T.astype(ctx_ref.dtype)
            lse_ref[h, i : i + 1, :] = top + jnp.log2(den)
            if i % 4 == 3:
                z.tick()
    z.finish()


def attend_bwd_kernel(zc, slope_ref, p_ref, g_ref, c_ref, lse_ref, *refs):
    zi, zo, zs = zc.counts()
    z_in, (out_ref, sums_ref), z_out, (kt_ref, dk_ref, dv_ref), z_scratch = split_refs(
        refs, zi, 2, zo, 3, zs
    )
    z = zc.make(z_in + z_out + z_scratch)
    enter_z(zc)
    z.start()
    B = BLOCK
    T, W = p_ref.shape
    H = W // (3 * HEAD)
    n = T // B
    factor = HEAD ** (-0.5)
    ones = jnp.ones((8, HEAD), jnp.float32)
    for h in range(H):
        qc, kc, vc = (pl.ds((part * H + h) * HEAD, HEAD) for part in range(3))
        cols = pl.ds(h * HEAD, HEAD)
        slope = slope_ref[h]
        kt_ref[...] = p_ref[:, kc].T
        qsum = jnp.zeros((1, HEAD), jnp.float32)
        for i in reversed(range(n)):
            L = (i + 1) * B
            q = p_ref[i * B : L, qc]
            g = g_ref[i * B : L, cols]
            head, tail = scores_t(q, p_ref[:L, kc], slope, i, B)
            prod = g.astype(jnp.float32) * c_ref[i * B : L, cols].astype(jnp.float32)
            inner = lax.dot_general(
                ones,
                prod,
                NT_DIMS,
                preferred_element_type=jnp.float32,
                precision=lax.Precision.HIGHEST,
            )[:1]
            lse = lse_ref[h, i : i + 1, :]
            dpt = nt(p_ref[:L, vc], g)
            dqt = None
            for part, lo, hi in ((head, 0, i * B), (tail, i * B, L)):
                if part is None:
                    continue
                pt = jnp.exp2(part - lse)
                ds = (pt * (dpt[lo:hi] - inner)).astype(jnp.bfloat16)
                pt = pt.astype(jnp.bfloat16)
                dk = nn(ds, q)
                dv = nn(pt, g)
                if i == n - 1:
                    dk_ref[lo:hi, :] = dk
                    dv_ref[lo:hi, :] = dv
                else:
                    dk_ref[lo:hi, :] += dk
                    dv_ref[lo:hi, :] += dv
                t = nn(kt_ref[:, lo:hi], ds)
                dqt = t if dqt is None else dqt + t
            dq = (dqt * factor).T.astype(jnp.bfloat16)
            out_ref[0, i * B : L, cols] = dq
            qsum += jnp.sum(dq.astype(jnp.float32), axis=0, keepdims=True)
            if i % 4 == 3:
                z.tick()
        out_ref[1, :, cols] = (dk_ref[...] * factor).astype(jnp.bfloat16)
        dv = dv_ref[...].astype(jnp.bfloat16)
        out_ref[2, :, cols] = dv
        sums_ref[0:1, cols] = qsum
        sums_ref[1:2, cols] = jnp.sum(dv.astype(jnp.float32), axis=0, keepdims=True)
    z.finish()


def attend_call(kernel, cid, name, slopes, arrays, outs, scratch, z):
    vmem = pl.BlockSpec(memory_space=pltpu.VMEM)
    out = pl.pallas_call(
        functools.partial(kernel, z),
        out_shape=(*outs, *z.out_shapes),
        in_specs=[pl.BlockSpec(memory_space=pltpu.SMEM)] + [vmem] * len(arrays) + z.in_specs(),
        out_specs=(vmem,) * len(outs) + z.out_specs(),
        scratch_shapes=[*scratch, *z.scratch],
        compiler_params=pltpu.CompilerParams(
            collective_id=cid if z.plan else None,
            has_side_effects=bool(z.plan),
            vmem_limit_bytes=60 << 20,
        ),
        input_output_aliases=z.aliases(1 + len(arrays), len(outs)),
        cost_estimate=cost(1 << 20),
        name=name,
    )(slopes, *arrays, *z.arrays)
    z.done(out[len(outs) :])
    return out[: len(outs)]


def attend_fwd(cid, project, slopes, z):
    T, W = project.shape
    H = W // (3 * HEAD)
    outs = (
        jax.ShapeDtypeStruct((T, H * HEAD), jnp.bfloat16),
        jax.ShapeDtypeStruct((H, T // BLOCK, BLOCK), jnp.float32),
    )
    scratch = (pltpu.VMEM((HEAD, T), jnp.bfloat16),)
    return attend_call(attend_fwd_kernel, cid, "attend_fwd", slopes, (project,), outs, scratch, z)


def attend_bwd(cid, project, grad_context, context, lse, slopes, z):
    T, W = project.shape
    H = W // (3 * HEAD)
    outs = (
        jax.ShapeDtypeStruct((3, T, H * HEAD), jnp.bfloat16),
        jax.ShapeDtypeStruct((2, H * HEAD), jnp.float32),
    )
    scratch = (
        pltpu.VMEM((HEAD, T), jnp.bfloat16),
        pltpu.VMEM((T, HEAD), jnp.float32),
        pltpu.VMEM((T, HEAD), jnp.float32),
    )
    arrays = (project, grad_context, context, lse)
    return attend_call(attend_bwd_kernel, cid, "attend_bwd", slopes, arrays, outs, scratch, z)


class Links:
    def __init__(self, z):
        self.me, self.core, self.bx, self.by, self.partner, self.xn, self.yn = peers()
        self.z, self.late = z, NoZ()
        self.more, self.made = False, ()
        self.sent, self.kept = [], []

    def owner(self, rel):
        return owner(rel, self.core, self.bx, self.by)

    def tick(self, n=1):
        for _ in range(n):
            if not self.z.tick():
                self.late.tick()

    def finish(self):
        self.z.finish()
        self.late.finish()
        for c in self.sent:
            c.wait_send()
        for c in self.kept:
            c.wait()


def fill(steps, n):
    for _ in range(min(n, len(steps))):
        steps.pop(0)()


class Gather:
    late = 0

    def __init__(
        self, R, D, x, ins, outs, body, more=(), more_out=(), scratch=(), filler=None, C=4
    ):
        self.R, self.D, self.C, self.given = R, D, C, x is not None
        self.body, self.filler = body, filler
        self.counts = (len(ins), len(more), len(outs), len(more_out))
        self.ins = [(x, True)] * self.given + [(a, True) for a in ins] + list(more)
        low = jnp.bfloat16
        self.outs = [(jax.ShapeDtypeStruct((8 * R, D), low), False)]
        self.outs += [(o, True) for o in outs] + list(more_out)
        self.scratch = [
            pltpu.VMEM((C, 8, R // C, D), low),
            pltpu.SemaphoreType.DMA((7, C)),
            pltpu.SemaphoreType.DMA((8, C)),
            pltpu.SemaphoreType.DMA((C, 8)),
            *scratch,
        ]

    def run(self, links, x_ref, ins, outs, scratch):
        n_in, n_more, n_out, n_more_out = self.counts
        if self.given:
            x_ref, ins = ins[0], ins[1:]
        ins, more = split_refs(ins, n_in, n_more)
        (full_ref,), outs, more_out = split_refs(outs, 1, n_out, n_more_out)
        buf, send, recv, loc = scratch[:4]
        steps = self.filler(ins, more, more_out, scratch[4:]) if self.filler else []
        R, D, C, body = self.R, self.D, self.C, self.body
        rc = R // C
        partner, xn, yn, core = links.partner, links.xn, links.yn, links.core

        def copy(src, rel, k, target, sidx):
            return pltpu.make_async_remote_copy(
                src_ref=src,
                dst_ref=buf.at[k, rel],
                send_sem=send.at[sidx, k],
                recv_sem=recv.at[rel, k],
                device_id={"mp": target},
                device_id_type=MESH,
            )

        def push(src, rel, k, target, sidx):
            c = copy(src, rel, k, target, sidx)
            c.start()
            links.sent.append(c)

        def arrive(rel, k):
            copy(buf.at[k, 0], rel, k, partner, 0).wait_recv()

        def keep(src, start, size, k, rel):
            c = pltpu.make_async_copy(src, full_ref.at[pl.ds(start, size), :], loc.at[k, rel])
            c.start()
            links.kept.append(c)

        def place(rel, k):
            return pl.multiple_of(links.owner(rel) * R + k * rc, rc)

        def run(k, lo, hi):
            starts = [place(rel, k) for rel in range(lo, hi)]
            for rel, start in zip(range(lo, hi), starts):
                keep(buf.at[k, rel], start, rc, k, rel)
            body(
                False,
                lambda: buf[k, lo:hi].reshape((hi - lo) * rc, D),
                [pl.ds(start, rc) for start in starts],
                ins,
                outs,
            )

        for k in range(C):
            own = x_ref.at[pl.ds(k * rc, rc), :]
            push(own, 2, k, xn, 1)
            push(own, 4, k, yn, 2)
            push(own, 1, k, partner, 0)
        start = pl.multiple_of(links.me * R, R)
        keep(x_ref, start, R, 0, 0)
        body(True, lambda: x_ref[...], [pl.ds(start, R)], ins, outs)
        links.tick()
        fill(steps, 2)
        across = jnp.where(core == 0, xn, yn)
        for k in range(C + 2):
            if k < C:
                arrive(2, k)
                arrive(4, k)
                push(buf.at[k, 4 - 2 * core], 6, k, across, 3)
                push(buf.at[k, 2], 3, k, partner, 4)
                push(buf.at[k, 4], 5, k, partner, 5)
            if k == 0:
                starts = [place(1, j) for j in range(C)]
                for j in range(C):
                    arrive(1, j)
                    keep(buf.at[j, 1], starts[j], rc, j, 1)
                body(
                    False,
                    lambda: buf[:, 1].reshape(R, D),
                    [pl.ds(start, rc) for start in starts],
                    ins,
                    outs,
                )
            if 1 <= k <= C:
                arrive(3, k - 1)
                arrive(5, k - 1)
                run(k - 1, 2, 6)
                arrive(6, k - 1)
                push(buf.at[k - 1, 6], 7, k - 1, partner, 6)
            if k >= 2:
                arrive(7, k - 2)
                run(k - 2, 6, 8)
            links.tick()
            fill(steps, 1)
        fill(steps, len(steps))


class Scatter:
    def __init__(
        self,
        T,
        D,
        ins,
        body,
        epilogue,
        more=(),
        more_out=(),
        scratch=(),
        filler=None,
        late=0,
        C=4,
    ):
        R = T // 8
        self.R, self.D, self.C = R, D, C
        self.body, self.epilogue, self.filler, self.late = body, epilogue, filler, late
        self.n_scratch = len(scratch)
        if late:
            w = more_out[0][0].shape[2]
            more_out = [*more_out, (jax.ShapeDtypeStruct((late * ZR, w), jnp.bfloat16), True)]
            scratch = [*scratch, *sum_scratch(late, w)]
        self.counts = (len(ins), len(epilogue.ins), len(more)), (len(epilogue.outs), len(more_out))
        self.ins = [(a, True) for a in ins] + [(a, True) for a in epilogue.ins] + list(more)
        self.outs = [(o, True) for o in epilogue.outs] + list(more_out)
        self.scratch = [
            pltpu.VMEM((8, R, D), jnp.bfloat16),
            pltpu.VMEM((7, R, D), jnp.bfloat16),
            pltpu.SemaphoreType.DMA((7, C)),
            pltpu.SemaphoreType.DMA((7, C)),
            *epilogue.scratch,
            *scratch,
        ]

    def run(self, links, _, ins, outs, scratch):
        ins, end_ins, more = split_refs(ins, *self.counts[0])
        end_outs, more_out = split_refs(outs, *self.counts[1])
        (pbuf, rbuf, send, recv), end_scratch, scratch, late_scratch = split_refs(
            scratch, 4, len(self.epilogue.scratch), self.n_scratch, 5 if self.late else 0
        )
        steps = []
        if self.late:
            plan = [(0, ZR * c) for c in range(self.late)]
            links.late = ZSum(plan, more_out[:1], more_out[-1:], late_scratch)
            more_out = more_out[:-1]
        if self.filler:
            steps = self.filler(ins, more, more_out, scratch) + [links.late.start]
        R, D, C = self.R, self.D, self.C
        rc = R // C
        core, bx, by, partner = links.core, links.bx, links.by, links.partner
        dn = jnp.where(core == 0, links.yn, links.xn)
        fn = jnp.where(core == 0, links.xn, links.yn)

        def copy(src, slot, k, target):
            rows = pl.ds(k * rc, rc)
            return pltpu.make_async_remote_copy(
                src_ref=src.at[rows, :],
                dst_ref=rbuf.at[slot, rows, :],
                send_sem=send.at[slot, k],
                recv_sem=recv.at[slot, k],
                device_id={"mp": target},
                device_id_type=MESH,
            )

        def push(slot, to, target, k):
            c = copy(pbuf.at[slot], to, k, target)
            c.start()
            links.sent.append(c)

        def arrive(slot, k):
            copy(pbuf.at[0], slot, k, partner).wait_recv()

        def dest_rank(which, c):
            if which == 0:
                return (1 - by) * 4 + (1 - bx) * 2 + c
            if which == 3:
                return by * 4 + bx * 2 + c
            flip_y = (1 - c) if which == 1 else c
            y = by + flip_y * (1 - 2 * by)
            x = bx + (1 - flip_y) * (1 - 2 * bx)
            return y * 4 + x * 2 + c

        def compute(which, c, slot):
            rows = pl.ds(pl.multiple_of(dest_rank(which, c) * R, R), R)
            self.body(rows, ins, pbuf.at[slot])

        def theirs(which):
            compute(which, 1 - core, which)
            for k in range(C):
                push(which, which, partner, k)

        def add(slot, rslot, k):
            @pl.loop(0, rc // 16)
            def _(i):
                rows = pl.ds(pl.multiple_of(k * rc + i * 16, 16), 16)
                pbuf[slot, rows, :] = (
                    pbuf[slot, rows, :].astype(jnp.float32)
                    + rbuf[rslot, rows, :].astype(jnp.float32)
                ).astype(pbuf.dtype)

        def join(which):
            for k in range(C):
                arrive(which, k)
                add(4 + which, which, k)
                if which < 2:
                    push(4 + which, 4 + which, dn, k)

        theirs(0)
        compute(0, core, 4)
        theirs(1)
        join(0)
        compute(1, core, 5)
        theirs(2)
        join(1)
        compute(2, core, 6)
        theirs(3)
        join(2)
        compute(3, core, 7)
        join(3)
        links.tick(2 if links.more else 3)
        for k in range(C):
            arrive(4, k)
            add(6, 4, k)
            push(6, 6, fn, k)
            links.tick(1 if links.more else 2)
            fill(steps, 2)
        fill(steps, len(steps))
        self.epilogue.begin(end_outs, end_scratch)
        for k in range(C):
            arrive(5, k)
            arrive(6, k)

            @pl.loop(0, rc // 16)
            def _(i):
                rows = pl.ds(pl.multiple_of(k * rc + i * 16, 16), 16)
                total = (
                    pbuf[7, rows, :].astype(jnp.float32)
                    + rbuf[5, rows, :].astype(jnp.float32)
                    + rbuf[6, rows, :].astype(jnp.float32)
                )
                self.epilogue.rows(rows, total, end_ins, end_outs, end_scratch)

        links.made = end_outs
        return self.epilogue.end(end_outs, end_scratch)


class AddNorm:
    def __init__(self, stream, bias, gain, shift, keep):
        self.ins = (stream, bias[None], gain[None], shift[None])
        self.keep = keep
        low = jax.ShapeDtypeStruct(stream.shape, jnp.bfloat16)
        self.outs = (jax.ShapeDtypeStruct(stream.shape, jnp.float32),) + (low,) * keep
        self.scratch = () if keep else (pltpu.VMEM(stream.shape, jnp.bfloat16),)

    def begin(self, outs, scratch):
        pass

    def rows(self, rows, total, ins, outs, scratch):
        stream, bias, gain, shift = ins
        value = stream[rows, :].astype(jnp.float32) + total + bias[...]
        outs[0][rows, :] = value
        low = outs[1] if self.keep else scratch[0]
        low[rows, :] = layer_norm(value, gain[...], shift[...]).astype(low.dtype)

    def end(self, outs, scratch):
        return None if self.keep else scratch[0]


class AddOnly:
    scratch = ()

    def __init__(self, stream, bias):
        self.ins = (stream, bias[None])
        self.outs = (jax.ShapeDtypeStruct(stream.shape, jnp.bfloat16),)

    def begin(self, outs, scratch):
        pass

    def rows(self, rows, total, ins, outs, scratch):
        outs[0][rows, :] = (ins[0][rows, :] + total + ins[1][...]).astype(jnp.bfloat16)

    def end(self, outs, scratch):
        return None


class NormBack:
    def __init__(self, grad, values, gain):
        R, D = values.shape
        self.ins = (grad, values, gain[None])
        self.outs = (
            jax.ShapeDtypeStruct((R, D), jnp.float32),
            jax.ShapeDtypeStruct((3, D), jnp.float32),
        )
        self.scratch = (pltpu.VMEM((R, D), jnp.bfloat16), pltpu.VMEM((3, 8, D), jnp.float32))

    def begin(self, outs, scratch):
        scratch[1][...] = jnp.zeros_like(scratch[1])

    def rows(self, rows, total, ins, outs, scratch):
        grad, values, gain = ins
        v = values[rows, :].astype(jnp.float32)
        centred = v - jnp.mean(v, axis=-1, keepdims=True)
        scale = lax.rsqrt(jnp.mean(centred * centred, axis=-1, keepdims=True) + norm_eps)
        unit = centred * scale
        inner = total * gain[...]
        mean = jnp.mean(inner, axis=-1, keepdims=True)
        along = jnp.mean(inner * unit, axis=-1, keepdims=True)
        new = grad[rows, :].astype(jnp.float32) + scale * (inner - mean - unit * along)
        outs[0][rows, :] = new
        scratch[0][rows, :] = new.astype(jnp.bfloat16)
        for i, x in enumerate((total * unit, total, new)):
            scratch[1][i] += x[:8] + x[8:]

    def end(self, outs, scratch):
        outs[1][...] = jnp.sum(scratch[1][...], axis=1)
        return scratch[0]


def shared_ins(phases):
    places = []
    flat = []
    for p in phases:
        mine = []
        for x, inside in p.ins:
            at = [i for i, (y, where) in enumerate(flat) if y is x and where == inside]
            if not at:
                flat.append((x, inside))
            mine.append(at[0] if at else len(flat) - 1)
        places.append(mine)
    return flat, places


def shared_scratch(phases):
    flat, places = [], []
    for p in phases:
        mine = []
        for x in p.scratch:
            common = any(x is y for y in STREAM_SCRATCH)
            at = [i for i, y in enumerate(flat) if y is x] if common else []
            if not at:
                flat.append(x)
            mine.append(at[0] if at else len(flat) - 1)
        places.append(mine)
    return flat, places


def chain_kernel(phases, zc, n_in, in_places, n_scratch, scratch_places, *refs):
    zi, zo, zs = zc.counts()
    ins, z_in, outs, z_out, scratch, z_scratch = split_refs(
        refs, n_in, zi, sum(len(p.outs) for p in phases), zo, n_scratch, zs
    )
    z = zc.make(z_in + z_out + z_scratch)
    if isinstance(phases[0], Scatter):
        z.ahead = max(z.ahead, 6)
    links = Links(z)
    enter(links.partner, links.xn, links.yn, bool(zc.plan) or any(p.late for p in phases))
    z.start()
    rows = None
    for p, here, there in zip(phases, in_places, scratch_places):
        links.more = p is not phases[-1]
        made, outs = outs[: len(p.outs)], outs[len(p.outs) :]
        mine, held = tuple(ins[i] for i in here), tuple(scratch[i] for i in there)
        rows = p.run(links, rows, mine, made, held)
    links.finish()


def chain_call(name, cid, phases, z=NO_Z):
    vmem = pl.BlockSpec(memory_space=pltpu.VMEM)
    anywhere = pl.BlockSpec(memory_space=pl.ANY)
    spec = lambda inside: vmem if inside else anywhere
    ins, in_places = shared_ins(phases)
    scratch, scratch_places = shared_scratch(phases)
    outs = [x for p in phases for x in p.outs]
    out = pl.pallas_call(
        functools.partial(
            chain_kernel, phases, z, len(ins), in_places, len(scratch), scratch_places
        ),
        out_shape=(*(shape for shape, _ in outs), *z.out_shapes),
        in_specs=[spec(i) for _, i in ins] + z.in_specs(),
        out_specs=tuple(spec(i) for _, i in outs) + z.out_specs(),
        scratch_shapes=[*scratch, *z.scratch],
        compiler_params=pltpu.CompilerParams(
            collective_id=cid, has_side_effects=True, vmem_limit_bytes=62 << 20
        ),
        input_output_aliases=z.aliases(len(ins), len(outs)),
        cost_estimate=cost(1 << 20),
        name=name,
    )(*(x for x, _ in ins), *z.arrays)
    z.done(out[len(outs) :])
    return split_refs(out, *(len(p.outs) for p in phases))


def gather_only_kernel(C, n, n_after, zc, *refs):
    zi, zo, zs = zc.counts()
    xs, _, z_in, fulls, z_out, (send, recv, loc), z_scratch = split_refs(
        refs, n, n_after, zi, n, zo, 3, zs
    )
    R, D = xs[0].shape
    rc = R // C
    me, core, bx, by, partner, xn, yn = peers()
    z = zc.make(z_in + z_out + z_scratch)
    enter(partner, xn, yn, bool(zc.plan))
    sent = []

    def copy(src, a, k, target, rel, sidx, whose):
        rows = pl.ds(pl.multiple_of(whose * R + k * rc, rc), rc)
        return pltpu.make_async_remote_copy(
            src_ref=fulls[a].at[rows, :] if src is None else src,
            dst_ref=fulls[a].at[rows, :],
            send_sem=send.at[a, sidx, k],
            recv_sem=recv.at[a, rel, k],
            device_id={"mp": target},
            device_id_type=MESH,
        )

    def push(*args):
        c = copy(*args)
        c.start()
        sent.append(c)

    def arrive(a, k, rel):
        copy(None, a, k, partner, rel, 0, owner(rel, core, bx, by)).wait_recv()

    kept = []
    for a in range(n):
        for k in range(C):
            own = xs[a].at[pl.ds(k * rc, rc), :]
            push(own, a, k, xn, 2, 1, me)
            push(own, a, k, yn, 4, 2, me)
            push(own, a, k, partner, 1, 0, me)
        c = pltpu.make_async_copy(
            xs[a], fulls[a].at[pl.ds(pl.multiple_of(me * R, R), R), :], loc.at[a]
        )
        c.start()
        kept.append(c)
    z.start()
    across = jnp.where(core == 0, xn, yn)
    x_core = owner(2, core, bx, by)
    y_core = owner(4, core, bx, by)
    through = jnp.where(core == 0, y_core, x_core)
    steps = [(a, k) for a in range(n) for k in range(C)]
    for i in range(len(steps) + 1):
        if i < len(steps):
            a, k = steps[i]
            arrive(a, k, 2)
            arrive(a, k, 4)
            push(None, a, k, across, 6, 3, through)
            push(None, a, k, partner, 3, 4, x_core)
            push(None, a, k, partner, 5, 5, y_core)
        if i >= 1:
            a, k = steps[i - 1]
            arrive(a, k, 6)
            push(None, a, k, partner, 7, 6, owner(6, core, bx, by))
        z.tick(-(-len(zc.plan) // (len(steps) + 1)))
    for a, k in steps:
        for rel in (1, 3, 5, 7):
            arrive(a, k, rel)
    z.finish()
    for c in sent:
        c.wait_send()
    for c in kept:
        c.wait()


def gather_only(cid, xs, after=(), z=NO_Z, C=4):
    R, D = xs[0].shape
    n = len(xs)
    anywhere = pl.BlockSpec(memory_space=pl.ANY)
    out = pl.pallas_call(
        functools.partial(gather_only_kernel, C, n, len(after), z),
        out_shape=tuple(jax.ShapeDtypeStruct((8 * R, D), x.dtype) for x in xs) + tuple(z.out_shapes),
        in_specs=[anywhere] * (n + len(after)) + z.in_specs(),
        out_specs=(anywhere,) * n + z.out_specs(),
        scratch_shapes=[
            pltpu.SemaphoreType.DMA((n, 7, C)),
            pltpu.SemaphoreType.DMA((n, 8, C)),
            pltpu.SemaphoreType.DMA((n,)),
            *z.scratch,
        ],
        compiler_params=pltpu.CompilerParams(collective_id=cid, has_side_effects=True),
        input_output_aliases=z.aliases(n + len(after), n),
        cost_estimate=cost(1 << 20),
        name="gather_rows",
    )(*xs, *after, *z.arrays)
    z.done(out[n:])
    return out[:n]


def tiles(n, step, f):
    step = min(step, n)

    @pl.loop(0, n // step)
    def _(j):
        f(pl.ds(pl.multiple_of(j * step, step), step))


def put(ref, pieces, cols, value):
    at = 0
    for rows in pieces:
        ref[rows, cols] = value[at : at + rows.size]
        at += rows.size


def take(ref, pieces, cols):
    parts = [ref[rows, cols] for rows in pieces]
    return parts[0] if len(parts) == 1 else jnp.concatenate(parts, axis=0)


def project_body(first, lhs, pieces, ins, outs):
    w, shift = ins

    def f(cols):
        put(outs[0], pieces, cols, (nn(lhs(), w[:, cols]) + shift[:, cols]).astype(jnp.bfloat16))

    tiles(w.shape[1], 256, f)


def gelu_both(v):
    t = jnp.tanh(0.7978845608028654 * (v + 0.044715 * v * v * v))
    d = 0.5 * (1.0 + t) + 0.5 * v * (1.0 - t * t) * (
        0.7978845608028654 * (1.0 + 3 * 0.044715 * v * v)
    )
    return (0.5 * v * (1.0 + t)).astype(jnp.bfloat16), d.astype(jnp.bfloat16)


def up_body(first, lhs, pieces, ins, outs):
    w, shift = ins

    def f(cols):
        active, slope = gelu_both(nn(lhs(), w[:, cols]) + shift[:, cols])
        put(outs[0], pieces, cols, active)
        put(outs[1], pieces, cols, slope)

    tiles(w.shape[1], 256, f)


def wide_nt(src, w, cols):
    Z, _, d = w.shape
    total = None
    for z in range(Z):
        t = nt(src[:, z * d : (z + 1) * d], w[z, cols, :])
        total = t if total is None else total + t
    return total


def down_back_body(first, lhs, pieces, ins, outs):
    w, slope = ins

    def f(cols):
        g = wide_nt(lhs(), w, cols) * take(slope, pieces, cols).astype(jnp.float32)
        g = g.astype(jnp.bfloat16)
        put(outs[0], pieces, cols, g)
        sums = jnp.sum(g.astype(jnp.float32), axis=0, keepdims=True)
        if first:
            outs[1][:, cols] = sums
        else:
            outs[1][:, cols] += sums

    tiles(w.shape[1], 256, f)


def dense_back_body(first, lhs, pieces, ins, outs):
    (w,) = ins

    def f(cols):
        put(outs[0], pieces, cols, wide_nt(lhs(), w, cols).astype(jnp.bfloat16))

    tiles(w.shape[1], 256, f)


def row_split_body(rows, ins, out):
    a, w = ins
    Z, _, d = w.shape
    for z in range(Z):
        out[:, z * d : (z + 1) * d] = nn(a[rows, :], w[z]).astype(out.dtype)


def up_back_body(rows, ins, out):
    a, w = ins

    def f(cols):
        out[:, cols] = nt(a[rows, :], w[cols, :]).astype(out.dtype)

    tiles(w.shape[0], 512, f)


def project_back_body(rows, ins, out):
    a, w = ins
    S, _, width = a.shape

    def f(cols):
        total = None
        for s in range(S):
            t = nt(a[s, rows, :], w[cols, s * width : (s + 1) * width])
            total = t if total is None else total + t
        out[:, cols] = total.astype(out.dtype)

    tiles(w.shape[0], 512, f)


class Stream:
    def __init__(self, chunks, buf, sems, stage, out_sems):
        self.chunks, self.buf, self.sems = chunks, buf, sems
        self.stage, self.out_sems = stage, out_sems
        self.turn, self.flying = 0, [[], []]

    def fetch(self, i):
        src, j = self.chunks[i]
        w = self.buf.shape[2]
        return pltpu.make_async_copy(
            src.at[:, pl.ds(j * w, w)], self.buf.at[i % 2], self.sems.at[i % 2]
        )

    def get(self, i):
        self.fetch(i).wait()
        if i + 1 < len(self.chunks):
            self.fetch(i + 1).start()
        return self.buf.at[i % 2]

    def result(self, make, targets):
        slot = self.turn % 2
        self.turn += 1
        for c in self.flying[slot]:
            c.wait()
        make(self.stage.at[slot])
        self.flying[slot] = []
        for n, (lo, width, dest) in enumerate(targets):
            c = pltpu.make_async_copy(
                self.stage.at[slot, :, pl.ds(lo, width)], dest, self.out_sems.at[slot, n]
            )
            c.start()
            self.flying[slot].append(c)

    def drain(self):
        for slot in range(2):
            for c in self.flying[slot]:
                c.wait()
            self.flying[slot] = []


STREAM_SCRATCH = (
    pltpu.VMEM((2, 2048, 256), jnp.bfloat16),
    pltpu.SemaphoreType.DMA((2,)),
    pltpu.VMEM((2, 256, 1024), jnp.bfloat16),
    pltpu.SemaphoreType.DMA((2, 4)),
    pltpu.VMEM((256, 2048), jnp.bfloat16),
)


def tile_product(turned, right, lo, half):
    def make(tile):
        def f(cols):
            at = pl.ds(pl.multiple_of(lo + cols.start, 256), cols.size)
            tile[:, cols] = nn(turned[...], right[:, at]).astype(tile.dtype)

        tiles(half, 256, f)

    return make


def down_steps(stream, out, turned, held, held_copy, chunk, n, w):
    half = stream.stage.shape[2]
    D = held.shape[1]
    d = out.shape[2]
    steps = []

    def step(j, h):
        if h == 0:
            turned[...] = chunk(j).T
        if j == 0 and h == 0 and held_copy is not None:
            held_copy.wait()
        targets = [
            (b * d, d, out.at[h * (half // d) + b, pl.ds(j * w, w), :]) for b in range(half // d)
        ]
        stream.result(tile_product(turned, held, h * half, half), targets)

    for j in range(n):
        for h in range(D // half):
            steps.append(functools.partial(step, j, h))
    return steps


def up_steps(stream, out, turned, hidden, first, D, w):
    F = hidden.shape[1]
    d = out.shape[2]

    def step(j):
        turned[...] = stream.get(first + j)[...].T
        z, r = (j * w) // d, (j * w) % d
        targets = [(b * d, d, out.at[z, pl.ds(b * d + r, w), :]) for b in range(F // d)]
        stream.result(tile_product(turned, hidden, 0, F), targets)

    return [functools.partial(step, j) for j in range(D // w)]


def down_filler(ins, more, more_out, scratch):
    active, grad = more
    (down_out,) = more_out
    buf, sems, stage, out_sems, turned, held, held_sem = scratch
    T, F = active.shape
    D = grad.shape[1]
    w = buf.shape[2]
    n = F // w
    stream = Stream([(active, j) for j in range(n)], buf, sems, stage, out_sems)
    held_copy = pltpu.make_async_copy(grad, held, held_sem)
    stream.fetch(0).start()
    held_copy.start()
    steps = down_steps(
        stream, down_out, turned, held, held_copy, lambda j: stream.get(j)[...], n, w
    )
    return steps + [stream.drain]


def up_filler(ins, more, more_out, scratch):
    hidden, normed = more
    buf, sems, stage, out_sems, turned = scratch
    D = normed.shape[1]
    w = buf.shape[2]
    stream = Stream([(normed, j) for j in range(D // w)], buf, sems, stage, out_sems)
    stream.fetch(0).start()
    return up_steps(stream, more_out[0], turned, hidden, 0, D, w) + [stream.drain]


def last_filler(ins, more, more_out, scratch):
    active, w_down = ins
    slope, grad = more
    hidden_out, sum_out, down_out = more_out
    stage, out_sems, turned, held, held_sem = scratch
    T, F = active.shape
    w = turned.shape[0]
    stream = Stream([], None, None, stage, out_sems)
    held_copy = pltpu.make_async_copy(grad, held, held_sem)
    held_copy.start()

    def back(i):
        if i == 0:
            held_copy.wait()
        rows = pl.ds(i * BLOCK, BLOCK)
        down_back_body(
            i == 0, lambda: held[rows, :], [rows], (w_down, slope), (hidden_out, sum_out)
        )

    steps = [functools.partial(back, i) for i in range(T // BLOCK)]
    steps += down_steps(
        stream, down_out, turned, held, None, lambda j: active[:, j * w : (j + 1) * w], F // w, w
    )
    return steps + [stream.drain]


def attn_filler(ins, more, more_out, scratch):
    parts = ins[0]
    context, grad, normed = more
    (out,) = more_out
    buf, sems, stage, out_sems, turned, ctx_t = scratch
    S, T, width = parts.shape
    D = grad.shape[1]
    Z = out.shape[0]
    d = D // Z
    w = buf.shape[2]
    n = D // w
    stream = Stream(
        [(context, 0)] + [(grad, j) for j in range(n)] + [(normed, j) for j in range(n)],
        buf,
        sems,
        stage,
        out_sems,
    )
    stream.fetch(0).start()
    steps = []

    def dense(j):
        def step():
            if j == 0:
                ctx_t[...] = stream.get(0)[...].T
            right = stream.get(1 + j)

            def make(tile):
                tile[:, :w] = nn(ctx_t[...], right[...]).astype(tile.dtype)

            z, r = (j * w) // d, (j * w) % d
            stream.result(make, [(0, w, out.at[z, pl.ds(0, width), pl.ds(r, w)])])

        return step

    def project(j):
        def step():
            turned[...] = stream.get(1 + n + j)[...].T

            def make(tile):
                for s in range(S):
                    tile[:, s * width : (s + 1) * width] = nn(turned[...], parts[s]).astype(
                        tile.dtype
                    )

            z, r = (j * w) // d, (j * w) % d
            side = pl.ds(r // w * width, width)
            stream.result(
                make,
                [(s * width, width, out.at[z, pl.ds(width + s * w, w), side]) for s in range(S)],
            )

        return step

    for j in range(n):
        steps.append(dense(j))
    for j in range(n):
        steps.append(project(j))
    steps.append(stream.drain)
    return steps


class Finish:
    late = 0

    def __init__(self, v, u):
        self.ins = [(v, True), (u, True)]
        self.outs = [
            (jax.ShapeDtypeStruct(v.shape, v.dtype), True),
            (jax.ShapeDtypeStruct(u.shape, u.dtype), True),
        ]
        self.scratch = [
            pltpu.VMEM((6, *v.shape), v.dtype),
            pltpu.VMEM((6, *u.shape), u.dtype),
            pltpu.VMEM((5, *v.shape), v.dtype),
            pltpu.VMEM((5, *u.shape), u.dtype),
            pltpu.SemaphoreType.DMA((2, 5)),
            pltpu.SemaphoreType.DMA((2, 5)),
        ]

    def run(self, links, _, ins, outs, scratch):
        v_ref, u_ref = ins
        v_out, u_out = outs
        vs, us, v_in, u_in, send, recv = scratch
        _, z1, z2, _ = z_peers()
        hops = [({"mp": n}, False) for n in (links.partner, links.xn, links.yn)]
        hops += [({"dp": z1}, True), ({"dp": z2}, True)]
        vs[0] = v_ref[...]
        vs[0, 0:2, :] = links.made[1][0:2, :]
        us[3] = u_ref[...]
        for i, (target, both) in enumerate(hops):
            copies = []
            for n, (src, dst) in enumerate(((vs, v_in), (us, u_in))[: 2 if both else 1]):
                c = pltpu.make_async_remote_copy(
                    src_ref=src.at[i],
                    dst_ref=dst.at[i],
                    send_sem=send.at[n, i],
                    recv_sem=recv.at[n, i],
                    device_id=target,
                    device_id_type=MESH,
                )
                c.start()
                copies.append(c)
            links.tick(2)
            for c in copies:
                c.wait()
            vs[i + 1] = vs[i] + v_in[i]
            if both:
                us[i + 1] = us[i] + u_in[i]
        v_out[...] = vs[5]
        u_out[...] = us[5]


def place_kernel(moves, n_src, *refs):
    srcs, outs, (low, wide, in_sem, out_sem) = split_refs(refs, n_src, 4, 4)
    depth = low.shape[0]

    def fetch(i):
        s, row, _ = moves[i]
        return pltpu.make_async_copy(
            srcs[s].at[pl.ds(row, ZR), :], low.at[i % depth], in_sem.at[i % depth]
        )

    def store(i):
        _, _, targets = moves[i]
        copies = []
        for n, (o, index, lo, width) in enumerate(targets):
            copies.append(
                pltpu.make_async_copy(
                    wide.at[i % depth, :, pl.ds(lo, width)],
                    outs[o].at[index],
                    out_sem.at[i % depth, n],
                )
            )
        return copies

    for i in range(min(depth, len(moves))):
        fetch(i).start()
    for i in range(len(moves)):
        fetch(i).wait()
        if i >= depth:
            for c in store(i - depth):
                c.wait()
        wide[i % depth] = low[i % depth].astype(jnp.float32)
        for c in store(i):
            c.start()
        if i + depth < len(moves):
            fetch(i + depth).start()
    for i in range(max(0, len(moves) - depth), len(moves)):
        for c in store(i):
            c.wait()


def place_call(sums, out_shapes, targets_of):
    arrays, moves = [], []
    for key, row, array, at in sums:
        if not any(a is array for a in arrays):
            arrays.append(array)
        i = [a is array for a in arrays].index(True)
        moves.append((i, at, targets_of(key, row)))
    w = arrays[0].shape[1]
    depth = 12
    anywhere = pl.BlockSpec(memory_space=pl.ANY)
    return pl.pallas_call(
        functools.partial(place_kernel, moves, len(arrays)),
        out_shape=tuple(out_shapes),
        in_specs=[anywhere] * len(arrays),
        out_specs=(anywhere,) * len(out_shapes),
        scratch_shapes=[
            pltpu.VMEM((depth, ZR, w), jnp.bfloat16),
            pltpu.VMEM((depth, ZR, w), jnp.float32),
            pltpu.SemaphoreType.DMA((depth,)),
            pltpu.SemaphoreType.DMA((depth, 2)),
        ],
        compiler_params=pltpu.CompilerParams(vmem_limit_bytes=62 << 20),
        cost_estimate=cost(1 << 20),
        name="place",
    )(*arrays)


def first_kernel(C, zc, n_project, *refs):
    zi, zo, zs = zc.counts()
    ins, z_in, outs, z_out, scratch, z_scratch = split_refs(refs, 6, zi, 6, zo, 13, zs)
    x_ref, gain_ref, bias_ref, shift_ref, up_ref, down_ref = ins
    full_ref, project_ref, up_out, down_out = *outs[:2], outs[2:4], outs[4:6]
    x_low, w_here, w_sem, wide, low, wide_sem, low_sem, *mine = scratch
    buf, send, recv, loc, wide2, low2 = mine
    R, D = x_ref.shape
    rc = R // C
    me, core, bx, by, partner, xn, yn = peers()
    z = zc.make(z_in + z_out + z_scratch)

    pieces = []
    both = ((up_ref, up_out, wide, low, 0), (down_ref, down_out, wide2, low2, 1))
    for l in range(2):
        for ref, out, w, n, stage in both:
            size = w.shape[1]
            pieces += [
                (ref.at[l, pl.ds(r, size), :], out[l].at[pl.ds(r, size), :], w, n, stage)
                for r in range(0, ref.shape[1], size)
            ]

    def read(i):
        src, _, w, _, stage = pieces[i]
        return pltpu.make_async_copy(src, w.at[i % 2], wide_sem.at[stage, i % 2])

    def write(i):
        _, dst, _, n, stage = pieces[i]
        return pltpu.make_async_copy(n.at[i % 2], dst, low_sem.at[stage, i % 2])

    def cast(i):
        _, _, w, n, _ = pieces[i]
        read(i).wait()
        if i >= 2:
            write(i - 2).wait()
        n[i % 2] = w[i % 2].astype(n.dtype)
        write(i).start()
        if i + 2 < len(pieces):
            read(i + 2).start()

    for i in range(2):
        read(i).start()
    enter(partner, xn, yn, True)
    z.start()

    @pl.loop(0, R // 16)
    def _(i):
        rows = pl.ds(pl.multiple_of(i * 16, 16), 16)
        v = x_ref[rows, :].astype(jnp.float32)
        x_low[rows, :] = layer_norm(v, gain_ref[...], bias_ref[...]).astype(x_low.dtype)

    sent = []

    def copy(src, rel, k, target, sidx):
        return pltpu.make_async_remote_copy(
            src_ref=src,
            dst_ref=buf.at[k, rel],
            send_sem=send.at[sidx, k],
            recv_sem=recv.at[rel, k],
            device_id={"mp": target},
            device_id_type=MESH,
        )

    def push(src, rel, k, target, sidx):
        c = copy(src, rel, k, target, sidx)
        c.start()
        sent.append(c)

    def arrive(rel, k):
        copy(buf.at[k, 0], rel, k, partner, 0).wait_recv()

    for k in range(C):
        own = x_low.at[pl.ds(k * rc, rc), :]
        push(own, 2, k, xn, 1)
        push(own, 4, k, yn, 2)
        push(own, 1, k, partner, 0)
    kept = [
        pltpu.make_async_copy(
            x_low, full_ref.at[pl.ds(pl.multiple_of(me * R, R), R), :], loc.at[0, 0]
        )
    ]
    kept[0].start()
    starts = [pl.multiple_of(owner(rel, core, bx, by) * R, R) for rel in range(8)]
    across = jnp.where(core == 0, xn, yn)
    z.tick()
    for k in range(C + 1):
        if k < C:
            arrive(2, k)
            arrive(4, k)
            push(buf.at[k, 4 - 2 * core], 6, k, across, 3)
            push(buf.at[k, 2], 3, k, partner, 4)
            push(buf.at[k, 4], 5, k, partner, 5)
        if k >= 1:
            arrive(6, k - 1)
            push(buf.at[k - 1, 6], 7, k - 1, partner, 6)
        z.tick()
        for i in range(2 * k, min(2 * k + 2, len(pieces))):
            cast(i)
        z.tick()
    for k in range(C):
        for rel in range(1, 8):
            if rel in (1, 3, 5, 7):
                arrive(rel, k)
            start = pl.multiple_of(starts[rel] + k * rc, rc)
            c = pltpu.make_async_copy(
                buf.at[k, rel], full_ref.at[pl.ds(start, rc), :], loc.at[k, rel]
            )
            c.start()
            kept.append(c)
    for i in range(2 * C + 2, len(pieces)):
        cast(i)
    for i in range(len(pieces) - 2, len(pieces)):
        write(i).wait()
    z.settle(n_project)
    weights = pltpu.make_async_copy(z_out[0], w_here, w_sem)
    weights.start()
    weights.wait()
    for rel in range(8):
        rows = pl.ds(starts[rel], R)

        def f(cols, rel=rel, rows=rows):
            lhs = x_low[...] if rel == 0 else buf[:, rel].reshape(R, D)
            w = w_here[:, :, cols].reshape(D, cols.size)
            project_ref[rows, cols] = (nn(lhs, w) + shift_ref[:, cols]).astype(jnp.bfloat16)

        tiles(project_ref.shape[1], 256, f)
        z.tick()
    z.finish()
    for c in sent:
        c.wait_send()
    for c in kept:
        c.wait()


def first_call(cid, x, gain, bias, shift, up, down, z, n_project, C=4):
    R, D = x.shape
    N = shift.shape[0]
    w = z.arrays[0]
    vmem = pl.BlockSpec(memory_space=pltpu.VMEM)
    anywhere = pl.BlockSpec(memory_space=pl.ANY)
    low = jnp.bfloat16
    out = pl.pallas_call(
        functools.partial(first_kernel, C, z, n_project),
        out_shape=(
            jax.ShapeDtypeStruct((8 * R, D), low),
            jax.ShapeDtypeStruct((8 * R, N), low),
            *[jax.ShapeDtypeStruct(up.shape[1:], low)] * 2,
            *[jax.ShapeDtypeStruct(down.shape[1:], low)] * 2,
            *z.out_shapes,
        ),
        in_specs=[vmem] * 4 + [anywhere] * 2 + z.in_specs(),
        out_specs=(anywhere, vmem) + (anywhere,) * 4 + z.out_specs(),
        scratch_shapes=[
            pltpu.VMEM((R, D), low),
            pltpu.VMEM((4, *w.shape[1:]), low),
            pltpu.SemaphoreType.DMA,
            pltpu.VMEM((2, 256, up.shape[2]), jnp.float32),
            pltpu.VMEM((2, 256, up.shape[2]), low),
            pltpu.SemaphoreType.DMA((2, 2)),
            pltpu.SemaphoreType.DMA((2, 2)),
            pltpu.VMEM((C, 8, R // C, D), low),
            pltpu.SemaphoreType.DMA((7, C)),
            pltpu.SemaphoreType.DMA((8, C)),
            pltpu.SemaphoreType.DMA((C, 8)),
            pltpu.VMEM((2, 512, down.shape[2]), jnp.float32),
            pltpu.VMEM((2, 512, down.shape[2]), low),
            *z.scratch,
        ],
        compiler_params=pltpu.CompilerParams(
            collective_id=cid, has_side_effects=True, vmem_limit_bytes=60 << 20
        ),
        cost_estimate=cost(1 << 20),
        name="first",
    )(x, gain[None], bias[None], shift[None], up, down, *z.arrays)
    z.done(out[6:])
    return out[:6]


def gather_sum(part):
    return lax.psum_scatter(
        part.astype(jnp.bfloat16), "mp", scatter_dimension=0, tiled=True
    ).astype(jnp.float32)


def gather_all(x):
    return lax.all_gather(x, "mp", axis=0, tiled=True)


def side_by_side(w):
    return jnp.concatenate([w[z] for z in range(w.shape[0])], axis=1)


def reduce_dp(part):
    return lax.psum_scatter(part.astype(jnp.bfloat16), "dp", scatter_dimension=0)


class Fast:
    def __init__(self, T, D):
        self.T, self.D = T, D
        self.backlog = Backlog()
        self.rows = None

    def start(self, x, gain, bias, shift, out_grad, weights):
        project, dense, up, down = weights
        low = jnp.bfloat16
        project = project.reshape(*project.shape[:2], -1).astype(low)
        dense = dense.astype(low)
        self.weights = queue = GatherQueue()
        queue.add(("project", 0), project, 0, 64)
        n_project = project.shape[1] // 64
        rows, out, up0, up1, down0, down1 = first_call(
            0, x, gain, bias, shift, up, down, queue.take(n_project), n_project
        )
        self.first = rows, out
        for key, shard in (
            (("up", 0), up0),
            (("down", 0), down0),
            (("project", 1), project[1]),
            (("up", 1), up1),
        ):
            queue.arrays[key] = lax.all_gather(shard, "dp", axis=0)
        queue.add(("dense", 0), dense, 0, 128)
        (self.grad_rows,) = gather_only(8, (out_grad,), z=queue.take(2))
        queue.add(("dense", 1), dense, 1, 128)
        queue.add(("down", 1), down1[None], 0, 128)

    def weight(self, name, l):
        w = self.weights.arrays[name, l]
        return w.reshape(-1, w.shape[2]) if name in ("project", "up") else w

    def shape(self, width, dtype=jnp.bfloat16):
        return jax.ShapeDtypeStruct((self.T, width), dtype)

    def packed(self, rows):
        return jax.ShapeDtypeStruct((4, rows, self.D // 4), jnp.bfloat16), False

    def scatter(self, ins, body, epilogue, **more):
        return Scatter(self.T, self.D, ins, body, epilogue, **more)

    def gather(self, x, ins, outs, body, **more):
        return Gather(self.T // 8, self.D, x, ins, outs, body, **more)

    def project(self, l, shift):
        if l == 0:
            return self.first
        w = self.weight("project", l)
        phase = self.gather(self.rows, (w, shift[None]), (self.shape(w.shape[1]),), project_body)
        return chain_call("gather_project", 10 * l, [phase], self.weights.take(2))[0]

    def attend(self, l, project, slopes):
        return attend_fwd(20 + l, project, slopes, NO_Z)

    def attn_out(self, l, stream, context, bias, gain, shift, up_shift):
        phase = self.scatter(
            (context, self.weight("dense", l)), row_split_body, AddNorm(stream, bias, gain, shift, True)
        )
        z = self.weights.take(3 * l)
        ((middle, rows),) = chain_call("dense_scatter", 10 * l + 1, [phase], z)
        w = self.weight("up", l)
        shape = self.shape(w.shape[1])
        phase = self.gather(rows, (w, up_shift[None]), (shape, shape), up_body)
        z = self.weights.take(5 * l)
        return middle, *chain_call("gather_up", 10 * l + 2, [phase], z)[0]

    def ffn_out(self, l, middle, active, bias, gain, shift):
        phase = self.scatter(
            (active, self.weight("down", l)),
            row_split_body,
            AddNorm(middle, bias, gain, shift, True),
            more=((self.grad_rows, False),),
        )
        ((stream, self.rows),) = chain_call("down_scatter", 10 * l + 3, [phase])
        return stream

    def last_out(self, l, middle, active, slope, bias):
        T, F = active.shape
        grad = self.grad_rows
        phase = self.scatter(
            (active, self.weight("down", l)),
            row_split_body,
            AddOnly(middle, bias),
            more=((slope, True), (grad, False)),
            more_out=(
                (self.shape(F), True),
                (jax.ShapeDtypeStruct((1, F), jnp.float32), True),
                self.packed(F),
            ),
            scratch=(*STREAM_SCRATCH[2:], pltpu.VMEM((T, self.D), jnp.bfloat16), pltpu.SemaphoreType.DMA),
            filler=last_filler,
        )
        ((rows, grad_hidden, sums, packed),) = chain_call("last_scatter", 10 * l + 3, [phase])
        self.backlog.add(("down", l), packed)
        return rows, grad, grad_hidden, sums

    def ffn_back(self, l, grad, middle, gain, grad_hidden, active, normed, grad_down):
        T, F = active.shape
        epilogue = NormBack(grad, middle, gain)
        ins = (grad_hidden, self.weight("up", l))
        if l:
            first = self.scatter(ins, up_back_body, epilogue)
        else:
            first = self.scatter(
                ins,
                up_back_body,
                epilogue,
                more=((active, False), (grad_down, False)),
                more_out=(self.packed(F),),
                scratch=STREAM_SCRATCH
                + (pltpu.VMEM((T, self.D), jnp.bfloat16), pltpu.SemaphoreType.DMA),
                filler=down_filler,
                late=5,
            )
        w = self.weight("dense", l)
        second = self.gather(
            None,
            (w,),
            (self.shape(w.shape[1]),),
            dense_back_body,
            more=((grad_hidden, True), (normed, False)),
            more_out=(self.packed(F),),
            scratch=STREAM_SCRATCH,
            filler=up_filler,
        )
        z = self.backlog.take(8 if l else 7)
        one, two = chain_call("ffn_back", 10 * l + 5, [first, second], z)
        if not l:
            self.backlog.add(("down", l), one[2], one[3])
        self.backlog.add(("up", l), two[2])
        return one[0], one[1], two[0], two[1]

    def attend_back(self, l, project, grad_context, context, log_norms, slopes):
        z = self.backlog.take(0 if l else 2)
        return attend_bwd(22 + l, project, grad_context, context, log_norms, slopes, z)

    def project_back(self, grad, stream, gain, grad_project, l, context, grad_branch, normed, late):
        S, T, width = grad_project.shape
        return self.scatter(
            (grad_project, self.weight("project", l)),
            project_back_body,
            NormBack(grad, stream, gain),
            more=((context, False), (grad_branch, False), (normed, False)),
            more_out=(self.packed((S + 1) * width),),
            scratch=STREAM_SCRATCH + (pltpu.VMEM((width, T), jnp.bfloat16),),
            filler=attn_filler,
            late=late,
        )

    def attn_back(self, l, grad, stream, gain, grad_project, context, grad_branch, normed, slope):
        first = self.project_back(
            grad, stream, gain, grad_project, l, context, grad_branch, normed, 4
        )
        F = slope.shape[1]
        w = self.weight("down", l - 1)
        second = self.gather(
            None,
            (w, slope),
            (self.shape(F), jax.ShapeDtypeStruct((1, F), jnp.float32)),
            down_back_body,
        )
        one, two = chain_call("attn_back", 10 * l + 7, [first, second], self.backlog.take(6))
        self.backlog.add(("attn", l), one[2], one[3])
        return one[0], one[1], two

    def first_attn_back(
        self, grad, stream, gain, grad_project, context, grad_branch, normed, rows, split
    ):
        chunks = 4 * grad_project.shape[2] // ZR
        first = self.project_back(
            grad, stream, gain, grad_project, 0, context, grad_branch, normed, chunks
        )
        n = len(rows)
        v = jnp.concatenate([jnp.zeros((2, self.D), jnp.float32), jnp.stack(rows)])
        v = jnp.pad(v, ((0, -v.shape[0] % 8), (0, 0)))
        second = Finish(v, split.reshape(8, -1))
        one, two = chain_call("first_attn_back", 7, [first, second], self.backlog.take(1000))
        self.backlog.add(("attn", 0), one[2], one[3])
        return one[0], two[0][: 2 + n], two[1].reshape(split.shape)

    def matrix_grads(self, shapes):
        layers, d, parts, width = shapes[0]
        group = self.D // lax.axis_size("dp")

        def targets(key, row):
            kind, l = key
            if kind == "down":
                return [(3, (l, pl.ds(row, ZR)), 0, group)]
            if kind == "up":
                b, r = divmod(row, group)
                return [(2, (l, pl.ds(r, ZR), pl.ds(b * group, group)), 0, group)]
            if row < width:
                return [(1, (l, pl.ds(row, ZR)), 0, group)]
            s, r = divmod(row - width, width)
            return [(0, (l, s, pl.ds(h * width + r, ZR)), h * width, width) for h in range(2)]

        shapes = [(layers, parts, d, width), *shapes[1:]]
        out = place_call(
            self.backlog.sums, [jax.ShapeDtypeStruct(x, jnp.float32) for x in shapes], targets
        )
        return (out[0].transpose(0, 2, 1, 3), *out[1:])


class Plain:
    def __init__(self, T, D):
        self.T, self.D = T, D
        self.ffn, self.attn = {}, {}

    def start(self, x, gain, bias, shift, out_grad, weights):
        self.rows = layer_norm(x.astype(jnp.float32), gain, bias).astype(jnp.bfloat16)
        self.out_grad = out_grad
        low = jnp.bfloat16
        self.weights = []
        for l in range(weights[0].shape[0]):
            project, dense, up, down = (x[l].astype(low) for x in weights)
            project = project.reshape(project.shape[0], -1)
            self.weights.append(
                (
                    lax.all_gather(project, "dp", axis=0, tiled=True),
                    lax.all_gather(dense, "dp", axis=0),
                    lax.all_gather(up, "dp", axis=0, tiled=True),
                    lax.all_gather(down, "dp", axis=0),
                )
            )

    def project(self, l, shift):
        full = gather_all(self.rows)
        return full, (nn(full, self.weights[l][0]) + shift).astype(jnp.bfloat16)

    def attend(self, l, project, slopes):
        return attend_fwd(0, project, slopes, NO_Z)

    def attn_out(self, l, stream, context, bias, gain, shift, up_shift):
        middle = stream + gather_sum(nn(context, side_by_side(self.weights[l][1]))) + bias
        full = gather_all(layer_norm(middle, gain, shift).astype(jnp.bfloat16))
        return middle, full, *gelu_both(nn(full, self.weights[l][2]) + up_shift)

    def ffn_out(self, l, middle, active, bias, gain, shift):
        stream = middle + gather_sum(nn(active, side_by_side(self.weights[l][3]))) + bias
        self.rows = layer_norm(stream, gain, shift).astype(jnp.bfloat16)
        return stream

    def down_back(self, l, grad, slope):
        full = gather_all(grad)
        g = (nt(full, side_by_side(self.weights[l][3])) * slope.astype(jnp.float32)).astype(
            jnp.bfloat16
        )
        return full, g, jnp.sum(g.astype(jnp.float32), axis=0, keepdims=True)

    def last_out(self, l, middle, active, slope, bias):
        rows = middle + gather_sum(nn(active, side_by_side(self.weights[l][3]))) + bias
        return rows.astype(jnp.bfloat16), *self.down_back(l, self.out_grad, slope)

    def norm_back(self, grad, values, gain, total):
        back = jax.vjp(layer_norm, values, gain, gain)[1]
        step, gain_sum, shift_sum = back(total)
        grad = grad + step
        return grad, jnp.stack([gain_sum, shift_sum, jnp.sum(grad, axis=0)])

    def ffn_back(self, l, grad, middle, gain, grad_hidden, active, normed, grad_down):
        Z = lax.axis_size("dp")
        F = grad_hidden.shape[1]
        d = self.D // Z
        up = jnp.einsum("td,tf->df", normed, grad_hidden, preferred_element_type=jnp.float32)
        down = jnp.einsum(
            "tf,tzd->zfd", active, grad_down.reshape(-1, Z, d), preferred_element_type=jnp.float32
        )
        self.ffn[l] = reduce_dp(up.reshape(Z, d, F)), reduce_dp(down)
        total = gather_sum(nt(grad_hidden, self.weights[l][2]))
        grad, sums = self.norm_back(grad, middle, gain, total)
        full = gather_all(grad.astype(jnp.bfloat16))
        return grad, sums, full, nt(full, side_by_side(self.weights[l][1])).astype(jnp.bfloat16)

    def attend_back(self, l, project, grad_context, context, log_norms, slopes):
        return attend_bwd(0, project, grad_context, context, log_norms, slopes, NO_Z)

    def project_back(self, l, grad, stream, gain, grad_project, context, grad_branch, normed):
        S, T, width = grad_project.shape
        w = self.weights[l][0]
        Z = lax.axis_size("dp")
        d = self.D // Z
        dense = jnp.einsum(
            "ti,tzd->zid", context, grad_branch.reshape(T, Z, d), preferred_element_type=jnp.float32
        )
        project = jnp.einsum(
            "td,sti->dsi", normed, grad_project, preferred_element_type=jnp.float32
        )
        self.attn[l] = reduce_dp(project.reshape(Z, d, S, width)), reduce_dp(dense)
        part = sum(nt(grad_project[s], w[:, s * width : (s + 1) * width]) for s in range(S))
        return self.norm_back(grad, stream, gain, gather_sum(part))

    def attn_back(self, l, grad, stream, gain, grad_project, context, grad_branch, normed, slope):
        grad, sums = self.project_back(
            l, grad, stream, gain, grad_project, context, grad_branch, normed
        )
        return grad, sums, self.down_back(l - 1, grad.astype(jnp.bfloat16), slope)

    def first_attn_back(
        self, grad, stream, gain, grad_project, context, grad_branch, normed, rows, split
    ):
        grad, sums = self.project_back(
            0, grad, stream, gain, grad_project, context, grad_branch, normed
        )
        rows = jnp.concatenate([sums[:2], jnp.stack(rows)])
        return grad, lax.psum(rows, ("dp", "mp")), lax.psum(split, "dp")

    def matrix_grads(self, shapes):
        grads = [(*self.attn[l], *self.ffn[l]) for l in range(shapes[0][0])]
        return tuple(jnp.stack(parts).astype(jnp.float32) for parts in zip(*grads))


def shards(
    inputs,
    out_grad,
    project_weight,
    dense_weight,
    up_weight,
    down_weight,
    project_bias,
    up_bias,
    norm_gain,
    norm_bias,
    output_bias,
):
    tensor_size = lax.axis_size("mp")
    tensor_rank = lax.axis_index("mp")
    row_count, model_width = inputs.shape
    total_rows = row_count * tensor_size
    inner_width = project_weight.shape[3]
    heads_here = N_HEADS // tensor_size
    layer_count = project_weight.shape[0]
    slopes = 2.0 ** (
        -8.0
        * (tensor_rank * heads_here + lax.iota(jnp.int32, heads_here) + 1).astype(jnp.float32)
        / N_HEADS
    )
    fast = tensor_size == 8 and lax.axis_size("dp") == 4 and row_count == 256
    ops = (Fast if fast else Plain)(total_rows, model_width)
    none = jnp.zeros((inner_width,), jnp.float32)
    shifts = [
        jnp.concatenate([project_bias[l, 0], none, project_bias[l, 1]]) for l in range(layer_count)
    ]
    weights = (project_weight, dense_weight, up_weight, down_weight)
    ops.start(inputs, norm_gain[0, 0], norm_bias[0, 0], shifts[0], out_grad, weights)
    stream = inputs.astype(jnp.float32)
    last = layer_count - 1
    stored = []
    for l in range(layer_count):
        normed_all, project = ops.project(l, shifts[l])
        context, log_norms = ops.attend(l, project, slopes)
        middle, normed2_all, active, slope = ops.attn_out(
            l,
            stream,
            context,
            output_bias[l, 0],
            norm_gain[l, 1],
            norm_bias[l, 1],
            up_bias[l],
        )
        stored.append(
            (stream, normed_all, project, log_norms, context, middle, normed2_all, active, slope)
        )
        if l < last:
            stream = ops.ffn_out(
                l, middle, active, output_bias[l, 1], norm_gain[l + 1, 0], norm_bias[l + 1, 0]
            )
    outputs, *step = ops.last_out(last, middle, active, slope, output_bias[last, 1])
    grad = out_grad.astype(jnp.float32)
    down_bias_grad = jnp.sum(grad, axis=0)
    sums = [None] * layer_count
    split = [None] * layer_count
    for l in reversed(range(layer_count)):
        stream, normed_all, project, log_norms, context, middle, normed2_all, active, _ = stored[l]
        grad_down, grad_hidden, up_bias_part = step
        grad, second, grad_branch, grad_context = ops.ffn_back(
            l, grad, middle, norm_gain[l, 1], grad_hidden, active, normed2_all, grad_down
        )
        grad_project, project_bias_part = ops.attend_back(
            l, project, grad_context, context, log_norms, slopes
        )
        sums[l] = [second[0], second[1], second[2], down_bias_grad]
        split[l] = jnp.concatenate([project_bias_part.reshape(-1), up_bias_part.reshape(-1)])
        args = (grad, stream, norm_gain[l, 0], grad_project, context, grad_branch, normed_all)
        if l:
            grad, first, step = ops.attn_back(l, *args, stored[l - 1][-1])
            sums[l] += [first[0], first[1]]
            down_bias_grad = first[2]
    rows = sums[0] + [x for parts in sums[1:] for x in parts]
    grad, total, split = ops.first_attn_back(*args, rows, jnp.stack(split))
    parts = [jnp.concatenate([total[2:6], total[:2]])]
    parts += [total[6 * l : 6 * l + 6] for l in range(1, layer_count)]
    copied = jnp.stack([jnp.stack([p[4], p[0], p[5], p[1], p[2], p[3]]) for p in parts])
    return (
        outputs,
        grad,
        *ops.matrix_grads([x.shape for x in weights]),
        split[:, : 2 * inner_width].reshape(layer_count, 2, inner_width),
        split[:, 2 * inner_width :],
        copied[:, 0:2],
        copied[:, 2:4],
        copied[:, 4:6],
    )


def solution(mesh):
    rows = P(("dp", "mp"), None)
    specs = (P(None, "dp", None, "mp"), P(None, "mp", "dp"), P(None, "dp", "mp"), P(None, "mp", "dp"))
    biases = (P(None, None, "mp"), P(None, "mp"), P(), P(), P())
    return jax.shard_map(
        shards,
        mesh=mesh,
        in_specs=(rows, rows, *specs, *biases),
        out_specs=(rows, rows, *specs, *biases),
        check_vma=False,
    )
```

```python
import functools

import jax
import jax.numpy as jnp
from jax import lax
from jax.experimental import pallas as pl
from jax.experimental.pallas import tpu as pltpu
from jax.sharding import PartitionSpec as P

N_HEADS = 16
BLOCK = 256
HEAD = 128
LOG2E = 1.4426950408889634
MESH = pl.DeviceIdType.MESH
NT_DIMS = (((1,), (1,)), ((), ()))
norm_eps = 1e-05


def nt(a, b):
    return lax.dot_general(a, b, NT_DIMS, preferred_element_type=jnp.float32)


def nn(a, b):
    return jnp.dot(a, b, preferred_element_type=jnp.float32)


def layer_norm(values, scale_row, shift_row):
    centre = jnp.mean(values, axis=-1, keepdims=True)
    centred = values - centre
    spread = jnp.mean(centred * centred, axis=-1, keepdims=True)
    return centred * lax.rsqrt(spread + norm_eps) * scale_row + shift_row


def peers():
    me = lax.axis_index("mp")
    core = me % 2
    bx = (me // 2) % 2
    by = me // 4
    return me, core, bx, by, me + 1 - 2 * core, me + 2 - 4 * bx, me + 4 - 8 * by


def owner(rel, core, bx, by):
    c = core if rel % 2 == 0 else 1 - core
    x = bx if (rel // 2) % 2 == 0 else 1 - bx
    y = by if rel // 4 == 0 else 1 - by
    return y * 4 + x * 2 + c


def z_peers():
    z = lax.axis_index("dp")
    z1 = z + 1 - 2 * (z % 2)
    return z, z1, (z + 2) % 4, (z1 + 2) % 4


def enter(partner, xn, yn, z=False):
    barrier = pltpu.get_barrier_semaphore()
    for n in (partner, xn, yn):
        pl.semaphore_signal(barrier, inc=1, device_id={"mp": n}, device_id_type=MESH)
    if z:
        _, z1, z2, _ = z_peers()
        for n in (z1, z2):
            pl.semaphore_signal(barrier, inc=1, device_id={"dp": n}, device_id_type=MESH)
    pl.semaphore_wait(barrier, 5 if z else 3)


ZR = 128


class ZSum:
    ahead = 3

    def __init__(self, plan, srcs, out, scratch):
        self.plan, self.srcs, self.out = plan, srcs, out[0]
        self.recv, self.own, self.send_sem, self.recv_sem, self.loc = scratch
        self.z, self.z1, self.z2, self.z3 = z_peers()
        self.sent, self.begun = [], False
        self.events = [functools.partial(self.event, c) for c in range(len(plan))]

    def block(self, c, z):
        i, row = self.plan[c]
        return self.srcs[i].at[z, pl.ds(row, ZR), :]

    def remote(self, src, kind, c, target):
        return pltpu.make_async_remote_copy(
            src_ref=src,
            dst_ref=self.recv.at[kind, c],
            send_sem=self.send_sem.at[kind, c],
            recv_sem=self.recv_sem.at[kind, c],
            device_id={"dp": target},
            device_id_type=MESH,
        )

    def push(self, *args):
        c = self.remote(*args)
        c.start()
        self.sent.append(c)

    def here(self, kind, c):
        return pltpu.make_async_copy(
            self.block(c, self.z2 if kind else self.z), self.own.at[kind, c], self.loc.at[kind, c]
        )

    def arrive(self, kind, c):
        self.remote(self.own.at[0, c], kind, c, self.z1).wait_recv()

    def start(self):
        self.begun = True
        for c in range(min(self.ahead, len(self.plan))):
            self.push(self.block(c, self.z3), 1, c, self.z1)
        for c in range(len(self.plan)):
            self.here(1, c).start()
            self.here(0, c).start()

    def event(self, c):
        if c + self.ahead < len(self.plan):
            n = c + self.ahead
            self.push(self.block(n, self.z3), 1, n, self.z1)
        self.arrive(1, c)
        self.here(1, c).wait()

        @pl.loop(0, ZR // 16)
        def _(i):
            rows = pl.ds(pl.multiple_of(i * 16, 16), 16)
            self.own[1, c, rows, :] = (
                self.own[1, c, rows, :].astype(jnp.float32)
                + self.recv[1, c, rows, :].astype(jnp.float32)
            ).astype(jnp.bfloat16)

        self.push(self.own.at[1, c], 2, c, self.z2)
        self.push(self.block(c, self.z1), 0, c, self.z1)

    def tick(self, n=1):
        n = min(n, len(self.events)) if self.begun else 0
        for _ in range(n):
            self.events.pop(0)()
        return n > 0

    def finish(self):
        self.tick(len(self.events))
        for c in range(len(self.plan)):
            self.here(0, c).wait()
            self.arrive(0, c)
            self.arrive(2, c)

            @pl.loop(0, ZR // 16)
            def _(i):
                rows = pl.ds(pl.multiple_of(i * 16, 16), 16)
                to = pl.ds(pl.multiple_of(c * ZR + i * 16, 16), 16)
                self.out[to, :] = (
                    self.own[0, c, rows, :].astype(jnp.float32)
                    + self.recv[0, c, rows, :].astype(jnp.float32)
                    + self.recv[2, c, rows, :].astype(jnp.float32)
                ).astype(jnp.bfloat16)

        for c in self.sent:
            c.wait_send()


class ZGather:
    ahead = 4

    def __init__(self, plan, srcs, outs, scratch):
        self.plan, self.srcs, self.outs = plan, srcs, outs
        self.send_sem, self.recv_sem, self.loc = scratch
        self.z, self.z1, self.z2, self.z3 = z_peers()
        self.sent = []
        self.passed, self.settled = 0, 0

    def place(self, c, z):
        i, row, size, _ = self.plan[c]
        return self.outs[i].at[z, pl.ds(row, size), :]

    def own(self, c):
        i, row, size, layer = self.plan[c]
        return self.srcs[i].at[layer, pl.ds(row, size), :]

    def remote(self, src, z, kind, c, target):
        return pltpu.make_async_remote_copy(
            src_ref=src,
            dst_ref=self.place(c, z),
            send_sem=self.send_sem.at[kind, c],
            recv_sem=self.recv_sem.at[kind, c],
            device_id={"dp": target},
            device_id_type=MESH,
        )

    def push(self, *args):
        c = self.remote(*args)
        c.start()
        self.sent.append(c)

    def here(self, c):
        return pltpu.make_async_copy(self.own(c), self.place(c, self.z), self.loc.at[c])

    def start(self):
        for c in range(len(self.plan)):
            if c < self.ahead:
                self.send_own(c)
            self.here(c).start()

    def send_own(self, c):
        self.push(self.own(c), self.z, 0, c, self.z2)
        self.push(self.own(c), self.z, 1, c, self.z1)

    def event(self, c):
        if c + self.ahead < len(self.plan):
            self.send_own(c + self.ahead)
        self.remote(self.own(c), self.z2, 0, c, self.z2).wait_recv()
        self.push(self.place(c, self.z2), self.z2, 2, c, self.z1)

    def tick(self, n=1):
        n = min(n, len(self.plan) - self.passed)
        for _ in range(n):
            self.event(self.passed)
            self.passed += 1
        return n > 0

    def settle(self, n):
        self.tick(n - self.passed)
        for c in range(self.settled, n):
            self.remote(self.own(c), self.z1, 1, c, self.z1).wait_recv()
            self.remote(self.own(c), self.z3, 2, c, self.z1).wait_recv()
            self.here(c).wait()
        self.settled = n

    def finish(self):
        self.settle(len(self.plan))
        for c in self.sent:
            c.wait_send()


class NoZ:
    ahead = 0

    def start(self):
        pass

    def tick(self, n=1):
        return False

    def finish(self):
        pass


class ZCall:
    plan, arrays, out_shapes, out_space, scratch = (), (), (), pltpu.VMEM, ()

    def make(self, refs):
        return NoZ()

    def done(self, results):
        pass

    def aliases(self, first_in, first_out):
        return {}

    def counts(self):
        return len(self.arrays), len(self.out_shapes), len(self.scratch)

    def in_specs(self):
        return [pl.BlockSpec(memory_space=pl.ANY)] * len(self.arrays)

    def out_specs(self):
        return (pl.BlockSpec(memory_space=self.out_space),) * len(self.out_shapes)


def sum_scratch(n, w):
    return (
        pltpu.VMEM((3, n, ZR, w), jnp.bfloat16),
        pltpu.VMEM((2, n, ZR, w), jnp.bfloat16),
        pltpu.SemaphoreType.DMA((3, n)),
        pltpu.SemaphoreType.DMA((3, n)),
        pltpu.SemaphoreType.DMA((2, n)),
    )


class SumCall(ZCall):
    def __init__(self, backlog, limit):
        self.plan, self.arrays, self.pieces = [], [], []
        while limit and backlog.queue:
            entry = backlog.queue[0]
            key, array, row = entry
            if not any(a is array for a in self.arrays):
                self.arrays.append(array)
            i = [a is array for a in self.arrays].index(True)
            self.pieces.append((key, row))
            self.plan.append((i, row))
            limit -= 1
            entry[2] += ZR
            if entry[2] == array.shape[1]:
                backlog.queue.pop(0)
        self.backlog = backlog
        n = len(self.plan)
        if n:
            w = self.arrays[0].shape[2]
            self.out_shapes = (jax.ShapeDtypeStruct((n * ZR, w), jnp.bfloat16),)
            self.scratch = sum_scratch(n, w)

    def make(self, refs):
        i, o, _ = self.counts()
        return ZSum(self.plan, refs[:i], refs[i : i + o], refs[i + o :]) if self.plan else NoZ()

    def done(self, results):
        for n, (key, row) in enumerate(self.pieces):
            self.backlog.sums.append((key, row, results[0], n * ZR))


class Backlog:
    def __init__(self):
        self.queue, self.sums = [], []

    def add(self, key, array, summed=None):
        done = 0 if summed is None else summed.shape[0]
        self.sums += [(key, row, summed, row) for row in range(0, done, ZR)]
        self.queue.append([key, array, done])

    def take(self, limit):
        return SumCall(self, limit)


class GatherCall(ZCall):
    out_space = pl.ANY

    def __init__(self, queue, limit):
        self.queue, self.keys, self.plan = queue, [], []
        shards, begun, shapes = [], [], []
        while limit and queue.entries:
            entry = queue.entries[0]
            key, shard, row, size, layer = entry
            if key not in self.keys:
                self.keys.append(key)
                shards.append(shard)
                shapes.append(jax.ShapeDtypeStruct((4, *shard.shape[1:]), shard.dtype))
                if key in queue.arrays:
                    begun.append((len(self.keys) - 1, queue.arrays[key]))
            self.plan.append((self.keys.index(key), row, size, layer))
            limit -= 1
            entry[2] += size
            if entry[2] == shard.shape[1]:
                queue.entries.pop(0)
        self.arrays = shards + [x for _, x in begun]
        self.begun = [i for i, _ in begun]
        self.out_shapes = tuple(shapes)
        n = len(self.plan)
        self.scratch = (
            pltpu.SemaphoreType.DMA((3, n)),
            pltpu.SemaphoreType.DMA((3, n)),
            pltpu.SemaphoreType.DMA((n,)),
        )

    def aliases(self, first_in, first_out):
        n = len(self.keys)
        return {first_in + n + j: first_out + i for j, i in enumerate(self.begun)}

    def make(self, refs):
        i, o, _ = self.counts()
        return ZGather(self.plan, refs[:i], refs[i : i + o], refs[i + o :])

    def done(self, results):
        for key, array in zip(self.keys, results):
            self.queue.arrays[key] = array


class GatherQueue:
    def __init__(self):
        self.entries, self.arrays = [], {}

    def add(self, key, shard, layer, size):
        self.entries.append([key, shard, 0, size, layer])

    def take(self, limit):
        return GatherCall(self, limit) if limit and self.entries else NO_Z


NO_Z = ZCall()


def cost(flops):
    return pl.CostEstimate(flops=flops, bytes_accessed=1 << 16, transcendentals=0)


def split_refs(refs, *counts):
    parts = []
    for n in counts:
        parts.append(refs[:n])
        refs = refs[n:]
    return parts


def bias_tile(slope, first_key, first_query, keys, queries):
    kp = first_key + lax.broadcasted_iota(jnp.int32, (keys, queries), 0)
    qp = first_query + lax.broadcasted_iota(jnp.int32, (keys, queries), 1)
    return (jnp.abs(qp - kp).astype(jnp.float32)) * (-slope * LOG2E)

def scores_t(q, k, slope, i, B):
    L = (i+1)*B
    factor = q.shape[1] ** (-0.5) * LOG2E
    st = nt(k, q) * factor
    key = lax.broadcasted_iota(jnp.int32, (L, 1), 0)
    if i > 0:
        m = i * B
        kp = lax.broadcasted_iota(jnp.int32, (m, 1), 0).astype(jnp.float32)
        qp = (m + lax.broadcasted_iota(jnp.int32, (1, B), 1)).astype(jnp.float32)
        head = st[:m] - (qp - kp) * (slope * LOG2E)
        tail = st[m:] + bias_tile(slope, 0, 0, B, B)
        return head, tail
    return None, st + bias_tile(slope, 0, 0, B, B)

def enter_z(zc):
    if zc.plan:
        _, z1, z2, _ = z_peers()
        barrier = pltpu.get_barrier_semaphore()
        for n in (z1, z2):
            pl.semaphore_signal(barrier, inc=1, device_id={"dp": n}, device_id_type=MESH)
        pl.semaphore_wait(barrier, 2)


def attend_fwd_kernel(zc, slope_ref, p_ref, *refs):
    zi, zo, zs = zc.counts()
    z_in, (ctx_ref, lse_ref), z_out, (vt_ref,), z_scratch = split_refs(refs, zi, 2, zo, 1, zs)
    z = zc.make(z_in + z_out + z_scratch)
    enter_z(zc)
    z.start()
    B = BLOCK
    T, W = p_ref.shape
    H = W // (3 * HEAD)
    for h in range(H):
        q, k, v = (pl.ds((part * H + h) * HEAD, HEAD) for part in range(3))
        slope = slope_ref[h]
        vt_ref[...] = p_ref[:, v].T
        for i in range(T // B):
            L = (i + 1) * B
            head, tail = scores_t(p_ref[i * B : L, q], p_ref[:L, k], slope, i, B)
            top = jnp.max(tail, axis=0, keepdims=True)
            if head is not None:
                top = jnp.maximum(top, jnp.max(head, axis=0, keepdims=True))
            pt = jnp.exp2(tail - top)
            den = jnp.sum(pt, axis=0, keepdims=True)
            ct = nn(vt_ref[:, i * B : L], pt.astype(jnp.bfloat16))
            if head is not None:
                ph = jnp.exp2(head - top)
                den = den + jnp.sum(ph, axis=0, keepdims=True)
                ct = ct + nn(vt_ref[:, : i * B], ph.astype(jnp.bfloat16))
            ctx_ref[i * B : L, pl.ds(h * HEAD, HEAD)] = (ct / den).T.astype(ctx_ref.dtype)
            lse_ref[h, i : i + 1, :] = top + jnp.log2(den)
            if i % 4 == 3:
                z.tick()
    z.finish()


def attend_bwd_kernel(zc, slope_ref, p_ref, g_ref, c_ref, lse_ref, *refs):
    zi, zo, zs = zc.counts()
    z_in, (out_ref, sums_ref), z_out, (kt_ref, dk_ref, dv_ref), z_scratch = split_refs(
        refs, zi, 2, zo, 3, zs
    )
    z = zc.make(z_in + z_out + z_scratch)
    enter_z(zc)
    z.start()
    B = BLOCK
    T, W = p_ref.shape
    H = W // (3 * HEAD)
    n = T // B
    factor = HEAD ** (-0.5)
    ones = jnp.ones((8, HEAD), jnp.float32)
    for h in range(H):
        qc, kc, vc = (pl.ds((part * H + h) * HEAD, HEAD) for part in range(3))
        cols = pl.ds(h * HEAD, HEAD)
        slope = slope_ref[h]
        kt_ref[...] = p_ref[:, kc].T
        qsum = jnp.zeros((1, HEAD), jnp.float32)
        for i in reversed(range(n)):
            L = (i + 1) * B
            q = p_ref[i * B : L, qc]
            g = g_ref[i * B : L, cols]
            head, tail = scores_t(q, p_ref[:L, kc], slope, i, B)
            prod = g.astype(jnp.float32) * c_ref[i * B : L, cols].astype(jnp.float32)
            inner = lax.dot_general(
                ones,
                prod,
                NT_DIMS,
                preferred_element_type=jnp.float32,
                precision=lax.Precision.HIGHEST,
            )[:1]
            lse = lse_ref[h, i : i + 1, :]
            dpt = nt(p_ref[:L, vc], g)
            dqt = None
            for part, lo, hi in ((head, 0, i * B), (tail, i * B, L)):
                if part is None:
                    continue
                pt = jnp.exp2(part - lse)
                ds = (pt * (dpt[lo:hi] - inner)).astype(jnp.bfloat16)
                pt = pt.astype(jnp.bfloat16)
                dk = nn(ds, q)
                dv = nn(pt, g)
                if i == n - 1:
                    dk_ref[lo:hi, :] = dk
                    dv_ref[lo:hi, :] = dv
                else:
                    dk_ref[lo:hi, :] += dk
                    dv_ref[lo:hi, :] += dv
                t = nn(kt_ref[:, lo:hi], ds)
                dqt = t if dqt is None else dqt + t
            dq = (dqt * factor).T.astype(jnp.bfloat16)
            out_ref[0, i * B : L, cols] = dq
            qsum += jnp.sum(dq.astype(jnp.float32), axis=0, keepdims=True)
            if i % 4 == 3:
                z.tick()
        out_ref[1, :, cols] = (dk_ref[...] * factor).astype(jnp.bfloat16)
        dv = dv_ref[...].astype(jnp.bfloat16)
        out_ref[2, :, cols] = dv
        sums_ref[0:1, cols] = qsum
        sums_ref[1:2, cols] = jnp.sum(dv.astype(jnp.float32), axis=0, keepdims=True)
    z.finish()


def attend_call(kernel, cid, name, slopes, arrays, outs, scratch, z):
    vmem = pl.BlockSpec(memory_space=pltpu.VMEM)
    out = pl.pallas_call(
        functools.partial(kernel, z),
        out_shape=(*outs, *z.out_shapes),
        in_specs=[pl.BlockSpec(memory_space=pltpu.SMEM)] + [vmem] * len(arrays) + z.in_specs(),
        out_specs=(vmem,) * len(outs) + z.out_specs(),
        scratch_shapes=[*scratch, *z.scratch],
        compiler_params=pltpu.CompilerParams(
            collective_id=cid if z.plan else None,
            has_side_effects=bool(z.plan),
            vmem_limit_bytes=60 << 20,
        ),
        input_output_aliases=z.aliases(1 + len(arrays), len(outs)),
        cost_estimate=cost(1 << 20),
        name=name,
    )(slopes, *arrays, *z.arrays)
    z.done(out[len(outs) :])
    return out[: len(outs)]


def attend_fwd(cid, project, slopes, z):
    T, W = project.shape
    H = W // (3 * HEAD)
    outs = (
        jax.ShapeDtypeStruct((T, H * HEAD), jnp.bfloat16),
        jax.ShapeDtypeStruct((H, T // BLOCK, BLOCK), jnp.float32),
    )
    scratch = (pltpu.VMEM((HEAD, T), jnp.bfloat16),)
    return attend_call(attend_fwd_kernel, cid, "attend_fwd", slopes, (project,), outs, scratch, z)


def attend_bwd(cid, project, grad_context, context, lse, slopes, z):
    T, W = project.shape
    H = W // (3 * HEAD)
    outs = (
        jax.ShapeDtypeStruct((3, T, H * HEAD), jnp.bfloat16),
        jax.ShapeDtypeStruct((2, H * HEAD), jnp.float32),
    )
    scratch = (
        pltpu.VMEM((HEAD, T), jnp.bfloat16),
        pltpu.VMEM((T, HEAD), jnp.float32),
        pltpu.VMEM((T, HEAD), jnp.float32),
    )
    arrays = (project, grad_context, context, lse)
    return attend_call(attend_bwd_kernel, cid, "attend_bwd", slopes, arrays, outs, scratch, z)


class Links:
    def __init__(self, z):
        self.me, self.core, self.bx, self.by, self.partner, self.xn, self.yn = peers()
        self.z, self.late = z, NoZ()
        self.more, self.made = False, ()
        self.sent, self.kept = [], []

    def owner(self, rel):
        return owner(rel, self.core, self.bx, self.by)

    def tick(self, n=1):
        for _ in range(n):
            if not self.z.tick() and not self.late.tick():
                break

    def finish(self):
        self.z.finish()
        self.late.finish()
        for c in self.sent:
            c.wait_send()
        for c in self.kept:
            c.wait()


class Fetched:
    def __init__(self, src, ref, sem):
        self.ref, self.copy, self.here = ref, pltpu.make_async_copy(src, ref, sem), False

    def wait(self):
        if not self.here:
            self.copy.wait()
        self.here = True


def need(operands):
    for x in operands:
        if isinstance(x, Fetched):
            x.wait()
    return refs_of(operands)


def refs_of(operands):
    return tuple(x.ref if isinstance(x, Fetched) else x for x in operands)


def fill(steps, n):
    for _ in range(min(n, len(steps))):
        steps.pop(0)()


class Gather:
    late = 0

    def __init__(
        self, R, D, x, ins, outs, body, more=(), more_out=(), scratch=(), filler=None, C=4
    ):
        self.R, self.D, self.C, self.given = R, D, C, x is not None
        self.body, self.filler = body, filler
        self.counts = (len(ins), len(more), len(outs), len(more_out))
        self.ins = [(x, True)] * self.given + [(a, True) for a in ins] + list(more)
        low = jnp.bfloat16
        self.outs = [(jax.ShapeDtypeStruct((8 * R, D), low), False)]
        self.outs += [(o, True) for o in outs] + list(more_out)
        self.scratch = [
            pltpu.VMEM((C, 8, R // C, D), low),
            pltpu.SemaphoreType.DMA((7, C)),
            pltpu.SemaphoreType.DMA((8, C)),
            pltpu.SemaphoreType.DMA((C, 8)),
            *scratch,
        ]

    def run(self, links, x_ref, ins, outs, scratch):
        n_in, n_more, n_out, n_more_out = self.counts
        if self.given:
            (x_ref,), ins = need(ins[:1]), ins[1:]
        ins, more = split_refs(ins, n_in, n_more)
        (full_ref,), outs, more_out = split_refs(outs, 1, n_out, n_more_out)
        buf, send, recv, loc = scratch[:4]
        steps = []
        if self.filler:
            steps = self.filler(refs_of(ins), refs_of(more), more_out, scratch[4:])
            steps = [functools.partial(need, more)] + steps
        R, D, C, body = self.R, self.D, self.C, self.body
        rc = R // C
        partner, xn, yn, core = links.partner, links.xn, links.yn, links.core

        def copy(src, rel, k, target, sidx):
            return pltpu.make_async_remote_copy(
                src_ref=src,
                dst_ref=buf.at[k, rel],
                send_sem=send.at[sidx, k],
                recv_sem=recv.at[rel, k],
                device_id={"mp": target},
                device_id_type=MESH,
            )

        def push(src, rel, k, target, sidx):
            c = copy(src, rel, k, target, sidx)
            c.start()
            links.sent.append(c)

        def arrive(rel, k):
            copy(buf.at[k, 0], rel, k, partner, 0).wait_recv()

        def keep(src, start, size, k, rel):
            c = pltpu.make_async_copy(src, full_ref.at[pl.ds(start, size), :], loc.at[k, rel])
            c.start()
            links.kept.append(c)

        def place(rel, k):
            return pl.multiple_of(links.owner(rel) * R + k * rc, rc)

        def run(k, lo, hi):
            starts = [place(rel, k) for rel in range(lo, hi)]
            for rel, start in zip(range(lo, hi), starts):
                keep(buf.at[k, rel], start, rc, k, rel)
            body(
                False,
                lambda: buf[k, lo:hi].reshape((hi - lo) * rc, D),
                [pl.ds(start, rc) for start in starts],
                ins,
                outs,
            )

        for k in range(C):
            own = x_ref.at[pl.ds(k * rc, rc), :]
            push(own, 2, k, xn, 1)
            push(own, 4, k, yn, 2)
            push(own, 1, k, partner, 0)
        start = pl.multiple_of(links.me * R, R)
        keep(x_ref, start, R, 0, 0)
        ins = need(ins)
        body(True, lambda: x_ref[...], [pl.ds(start, R)], ins, outs)
        links.tick()
        fill(steps, 2)
        across = jnp.where(core == 0, xn, yn)
        for k in range(C + 2):
            if k < C:
                arrive(2, k)
                arrive(4, k)
                push(buf.at[k, 4 - 2 * core], 6, k, across, 3)
                push(buf.at[k, 2], 3, k, partner, 4)
                push(buf.at[k, 4], 5, k, partner, 5)
            if k == 0:
                starts = [place(1, j) for j in range(C)]
                for j in range(C):
                    arrive(1, j)
                    keep(buf.at[j, 1], starts[j], rc, j, 1)
                body(
                    False,
                    lambda: buf[:, 1].reshape(R, D),
                    [pl.ds(start, rc) for start in starts],
                    ins,
                    outs,
                )
            if 1 <= k <= C:
                arrive(3, k - 1)
                arrive(5, k - 1)
                run(k - 1, 2, 6)
                arrive(6, k - 1)
                push(buf.at[k - 1, 6], 7, k - 1, partner, 6)
            if k >= 2:
                arrive(7, k - 2)
                run(k - 2, 6, 8)
            links.tick()
            fill(steps, 1)
        fill(steps, len(steps))


class Scatter:
    def __init__(
        self,
        T,
        D,
        ins,
        body,
        epilogue,
        more=(),
        more_out=(),
        scratch=(),
        filler=None,
        late=0,
        C=4,
    ):
        R = T // 8
        self.R, self.D, self.C = R, D, C
        self.body, self.epilogue, self.filler, self.late = body, epilogue, filler, late
        self.n_scratch = len(scratch)
        if late:
            w = more_out[0][0].shape[2]
            more_out = [*more_out, (jax.ShapeDtypeStruct((late * ZR, w), jnp.bfloat16), True)]
            scratch = [*scratch, *sum_scratch(late, w)]
        self.counts = (len(ins), len(epilogue.ins), len(more)), (len(epilogue.outs), len(more_out))
        self.ins = [(a, True) for a in ins] + [(a, True) for a in epilogue.ins] + list(more)
        self.outs = [(o, True) for o in epilogue.outs] + list(more_out)
        self.scratch = [
            pltpu.VMEM((8, R, D), jnp.bfloat16),
            pltpu.VMEM((7, R, D), jnp.bfloat16),
            pltpu.SemaphoreType.DMA((7, C)),
            pltpu.SemaphoreType.DMA((7, C)),
            *epilogue.scratch,
            *scratch,
        ]

    def run(self, links, _, ins, outs, scratch):
        ins, end_ins, more = split_refs(ins, *self.counts[0])
        end_outs, more_out = split_refs(outs, *self.counts[1])
        (pbuf, rbuf, send, recv), end_scratch, scratch, late_scratch = split_refs(
            scratch, 4, len(self.epilogue.scratch), self.n_scratch, 5 if self.late else 0
        )
        steps = []
        if self.late:
            plan = [(0, ZR * c) for c in range(self.late)]
            links.late = ZSum(plan, more_out[:1], more_out[-1:], late_scratch)
            more_out = more_out[:-1]
        if self.filler:
            steps = self.filler(refs_of(ins), refs_of(more), more_out, scratch)
            steps = [functools.partial(need, more)] + steps + [links.late.start]
        ins = need(ins)
        R, D, C = self.R, self.D, self.C
        rc = R // C
        core, bx, by, partner = links.core, links.bx, links.by, links.partner
        dn = jnp.where(core == 0, links.yn, links.xn)
        fn = jnp.where(core == 0, links.xn, links.yn)

        def copy(src, slot, k, target):
            rows = pl.ds(k * rc, rc)
            return pltpu.make_async_remote_copy(
                src_ref=src.at[rows, :],
                dst_ref=rbuf.at[slot, rows, :],
                send_sem=send.at[slot, k],
                recv_sem=recv.at[slot, k],
                device_id={"mp": target},
                device_id_type=MESH,
            )

        def push(slot, to, target, k):
            c = copy(pbuf.at[slot], to, k, target)
            c.start()
            links.sent.append(c)

        def arrive(slot, k):
            copy(pbuf.at[0], slot, k, partner).wait_recv()

        def dest_rank(which, c):
            if which == 0:
                return (1 - by) * 4 + (1 - bx) * 2 + c
            if which == 3:
                return by * 4 + bx * 2 + c
            flip_y = (1 - c) if which == 1 else c
            y = by + flip_y * (1 - 2 * by)
            x = bx + (1 - flip_y) * (1 - 2 * bx)
            return y * 4 + x * 2 + c

        def compute(which, c, slot, part=0, parts=1):
            n = R // parts
            rows = pl.ds(pl.multiple_of(dest_rank(which, c) * R + part * n, n), n)
            self.body(rows, ins, pbuf.at[slot, pl.ds(part * n, n), :])

        def theirs(which, part=0, parts=1):
            compute(which, 1 - core, which, part, parts)
            for k in range(part * C // parts, (part + 1) * C // parts):
                push(which, which, partner, k)

        def add(slot, rslot, k):
            @pl.loop(0, rc // 16)
            def _(i):
                rows = pl.ds(pl.multiple_of(k * rc + i * 16, 16), 16)
                pbuf[slot, rows, :] = (
                    pbuf[slot, rows, :].astype(jnp.float32)
                    + rbuf[rslot, rows, :].astype(jnp.float32)
                ).astype(pbuf.dtype)

        def join(which, part=0, parts=1):
            for k in range(part * C // parts, (part + 1) * C // parts):
                arrive(which, k)
                add(4 + which, which, k)
                if which < 2:
                    push(4 + which, 4 + which, dn, k)

        theirs(0, 0, 2)
        theirs(0, 1, 2)
        compute(0, core, 4, 0, 2)
        compute(0, core, 4, 1, 2)
        join(0, 0, 2)
        theirs(1)
        join(0, 1, 2)
        compute(1, core, 5)
        theirs(2)
        join(1)
        compute(2, core, 6)
        theirs(3)
        join(2)
        compute(3, core, 7)
        join(3)
        links.tick(2 if links.more else 3)
        for k in range(C):
            arrive(4, k)
            add(6, 4, k)
            push(6, 6, fn, k)
            links.tick(1 if links.more else 2)
            fill(steps, 2)
        fill(steps, len(steps))
        end_ins = need(end_ins)
        self.epilogue.begin(end_outs, end_scratch)
        for k in range(C):
            arrive(5, k)
            arrive(6, k)

            @pl.loop(0, rc // 16)
            def _(i):
                rows = pl.ds(pl.multiple_of(k * rc + i * 16, 16), 16)
                total = (
                    pbuf[7, rows, :].astype(jnp.float32)
                    + rbuf[5, rows, :].astype(jnp.float32)
                    + rbuf[6, rows, :].astype(jnp.float32)
                )
                self.epilogue.rows(rows, total, end_ins, end_outs, end_scratch)

        links.made = end_outs
        return self.epilogue.end(end_outs, end_scratch)


class AddNorm:
    def __init__(self, stream, bias, gain, shift, keep):
        self.ins = (stream, bias[None], gain[None], shift[None])
        self.keep = keep
        low = jax.ShapeDtypeStruct(stream.shape, jnp.bfloat16)
        self.outs = (jax.ShapeDtypeStruct(stream.shape, jnp.float32),) + (low,) * keep
        self.scratch = () if keep else (pltpu.VMEM(stream.shape, jnp.bfloat16),)

    def begin(self, outs, scratch):
        pass

    def rows(self, rows, total, ins, outs, scratch):
        stream, bias, gain, shift = ins
        value = stream[rows, :].astype(jnp.float32) + total + bias[...]
        outs[0][rows, :] = value
        low = outs[1] if self.keep else scratch[0]
        low[rows, :] = layer_norm(value, gain[...], shift[...]).astype(low.dtype)

    def end(self, outs, scratch):
        return None if self.keep else scratch[0]


class AddOnly:
    scratch = ()

    def __init__(self, stream, bias):
        self.ins = (stream, bias[None])
        self.outs = (jax.ShapeDtypeStruct(stream.shape, jnp.bfloat16),)

    def begin(self, outs, scratch):
        pass

    def rows(self, rows, total, ins, outs, scratch):
        outs[0][rows, :] = (ins[0][rows, :] + total + ins[1][...]).astype(jnp.bfloat16)

    def end(self, outs, scratch):
        return None


class NormBack:
    def __init__(self, grad, values, gain):
        R, D = values.shape
        self.ins = (grad, values, gain[None])
        self.outs = (
            jax.ShapeDtypeStruct((R, D), jnp.float32),
            jax.ShapeDtypeStruct((3, D), jnp.float32),
        )
        self.scratch = (pltpu.VMEM((R, D), jnp.bfloat16), pltpu.VMEM((3, 8, D), jnp.float32))

    def begin(self, outs, scratch):
        scratch[1][...] = jnp.zeros_like(scratch[1])

    def rows(self, rows, total, ins, outs, scratch):
        grad, values, gain = ins
        v = values[rows, :].astype(jnp.float32)
        centred = v - jnp.mean(v, axis=-1, keepdims=True)
        scale = lax.rsqrt(jnp.mean(centred * centred, axis=-1, keepdims=True) + norm_eps)
        unit = centred * scale
        inner = total * gain[...]
        mean = jnp.mean(inner, axis=-1, keepdims=True)
        along = jnp.mean(inner * unit, axis=-1, keepdims=True)
        new = grad[rows, :].astype(jnp.float32) + scale * (inner - mean - unit * along)
        outs[0][rows, :] = new
        scratch[0][rows, :] = new.astype(jnp.bfloat16)
        for i, x in enumerate((total * unit, total, new)):
            scratch[1][i] += x[:8] + x[8:]

    def end(self, outs, scratch):
        outs[1][...] = jnp.sum(scratch[1][...], axis=1)
        return scratch[0]


def shared_ins(phases):
    places = []
    flat = []
    for p in phases:
        mine = []
        for x, inside in p.ins:
            at = [i for i, (y, where) in enumerate(flat) if y is x and where == inside]
            if not at:
                flat.append((x, inside))
            mine.append(at[0] if at else len(flat) - 1)
        places.append(mine)
    return flat, places


def shared_scratch(phases):
    flat, places = [], []
    for p in phases:
        mine = []
        for x in p.scratch:
            common = any(x is y for y in STREAM_SCRATCH)
            at = [i for i, y in enumerate(flat) if y is x] if common else []
            if not at:
                flat.append(x)
            mine.append(at[0] if at else len(flat) - 1)
        places.append(mine)
    return flat, places


def chain_kernel(phases, zc, inside, in_places, n_scratch, scratch_places, *refs):
    zi, zo, zs = zc.counts()
    n_fetch = sum(inside)
    ins, z_in, outs, z_out, scratch, z_scratch, held, sems = split_refs(
        refs,
        len(inside),
        zi,
        sum(len(p.outs) for p in phases),
        zo,
        n_scratch,
        zs,
        n_fetch,
        1,
    )
    operands, n = [], 0
    for ref, fetch in zip(ins, inside):
        operands.append(Fetched(ref, held[n], sems[0].at[n]) if fetch else ref)
        n += fetch
    for x in operands:
        if isinstance(x, Fetched):
            x.copy.start()
    z = zc.make(z_in + z_out + z_scratch)
    if isinstance(phases[0], Scatter):
        z.ahead = max(z.ahead, 6)
    links = Links(z)
    enter(links.partner, links.xn, links.yn, bool(zc.plan) or any(p.late for p in phases))
    z.start()
    rows = None
    for p, here, there in zip(phases, in_places, scratch_places):
        links.more = p is not phases[-1]
        made, outs = outs[: len(p.outs)], outs[len(p.outs) :]
        mine, room = tuple(operands[i] for i in here), tuple(scratch[i] for i in there)
        rows = p.run(links, rows, mine, made, room)
    links.finish()
    need(operands)


def chain_call(name, cid, phases, z=NO_Z):
    vmem = pl.BlockSpec(memory_space=pltpu.VMEM)
    anywhere = pl.BlockSpec(memory_space=pl.ANY)
    spec = lambda inside: vmem if inside else anywhere
    ins, in_places = shared_ins(phases)
    scratch, scratch_places = shared_scratch(phases)
    outs = [x for p in phases for x in p.outs]
    out = pl.pallas_call(
        functools.partial(
            chain_kernel,
            phases,
            z,
            [i for _, i in ins],
            in_places,
            len(scratch),
            scratch_places,
        ),
        out_shape=(*(shape for shape, _ in outs), *z.out_shapes),
        in_specs=[anywhere] * len(ins) + z.in_specs(),
        out_specs=tuple(spec(i) for _, i in outs) + z.out_specs(),
        scratch_shapes=[
            *scratch,
            *z.scratch,
            *(pltpu.VMEM(x.shape, x.dtype) for x, i in ins if i),
            pltpu.SemaphoreType.DMA((max(1, sum(i for _, i in ins)),)),
        ],
        compiler_params=pltpu.CompilerParams(
            collective_id=cid, has_side_effects=True, vmem_limit_bytes=62 << 20
        ),
        input_output_aliases=z.aliases(len(ins), len(outs)),
        cost_estimate=cost(1 << 20),
        name=name,
    )(*(x for x, _ in ins), *z.arrays)
    z.done(out[len(outs) :])
    return split_refs(out, *(len(p.outs) for p in phases))


def gather_only_kernel(C, n, n_after, zc, *refs):
    zi, zo, zs = zc.counts()
    xs, _, z_in, fulls, z_out, (send, recv, loc), z_scratch = split_refs(
        refs, n, n_after, zi, n, zo, 3, zs
    )
    R, D = xs[0].shape
    rc = R // C
    me, core, bx, by, partner, xn, yn = peers()
    z = zc.make(z_in + z_out + z_scratch)
    enter(partner, xn, yn, bool(zc.plan))
    sent = []

    def copy(src, a, k, target, rel, sidx, whose):
        rows = pl.ds(pl.multiple_of(whose * R + k * rc, rc), rc)
        return pltpu.make_async_remote_copy(
            src_ref=fulls[a].at[rows, :] if src is None else src,
            dst_ref=fulls[a].at[rows, :],
            send_sem=send.at[a, sidx, k],
            recv_sem=recv.at[a, rel, k],
            device_id={"mp": target},
            device_id_type=MESH,
        )

    def push(*args):
        c = copy(*args)
        c.start()
        sent.append(c)

    def arrive(a, k, rel):
        copy(None, a, k, partner, rel, 0, owner(rel, core, bx, by)).wait_recv()

    kept = []
    for a in range(n):
        for k in range(C):
            own = xs[a].at[pl.ds(k * rc, rc), :]
            push(own, a, k, xn, 2, 1, me)
            push(own, a, k, yn, 4, 2, me)
            push(own, a, k, partner, 1, 0, me)
        c = pltpu.make_async_copy(
            xs[a], fulls[a].at[pl.ds(pl.multiple_of(me * R, R), R), :], loc.at[a]
        )
        c.start()
        kept.append(c)
    z.start()
    across = jnp.where(core == 0, xn, yn)
    x_core = owner(2, core, bx, by)
    y_core = owner(4, core, bx, by)
    through = jnp.where(core == 0, y_core, x_core)
    steps = [(a, k) for a in range(n) for k in range(C)]
    for i in range(len(steps) + 1):
        if i < len(steps):
            a, k = steps[i]
            arrive(a, k, 2)
            arrive(a, k, 4)
            push(None, a, k, across, 6, 3, through)
            push(None, a, k, partner, 3, 4, x_core)
            push(None, a, k, partner, 5, 5, y_core)
        if i >= 1:
            a, k = steps[i - 1]
            arrive(a, k, 6)
            push(None, a, k, partner, 7, 6, owner(6, core, bx, by))
        z.tick(-(-len(zc.plan) // (len(steps) + 1)))
    for a, k in steps:
        for rel in (1, 3, 5, 7):
            arrive(a, k, rel)
    z.finish()
    for c in sent:
        c.wait_send()
    for c in kept:
        c.wait()


def gather_only(cid, xs, after=(), z=NO_Z, C=4):
    R, D = xs[0].shape
    n = len(xs)
    anywhere = pl.BlockSpec(memory_space=pl.ANY)
    out = pl.pallas_call(
        functools.partial(gather_only_kernel, C, n, len(after), z),
        out_shape=tuple(jax.ShapeDtypeStruct((8 * R, D), x.dtype) for x in xs) + tuple(z.out_shapes),
        in_specs=[anywhere] * (n + len(after)) + z.in_specs(),
        out_specs=(anywhere,) * n + z.out_specs(),
        scratch_shapes=[
            pltpu.SemaphoreType.DMA((n, 7, C)),
            pltpu.SemaphoreType.DMA((n, 8, C)),
            pltpu.SemaphoreType.DMA((n,)),
            *z.scratch,
        ],
        compiler_params=pltpu.CompilerParams(collective_id=cid, has_side_effects=True),
        input_output_aliases=z.aliases(n + len(after), n),
        cost_estimate=cost(1 << 20),
        name="gather_rows",
    )(*xs, *after, *z.arrays)
    z.done(out[n:])
    return out[:n]


def tiles(n, step, f):
    step = min(step, n)

    @pl.loop(0, n // step)
    def _(j):
        f(pl.ds(pl.multiple_of(j * step, step), step))


def put(ref, pieces, cols, value):
    at = 0
    for rows in pieces:
        ref[rows, cols] = value[at : at + rows.size]
        at += rows.size


def take(ref, pieces, cols):
    parts = [ref[rows, cols] for rows in pieces]
    return parts[0] if len(parts) == 1 else jnp.concatenate(parts, axis=0)


def project_body(first, lhs, pieces, ins, outs):
    w, shift = ins

    def f(cols):
        put(outs[0], pieces, cols, (nn(lhs(), w[:, cols]) + shift[:, cols]).astype(jnp.bfloat16))

    tiles(w.shape[1], 256, f)


def gelu_both(v):
    t = jnp.tanh(0.7978845608028654 * (v + 0.044715 * v * v * v))
    d = 0.5 * (1.0 + t) + 0.5 * v * (1.0 - t * t) * (
        0.7978845608028654 * (1.0 + 3 * 0.044715 * v * v)
    )
    return (0.5 * v * (1.0 + t)).astype(jnp.bfloat16), d.astype(jnp.bfloat16)


def up_body(first, lhs, pieces, ins, outs):
    w, shift = ins

    def f(cols):
        active, slope = gelu_both(nn(lhs(), w[:, cols]) + shift[:, cols])
        put(outs[0], pieces, cols, active)
        put(outs[1], pieces, cols, slope)

    tiles(w.shape[1], 256, f)


def wide_nt(src, w, cols):
    Z, _, d = w.shape
    total = None
    for z in range(Z):
        t = nt(src[:, z * d : (z + 1) * d], w[z, cols, :])
        total = t if total is None else total + t
    return total


def down_back_body(first, lhs, pieces, ins, outs):
    w, slope = ins

    def f(cols):
        g = wide_nt(lhs(), w, cols) * take(slope, pieces, cols).astype(jnp.float32)
        g = g.astype(jnp.bfloat16)
        put(outs[0], pieces, cols, g)
        sums = jnp.sum(g.astype(jnp.float32), axis=0, keepdims=True)
        if first:
            outs[1][:, cols] = sums
        else:
            outs[1][:, cols] += sums

    tiles(w.shape[1], 256, f)


def dense_back_body(first, lhs, pieces, ins, outs):
    (w,) = ins

    def f(cols):
        put(outs[0], pieces, cols, wide_nt(lhs(), w, cols).astype(jnp.bfloat16))

    tiles(w.shape[1], 256, f)


def row_split_body(rows, ins, out):
    a, w = ins
    Z, _, d = w.shape
    for z in range(Z):
        out[:, z * d : (z + 1) * d] = nn(a[rows, :], w[z]).astype(out.dtype)


def up_back_body(rows, ins, out):
    a, w = ins

    def f(cols):
        out[:, cols] = nt(a[rows, :], w[cols, :]).astype(out.dtype)

    tiles(w.shape[0], 512, f)


def project_back_body(rows, ins, out):
    a, w = ins
    S, _, width = a.shape

    def f(cols):
        total = None
        for s in range(S):
            t = nt(a[s, rows, :], w[cols, s * width : (s + 1) * width])
            total = t if total is None else total + t
        out[:, cols] = total.astype(out.dtype)

    tiles(w.shape[0], 512, f)


class Stream:
    def __init__(self, chunks, buf, sems, stage, out_sems):
        self.chunks, self.buf, self.sems = chunks, buf, sems
        self.stage, self.out_sems = stage, out_sems
        self.turn, self.flying = 0, [[], []]

    def fetch(self, i):
        src, j = self.chunks[i]
        w = self.buf.shape[2]
        return pltpu.make_async_copy(
            src.at[:, pl.ds(j * w, w)], self.buf.at[i % 2], self.sems.at[i % 2]
        )

    def get(self, i):
        self.fetch(i).wait()
        if i + 1 < len(self.chunks):
            self.fetch(i + 1).start()
        return self.buf.at[i % 2]

    def result(self, make, targets):
        slot = self.turn % 2
        self.turn += 1
        for c in self.flying[slot]:
            c.wait()
        make(self.stage.at[slot])
        self.flying[slot] = []
        for n, (lo, width, dest) in enumerate(targets):
            c = pltpu.make_async_copy(
                self.stage.at[slot, :, pl.ds(lo, width)], dest, self.out_sems.at[slot, n]
            )
            c.start()
            self.flying[slot].append(c)

    def drain(self):
        for slot in range(2):
            for c in self.flying[slot]:
                c.wait()
            self.flying[slot] = []


STREAM_SCRATCH = (
    pltpu.VMEM((2, 2048, 256), jnp.bfloat16),
    pltpu.SemaphoreType.DMA((2,)),
    pltpu.VMEM((2, 256, 1024), jnp.bfloat16),
    pltpu.SemaphoreType.DMA((2, 4)),
    pltpu.VMEM((256, 2048), jnp.bfloat16),
)


def tile_product(turned, right, lo, half):
    def make(tile):
        def f(cols):
            at = pl.ds(pl.multiple_of(lo + cols.start, 256), cols.size)
            tile[:, cols] = nn(turned[...], right[:, at]).astype(tile.dtype)

        tiles(half, 256, f)

    return make


def down_steps(stream, out, turned, held, held_copy, chunk, n, w):
    half = stream.stage.shape[2]
    D = held.shape[1]
    d = out.shape[2]
    steps = []

    def step(j, h):
        if h == 0:
            turned[...] = chunk(j).T
        if j == 0 and h == 0 and held_copy is not None:
            held_copy.wait()
        targets = [
            (b * d, d, out.at[h * (half // d) + b, pl.ds(j * w, w), :]) for b in range(half // d)
        ]
        stream.result(tile_product(turned, held, h * half, half), targets)

    for j in range(n):
        for h in range(D // half):
            steps.append(functools.partial(step, j, h))
    return steps


def up_steps(stream, out, turned, hidden, first, D, w):
    F = hidden.shape[1]
    d = out.shape[2]

    def step(j):
        turned[...] = stream.get(first + j)[...].T
        z, r = (j * w) // d, (j * w) % d
        targets = [(b * d, d, out.at[z, pl.ds(b * d + r, w), :]) for b in range(F // d)]
        stream.result(tile_product(turned, hidden, 0, F), targets)

    return [functools.partial(step, j) for j in range(D // w)]


def down_filler(ins, more, more_out, scratch):
    active, grad = more
    (down_out,) = more_out
    buf, sems, stage, out_sems, turned, held, held_sem = scratch
    T, F = active.shape
    D = grad.shape[1]
    w = buf.shape[2]
    n = F // w
    stream = Stream([(active, j) for j in range(n)], buf, sems, stage, out_sems)
    held_copy = pltpu.make_async_copy(grad, held, held_sem)
    stream.fetch(0).start()
    held_copy.start()
    steps = down_steps(
        stream, down_out, turned, held, held_copy, lambda j: stream.get(j)[...], n, w
    )
    return steps + [stream.drain]


def up_filler(ins, more, more_out, scratch):
    hidden, normed = more
    buf, sems, stage, out_sems, turned = scratch
    D = normed.shape[1]
    w = buf.shape[2]
    stream = Stream([(normed, j) for j in range(D // w)], buf, sems, stage, out_sems)
    stream.fetch(0).start()
    return up_steps(stream, more_out[0], turned, hidden, 0, D, w) + [stream.drain]


def last_filler(ins, more, more_out, scratch):
    active, w_down = ins
    slope, grad = more
    hidden_out, sum_out, down_out = more_out
    stage, out_sems, turned, held, held_sem = scratch
    T, F = active.shape
    w = turned.shape[0]
    stream = Stream([], None, None, stage, out_sems)
    held_copy = pltpu.make_async_copy(grad, held, held_sem)
    held_copy.start()

    def back(i):
        if i == 0:
            held_copy.wait()
        rows = pl.ds(i * BLOCK, BLOCK)
        down_back_body(
            i == 0, lambda: held[rows, :], [rows], (w_down, slope), (hidden_out, sum_out)
        )

    steps = [functools.partial(back, i) for i in range(T // BLOCK)]
    steps += down_steps(
        stream, down_out, turned, held, None, lambda j: active[:, j * w : (j + 1) * w], F // w, w
    )
    return steps + [stream.drain]


def attn_filler(ins, more, more_out, scratch):
    parts = ins[0]
    context, grad, normed = more
    (out,) = more_out
    buf, sems, stage, out_sems, turned, ctx_t = scratch
    S, T, width = parts.shape
    D = grad.shape[1]
    Z = out.shape[0]
    d = D // Z
    w = buf.shape[2]
    n = D // w
    stream = Stream(
        [(context, 0)] + [(grad, j) for j in range(n)] + [(normed, j) for j in range(n)],
        buf,
        sems,
        stage,
        out_sems,
    )
    stream.fetch(0).start()
    steps = []

    def dense(j):
        def step():
            if j == 0:
                ctx_t[...] = stream.get(0)[...].T
            right = stream.get(1 + j)

            def make(tile):
                tile[:, :w] = nn(ctx_t[...], right[...]).astype(tile.dtype)

            z, r = (j * w) // d, (j * w) % d
            stream.result(make, [(0, w, out.at[z, pl.ds(0, width), pl.ds(r, w)])])

        return step

    def project(j):
        def step():
            turned[...] = stream.get(1 + n + j)[...].T

            def make(tile):
                for s in range(S):
                    tile[:, s * width : (s + 1) * width] = nn(turned[...], parts[s]).astype(
                        tile.dtype
                    )

            z, r = (j * w) // d, (j * w) % d
            side = pl.ds(r // w * width, width)
            stream.result(
                make,
                [(s * width, width, out.at[z, pl.ds(width + s * w, w), side]) for s in range(S)],
            )

        return step

    for j in range(n):
        steps.append(dense(j))
    for j in range(n):
        steps.append(project(j))
    steps.append(stream.drain)
    return steps


class Finish:
    late = 0

    def __init__(self, v, u):
        self.ins = [(v, True), (u, True)]
        self.outs = [
            (jax.ShapeDtypeStruct(v.shape, v.dtype), True),
            (jax.ShapeDtypeStruct(u.shape, u.dtype), True),
        ]
        self.scratch = [
            pltpu.VMEM((6, *v.shape), v.dtype),
            pltpu.VMEM((6, *u.shape), u.dtype),
            pltpu.VMEM((5, *v.shape), v.dtype),
            pltpu.VMEM((5, *u.shape), u.dtype),
            pltpu.SemaphoreType.DMA((2, 5)),
            pltpu.SemaphoreType.DMA((2, 5)),
        ]

    def run(self, links, _, ins, outs, scratch):
        v_ref, u_ref = need(ins)
        v_out, u_out = outs
        vs, us, v_in, u_in, send, recv = scratch
        _, z1, z2, _ = z_peers()
        hops = [({"mp": n}, False) for n in (links.partner, links.xn, links.yn)]
        hops += [({"dp": z1}, True), ({"dp": z2}, True)]
        vs[0] = v_ref[...]
        vs[0, 0:2, :] = links.made[1][0:2, :]
        us[3] = u_ref[...]
        for i, (target, both) in enumerate(hops):
            copies = []
            for n, (src, dst) in enumerate(((vs, v_in), (us, u_in))[: 2 if both else 1]):
                c = pltpu.make_async_remote_copy(
                    src_ref=src.at[i],
                    dst_ref=dst.at[i],
                    send_sem=send.at[n, i],
                    recv_sem=recv.at[n, i],
                    device_id=target,
                    device_id_type=MESH,
                )
                c.start()
                copies.append(c)
            links.tick(2)
            for c in copies:
                c.wait()
            vs[i + 1] = vs[i] + v_in[i]
            if both:
                us[i + 1] = us[i] + u_in[i]
        v_out[...] = vs[5]
        u_out[...] = us[5]


def place_kernel(moves, n_src, *refs):
    (v, u), srcs, outs, small, (low, wide, in_sem, out_sem) = split_refs(refs, 2, n_src, 4, 5, 4)
    gain, shift, bias, of_project, of_up = small
    for l in range(gain.shape[0]):
        at = 6 * l
        order = (0, 2, 1, 3, 4, 5) if l == 0 else (at + 4, at, at + 5, at + 1, at + 2, at + 3)
        for i, ref in enumerate((gain, shift, bias)):
            for j in range(2):
                r = order[2 * i + j]
                ref[l, j : j + 1, :] = v[r : r + 1, :]
        width = of_project.shape[2]
        for j in range(2):
            of_project[l, j : j + 1, :] = u[l : l + 1, j * width : (j + 1) * width]
        of_up[l : l + 1, :] = u[l : l + 1, 2 * width :]
    depth = low.shape[0]

    def fetch(i):
        s, row, _ = moves[i]
        return pltpu.make_async_copy(
            srcs[s].at[pl.ds(row, ZR), :], low.at[i % depth], in_sem.at[i % depth]
        )

    def store(i):
        _, _, targets = moves[i]
        copies = []
        for n, (o, index, lo, width) in enumerate(targets):
            copies.append(
                pltpu.make_async_copy(
                    wide.at[i % depth, :, pl.ds(lo, width)],
                    outs[o].at[index],
                    out_sem.at[i % depth, n],
                )
            )
        return copies

    for i in range(min(depth, len(moves))):
        fetch(i).start()
    for i in range(len(moves)):
        fetch(i).wait()
        if i >= depth:
            for c in store(i - depth):
                c.wait()
        wide[i % depth] = low[i % depth].astype(jnp.float32)
        for c in store(i):
            c.start()
        if i + depth < len(moves):
            fetch(i + depth).start()
    for i in range(max(0, len(moves) - depth), len(moves)):
        for c in store(i):
            c.wait()


def place_call(sums, out_shapes, targets_of, v, u, small):
    vmem = pl.BlockSpec(memory_space=pltpu.VMEM)
    arrays, moves = [], []
    for key, row, array, at in sums:
        if not any(a is array for a in arrays):
            arrays.append(array)
        i = [a is array for a in arrays].index(True)
        moves.append((i, at, targets_of(key, row)))
    w = arrays[0].shape[1]
    depth = 12
    anywhere = pl.BlockSpec(memory_space=pl.ANY)
    return pl.pallas_call(
        functools.partial(place_kernel, moves, len(arrays)),
        out_shape=tuple(out_shapes) + tuple(small),
        in_specs=[vmem] * 2 + [anywhere] * len(arrays),
        out_specs=(anywhere,) * len(out_shapes) + (vmem,) * len(small),
        scratch_shapes=[
            pltpu.VMEM((depth, ZR, w), jnp.bfloat16),
            pltpu.VMEM((depth, ZR, w), jnp.float32),
            pltpu.SemaphoreType.DMA((depth,)),
            pltpu.SemaphoreType.DMA((depth, 2)),
        ],
        compiler_params=pltpu.CompilerParams(vmem_limit_bytes=62 << 20),
        cost_estimate=cost(1 << 20),
        name="place",
    )(v, u, *arrays)


def first_kernel(C, zc, n_project, *refs):
    zi, zo, zs = zc.counts()
    ins, z_in, outs, z_out, scratch, z_scratch = split_refs(refs, 6, zi, 6, zo, 14, zs)
    x_ref, gain_ref, bias_ref, shift_ref, up_ref, down_ref = ins
    full_ref, project_ref, up_out, down_out = *outs[:2], outs[2:4], outs[4:6]
    x_low, w_here, w_sem, wide, low, wide_sem, low_sem, *mine = scratch
    buf, send, recv, loc, wide2, low2, total_ref = mine
    R, D = x_ref.shape
    rc = R // C
    me, core, bx, by, partner, xn, yn = peers()
    z = zc.make(z_in + z_out + z_scratch)

    pieces = []
    both = ((up_ref, up_out, wide, low, 0), (down_ref, down_out, wide2, low2, 1))
    for l in range(2):
        for ref, out, w, n, stage in both:
            size = w.shape[1]
            pieces += [
                (ref.at[l, pl.ds(r, size), :], out[l].at[pl.ds(r, size), :], w, n, stage)
                for r in range(0, ref.shape[1], size)
            ]

    def read(i):
        src, _, w, _, stage = pieces[i]
        return pltpu.make_async_copy(src, w.at[i % 2], wide_sem.at[stage, i % 2])

    def write(i):
        _, dst, _, n, stage = pieces[i]
        return pltpu.make_async_copy(n.at[i % 2], dst, low_sem.at[stage, i % 2])

    def cast(i):
        _, _, w, n, _ = pieces[i]
        read(i).wait()
        if i >= 2:
            write(i - 2).wait()
        n[i % 2] = w[i % 2].astype(n.dtype)
        write(i).start()
        if i + 2 < len(pieces):
            read(i + 2).start()

    for i in range(2):
        read(i).start()
    z.ahead = n_project
    enter(partner, xn, yn, True)
    z.start()

    @pl.loop(0, R // 16)
    def _(i):
        rows = pl.ds(pl.multiple_of(i * 16, 16), 16)
        v = x_ref[rows, :].astype(jnp.float32)
        x_low[rows, :] = layer_norm(v, gain_ref[...], bias_ref[...]).astype(x_low.dtype)

    sent = []

    def copy(src, rel, k, target, sidx):
        return pltpu.make_async_remote_copy(
            src_ref=src,
            dst_ref=buf.at[k, rel],
            send_sem=send.at[sidx, k],
            recv_sem=recv.at[rel, k],
            device_id={"mp": target},
            device_id_type=MESH,
        )

    def push(src, rel, k, target, sidx):
        c = copy(src, rel, k, target, sidx)
        c.start()
        sent.append(c)

    def arrive(rel, k):
        copy(buf.at[k, 0], rel, k, partner, 0).wait_recv()

    for k in range(C):
        own = x_low.at[pl.ds(k * rc, rc), :]
        push(own, 2, k, xn, 1)
        push(own, 4, k, yn, 2)
        push(own, 1, k, partner, 0)
    kept = [
        pltpu.make_async_copy(
            x_low, full_ref.at[pl.ds(pl.multiple_of(me * R, R), R), :], loc.at[0, 0]
        )
    ]
    kept[0].start()
    starts = [pl.multiple_of(owner(rel, core, bx, by) * R, R) for rel in range(8)]
    across = jnp.where(core == 0, xn, yn)
    for k in range(C + 1):
        if k < C:
            arrive(2, k)
            arrive(4, k)
            push(buf.at[k, 4 - 2 * core], 6, k, across, 3)
            push(buf.at[k, 2], 3, k, partner, 4)
            push(buf.at[k, 4], 5, k, partner, 5)
        if k >= 1:
            arrive(6, k - 1)
            push(buf.at[k - 1, 6], 7, k - 1, partner, 6)
        for i in range(2 * k, min(2 * k + 2, len(pieces))):
            cast(i)
        z.tick((0, 0, 3, 2, 1)[k])
    for k in range(C):
        for rel in range(1, 8):
            if rel in (1, 3, 5, 7):
                arrive(rel, k)
            start = pl.multiple_of(starts[rel] + k * rc, rc)
            c = pltpu.make_async_copy(
                buf.at[k, rel], full_ref.at[pl.ds(start, rc), :], loc.at[k, rel]
            )
            c.start()
            kept.append(c)
    for i in range(2 * C + 2, len(pieces)):
        cast(i)
    for i in range(len(pieces) - 2, len(pieces)):
        write(i).wait()
    z.tick(n_project)
    Z, per, _ = w_here.shape
    parts = w_sem.shape[0]
    size = per // parts
    for p in range(parts):
        z.settle((p + 1) * n_project // parts)
        here = pl.ds(p * size, size)
        weights = pltpu.make_async_copy(z_out[0].at[:, here, :], w_here.at[:, here, :], w_sem.at[p])
        weights.start()
        weights.wait()
        for rel in range(8):
            rows = pl.ds(starts[rel], R)

            def f(cols, rel=rel, rows=rows):
                lhs = []
                for i in range(Z):
                    depth = pl.ds(i * per + p * size, size)
                    x = x_low[:, depth] if rel == 0 else buf[:, rel, :, depth].reshape(R, size)
                    lhs.append(x)
                w = w_here[:, here, cols].reshape(Z * size, cols.size)
                term = nn(jnp.concatenate(lhs, axis=1), w)
                if p > 0:
                    term = term + total_ref[rows, cols]
                if p < parts - 1:
                    total_ref[rows, cols] = term
                else:
                    project_ref[rows, cols] = (term + shift_ref[:, cols]).astype(jnp.bfloat16)

            tiles(project_ref.shape[1], 256, f)
            z.tick()
    z.finish()
    for c in sent:
        c.wait_send()
    for c in kept:
        c.wait()


def first_call(cid, x, gain, bias, shift, up, down, z, n_project, C=4):
    R, D = x.shape
    N = shift.shape[0]
    w = z.arrays[0]
    vmem = pl.BlockSpec(memory_space=pltpu.VMEM)
    anywhere = pl.BlockSpec(memory_space=pl.ANY)
    low = jnp.bfloat16
    out = pl.pallas_call(
        functools.partial(first_kernel, C, z, n_project),
        out_shape=(
            jax.ShapeDtypeStruct((8 * R, D), low),
            jax.ShapeDtypeStruct((8 * R, N), low),
            *[jax.ShapeDtypeStruct(up.shape[1:], low)] * 2,
            *[jax.ShapeDtypeStruct(down.shape[1:], low)] * 2,
            *z.out_shapes,
        ),
        in_specs=[vmem] * 4 + [anywhere] * 2 + z.in_specs(),
        out_specs=(anywhere, vmem) + (anywhere,) * 4 + z.out_specs(),
        scratch_shapes=[
            pltpu.VMEM((R, D), low),
            pltpu.VMEM((4, *w.shape[1:]), low),
            pltpu.SemaphoreType.DMA((2,)),
            pltpu.VMEM((2, 256, up.shape[2]), jnp.float32),
            pltpu.VMEM((2, 256, up.shape[2]), low),
            pltpu.SemaphoreType.DMA((2, 2)),
            pltpu.SemaphoreType.DMA((2, 2)),
            pltpu.VMEM((C, 8, R // C, D), low),
            pltpu.SemaphoreType.DMA((7, C)),
            pltpu.SemaphoreType.DMA((8, C)),
            pltpu.SemaphoreType.DMA((C, 8)),
            pltpu.VMEM((2, 512, down.shape[2]), jnp.float32),
            pltpu.VMEM((2, 512, down.shape[2]), low),
            pltpu.VMEM((8 * R, N), jnp.float32),
            *z.scratch,
        ],
        compiler_params=pltpu.CompilerParams(
            collective_id=cid, has_side_effects=True, vmem_limit_bytes=60 << 20
        ),
        cost_estimate=cost(1 << 20),
        name="first",
    )(x, gain[None], bias[None], shift[None], up, down, *z.arrays)
    z.done(out[6:])
    return out[:6]


def gather_sum(part):
    return lax.psum_scatter(
        part.astype(jnp.bfloat16), "mp", scatter_dimension=0, tiled=True
    ).astype(jnp.float32)


def gather_all(x):
    return lax.all_gather(x, "mp", axis=0, tiled=True)


def side_by_side(w):
    return jnp.concatenate([w[z] for z in range(w.shape[0])], axis=1)


def reduce_dp(part):
    return lax.psum_scatter(part.astype(jnp.bfloat16), "dp", scatter_dimension=0)


class Fast:
    def __init__(self, T, D):
        self.T, self.D = T, D
        self.backlog = Backlog()
        self.rows = None

    def start(self, x, gain, bias, shift, out_grad, weights):
        project, dense, up, down = weights
        low = jnp.bfloat16
        project = project.reshape(*project.shape[:2], -1).astype(low)
        dense = dense.astype(low)
        self.weights = queue = GatherQueue()
        queue.add(("project", 0), project, 0, 64)
        n_project = project.shape[1] // 64
        rows, out, up0, up1, down0, down1 = first_call(
            0, x, gain, bias, shift, up, down, queue.take(n_project), n_project
        )
        self.first = rows, out
        for key, shard in (
            (("up", 0), up0),
            (("down", 0), down0),
            (("project", 1), project[1]),
            (("up", 1), up1),
        ):
            queue.arrays[key] = lax.all_gather(shard, "dp", axis=0)
        queue.add(("dense", 0), dense, 0, 128)
        (self.grad_rows,) = gather_only(8, (out_grad,), z=queue.take(2))
        queue.add(("dense", 1), dense, 1, 128)
        queue.add(("down", 1), down1[None], 0, 128)

    def weight(self, name, l):
        w = self.weights.arrays[name, l]
        return w.reshape(-1, w.shape[2]) if name in ("project", "up") else w

    def shape(self, width, dtype=jnp.bfloat16):
        return jax.ShapeDtypeStruct((self.T, width), dtype)

    def packed(self, rows):
        return jax.ShapeDtypeStruct((4, rows, self.D // 4), jnp.bfloat16), False

    def scatter(self, ins, body, epilogue, **more):
        return Scatter(self.T, self.D, ins, body, epilogue, **more)

    def gather(self, x, ins, outs, body, **more):
        return Gather(self.T // 8, self.D, x, ins, outs, body, **more)

    def project(self, l, shift):
        if l == 0:
            return self.first
        w = self.weight("project", l)
        phase = self.gather(self.rows, (w, shift[None]), (self.shape(w.shape[1]),), project_body)
        return chain_call("gather_project", 10 * l, [phase], self.weights.take(2))[0]

    def attend(self, l, project, slopes):
        return attend_fwd(20 + l, project, slopes, NO_Z)

    def attn_out(self, l, stream, context, bias, gain, shift, up_shift):
        phase = self.scatter(
            (context, self.weight("dense", l)), row_split_body, AddNorm(stream, bias, gain, shift, True)
        )
        z = self.weights.take(3 * l)
        ((middle, rows),) = chain_call("dense_scatter", 10 * l + 1, [phase], z)
        w = self.weight("up", l)
        shape = self.shape(w.shape[1])
        phase = self.gather(rows, (w, up_shift[None]), (shape, shape), up_body)
        z = self.weights.take(5 * l)
        return middle, *chain_call("gather_up", 10 * l + 2, [phase], z)[0]

    def ffn_out(self, l, middle, active, bias, gain, shift):
        phase = self.scatter(
            (active, self.weight("down", l)),
            row_split_body,
            AddNorm(middle, bias, gain, shift, True),
            more=((self.grad_rows, False),),
        )
        ((stream, self.rows),) = chain_call("down_scatter", 10 * l + 3, [phase])
        return stream

    def last_out(self, l, middle, active, slope, bias):
        T, F = active.shape
        grad = self.grad_rows
        phase = self.scatter(
            (active, self.weight("down", l)),
            row_split_body,
            AddOnly(middle, bias),
            more=((slope, True), (grad, False)),
            more_out=(
                (self.shape(F), True),
                (jax.ShapeDtypeStruct((1, F), jnp.float32), True),
                self.packed(F),
            ),
            scratch=(*STREAM_SCRATCH[2:], pltpu.VMEM((T, self.D), jnp.bfloat16), pltpu.SemaphoreType.DMA),
            filler=last_filler,
        )
        ((rows, grad_hidden, sums, packed),) = chain_call("last_scatter", 10 * l + 3, [phase])
        self.backlog.add(("down", l), packed)
        return rows, grad, grad_hidden, sums

    def ffn_back(self, l, grad, middle, gain, grad_hidden, active, normed, grad_down):
        T, F = active.shape
        epilogue = NormBack(grad, middle, gain)
        ins = (grad_hidden, self.weight("up", l))
        up = dict(
            more=((grad_hidden, True), (normed, False)),
            more_out=(self.packed(F),),
            scratch=STREAM_SCRATCH,
            filler=up_filler,
        )
        down = dict(
            more=((active, False), (grad_down, False)),
            more_out=(self.packed(F),),
            scratch=STREAM_SCRATCH
            + (pltpu.VMEM((T, self.D), jnp.bfloat16), pltpu.SemaphoreType.DMA),
            filler=down_filler,
        )
        beside = dict(up, late=1) if l else dict(down, late=5)
        first = self.scatter(ins, up_back_body, epilogue, **beside)
        w = self.weight("dense", l)
        beside = {} if l else up
        second = self.gather(None, (w,), (self.shape(w.shape[1]),), dense_back_body, **beside)
        z = self.backlog.take(8 if l else 6)
        one, two = chain_call("ffn_back", 10 * l + 5, [first, second], z)
        self.backlog.add(("up" if l else "down", l), one[2], one[3])
        if not l:
            self.backlog.add(("up", l), two[2])
        return one[0], one[1], two[0], two[1]

    def attend_back(self, l, project, grad_context, context, log_norms, slopes):
        z = self.backlog.take(0 if l else 2)
        return attend_bwd(22 + l, project, grad_context, context, log_norms, slopes, z)

    def project_back(self, grad, stream, gain, grad_project, l, context, grad_branch, normed, late):
        S, T, width = grad_project.shape
        return self.scatter(
            (grad_project, self.weight("project", l)),
            project_back_body,
            NormBack(grad, stream, gain),
            more=((context, False), (grad_branch, False), (normed, False)),
            more_out=(self.packed((S + 1) * width),),
            scratch=STREAM_SCRATCH + (pltpu.VMEM((width, T), jnp.bfloat16),),
            filler=attn_filler,
            late=late,
        )

    def attn_back(self, l, grad, stream, gain, grad_project, context, grad_branch, normed, slope):
        first = self.project_back(
            grad, stream, gain, grad_project, l, context, grad_branch, normed, 2
        )
        F = slope.shape[1]
        w = self.weight("down", l - 1)
        second = self.gather(
            None,
            (w, slope),
            (self.shape(F), jax.ShapeDtypeStruct((1, F), jnp.float32)),
            down_back_body,
        )
        one, two = chain_call("attn_back", 10 * l + 7, [first, second], self.backlog.take(7))
        self.backlog.add(("attn", l), one[2], one[3])
        return one[0], one[1], two

    def first_attn_back(
        self, grad, stream, gain, grad_project, context, grad_branch, normed, rows, split
    ):
        chunks = 4 * grad_project.shape[2] // ZR
        first = self.project_back(
            grad, stream, gain, grad_project, 0, context, grad_branch, normed, chunks
        )
        v = jnp.concatenate([jnp.zeros((2, self.D), jnp.float32), jnp.stack(rows)])
        u = jnp.pad(split, ((0, -split.shape[0] % 8), (0, 0)))
        second = Finish(jnp.pad(v, ((0, -v.shape[0] % 8), (0, 0))), u)
        one, two = chain_call("first_attn_back", 7, [first, second], self.backlog.take(1000))
        self.backlog.add(("attn", 0), one[2], one[3])
        return one[0], two[0], two[1]

    def results(self, shapes, small, v, u):
        layers, d, parts, width = shapes[0]
        group = self.D // lax.axis_size("dp")

        def targets(key, row):
            kind, l = key
            if kind == "down":
                return [(3, (l, pl.ds(row, ZR)), 0, group)]
            if kind == "up":
                b, r = divmod(row, group)
                return [(2, (l, pl.ds(r, ZR), pl.ds(b * group, group)), 0, group)]
            if row < width:
                return [(1, (l, pl.ds(row, ZR)), 0, group)]
            s, r = divmod(row - width, width)
            return [(0, (l, s, pl.ds(h * width + r, ZR)), h * width, width) for h in range(2)]

        shapes = [(layers, parts, d, width), *shapes[1:]]
        shape = lambda x: jax.ShapeDtypeStruct(x, jnp.float32)
        out = place_call(
            self.backlog.sums,
            [shape(x) for x in shapes],
            targets,
            v,
            u,
            [shape(x) for x in (small[2], small[2], small[2], small[0], small[1])],
        )
        out = (*out[:4], out[7], out[8], *out[4:7])
        return (out[0].transpose(0, 2, 1, 3), *out[1:])


class Plain:
    def __init__(self, T, D):
        self.T, self.D = T, D
        self.ffn, self.attn = {}, {}

    def start(self, x, gain, bias, shift, out_grad, weights):
        self.rows = layer_norm(x.astype(jnp.float32), gain, bias).astype(jnp.bfloat16)
        self.out_grad = out_grad
        low = jnp.bfloat16
        self.weights = []
        for l in range(weights[0].shape[0]):
            project, dense, up, down = (x[l].astype(low) for x in weights)
            project = project.reshape(project.shape[0], -1)
            self.weights.append(
                (
                    lax.all_gather(project, "dp", axis=0, tiled=True),
                    lax.all_gather(dense, "dp", axis=0),
                    lax.all_gather(up, "dp", axis=0, tiled=True),
                    lax.all_gather(down, "dp", axis=0),
                )
            )

    def project(self, l, shift):
        full = gather_all(self.rows)
        return full, (nn(full, self.weights[l][0]) + shift).astype(jnp.bfloat16)

    def attend(self, l, project, slopes):
        return attend_fwd(0, project, slopes, NO_Z)

    def attn_out(self, l, stream, context, bias, gain, shift, up_shift):
        middle = stream + gather_sum(nn(context, side_by_side(self.weights[l][1]))) + bias
        full = gather_all(layer_norm(middle, gain, shift).astype(jnp.bfloat16))
        return middle, full, *gelu_both(nn(full, self.weights[l][2]) + up_shift)

    def ffn_out(self, l, middle, active, bias, gain, shift):
        stream = middle + gather_sum(nn(active, side_by_side(self.weights[l][3]))) + bias
        self.rows = layer_norm(stream, gain, shift).astype(jnp.bfloat16)
        return stream

    def down_back(self, l, grad, slope):
        full = gather_all(grad)
        g = (nt(full, side_by_side(self.weights[l][3])) * slope.astype(jnp.float32)).astype(
            jnp.bfloat16
        )
        return full, g, jnp.sum(g.astype(jnp.float32), axis=0, keepdims=True)

    def last_out(self, l, middle, active, slope, bias):
        rows = middle + gather_sum(nn(active, side_by_side(self.weights[l][3]))) + bias
        return rows.astype(jnp.bfloat16), *self.down_back(l, self.out_grad, slope)

    def norm_back(self, grad, values, gain, total):
        back = jax.vjp(layer_norm, values.astype(jnp.float32), gain, gain)[1]
        step, gain_sum, shift_sum = back(total)
        grad = grad + step
        return grad, jnp.stack([gain_sum, shift_sum, jnp.sum(grad, axis=0)])

    def ffn_back(self, l, grad, middle, gain, grad_hidden, active, normed, grad_down):
        Z = lax.axis_size("dp")
        F = grad_hidden.shape[1]
        d = self.D // Z
        up = jnp.einsum("td,tf->df", normed, grad_hidden, preferred_element_type=jnp.float32)
        down = jnp.einsum(
            "tf,tzd->zfd", active, grad_down.reshape(-1, Z, d), preferred_element_type=jnp.float32
        )
        self.ffn[l] = reduce_dp(up.reshape(Z, d, F)), reduce_dp(down)
        total = gather_sum(nt(grad_hidden, self.weights[l][2]))
        grad, sums = self.norm_back(grad, middle, gain, total)
        full = gather_all(grad.astype(jnp.bfloat16))
        return grad, sums, full, nt(full, side_by_side(self.weights[l][1])).astype(jnp.bfloat16)

    def attend_back(self, l, project, grad_context, context, log_norms, slopes):
        return attend_bwd(0, project, grad_context, context, log_norms, slopes, NO_Z)

    def project_back(self, l, grad, stream, gain, grad_project, context, grad_branch, normed):
        S, T, width = grad_project.shape
        w = self.weights[l][0]
        Z = lax.axis_size("dp")
        d = self.D // Z
        dense = jnp.einsum(
            "ti,tzd->zid", context, grad_branch.reshape(T, Z, d), preferred_element_type=jnp.float32
        )
        project = jnp.einsum(
            "td,sti->dsi", normed, grad_project, preferred_element_type=jnp.float32
        )
        self.attn[l] = reduce_dp(project.reshape(Z, d, S, width)), reduce_dp(dense)
        part = sum(nt(grad_project[s], w[:, s * width : (s + 1) * width]) for s in range(S))
        return self.norm_back(grad, stream, gain, gather_sum(part))

    def attn_back(self, l, grad, stream, gain, grad_project, context, grad_branch, normed, slope):
        grad, sums = self.project_back(
            l, grad, stream, gain, grad_project, context, grad_branch, normed
        )
        return grad, sums, self.down_back(l - 1, grad.astype(jnp.bfloat16), slope)

    def first_attn_back(
        self, grad, stream, gain, grad_project, context, grad_branch, normed, rows, split
    ):
        grad, sums = self.project_back(
            0, grad, stream, gain, grad_project, context, grad_branch, normed
        )
        rows = jnp.concatenate([sums[:2], jnp.stack(rows)])
        return grad, lax.psum(rows, ("dp", "mp")), lax.psum(split, "dp")

    def results(self, shapes, small, total, split):
        grads = [(*self.attn[l], *self.ffn[l]) for l in range(shapes[0][0])]
        matrices = tuple(jnp.stack(parts).astype(jnp.float32) for parts in zip(*grads))
        parts = [jnp.concatenate([total[2:6], total[:2]])]
        parts += [total[6 * l : 6 * l + 6] for l in range(1, len(grads))]
        pick = lambda i, j: jnp.stack([jnp.stack([p[i], p[j]]) for p in parts])
        n = small[0][1] * small[0][2]
        split = split[:, :n].reshape(small[0]), split[:, n:]
        return (*matrices, *split, pick(4, 0), pick(5, 1), pick(2, 3))


def shards(
    inputs,
    out_grad,
    project_weight,
    dense_weight,
    up_weight,
    down_weight,
    project_bias,
    up_bias,
    norm_gain,
    norm_bias,
    output_bias,
):
    tensor_size = lax.axis_size("mp")
    tensor_rank = lax.axis_index("mp")
    row_count, model_width = inputs.shape
    total_rows = row_count * tensor_size
    inner_width = project_weight.shape[3]
    heads_here = N_HEADS // tensor_size
    layer_count = project_weight.shape[0]
    slopes = 2.0 ** (
        -8.0
        * (tensor_rank * heads_here + lax.iota(jnp.int32, heads_here) + 1).astype(jnp.float32)
        / N_HEADS
    )
    fast = tensor_size == 8 and lax.axis_size("dp") == 4 and row_count == 256
    ops = (Fast if fast else Plain)(total_rows, model_width)
    none = jnp.zeros((inner_width,), jnp.float32)
    shifts = [
        jnp.concatenate([project_bias[l, 0], none, project_bias[l, 1]]) for l in range(layer_count)
    ]
    weights = (project_weight, dense_weight, up_weight, down_weight)
    ops.start(inputs, norm_gain[0, 0], norm_bias[0, 0], shifts[0], out_grad, weights)
    stream = inputs
    last = layer_count - 1
    stored = []
    for l in range(layer_count):
        normed_all, project = ops.project(l, shifts[l])
        context, log_norms = ops.attend(l, project, slopes)
        middle, normed2_all, active, slope = ops.attn_out(
            l,
            stream,
            context,
            output_bias[l, 0],
            norm_gain[l, 1],
            norm_bias[l, 1],
            up_bias[l],
        )
        stored.append(
            (stream, normed_all, project, log_norms, context, middle, normed2_all, active, slope)
        )
        if l < last:
            stream = ops.ffn_out(
                l, middle, active, output_bias[l, 1], norm_gain[l + 1, 0], norm_bias[l + 1, 0]
            )
    outputs, *step = ops.last_out(last, middle, active, slope, output_bias[last, 1])
    grad = out_grad
    down_bias_grad = jnp.sum(grad.astype(jnp.float32), axis=0)
    sums = [None] * layer_count
    split = [None] * layer_count
    for l in reversed(range(layer_count)):
        stream, normed_all, project, log_norms, context, middle, normed2_all, active, _ = stored[l]
        grad_down, grad_hidden, up_bias_part = step
        grad, second, grad_branch, grad_context = ops.ffn_back(
            l, grad, middle, norm_gain[l, 1], grad_hidden, active, normed2_all, grad_down
        )
        grad_project, project_bias_part = ops.attend_back(
            l, project, grad_context, context, log_norms, slopes
        )
        sums[l] = [second[0], second[1], second[2], down_bias_grad]
        split[l] = jnp.concatenate([project_bias_part.reshape(-1), up_bias_part.reshape(-1)])
        args = (grad, stream, norm_gain[l, 0], grad_project, context, grad_branch, normed_all)
        if l:
            grad, first, step = ops.attn_back(l, *args, stored[l - 1][-1])
            sums[l] += [first[0], first[1]]
            down_bias_grad = first[2]
    rows = sums[0] + [x for parts in sums[1:] for x in parts]
    grad, total, split = ops.first_attn_back(*args, rows, jnp.stack(split))
    shapes = [x.shape for x in weights]
    small = [x.shape for x in (project_bias, up_bias, norm_gain)]
    return outputs, grad, *ops.results(shapes, small, total, split)


def solution(mesh):
    rows = P(("dp", "mp"), None)
    specs = (P(None, "dp", None, "mp"), P(None, "mp", "dp"), P(None, "dp", "mp"), P(None, "mp", "dp"))
    biases = (P(None, None, "mp"), P(None, "mp"), P(), P(), P())
    return jax.shard_map(
        shards,
        mesh=mesh,
        in_specs=(rows, rows, *specs, *biases),
        out_specs=(rows, rows, *specs, *biases),
        check_vma=False,
    )
```

```python
import functools

import jax
import jax.numpy as jnp
from jax import lax
from jax.experimental import pallas as pl
from jax.experimental.pallas import tpu as pltpu
from jax.sharding import PartitionSpec as P

N_HEADS = 16
BLOCK = 256
HEAD = 128
LOG2E = 1.4426950408889634
MESH = pl.DeviceIdType.MESH
NT_DIMS = (((1,), (1,)), ((), ()))
norm_eps = 1e-05


def nt(a, b):
    return lax.dot_general(a, b, NT_DIMS, preferred_element_type=jnp.float32)


def nn(a, b):
    return jnp.dot(a, b, preferred_element_type=jnp.float32)


def layer_norm(values, scale_row, shift_row):
    centre = jnp.mean(values, axis=-1, keepdims=True)
    centred = values - centre
    spread = jnp.mean(centred * centred, axis=-1, keepdims=True)
    return centred * lax.rsqrt(spread + norm_eps) * scale_row + shift_row


def peers():
    me = lax.axis_index("mp")
    core = me % 2
    bx = (me // 2) % 2
    by = me // 4
    return me, core, bx, by, me + 1 - 2 * core, me + 2 - 4 * bx, me + 4 - 8 * by


def owner(rel, core, bx, by):
    c = core if rel % 2 == 0 else 1 - core
    x = bx if (rel // 2) % 2 == 0 else 1 - bx
    y = by if rel // 4 == 0 else 1 - by
    return y * 4 + x * 2 + c


def z_peers():
    z = lax.axis_index("dp")
    z1 = z + 1 - 2 * (z % 2)
    return z, z1, (z + 2) % 4, (z1 + 2) % 4


def enter(partner, xn, yn, z=False):
    barrier = pltpu.get_barrier_semaphore()
    for n in (partner, xn, yn):
        pl.semaphore_signal(barrier, inc=1, device_id={"mp": n}, device_id_type=MESH)
    if z:
        _, z1, z2, _ = z_peers()
        for n in (z1, z2):
            pl.semaphore_signal(barrier, inc=1, device_id={"dp": n}, device_id_type=MESH)
    pl.semaphore_wait(barrier, 5 if z else 3)


ZR = 128


class ZSum:
    ahead = 3

    def __init__(self, plan, srcs, out, scratch):
        self.plan, self.srcs, self.out = plan, srcs, out[0]
        self.recv, self.own, self.send_sem, self.recv_sem, self.loc = scratch
        self.z, self.z1, self.z2, self.z3 = z_peers()
        self.sent, self.begun = [], False
        self.events = [functools.partial(self.event, c) for c in range(len(plan))]

    def block(self, c, z):
        i, row = self.plan[c]
        return self.srcs[i].at[z, pl.ds(row, ZR), :]

    def remote(self, src, kind, c, target):
        return pltpu.make_async_remote_copy(
            src_ref=src,
            dst_ref=self.recv.at[kind, c],
            send_sem=self.send_sem.at[kind, c],
            recv_sem=self.recv_sem.at[kind, c],
            device_id={"dp": target},
            device_id_type=MESH,
        )

    def push(self, *args):
        c = self.remote(*args)
        c.start()
        self.sent.append(c)

    def here(self, kind, c):
        return pltpu.make_async_copy(
            self.block(c, self.z2 if kind else self.z), self.own.at[kind, c], self.loc.at[kind, c]
        )

    def arrive(self, kind, c):
        self.remote(self.own.at[0, c], kind, c, self.z1).wait_recv()

    def start(self):
        self.begun = True
        for c in range(min(self.ahead, len(self.plan))):
            self.push(self.block(c, self.z3), 1, c, self.z1)
        for c in range(len(self.plan)):
            self.here(1, c).start()
            self.here(0, c).start()

    def event(self, c):
        if c + self.ahead < len(self.plan):
            n = c + self.ahead
            self.push(self.block(n, self.z3), 1, n, self.z1)
        self.arrive(1, c)
        self.here(1, c).wait()

        @pl.loop(0, ZR // 16)
        def _(i):
            rows = pl.ds(pl.multiple_of(i * 16, 16), 16)
            self.own[1, c, rows, :] = (
                self.own[1, c, rows, :].astype(jnp.float32)
                + self.recv[1, c, rows, :].astype(jnp.float32)
            ).astype(jnp.bfloat16)

        self.push(self.own.at[1, c], 2, c, self.z2)
        self.push(self.block(c, self.z1), 0, c, self.z1)

    def tick(self, n=1):
        n = min(n, len(self.events)) if self.begun else 0
        for _ in range(n):
            self.events.pop(0)()
        return n > 0

    def finish(self):
        self.tick(len(self.events))
        for c in range(len(self.plan)):
            self.here(0, c).wait()
            self.arrive(0, c)
            self.arrive(2, c)

            @pl.loop(0, ZR // 16)
            def _(i):
                rows = pl.ds(pl.multiple_of(i * 16, 16), 16)
                to = pl.ds(pl.multiple_of(c * ZR + i * 16, 16), 16)
                self.out[to, :] = (
                    self.own[0, c, rows, :].astype(jnp.float32)
                    + self.recv[0, c, rows, :].astype(jnp.float32)
                    + self.recv[2, c, rows, :].astype(jnp.float32)
                ).astype(jnp.bfloat16)

        for c in self.sent:
            c.wait_send()


class ZGather:
    ahead = 4

    def __init__(self, plan, srcs, outs, scratch):
        self.plan, self.srcs, self.outs = plan, srcs, outs
        self.send_sem, self.recv_sem, self.loc = scratch
        self.z, self.z1, self.z2, self.z3 = z_peers()
        self.sent = []
        self.passed, self.settled = 0, 0

    def place(self, c, z):
        i, row, size, _ = self.plan[c]
        return self.outs[i].at[z, pl.ds(row, size), :]

    def own(self, c):
        i, row, size, layer = self.plan[c]
        return self.srcs[i].at[layer, pl.ds(row, size), :]

    def remote(self, src, z, kind, c, target):
        return pltpu.make_async_remote_copy(
            src_ref=src,
            dst_ref=self.place(c, z),
            send_sem=self.send_sem.at[kind, c],
            recv_sem=self.recv_sem.at[kind, c],
            device_id={"dp": target},
            device_id_type=MESH,
        )

    def push(self, *args):
        c = self.remote(*args)
        c.start()
        self.sent.append(c)

    def here(self, c):
        return pltpu.make_async_copy(self.own(c), self.place(c, self.z), self.loc.at[c])

    def start(self):
        for c in range(len(self.plan)):
            if c < self.ahead:
                self.send_own(c)
            self.here(c).start()

    def send_own(self, c):
        self.push(self.own(c), self.z, 0, c, self.z2)
        self.push(self.own(c), self.z, 1, c, self.z1)

    def event(self, c):
        if c + self.ahead < len(self.plan):
            self.send_own(c + self.ahead)
        self.remote(self.own(c), self.z2, 0, c, self.z2).wait_recv()
        self.push(self.place(c, self.z2), self.z2, 2, c, self.z1)

    def tick(self, n=1):
        n = min(n, len(self.plan) - self.passed)
        for _ in range(n):
            self.event(self.passed)
            self.passed += 1
        return n > 0

    def settle(self, n):
        self.tick(n - self.passed)
        for c in range(self.settled, n):
            self.remote(self.own(c), self.z1, 1, c, self.z1).wait_recv()
            self.remote(self.own(c), self.z3, 2, c, self.z1).wait_recv()
            self.here(c).wait()
        self.settled = n

    def finish(self):
        self.settle(len(self.plan))
        for c in self.sent:
            c.wait_send()


class NoZ:
    ahead = 0

    def start(self):
        pass

    def tick(self, n=1):
        return False

    def finish(self):
        pass


class ZCall:
    plan, arrays, out_shapes, out_space, scratch = (), (), (), pltpu.VMEM, ()

    def make(self, refs):
        return NoZ()

    def done(self, results):
        pass

    def aliases(self, first_in, first_out):
        return {}

    def counts(self):
        return len(self.arrays), len(self.out_shapes), len(self.scratch)

    def in_specs(self):
        return [pl.BlockSpec(memory_space=pl.ANY)] * len(self.arrays)

    def out_specs(self):
        return (pl.BlockSpec(memory_space=self.out_space),) * len(self.out_shapes)


def sum_scratch(n, w):
    return (
        pltpu.VMEM((3, n, ZR, w), jnp.bfloat16),
        pltpu.VMEM((2, n, ZR, w), jnp.bfloat16),
        pltpu.SemaphoreType.DMA((3, n)),
        pltpu.SemaphoreType.DMA((3, n)),
        pltpu.SemaphoreType.DMA((2, n)),
    )


class SumCall(ZCall):
    def __init__(self, backlog, limit):
        self.plan, self.arrays, self.pieces = [], [], []
        while limit and backlog.queue:
            entry = backlog.queue[0]
            key, array, row = entry
            if not any(a is array for a in self.arrays):
                self.arrays.append(array)
            i = [a is array for a in self.arrays].index(True)
            self.pieces.append((key, row))
            self.plan.append((i, row))
            limit -= 1
            entry[2] += ZR
            if entry[2] == array.shape[1]:
                backlog.queue.pop(0)
        self.backlog = backlog
        n = len(self.plan)
        if n:
            w = self.arrays[0].shape[2]
            self.out_shapes = (jax.ShapeDtypeStruct((n * ZR, w), jnp.bfloat16),)
            self.scratch = sum_scratch(n, w)

    def make(self, refs):
        i, o, _ = self.counts()
        return ZSum(self.plan, refs[:i], refs[i : i + o], refs[i + o :]) if self.plan else NoZ()

    def done(self, results):
        for n, (key, row) in enumerate(self.pieces):
            self.backlog.sums.append((key, row, results[0], n * ZR))


class Backlog:
    def __init__(self):
        self.queue, self.sums = [], []

    def add(self, key, array, summed=None):
        done = 0 if summed is None else summed.shape[0]
        self.sums += [(key, row, summed, row) for row in range(0, done, ZR)]
        self.queue.append([key, array, done])

    def take(self, limit):
        return SumCall(self, limit)


class GatherCall(ZCall):
    out_space = pl.ANY

    def __init__(self, queue, limit):
        self.queue, self.keys, self.plan = queue, [], []
        shards, begun, shapes = [], [], []
        while limit and queue.entries:
            entry = queue.entries[0]
            key, shard, row, size, layer = entry
            if key not in self.keys:
                self.keys.append(key)
                shards.append(shard)
                shapes.append(jax.ShapeDtypeStruct((4, *shard.shape[1:]), shard.dtype))
                if key in queue.arrays:
                    begun.append((len(self.keys) - 1, queue.arrays[key]))
            self.plan.append((self.keys.index(key), row, size, layer))
            limit -= 1
            entry[2] += size
            if entry[2] == shard.shape[1]:
                queue.entries.pop(0)
        self.arrays = shards + [x for _, x in begun]
        self.begun = [i for i, _ in begun]
        self.out_shapes = tuple(shapes)
        n = len(self.plan)
        self.scratch = (
            pltpu.SemaphoreType.DMA((3, n)),
            pltpu.SemaphoreType.DMA((3, n)),
            pltpu.SemaphoreType.DMA((n,)),
        )

    def aliases(self, first_in, first_out):
        n = len(self.keys)
        return {first_in + n + j: first_out + i for j, i in enumerate(self.begun)}

    def make(self, refs):
        i, o, _ = self.counts()
        return ZGather(self.plan, refs[:i], refs[i : i + o], refs[i + o :])

    def done(self, results):
        for key, array in zip(self.keys, results):
            self.queue.arrays[key] = array


class GatherQueue:
    def __init__(self):
        self.entries, self.arrays = [], {}

    def add(self, key, shard, layer, size):
        self.entries.append([key, shard, 0, size, layer])

    def take(self, limit):
        return GatherCall(self, limit) if limit and self.entries else NO_Z


NO_Z = ZCall()


def cost(flops):
    return pl.CostEstimate(flops=flops, bytes_accessed=1 << 16, transcendentals=0)


def split_refs(refs, *counts):
    parts = []
    for n in counts:
        parts.append(refs[:n])
        refs = refs[n:]
    return parts


def bias_tile(slope, first_key, first_query, keys, queries):
    kp = first_key + lax.broadcasted_iota(jnp.int32, (keys, queries), 0)
    qp = first_query + lax.broadcasted_iota(jnp.int32, (keys, queries), 1)
    return (jnp.abs(qp - kp).astype(jnp.float32)) * (-slope * LOG2E)

def scores_t(q, k, slope, i, B):
    L = (i+1)*B
    factor = q.shape[1] ** (-0.5) * LOG2E
    st = nt(k, q) * factor
    key = lax.broadcasted_iota(jnp.int32, (L, 1), 0)
    if i > 0:
        m = i * B
        kp = lax.broadcasted_iota(jnp.int32, (m, 1), 0).astype(jnp.float32)
        qp = (m + lax.broadcasted_iota(jnp.int32, (1, B), 1)).astype(jnp.float32)
        head = st[:m] - (qp - kp) * (slope * LOG2E)
        tail = st[m:] + bias_tile(slope, 0, 0, B, B)
        return head, tail
    return None, st + bias_tile(slope, 0, 0, B, B)

def enter_z(zc):
    if zc.plan:
        _, z1, z2, _ = z_peers()
        barrier = pltpu.get_barrier_semaphore()
        for n in (z1, z2):
            pl.semaphore_signal(barrier, inc=1, device_id={"dp": n}, device_id_type=MESH)
        pl.semaphore_wait(barrier, 2)


def attend_fwd_kernel(zc, slope_ref, p_ref, *refs):
    zi, zo, zs = zc.counts()
    z_in, (ctx_ref, lse_ref), z_out, (vt_ref,), z_scratch = split_refs(refs, zi, 2, zo, 1, zs)
    z = zc.make(z_in + z_out + z_scratch)
    enter_z(zc)
    z.start()
    B = BLOCK
    T, W = p_ref.shape
    H = W // (3 * HEAD)
    for h in range(H):
        q, k, v = (pl.ds((part * H + h) * HEAD, HEAD) for part in range(3))
        slope = slope_ref[h]
        vt_ref[...] = p_ref[:, v].T
        for i in range(T // B):
            L = (i + 1) * B
            head, tail = scores_t(p_ref[i * B : L, q], p_ref[:L, k], slope, i, B)
            top = jnp.max(tail, axis=0, keepdims=True)
            if head is not None:
                top = jnp.maximum(top, jnp.max(head, axis=0, keepdims=True))
            pt = jnp.exp2(tail - top)
            den = jnp.sum(pt, axis=0, keepdims=True)
            ct = nn(vt_ref[:, i * B : L], pt.astype(jnp.bfloat16))
            if head is not None:
                ph = jnp.exp2(head - top)
                den = den + jnp.sum(ph, axis=0, keepdims=True)
                ct = ct + nn(vt_ref[:, : i * B], ph.astype(jnp.bfloat16))
            ctx_ref[i * B : L, pl.ds(h * HEAD, HEAD)] = (ct / den).T.astype(ctx_ref.dtype)
            lse_ref[h, i : i + 1, :] = top + jnp.log2(den)
            if i % 4 == 3:
                z.tick()
    z.finish()


def attend_bwd_kernel(zc, slope_ref, p_ref, g_ref, c_ref, lse_ref, *refs):
    zi, zo, zs = zc.counts()
    z_in, (out_ref, sums_ref), z_out, (kt_ref, dk_ref, dv_ref), z_scratch = split_refs(
        refs, zi, 2, zo, 3, zs
    )
    z = zc.make(z_in + z_out + z_scratch)
    enter_z(zc)
    z.start()
    B = BLOCK
    T, W = p_ref.shape
    H = W // (3 * HEAD)
    n = T // B
    factor = HEAD ** (-0.5)
    ones = jnp.ones((8, HEAD), jnp.float32)
    for h in range(H):
        qc, kc, vc = (pl.ds((part * H + h) * HEAD, HEAD) for part in range(3))
        cols = pl.ds(h * HEAD, HEAD)
        slope = slope_ref[h]
        kt_ref[...] = p_ref[:, kc].T
        qsum = jnp.zeros((1, HEAD), jnp.float32)
        for i in reversed(range(n)):
            L = (i + 1) * B
            q = p_ref[i * B : L, qc]
            g = g_ref[i * B : L, cols]
            head, tail = scores_t(q, p_ref[:L, kc], slope, i, B)
            prod = g.astype(jnp.float32) * c_ref[i * B : L, cols].astype(jnp.float32)
            inner = lax.dot_general(
                ones,
                prod,
                NT_DIMS,
                preferred_element_type=jnp.float32,
                precision=lax.Precision.HIGHEST,
            )[:1]
            lse = lse_ref[h, i : i + 1, :]
            dpt = nt(p_ref[:L, vc], g)
            dqt = None
            for part, lo, hi in ((head, 0, i * B), (tail, i * B, L)):
                if part is None:
                    continue
                pt = jnp.exp2(part - lse)
                ds = (pt * (dpt[lo:hi] - inner)).astype(jnp.bfloat16)
                pt = pt.astype(jnp.bfloat16)
                dk = nn(ds, q)
                dv = nn(pt, g)
                if i == n - 1:
                    dk_ref[lo:hi, :] = dk
                    dv_ref[lo:hi, :] = dv
                else:
                    dk_ref[lo:hi, :] += dk
                    dv_ref[lo:hi, :] += dv
                t = nn(kt_ref[:, lo:hi], ds)
                dqt = t if dqt is None else dqt + t
            dq = (dqt * factor).T.astype(jnp.bfloat16)
            out_ref[0, i * B : L, cols] = dq
            qsum += jnp.sum(dq.astype(jnp.float32), axis=0, keepdims=True)
            if i % 4 == 3:
                z.tick()
        out_ref[1, :, cols] = (dk_ref[...] * factor).astype(jnp.bfloat16)
        dv = dv_ref[...].astype(jnp.bfloat16)
        out_ref[2, :, cols] = dv
        sums_ref[0:1, cols] = qsum
        sums_ref[1:2, cols] = jnp.sum(dv.astype(jnp.float32), axis=0, keepdims=True)
    z.finish()


def attend_call(kernel, cid, name, slopes, arrays, outs, scratch, z):
    vmem = pl.BlockSpec(memory_space=pltpu.VMEM)
    out = pl.pallas_call(
        functools.partial(kernel, z),
        out_shape=(*outs, *z.out_shapes),
        in_specs=[pl.BlockSpec(memory_space=pltpu.SMEM)] + [vmem] * len(arrays) + z.in_specs(),
        out_specs=(vmem,) * len(outs) + z.out_specs(),
        scratch_shapes=[*scratch, *z.scratch],
        compiler_params=pltpu.CompilerParams(
            collective_id=cid if z.plan else None,
            has_side_effects=bool(z.plan),
            vmem_limit_bytes=60 << 20,
        ),
        input_output_aliases=z.aliases(1 + len(arrays), len(outs)),
        cost_estimate=cost(1 << 20),
        name=name,
    )(slopes, *arrays, *z.arrays)
    z.done(out[len(outs) :])
    return out[: len(outs)]


def attend_fwd(cid, project, slopes, z):
    T, W = project.shape
    H = W // (3 * HEAD)
    outs = (
        jax.ShapeDtypeStruct((T, H * HEAD), jnp.bfloat16),
        jax.ShapeDtypeStruct((H, T // BLOCK, BLOCK), jnp.float32),
    )
    scratch = (pltpu.VMEM((HEAD, T), jnp.bfloat16),)
    return attend_call(attend_fwd_kernel, cid, "attend_fwd", slopes, (project,), outs, scratch, z)


def attend_bwd(cid, project, grad_context, context, lse, slopes, z):
    T, W = project.shape
    H = W // (3 * HEAD)
    outs = (
        jax.ShapeDtypeStruct((3, T, H * HEAD), jnp.bfloat16),
        jax.ShapeDtypeStruct((2, H * HEAD), jnp.float32),
    )
    scratch = (
        pltpu.VMEM((HEAD, T), jnp.bfloat16),
        pltpu.VMEM((T, HEAD), jnp.float32),
        pltpu.VMEM((T, HEAD), jnp.float32),
    )
    arrays = (project, grad_context, context, lse)
    return attend_call(attend_bwd_kernel, cid, "attend_bwd", slopes, arrays, outs, scratch, z)


class Links:
    def __init__(self, z):
        self.me, self.core, self.bx, self.by, self.partner, self.xn, self.yn = peers()
        self.z, self.late = z, NoZ()
        self.more, self.made = False, ()
        self.sent, self.kept = [], []

    def owner(self, rel):
        return owner(rel, self.core, self.bx, self.by)

    def tick(self, n=1):
        for _ in range(n):
            if not self.z.tick() and not self.late.tick():
                break

    def finish(self):
        self.z.finish()
        self.late.finish()
        for c in self.sent:
            c.wait_send()
        for c in self.kept:
            c.wait()


class Fetched:
    def __init__(self, src, ref, sem):
        self.ref, self.copy, self.here = ref, pltpu.make_async_copy(src, ref, sem), False

    def wait(self):
        if not self.here:
            self.copy.wait()
        self.here = True


def need(operands):
    for x in operands:
        if isinstance(x, Fetched):
            x.wait()
    return refs_of(operands)


def refs_of(operands):
    return tuple(x.ref if isinstance(x, Fetched) else x for x in operands)


def fill(steps, n):
    for _ in range(min(n, len(steps))):
        steps.pop(0)()


class Gather:
    late = 0

    def __init__(
        self, R, D, x, ins, outs, body, more=(), more_out=(), scratch=(), filler=None, C=4
    ):
        self.R, self.D, self.C, self.given = R, D, C, x is not None
        self.body, self.filler = body, filler
        self.counts = (len(ins), len(more), len(outs), len(more_out))
        self.ins = [(x, True)] * self.given + [(a, True) for a in ins] + list(more)
        low = jnp.bfloat16
        self.outs = [(jax.ShapeDtypeStruct((8 * R, D), low), False)]
        self.outs += [(o, True) for o in outs] + list(more_out)
        self.scratch = [
            pltpu.VMEM((C, 8, R // C, D), low),
            pltpu.SemaphoreType.DMA((7, C)),
            pltpu.SemaphoreType.DMA((8, C)),
            pltpu.SemaphoreType.DMA((C, 8)),
            *scratch,
        ]

    def run(self, links, x_ref, ins, outs, scratch):
        n_in, n_more, n_out, n_more_out = self.counts
        if self.given:
            (x_ref,), ins = need(ins[:1]), ins[1:]
        ins, more = split_refs(ins, n_in, n_more)
        (full_ref,), outs, more_out = split_refs(outs, 1, n_out, n_more_out)
        buf, send, recv, loc = scratch[:4]
        steps = []
        if self.filler:
            steps = self.filler(refs_of(ins), refs_of(more), more_out, scratch[4:])
            steps = [functools.partial(need, more)] + steps
        R, D, C, body = self.R, self.D, self.C, self.body
        rc = R // C
        partner, xn, yn, core = links.partner, links.xn, links.yn, links.core

        def copy(src, rel, k, target, sidx):
            return pltpu.make_async_remote_copy(
                src_ref=src,
                dst_ref=buf.at[k, rel],
                send_sem=send.at[sidx, k],
                recv_sem=recv.at[rel, k],
                device_id={"mp": target},
                device_id_type=MESH,
            )

        def push(src, rel, k, target, sidx):
            c = copy(src, rel, k, target, sidx)
            c.start()
            links.sent.append(c)

        def arrive(rel, k):
            copy(buf.at[k, 0], rel, k, partner, 0).wait_recv()

        def keep(src, start, size, k, rel):
            c = pltpu.make_async_copy(src, full_ref.at[pl.ds(start, size), :], loc.at[k, rel])
            c.start()
            links.kept.append(c)

        def place(rel, k):
            return pl.multiple_of(links.owner(rel) * R + k * rc, rc)

        def run(k, lo, hi):
            starts = [place(rel, k) for rel in range(lo, hi)]
            for rel, start in zip(range(lo, hi), starts):
                keep(buf.at[k, rel], start, rc, k, rel)
            body(
                False,
                lambda: buf[k, lo:hi].reshape((hi - lo) * rc, D),
                [pl.ds(start, rc) for start in starts],
                ins,
                outs,
            )

        for k in range(C):
            own = x_ref.at[pl.ds(k * rc, rc), :]
            push(own, 2, k, xn, 1)
            push(own, 4, k, yn, 2)
            push(own, 1, k, partner, 0)
        start = pl.multiple_of(links.me * R, R)
        keep(x_ref, start, R, 0, 0)
        ins = need(ins)
        body(True, lambda: x_ref[...], [pl.ds(start, R)], ins, outs)
        links.tick()
        fill(steps, 2)
        across = jnp.where(core == 0, xn, yn)
        for k in range(C + 2):
            if k < C:
                arrive(2, k)
                arrive(4, k)
                push(buf.at[k, 4 - 2 * core], 6, k, across, 3)
                push(buf.at[k, 2], 3, k, partner, 4)
                push(buf.at[k, 4], 5, k, partner, 5)
            if k == 0:
                starts = [place(1, j) for j in range(C)]
                for j in range(C):
                    arrive(1, j)
                    keep(buf.at[j, 1], starts[j], rc, j, 1)
                body(
                    False,
                    lambda: buf[:, 1].reshape(R, D),
                    [pl.ds(start, rc) for start in starts],
                    ins,
                    outs,
                )
            if 1 <= k <= C:
                arrive(3, k - 1)
                arrive(5, k - 1)
                run(k - 1, 2, 6)
                arrive(6, k - 1)
                push(buf.at[k - 1, 6], 7, k - 1, partner, 6)
            if k >= 2:
                arrive(7, k - 2)
                run(k - 2, 6, 8)
            links.tick()
            fill(steps, 1)
        fill(steps, len(steps))


class Scatter:
    def __init__(
        self,
        T,
        D,
        ins,
        body,
        epilogue,
        more=(),
        more_out=(),
        scratch=(),
        filler=None,
        late=0,
        C=4,
    ):
        R = T // 8
        self.R, self.D, self.C = R, D, C
        self.body, self.epilogue, self.filler, self.late = body, epilogue, filler, late
        self.n_scratch = len(scratch)
        if late:
            w = more_out[0][0].shape[2]
            more_out = [*more_out, (jax.ShapeDtypeStruct((late * ZR, w), jnp.bfloat16), True)]
            scratch = [*scratch, *sum_scratch(late, w)]
        self.counts = (len(ins), len(epilogue.ins), len(more)), (len(epilogue.outs), len(more_out))
        self.ins = [(a, True) for a in ins] + [(a, True) for a in epilogue.ins] + list(more)
        self.outs = [(o, True) for o in epilogue.outs] + list(more_out)
        self.scratch = [
            pltpu.VMEM((8, R, D), jnp.bfloat16),
            pltpu.VMEM((7, R, D), jnp.bfloat16),
            pltpu.SemaphoreType.DMA((7, C)),
            pltpu.SemaphoreType.DMA((7, C)),
            *epilogue.scratch,
            *scratch,
        ]

    def run(self, links, _, ins, outs, scratch):
        ins, end_ins, more = split_refs(ins, *self.counts[0])
        end_outs, more_out = split_refs(outs, *self.counts[1])
        (pbuf, rbuf, send, recv), end_scratch, scratch, late_scratch = split_refs(
            scratch, 4, len(self.epilogue.scratch), self.n_scratch, 5 if self.late else 0
        )
        steps = []
        if self.late:
            plan = [(0, ZR * c) for c in range(self.late)]
            links.late = ZSum(plan, more_out[:1], more_out[-1:], late_scratch)
            more_out = more_out[:-1]
        if self.filler:
            steps = self.filler(refs_of(ins), refs_of(more), more_out, scratch)
            steps = [functools.partial(need, more)] + steps + [links.late.start]
        ins = need(ins)
        R, D, C = self.R, self.D, self.C
        rc = R // C
        core, bx, by, partner = links.core, links.bx, links.by, links.partner
        dn = jnp.where(core == 0, links.yn, links.xn)
        fn = jnp.where(core == 0, links.xn, links.yn)

        def copy(src, slot, k, target):
            rows = pl.ds(k * rc, rc)
            return pltpu.make_async_remote_copy(
                src_ref=src.at[rows, :],
                dst_ref=rbuf.at[slot, rows, :],
                send_sem=send.at[slot, k],
                recv_sem=recv.at[slot, k],
                device_id={"mp": target},
                device_id_type=MESH,
            )

        def push(slot, to, target, k):
            c = copy(pbuf.at[slot], to, k, target)
            c.start()
            links.sent.append(c)

        def arrive(slot, k):
            copy(pbuf.at[0], slot, k, partner).wait_recv()

        def dest_rank(which, c):
            if which == 0:
                return (1 - by) * 4 + (1 - bx) * 2 + c
            if which == 3:
                return by * 4 + bx * 2 + c
            flip_y = (1 - c) if which == 1 else c
            y = by + flip_y * (1 - 2 * by)
            x = bx + (1 - flip_y) * (1 - 2 * bx)
            return y * 4 + x * 2 + c

        def compute(which, c, slot, part=0, parts=1):
            n = R // parts
            rows = pl.ds(pl.multiple_of(dest_rank(which, c) * R + part * n, n), n)
            self.body(rows, ins, pbuf.at[slot, pl.ds(part * n, n), :])

        def theirs(which, part=0, parts=1):
            compute(which, 1 - core, which, part, parts)
            for k in range(part * C // parts, (part + 1) * C // parts):
                push(which, which, partner, k)

        def add(slot, rslot, k):
            @pl.loop(0, rc // 16)
            def _(i):
                rows = pl.ds(pl.multiple_of(k * rc + i * 16, 16), 16)
                pbuf[slot, rows, :] = (
                    pbuf[slot, rows, :].astype(jnp.float32)
                    + rbuf[rslot, rows, :].astype(jnp.float32)
                ).astype(pbuf.dtype)

        def join(which, part=0, parts=1):
            for k in range(part * C // parts, (part + 1) * C // parts):
                arrive(which, k)
                add(4 + which, which, k)
                if which < 2:
                    push(4 + which, 4 + which, dn, k)

        theirs(0, 0, 2)
        theirs(0, 1, 2)
        compute(0, core, 4, 0, 2)
        compute(0, core, 4, 1, 2)
        join(0, 0, 2)
        theirs(1)
        join(0, 1, 2)
        compute(1, core, 5)
        theirs(2)
        join(1)
        compute(2, core, 6)
        theirs(3)
        join(2)
        compute(3, core, 7)
        join(3)
        links.tick(2 if links.more else 3)
        share = -(-len(steps) // C) if self.late else 2
        for k in range(C):
            arrive(4, k)
            add(6, 4, k)
            push(6, 6, fn, k)
            links.tick(1 if links.more else 2)
            fill(steps, share)
        fill(steps, len(steps))
        end_ins = need(end_ins)
        self.epilogue.begin(end_outs, end_scratch)
        for k in range(C):
            arrive(5, k)
            arrive(6, k)

            @pl.loop(0, rc // 16)
            def _(i):
                rows = pl.ds(pl.multiple_of(k * rc + i * 16, 16), 16)
                total = (
                    pbuf[7, rows, :].astype(jnp.float32)
                    + rbuf[5, rows, :].astype(jnp.float32)
                    + rbuf[6, rows, :].astype(jnp.float32)
                )
                self.epilogue.rows(rows, total, end_ins, end_outs, end_scratch)

        links.made = end_outs
        return self.epilogue.end(end_outs, end_scratch)


class AddNorm:
    def __init__(self, stream, bias, gain, shift, keep):
        self.ins = (stream, bias[None], gain[None], shift[None])
        self.keep = keep
        low = jax.ShapeDtypeStruct(stream.shape, jnp.bfloat16)
        self.outs = (jax.ShapeDtypeStruct(stream.shape, jnp.float32),) + (low,) * keep
        self.scratch = () if keep else (pltpu.VMEM(stream.shape, jnp.bfloat16),)

    def begin(self, outs, scratch):
        pass

    def rows(self, rows, total, ins, outs, scratch):
        stream, bias, gain, shift = ins
        value = stream[rows, :].astype(jnp.float32) + total + bias[...]
        outs[0][rows, :] = value
        low = outs[1] if self.keep else scratch[0]
        low[rows, :] = layer_norm(value, gain[...], shift[...]).astype(low.dtype)

    def end(self, outs, scratch):
        return None if self.keep else scratch[0]


class AddOnly:
    scratch = ()

    def __init__(self, stream, bias):
        self.ins = (stream, bias[None])
        self.outs = (jax.ShapeDtypeStruct(stream.shape, jnp.bfloat16),)

    def begin(self, outs, scratch):
        pass

    def rows(self, rows, total, ins, outs, scratch):
        outs[0][rows, :] = (ins[0][rows, :] + total + ins[1][...]).astype(jnp.bfloat16)

    def end(self, outs, scratch):
        return None


class NormBack:
    def __init__(self, grad, values, gain):
        R, D = values.shape
        self.ins = (grad, values, gain[None])
        self.outs = (
            jax.ShapeDtypeStruct((R, D), jnp.float32),
            jax.ShapeDtypeStruct((3, D), jnp.float32),
        )
        self.scratch = (pltpu.VMEM((R, D), jnp.bfloat16), pltpu.VMEM((3, 8, D), jnp.float32))

    def begin(self, outs, scratch):
        scratch[1][...] = jnp.zeros_like(scratch[1])

    def rows(self, rows, total, ins, outs, scratch):
        grad, values, gain = ins
        v = values[rows, :].astype(jnp.float32)
        centred = v - jnp.mean(v, axis=-1, keepdims=True)
        scale = lax.rsqrt(jnp.mean(centred * centred, axis=-1, keepdims=True) + norm_eps)
        unit = centred * scale
        inner = total * gain[...]
        mean = jnp.mean(inner, axis=-1, keepdims=True)
        along = jnp.mean(inner * unit, axis=-1, keepdims=True)
        new = grad[rows, :].astype(jnp.float32) + scale * (inner - mean - unit * along)
        outs[0][rows, :] = new
        scratch[0][rows, :] = new.astype(jnp.bfloat16)
        for i, x in enumerate((total * unit, total, new)):
            scratch[1][i] += x[:8] + x[8:]

    def end(self, outs, scratch):
        outs[1][...] = jnp.sum(scratch[1][...], axis=1)
        return scratch[0]


def shared_ins(phases):
    places = []
    flat = []
    for p in phases:
        mine = []
        for x, inside in p.ins:
            at = [i for i, (y, where) in enumerate(flat) if y is x and where == inside]
            if not at:
                flat.append((x, inside))
            mine.append(at[0] if at else len(flat) - 1)
        places.append(mine)
    return flat, places


def shared_scratch(phases):
    flat, places = [], []
    for p in phases:
        mine = []
        for x in p.scratch:
            common = any(x is y for y in STREAM_SCRATCH)
            at = [i for i, y in enumerate(flat) if y is x] if common else []
            if not at:
                flat.append(x)
            mine.append(at[0] if at else len(flat) - 1)
        places.append(mine)
    return flat, places


def chain_kernel(phases, zc, inside, in_places, n_scratch, scratch_places, *refs):
    zi, zo, zs = zc.counts()
    n_fetch = sum(inside)
    ins, z_in, outs, z_out, scratch, z_scratch, held, sems = split_refs(
        refs,
        len(inside),
        zi,
        sum(len(p.outs) for p in phases),
        zo,
        n_scratch,
        zs,
        n_fetch,
        1,
    )
    operands, n = [], 0
    for ref, fetch in zip(ins, inside):
        operands.append(Fetched(ref, held[n], sems[0].at[n]) if fetch else ref)
        n += fetch
    for x in operands:
        if isinstance(x, Fetched):
            x.copy.start()
    z = zc.make(z_in + z_out + z_scratch)
    if isinstance(phases[0], Scatter):
        z.ahead = max(z.ahead, 6)
    links = Links(z)
    enter(links.partner, links.xn, links.yn, bool(zc.plan) or any(p.late for p in phases))
    z.start()
    rows = None
    for p, here, there in zip(phases, in_places, scratch_places):
        links.more = p is not phases[-1]
        made, outs = outs[: len(p.outs)], outs[len(p.outs) :]
        mine, room = tuple(operands[i] for i in here), tuple(scratch[i] for i in there)
        rows = p.run(links, rows, mine, made, room)
    links.finish()
    need(operands)


def chain_call(name, cid, phases, z=NO_Z):
    vmem = pl.BlockSpec(memory_space=pltpu.VMEM)
    anywhere = pl.BlockSpec(memory_space=pl.ANY)
    spec = lambda inside: vmem if inside else anywhere
    ins, in_places = shared_ins(phases)
    scratch, scratch_places = shared_scratch(phases)
    outs = [x for p in phases for x in p.outs]
    out = pl.pallas_call(
        functools.partial(
            chain_kernel,
            phases,
            z,
            [i for _, i in ins],
            in_places,
            len(scratch),
            scratch_places,
        ),
        out_shape=(*(shape for shape, _ in outs), *z.out_shapes),
        in_specs=[anywhere] * len(ins) + z.in_specs(),
        out_specs=tuple(spec(i) for _, i in outs) + z.out_specs(),
        scratch_shapes=[
            *scratch,
            *z.scratch,
            *(pltpu.VMEM(x.shape, x.dtype) for x, i in ins if i),
            pltpu.SemaphoreType.DMA((max(1, sum(i for _, i in ins)),)),
        ],
        compiler_params=pltpu.CompilerParams(
            collective_id=cid, has_side_effects=True, vmem_limit_bytes=62 << 20
        ),
        input_output_aliases=z.aliases(len(ins), len(outs)),
        cost_estimate=cost(1 << 20),
        name=name,
    )(*(x for x, _ in ins), *z.arrays)
    z.done(out[len(outs) :])
    return split_refs(out, *(len(p.outs) for p in phases))


def gather_only_kernel(C, n, n_after, zc, *refs):
    zi, zo, zs = zc.counts()
    xs, _, z_in, fulls, z_out, (send, recv, loc), z_scratch = split_refs(
        refs, n, n_after, zi, n, zo, 3, zs
    )
    R, D = xs[0].shape
    rc = R // C
    me, core, bx, by, partner, xn, yn = peers()
    z = zc.make(z_in + z_out + z_scratch)
    enter(partner, xn, yn, bool(zc.plan))
    sent = []

    def copy(src, a, k, target, rel, sidx, whose):
        rows = pl.ds(pl.multiple_of(whose * R + k * rc, rc), rc)
        return pltpu.make_async_remote_copy(
            src_ref=fulls[a].at[rows, :] if src is None else src,
            dst_ref=fulls[a].at[rows, :],
            send_sem=send.at[a, sidx, k],
            recv_sem=recv.at[a, rel, k],
            device_id={"mp": target},
            device_id_type=MESH,
        )

    def push(*args):
        c = copy(*args)
        c.start()
        sent.append(c)

    def arrive(a, k, rel):
        copy(None, a, k, partner, rel, 0, owner(rel, core, bx, by)).wait_recv()

    kept = []
    for a in range(n):
        for k in range(C):
            own = xs[a].at[pl.ds(k * rc, rc), :]
            push(own, a, k, xn, 2, 1, me)
            push(own, a, k, yn, 4, 2, me)
            push(own, a, k, partner, 1, 0, me)
        c = pltpu.make_async_copy(
            xs[a], fulls[a].at[pl.ds(pl.multiple_of(me * R, R), R), :], loc.at[a]
        )
        c.start()
        kept.append(c)
    z.start()
    across = jnp.where(core == 0, xn, yn)
    x_core = owner(2, core, bx, by)
    y_core = owner(4, core, bx, by)
    through = jnp.where(core == 0, y_core, x_core)
    steps = [(a, k) for a in range(n) for k in range(C)]
    for i in range(len(steps) + 1):
        if i < len(steps):
            a, k = steps[i]
            arrive(a, k, 2)
            arrive(a, k, 4)
            push(None, a, k, across, 6, 3, through)
            push(None, a, k, partner, 3, 4, x_core)
            push(None, a, k, partner, 5, 5, y_core)
        if i >= 1:
            a, k = steps[i - 1]
            arrive(a, k, 6)
            push(None, a, k, partner, 7, 6, owner(6, core, bx, by))
        z.tick(-(-len(zc.plan) // (len(steps) + 1)))
    for a, k in steps:
        for rel in (1, 3, 5, 7):
            arrive(a, k, rel)
    z.finish()
    for c in sent:
        c.wait_send()
    for c in kept:
        c.wait()


def gather_only(cid, xs, after=(), z=NO_Z, C=4):
    R, D = xs[0].shape
    n = len(xs)
    anywhere = pl.BlockSpec(memory_space=pl.ANY)
    out = pl.pallas_call(
        functools.partial(gather_only_kernel, C, n, len(after), z),
        out_shape=tuple(jax.ShapeDtypeStruct((8 * R, D), x.dtype) for x in xs) + tuple(z.out_shapes),
        in_specs=[anywhere] * (n + len(after)) + z.in_specs(),
        out_specs=(anywhere,) * n + z.out_specs(),
        scratch_shapes=[
            pltpu.SemaphoreType.DMA((n, 7, C)),
            pltpu.SemaphoreType.DMA((n, 8, C)),
            pltpu.SemaphoreType.DMA((n,)),
            *z.scratch,
        ],
        compiler_params=pltpu.CompilerParams(collective_id=cid, has_side_effects=True),
        input_output_aliases=z.aliases(n + len(after), n),
        cost_estimate=cost(1 << 20),
        name="gather_rows",
    )(*xs, *after, *z.arrays)
    z.done(out[n:])
    return out[:n]


def tiles(n, step, f):
    step = min(step, n)

    @pl.loop(0, n // step)
    def _(j):
        f(pl.ds(pl.multiple_of(j * step, step), step))


def put(ref, pieces, cols, value):
    at = 0
    for rows in pieces:
        ref[rows, cols] = value[at : at + rows.size]
        at += rows.size


def take(ref, pieces, cols):
    parts = [ref[rows, cols] for rows in pieces]
    return parts[0] if len(parts) == 1 else jnp.concatenate(parts, axis=0)


def project_body(first, lhs, pieces, ins, outs):
    w, shift = ins

    def f(cols):
        put(outs[0], pieces, cols, (nn(lhs(), w[:, cols]) + shift[:, cols]).astype(jnp.bfloat16))

    tiles(w.shape[1], 256, f)


def gelu_both(v):
    t = jnp.tanh(0.7978845608028654 * (v + 0.044715 * v * v * v))
    d = 0.5 * (1.0 + t) + 0.5 * v * (1.0 - t * t) * (
        0.7978845608028654 * (1.0 + 3 * 0.044715 * v * v)
    )
    return (0.5 * v * (1.0 + t)).astype(jnp.bfloat16), d.astype(jnp.bfloat16)


def up_body(first, lhs, pieces, ins, outs):
    w, shift = ins

    def f(cols):
        active, slope = gelu_both(nn(lhs(), w[:, cols]) + shift[:, cols])
        put(outs[0], pieces, cols, active)
        put(outs[1], pieces, cols, slope)

    tiles(w.shape[1], 256, f)


def wide_nt(src, w, cols):
    Z, _, d = w.shape
    total = None
    for z in range(Z):
        t = nt(src[:, z * d : (z + 1) * d], w[z, cols, :])
        total = t if total is None else total + t
    return total


def down_back_body(first, lhs, pieces, ins, outs):
    w, slope = ins

    def f(cols):
        g = wide_nt(lhs(), w, cols) * take(slope, pieces, cols).astype(jnp.float32)
        g = g.astype(jnp.bfloat16)
        put(outs[0], pieces, cols, g)
        sums = jnp.sum(g.astype(jnp.float32), axis=0, keepdims=True)
        if first:
            outs[1][:, cols] = sums
        else:
            outs[1][:, cols] += sums

    tiles(w.shape[1], 256, f)


def dense_back_body(first, lhs, pieces, ins, outs):
    (w,) = ins

    def f(cols):
        put(outs[0], pieces, cols, wide_nt(lhs(), w, cols).astype(jnp.bfloat16))

    tiles(w.shape[1], 256, f)


def row_split_body(rows, ins, out):
    a, w = ins
    Z, _, d = w.shape
    for z in range(Z):
        out[:, z * d : (z + 1) * d] = nn(a[rows, :], w[z]).astype(out.dtype)


def up_back_body(rows, ins, out):
    a, w = ins

    def f(cols):
        out[:, cols] = nt(a[rows, :], w[cols, :]).astype(out.dtype)

    tiles(w.shape[0], 512, f)


def project_back_body(rows, ins, out):
    a, w = ins
    S, _, width = a.shape

    def f(cols):
        total = None
        for s in range(S):
            t = nt(a[s, rows, :], w[cols, s * width : (s + 1) * width])
            total = t if total is None else total + t
        out[:, cols] = total.astype(out.dtype)

    tiles(w.shape[0], 512, f)


class Stream:
    def __init__(self, chunks, buf, sems, stage, out_sems):
        self.chunks, self.buf, self.sems = chunks, buf, sems
        self.stage, self.out_sems = stage, out_sems
        self.turn, self.flying = 0, [[], []]

    def fetch(self, i):
        src, j = self.chunks[i]
        w = self.buf.shape[2]
        return pltpu.make_async_copy(
            src.at[:, pl.ds(j * w, w)], self.buf.at[i % 2], self.sems.at[i % 2]
        )

    def get(self, i):
        self.fetch(i).wait()
        if i + 1 < len(self.chunks):
            self.fetch(i + 1).start()
        return self.buf.at[i % 2]

    def result(self, make, targets):
        slot = self.turn % 2
        self.turn += 1
        for c in self.flying[slot]:
            c.wait()
        make(self.stage.at[slot])
        self.flying[slot] = []
        for n, (lo, width, dest) in enumerate(targets):
            c = pltpu.make_async_copy(
                self.stage.at[slot, :, pl.ds(lo, width)], dest, self.out_sems.at[slot, n]
            )
            c.start()
            self.flying[slot].append(c)

    def drain(self):
        for slot in range(2):
            for c in self.flying[slot]:
                c.wait()
            self.flying[slot] = []


STREAM_SCRATCH = (
    pltpu.VMEM((2, 2048, 256), jnp.bfloat16),
    pltpu.SemaphoreType.DMA((2,)),
    pltpu.VMEM((2, 256, 1024), jnp.bfloat16),
    pltpu.SemaphoreType.DMA((2, 4)),
    pltpu.VMEM((256, 2048), jnp.bfloat16),
)


def tile_product(turned, right, lo, half):
    def make(tile):
        def f(cols):
            at = pl.ds(pl.multiple_of(lo + cols.start, 256), cols.size)
            tile[:, cols] = nn(turned[...], right[:, at]).astype(tile.dtype)

        tiles(half, 256, f)

    return make


def down_steps(stream, out, turned, held, held_copy, chunk, n, w):
    half = stream.stage.shape[2]
    D = held.shape[1]
    d = out.shape[2]
    steps = []

    def step(j, h):
        if h == 0:
            turned[...] = chunk(j).T
        if j == 0 and h == 0 and held_copy is not None:
            held_copy.wait()
        targets = [
            (b * d, d, out.at[h * (half // d) + b, pl.ds(j * w, w), :]) for b in range(half // d)
        ]
        stream.result(tile_product(turned, held, h * half, half), targets)

    for j in range(n):
        for h in range(D // half):
            steps.append(functools.partial(step, j, h))
    return steps


def up_steps(stream, out, turned, hidden, first, D, w):
    F = hidden.shape[1]
    d = out.shape[2]

    def step(j):
        turned[...] = stream.get(first + j)[...].T
        z, r = (j * w) // d, (j * w) % d
        targets = [(b * d, d, out.at[z, pl.ds(b * d + r, w), :]) for b in range(F // d)]
        stream.result(tile_product(turned, hidden, 0, F), targets)

    return [functools.partial(step, j) for j in range(D // w)]


def down_filler(ins, more, more_out, scratch):
    active, grad = more
    (down_out,) = more_out
    buf, sems, stage, out_sems, turned, held, held_sem = scratch
    T, F = active.shape
    D = grad.shape[1]
    w = buf.shape[2]
    n = F // w
    stream = Stream([(active, j) for j in range(n)], buf, sems, stage, out_sems)
    held_copy = pltpu.make_async_copy(grad, held, held_sem)
    stream.fetch(0).start()
    held_copy.start()
    steps = down_steps(
        stream, down_out, turned, held, held_copy, lambda j: stream.get(j)[...], n, w
    )
    return steps + [stream.drain]


def up_filler(ins, more, more_out, scratch):
    hidden, normed = more
    buf, sems, stage, out_sems, turned = scratch
    D = normed.shape[1]
    w = buf.shape[2]
    stream = Stream([(normed, j) for j in range(D // w)], buf, sems, stage, out_sems)
    stream.fetch(0).start()
    return up_steps(stream, more_out[0], turned, hidden, 0, D, w) + [stream.drain]


def last_filler(ins, more, more_out, scratch):
    active, w_down = ins
    slope, grad = more
    hidden_out, sum_out, down_out = more_out
    stage, out_sems, turned, held, held_sem = scratch
    T, F = active.shape
    w = turned.shape[0]
    stream = Stream([], None, None, stage, out_sems)
    held_copy = pltpu.make_async_copy(grad, held, held_sem)
    held_copy.start()

    def back(i):
        if i == 0:
            held_copy.wait()
        rows = pl.ds(i * BLOCK, BLOCK)
        down_back_body(
            i == 0, lambda: held[rows, :], [rows], (w_down, slope), (hidden_out, sum_out)
        )

    steps = [functools.partial(back, i) for i in range(T // BLOCK)]
    steps += down_steps(
        stream, down_out, turned, held, None, lambda j: active[:, j * w : (j + 1) * w], F // w, w
    )
    return steps + [stream.drain]


def attn_filler(ins, more, more_out, scratch):
    parts = ins[0]
    context, grad, normed = more
    (out,) = more_out
    buf, sems, stage, out_sems, turned, ctx_t = scratch
    S, T, width = parts.shape
    D = grad.shape[1]
    Z = out.shape[0]
    d = D // Z
    w = buf.shape[2]
    n = D // w
    stream = Stream(
        [(context, 0)] + [(grad, j) for j in range(n)] + [(normed, j) for j in range(n)],
        buf,
        sems,
        stage,
        out_sems,
    )
    stream.fetch(0).start()
    steps = []

    def dense(j):
        def step():
            if j == 0:
                ctx_t[...] = stream.get(0)[...].T
            right = stream.get(1 + j)

            def make(tile):
                tile[:, :w] = nn(ctx_t[...], right[...]).astype(tile.dtype)

            z, r = (j * w) // d, (j * w) % d
            stream.result(make, [(0, w, out.at[z, pl.ds(0, width), pl.ds(r, w)])])

        return step

    def project(j):
        def step():
            turned[...] = stream.get(1 + n + j)[...].T

            def make(tile):
                for s in range(S):
                    tile[:, s * width : (s + 1) * width] = nn(turned[...], parts[s]).astype(
                        tile.dtype
                    )

            z, r = (j * w) // d, (j * w) % d
            side = pl.ds(r // w * width, width)
            stream.result(
                make,
                [(s * width, width, out.at[z, pl.ds(width + s * w, w), side]) for s in range(S)],
            )

        return step

    for j in range(n):
        steps.append(dense(j))
    for j in range(n):
        steps.append(project(j))
    steps.append(stream.drain)
    return steps


class Finish:
    late = 0

    def __init__(self, v, u):
        self.ins = [(v, True), (u, True)]
        self.outs = [
            (jax.ShapeDtypeStruct(v.shape, v.dtype), True),
            (jax.ShapeDtypeStruct(u.shape, u.dtype), True),
        ]
        self.scratch = [
            pltpu.VMEM((6, *v.shape), v.dtype),
            pltpu.VMEM((6, *u.shape), u.dtype),
            pltpu.VMEM((5, *v.shape), v.dtype),
            pltpu.VMEM((5, *u.shape), u.dtype),
            pltpu.SemaphoreType.DMA((2, 5)),
            pltpu.SemaphoreType.DMA((2, 5)),
        ]

    def run(self, links, _, ins, outs, scratch):
        v_ref, u_ref = need(ins)
        v_out, u_out = outs
        vs, us, v_in, u_in, send, recv = scratch
        _, z1, z2, _ = z_peers()
        hops = [({"mp": n}, False) for n in (links.partner, links.xn, links.yn)]
        hops += [({"dp": z1}, True), ({"dp": z2}, True)]
        vs[0] = v_ref[...]
        vs[0, 0:2, :] = links.made[1][0:2, :]
        us[3] = u_ref[...]
        for i, (target, both) in enumerate(hops):
            copies = []
            for n, (src, dst) in enumerate(((vs, v_in), (us, u_in))[: 2 if both else 1]):
                c = pltpu.make_async_remote_copy(
                    src_ref=src.at[i],
                    dst_ref=dst.at[i],
                    send_sem=send.at[n, i],
                    recv_sem=recv.at[n, i],
                    device_id=target,
                    device_id_type=MESH,
                )
                c.start()
                copies.append(c)
            links.tick(2)
            for c in copies:
                c.wait()
            vs[i + 1] = vs[i] + v_in[i]
            if both:
                us[i + 1] = us[i] + u_in[i]
        v_out[...] = vs[5]
        u_out[...] = us[5]


def place_kernel(moves, n_src, *refs):
    (v, u), srcs, outs, small, (low, wide, in_sem, out_sem) = split_refs(refs, 2, n_src, 4, 5, 4)
    gain, shift, bias, of_project, of_up = small
    for l in range(gain.shape[0]):
        at = 6 * l
        order = (0, 2, 1, 3, 4, 5) if l == 0 else (at + 4, at, at + 5, at + 1, at + 2, at + 3)
        for i, ref in enumerate((gain, shift, bias)):
            for j in range(2):
                r = order[2 * i + j]
                ref[l, j : j + 1, :] = v[r : r + 1, :]
        width = of_project.shape[2]
        for j in range(2):
            of_project[l, j : j + 1, :] = u[l : l + 1, j * width : (j + 1) * width]
        of_up[l : l + 1, :] = u[l : l + 1, 2 * width :]
    depth = low.shape[0]

    def fetch(i):
        s, row, _ = moves[i]
        return pltpu.make_async_copy(
            srcs[s].at[pl.ds(row, ZR), :], low.at[i % depth], in_sem.at[i % depth]
        )

    def store(i):
        _, _, targets = moves[i]
        copies = []
        for n, (o, index, lo, width) in enumerate(targets):
            copies.append(
                pltpu.make_async_copy(
                    wide.at[i % depth, :, pl.ds(lo, width)],
                    outs[o].at[index],
                    out_sem.at[i % depth, n],
                )
            )
        return copies

    for i in range(min(depth, len(moves))):
        fetch(i).start()
    for i in range(len(moves)):
        fetch(i).wait()
        if i >= depth:
            for c in store(i - depth):
                c.wait()
        wide[i % depth] = low[i % depth].astype(jnp.float32)
        for c in store(i):
            c.start()
        if i + depth < len(moves):
            fetch(i + depth).start()
    for i in range(max(0, len(moves) - depth), len(moves)):
        for c in store(i):
            c.wait()


def place_call(sums, out_shapes, targets_of, v, u, small):
    vmem = pl.BlockSpec(memory_space=pltpu.VMEM)
    arrays, moves = [], []
    for key, row, array, at in sums:
        if not any(a is array for a in arrays):
            arrays.append(array)
        i = [a is array for a in arrays].index(True)
        moves.append((i, at, targets_of(key, row)))
    w = arrays[0].shape[1]
    depth = 12
    anywhere = pl.BlockSpec(memory_space=pl.ANY)
    return pl.pallas_call(
        functools.partial(place_kernel, moves, len(arrays)),
        out_shape=tuple(out_shapes) + tuple(small),
        in_specs=[vmem] * 2 + [anywhere] * len(arrays),
        out_specs=(anywhere,) * len(out_shapes) + (vmem,) * len(small),
        scratch_shapes=[
            pltpu.VMEM((depth, ZR, w), jnp.bfloat16),
            pltpu.VMEM((depth, ZR, w), jnp.float32),
            pltpu.SemaphoreType.DMA((depth,)),
            pltpu.SemaphoreType.DMA((depth, 2)),
        ],
        compiler_params=pltpu.CompilerParams(vmem_limit_bytes=62 << 20),
        cost_estimate=cost(1 << 20),
        name="place",
    )(v, u, *arrays)


def first_kernel(C, zc, n_project, *refs):
    zi, zo, zs = zc.counts()
    ins, z_in, outs, z_out, scratch, z_scratch = split_refs(refs, 6, zi, 6, zo, 14, zs)
    x_ref, gain_ref, bias_ref, shift_ref, up_ref, down_ref = ins
    full_ref, project_ref, up_out, down_out = *outs[:2], outs[2:4], outs[4:6]
    x_low, w_here, w_sem, wide, low, wide_sem, low_sem, *mine = scratch
    buf, send, recv, loc, wide2, low2, total_ref = mine
    R, D = x_ref.shape
    rc = R // C
    me, core, bx, by, partner, xn, yn = peers()
    z = zc.make(z_in + z_out + z_scratch)

    pieces = []
    both = ((up_ref, up_out, wide, low, 0), (down_ref, down_out, wide2, low2, 1))
    for l in range(2):
        for ref, out, w, n, stage in both:
            size = w.shape[1]
            pieces += [
                (ref.at[l, pl.ds(r, size), :], out[l].at[pl.ds(r, size), :], w, n, stage)
                for r in range(0, ref.shape[1], size)
            ]

    def read(i):
        src, _, w, _, stage = pieces[i]
        return pltpu.make_async_copy(src, w.at[i % 2], wide_sem.at[stage, i % 2])

    def write(i):
        _, dst, _, n, stage = pieces[i]
        return pltpu.make_async_copy(n.at[i % 2], dst, low_sem.at[stage, i % 2])

    def cast(i):
        _, _, w, n, _ = pieces[i]
        read(i).wait()
        if i >= 2:
            write(i - 2).wait()
        n[i % 2] = w[i % 2].astype(n.dtype)
        write(i).start()
        if i + 2 < len(pieces):
            read(i + 2).start()

    for i in range(2):
        read(i).start()
    z.ahead = n_project
    enter(partner, xn, yn, True)
    z.start()

    @pl.loop(0, R // 16)
    def _(i):
        rows = pl.ds(pl.multiple_of(i * 16, 16), 16)
        v = x_ref[rows, :].astype(jnp.float32)
        x_low[rows, :] = layer_norm(v, gain_ref[...], bias_ref[...]).astype(x_low.dtype)

    sent = []

    def copy(src, rel, k, target, sidx):
        return pltpu.make_async_remote_copy(
            src_ref=src,
            dst_ref=buf.at[k, rel],
            send_sem=send.at[sidx, k],
            recv_sem=recv.at[rel, k],
            device_id={"mp": target},
            device_id_type=MESH,
        )

    def push(src, rel, k, target, sidx):
        c = copy(src, rel, k, target, sidx)
        c.start()
        sent.append(c)

    def arrive(rel, k):
        copy(buf.at[k, 0], rel, k, partner, 0).wait_recv()

    for k in range(C):
        own = x_low.at[pl.ds(k * rc, rc), :]
        push(own, 2, k, xn, 1)
        push(own, 4, k, yn, 2)
        push(own, 1, k, partner, 0)
    kept = [
        pltpu.make_async_copy(
            x_low, full_ref.at[pl.ds(pl.multiple_of(me * R, R), R), :], loc.at[0, 0]
        )
    ]
    kept[0].start()
    starts = [pl.multiple_of(owner(rel, core, bx, by) * R, R) for rel in range(8)]
    across = jnp.where(core == 0, xn, yn)
    for k in range(C + 1):
        if k < C:
            arrive(2, k)
            arrive(4, k)
            push(buf.at[k, 4 - 2 * core], 6, k, across, 3)
            push(buf.at[k, 2], 3, k, partner, 4)
            push(buf.at[k, 4], 5, k, partner, 5)
        if k >= 1:
            arrive(6, k - 1)
            push(buf.at[k - 1, 6], 7, k - 1, partner, 6)
        for i in range(2 * k, min(2 * k + 2, len(pieces))):
            cast(i)
        z.tick((0, 0, 3, 2, 1)[k])
    for k in range(C):
        for rel in range(1, 8):
            if rel in (1, 3, 5, 7):
                arrive(rel, k)
            start = pl.multiple_of(starts[rel] + k * rc, rc)
            c = pltpu.make_async_copy(
                buf.at[k, rel], full_ref.at[pl.ds(start, rc), :], loc.at[k, rel]
            )
            c.start()
            kept.append(c)
    for i in range(2 * C + 2, len(pieces)):
        cast(i)
    for i in range(len(pieces) - 2, len(pieces)):
        write(i).wait()
    z.tick(n_project)
    Z, per, _ = w_here.shape
    parts = w_sem.shape[0]
    size = per // parts
    for p in range(parts):
        z.settle((p + 1) * n_project // parts)
        here = pl.ds(p * size, size)
        weights = pltpu.make_async_copy(z_out[0].at[:, here, :], w_here.at[:, here, :], w_sem.at[p])
        weights.start()
        weights.wait()
        for rel in range(8):
            rows = pl.ds(starts[rel], R)

            def f(cols, rel=rel, rows=rows):
                lhs = []
                for i in range(Z):
                    depth = pl.ds(i * per + p * size, size)
                    x = x_low[:, depth] if rel == 0 else buf[:, rel, :, depth].reshape(R, size)
                    lhs.append(x)
                w = w_here[:, here, cols].reshape(Z * size, cols.size)
                term = nn(jnp.concatenate(lhs, axis=1), w)
                if p > 0:
                    term = term + total_ref[rows, cols]
                if p < parts - 1:
                    total_ref[rows, cols] = term
                else:
                    project_ref[rows, cols] = (term + shift_ref[:, cols]).astype(jnp.bfloat16)

            tiles(project_ref.shape[1], 256, f)
            z.tick()
    z.finish()
    for c in sent:
        c.wait_send()
    for c in kept:
        c.wait()


def first_call(cid, x, gain, bias, shift, up, down, z, n_project, C=4):
    R, D = x.shape
    N = shift.shape[0]
    w = z.arrays[0]
    vmem = pl.BlockSpec(memory_space=pltpu.VMEM)
    anywhere = pl.BlockSpec(memory_space=pl.ANY)
    low = jnp.bfloat16
    out = pl.pallas_call(
        functools.partial(first_kernel, C, z, n_project),
        out_shape=(
            jax.ShapeDtypeStruct((8 * R, D), low),
            jax.ShapeDtypeStruct((8 * R, N), low),
            *[jax.ShapeDtypeStruct(up.shape[1:], low)] * 2,
            *[jax.ShapeDtypeStruct(down.shape[1:], low)] * 2,
            *z.out_shapes,
        ),
        in_specs=[vmem] * 4 + [anywhere] * 2 + z.in_specs(),
        out_specs=(anywhere, vmem) + (anywhere,) * 4 + z.out_specs(),
        scratch_shapes=[
            pltpu.VMEM((R, D), low),
            pltpu.VMEM((4, *w.shape[1:]), low),
            pltpu.SemaphoreType.DMA((2,)),
            pltpu.VMEM((2, 256, up.shape[2]), jnp.float32),
            pltpu.VMEM((2, 256, up.shape[2]), low),
            pltpu.SemaphoreType.DMA((2, 2)),
            pltpu.SemaphoreType.DMA((2, 2)),
            pltpu.VMEM((C, 8, R // C, D), low),
            pltpu.SemaphoreType.DMA((7, C)),
            pltpu.SemaphoreType.DMA((8, C)),
            pltpu.SemaphoreType.DMA((C, 8)),
            pltpu.VMEM((2, 512, down.shape[2]), jnp.float32),
            pltpu.VMEM((2, 512, down.shape[2]), low),
            pltpu.VMEM((8 * R, N), jnp.float32),
            *z.scratch,
        ],
        compiler_params=pltpu.CompilerParams(
            collective_id=cid, has_side_effects=True, vmem_limit_bytes=60 << 20
        ),
        cost_estimate=cost(1 << 20),
        name="first",
    )(x, gain[None], bias[None], shift[None], up, down, *z.arrays)
    z.done(out[6:])
    return out[:6]


def gather_sum(part):
    return lax.psum_scatter(
        part.astype(jnp.bfloat16), "mp", scatter_dimension=0, tiled=True
    ).astype(jnp.float32)


def gather_all(x):
    return lax.all_gather(x, "mp", axis=0, tiled=True)


def side_by_side(w):
    return jnp.concatenate([w[z] for z in range(w.shape[0])], axis=1)


def reduce_dp(part):
    return lax.psum_scatter(part.astype(jnp.bfloat16), "dp", scatter_dimension=0)


class Fast:
    def __init__(self, T, D):
        self.T, self.D = T, D
        self.backlog = Backlog()
        self.rows = None

    def start(self, x, gain, bias, shift, out_grad, weights):
        project, dense, up, down = weights
        low = jnp.bfloat16
        project = project.reshape(*project.shape[:2], -1).astype(low)
        dense = dense.astype(low)
        self.weights = queue = GatherQueue()
        queue.add(("project", 0), project, 0, 64)
        n_project = project.shape[1] // 64
        rows, out, up0, up1, down0, down1 = first_call(
            0, x, gain, bias, shift, up, down, queue.take(n_project), n_project
        )
        self.first = rows, out
        for key, shard in (
            (("up", 0), up0),
            (("down", 0), down0),
            (("project", 1), project[1]),
            (("up", 1), up1),
        ):
            queue.arrays[key] = lax.all_gather(shard, "dp", axis=0)
        queue.add(("dense", 0), dense, 0, 128)
        (self.grad_rows,) = gather_only(8, (out_grad,), z=queue.take(2))
        queue.add(("dense", 1), dense, 1, 128)
        queue.add(("down", 1), down1[None], 0, 128)

    def weight(self, name, l):
        w = self.weights.arrays[name, l]
        return w.reshape(-1, w.shape[2]) if name in ("project", "up") else w

    def shape(self, width, dtype=jnp.bfloat16):
        return jax.ShapeDtypeStruct((self.T, width), dtype)

    def packed(self, rows):
        return jax.ShapeDtypeStruct((4, rows, self.D // 4), jnp.bfloat16), False

    def scatter(self, ins, body, epilogue, **more):
        return Scatter(self.T, self.D, ins, body, epilogue, **more)

    def gather(self, x, ins, outs, body, **more):
        return Gather(self.T // 8, self.D, x, ins, outs, body, **more)

    def project(self, l, shift):
        if l == 0:
            return self.first
        w = self.weight("project", l)
        phase = self.gather(self.rows, (w, shift[None]), (self.shape(w.shape[1]),), project_body)
        return chain_call("gather_project", 10 * l, [phase], self.weights.take(2))[0]

    def attend(self, l, project, slopes):
        return attend_fwd(20 + l, project, slopes, NO_Z)

    def attn_out(self, l, stream, context, bias, gain, shift, up_shift):
        phase = self.scatter(
            (context, self.weight("dense", l)), row_split_body, AddNorm(stream, bias, gain, shift, True)
        )
        z = self.weights.take(3 * l)
        ((middle, rows),) = chain_call("dense_scatter", 10 * l + 1, [phase], z)
        w = self.weight("up", l)
        shape = self.shape(w.shape[1])
        phase = self.gather(rows, (w, up_shift[None]), (shape, shape), up_body)
        z = self.weights.take(5 * l)
        return middle, *chain_call("gather_up", 10 * l + 2, [phase], z)[0]

    def ffn_out(self, l, middle, active, bias, gain, shift):
        phase = self.scatter(
            (active, self.weight("down", l)),
            row_split_body,
            AddNorm(middle, bias, gain, shift, True),
            more=((self.grad_rows, False),),
        )
        ((stream, self.rows),) = chain_call("down_scatter", 10 * l + 3, [phase])
        return stream

    def last_out(self, l, middle, active, slope, bias):
        T, F = active.shape
        grad = self.grad_rows
        phase = self.scatter(
            (active, self.weight("down", l)),
            row_split_body,
            AddOnly(middle, bias),
            more=((slope, True), (grad, False)),
            more_out=(
                (self.shape(F), True),
                (jax.ShapeDtypeStruct((1, F), jnp.float32), True),
                self.packed(F),
            ),
            scratch=(*STREAM_SCRATCH[2:], pltpu.VMEM((T, self.D), jnp.bfloat16), pltpu.SemaphoreType.DMA),
            filler=last_filler,
        )
        ((rows, grad_hidden, sums, packed),) = chain_call("last_scatter", 10 * l + 3, [phase])
        self.backlog.add(("down", l), packed)
        return rows, grad, grad_hidden, sums

    def ffn_back(self, l, grad, middle, gain, grad_hidden, active, normed, grad_down):
        T, F = active.shape
        epilogue = NormBack(grad, middle, gain)
        ins = (grad_hidden, self.weight("up", l))
        up = dict(
            more=((grad_hidden, True), (normed, False)),
            more_out=(self.packed(F),),
            scratch=STREAM_SCRATCH,
            filler=up_filler,
        )
        down = dict(
            more=((active, False), (grad_down, False)),
            more_out=(self.packed(F),),
            scratch=STREAM_SCRATCH
            + (pltpu.VMEM((T, self.D), jnp.bfloat16), pltpu.SemaphoreType.DMA),
            filler=down_filler,
        )
        beside = dict(up, late=1) if l else dict(down, late=6)
        first = self.scatter(ins, up_back_body, epilogue, **beside)
        w = self.weight("dense", l)
        beside = {} if l else up
        second = self.gather(None, (w,), (self.shape(w.shape[1]),), dense_back_body, **beside)
        z = self.backlog.take(8 if l else 5)
        one, two = chain_call("ffn_back", 10 * l + 5, [first, second], z)
        self.backlog.add(("up" if l else "down", l), one[2], one[3])
        if not l:
            self.backlog.add(("up", l), two[2])
        return one[0], one[1], two[0], two[1]

    def attend_back(self, l, project, grad_context, context, log_norms, slopes):
        z = self.backlog.take(0 if l else 2)
        return attend_bwd(22 + l, project, grad_context, context, log_norms, slopes, z)

    def project_back(self, grad, stream, gain, grad_project, l, context, grad_branch, normed, late):
        S, T, width = grad_project.shape
        return self.scatter(
            (grad_project, self.weight("project", l)),
            project_back_body,
            NormBack(grad, stream, gain),
            more=((context, False), (grad_branch, False), (normed, False)),
            more_out=(self.packed((S + 1) * width),),
            scratch=STREAM_SCRATCH + (pltpu.VMEM((width, T), jnp.bfloat16),),
            filler=attn_filler,
            late=late,
        )

    def attn_back(self, l, grad, stream, gain, grad_project, context, grad_branch, normed, slope):
        first = self.project_back(
            grad, stream, gain, grad_project, l, context, grad_branch, normed, 3
        )
        F = slope.shape[1]
        w = self.weight("down", l - 1)
        second = self.gather(
            None,
            (w, slope),
            (self.shape(F), jax.ShapeDtypeStruct((1, F), jnp.float32)),
            down_back_body,
        )
        one, two = chain_call("attn_back", 10 * l + 7, [first, second], self.backlog.take(7))
        self.backlog.add(("attn", l), one[2], one[3])
        return one[0], one[1], two

    def first_attn_back(
        self, grad, stream, gain, grad_project, context, grad_branch, normed, rows, split
    ):
        chunks = 4 * grad_project.shape[2] // ZR
        first = self.project_back(
            grad, stream, gain, grad_project, 0, context, grad_branch, normed, chunks
        )
        v = jnp.concatenate([jnp.zeros((2, self.D), jnp.float32), jnp.stack(rows)])
        u = jnp.pad(split, ((0, -split.shape[0] % 8), (0, 0)))
        second = Finish(jnp.pad(v, ((0, -v.shape[0] % 8), (0, 0))), u)
        one, two = chain_call("first_attn_back", 7, [first, second], self.backlog.take(1000))
        self.backlog.add(("attn", 0), one[2], one[3])
        return one[0], two[0], two[1]

    def results(self, shapes, small, v, u):
        layers, d, parts, width = shapes[0]
        group = self.D // lax.axis_size("dp")

        def targets(key, row):
            kind, l = key
            if kind == "down":
                return [(3, (l, pl.ds(row, ZR)), 0, group)]
            if kind == "up":
                b, r = divmod(row, group)
                return [(2, (l, pl.ds(r, ZR), pl.ds(b * group, group)), 0, group)]
            if row < width:
                return [(1, (l, pl.ds(row, ZR)), 0, group)]
            s, r = divmod(row - width, width)
            return [(0, (l, s, pl.ds(h * width + r, ZR)), h * width, width) for h in range(2)]

        shapes = [(layers, parts, d, width), *shapes[1:]]
        shape = lambda x: jax.ShapeDtypeStruct(x, jnp.float32)
        out = place_call(
            self.backlog.sums,
            [shape(x) for x in shapes],
            targets,
            v,
            u,
            [shape(x) for x in (small[2], small[2], small[2], small[0], small[1])],
        )
        out = (*out[:4], out[7], out[8], *out[4:7])
        return (out[0].transpose(0, 2, 1, 3), *out[1:])


class Plain:
    def __init__(self, T, D):
        self.T, self.D = T, D
        self.ffn, self.attn = {}, {}

    def start(self, x, gain, bias, shift, out_grad, weights):
        self.rows = layer_norm(x.astype(jnp.float32), gain, bias).astype(jnp.bfloat16)
        self.out_grad = out_grad
        low = jnp.bfloat16
        self.weights = []
        for l in range(weights[0].shape[0]):
            project, dense, up, down = (x[l].astype(low) for x in weights)
            project = project.reshape(project.shape[0], -1)
            self.weights.append(
                (
                    lax.all_gather(project, "dp", axis=0, tiled=True),
                    lax.all_gather(dense, "dp", axis=0),
                    lax.all_gather(up, "dp", axis=0, tiled=True),
                    lax.all_gather(down, "dp", axis=0),
                )
            )

    def project(self, l, shift):
        full = gather_all(self.rows)
        return full, (nn(full, self.weights[l][0]) + shift).astype(jnp.bfloat16)

    def attend(self, l, project, slopes):
        return attend_fwd(0, project, slopes, NO_Z)

    def attn_out(self, l, stream, context, bias, gain, shift, up_shift):
        middle = stream + gather_sum(nn(context, side_by_side(self.weights[l][1]))) + bias
        full = gather_all(layer_norm(middle, gain, shift).astype(jnp.bfloat16))
        return middle, full, *gelu_both(nn(full, self.weights[l][2]) + up_shift)

    def ffn_out(self, l, middle, active, bias, gain, shift):
        stream = middle + gather_sum(nn(active, side_by_side(self.weights[l][3]))) + bias
        self.rows = layer_norm(stream, gain, shift).astype(jnp.bfloat16)
        return stream

    def down_back(self, l, grad, slope):
        full = gather_all(grad)
        g = (nt(full, side_by_side(self.weights[l][3])) * slope.astype(jnp.float32)).astype(
            jnp.bfloat16
        )
        return full, g, jnp.sum(g.astype(jnp.float32), axis=0, keepdims=True)

    def last_out(self, l, middle, active, slope, bias):
        rows = middle + gather_sum(nn(active, side_by_side(self.weights[l][3]))) + bias
        return rows.astype(jnp.bfloat16), *self.down_back(l, self.out_grad, slope)

    def norm_back(self, grad, values, gain, total):
        back = jax.vjp(layer_norm, values.astype(jnp.float32), gain, gain)[1]
        step, gain_sum, shift_sum = back(total)
        grad = grad + step
        return grad, jnp.stack([gain_sum, shift_sum, jnp.sum(grad, axis=0)])

    def ffn_back(self, l, grad, middle, gain, grad_hidden, active, normed, grad_down):
        Z = lax.axis_size("dp")
        F = grad_hidden.shape[1]
        d = self.D // Z
        up = jnp.einsum("td,tf->df", normed, grad_hidden, preferred_element_type=jnp.float32)
        down = jnp.einsum(
            "tf,tzd->zfd", active, grad_down.reshape(-1, Z, d), preferred_element_type=jnp.float32
        )
        self.ffn[l] = reduce_dp(up.reshape(Z, d, F)), reduce_dp(down)
        total = gather_sum(nt(grad_hidden, self.weights[l][2]))
        grad, sums = self.norm_back(grad, middle, gain, total)
        full = gather_all(grad.astype(jnp.bfloat16))
        return grad, sums, full, nt(full, side_by_side(self.weights[l][1])).astype(jnp.bfloat16)

    def attend_back(self, l, project, grad_context, context, log_norms, slopes):
        return attend_bwd(0, project, grad_context, context, log_norms, slopes, NO_Z)

    def project_back(self, l, grad, stream, gain, grad_project, context, grad_branch, normed):
        S, T, width = grad_project.shape
        w = self.weights[l][0]
        Z = lax.axis_size("dp")
        d = self.D // Z
        dense = jnp.einsum(
            "ti,tzd->zid", context, grad_branch.reshape(T, Z, d), preferred_element_type=jnp.float32
        )
        project = jnp.einsum(
            "td,sti->dsi", normed, grad_project, preferred_element_type=jnp.float32
        )
        self.attn[l] = reduce_dp(project.reshape(Z, d, S, width)), reduce_dp(dense)
        part = sum(nt(grad_project[s], w[:, s * width : (s + 1) * width]) for s in range(S))
        return self.norm_back(grad, stream, gain, gather_sum(part))

    def attn_back(self, l, grad, stream, gain, grad_project, context, grad_branch, normed, slope):
        grad, sums = self.project_back(
            l, grad, stream, gain, grad_project, context, grad_branch, normed
        )
        return grad, sums, self.down_back(l - 1, grad.astype(jnp.bfloat16), slope)

    def first_attn_back(
        self, grad, stream, gain, grad_project, context, grad_branch, normed, rows, split
    ):
        grad, sums = self.project_back(
            0, grad, stream, gain, grad_project, context, grad_branch, normed
        )
        rows = jnp.concatenate([sums[:2], jnp.stack(rows)])
        return grad, lax.psum(rows, ("dp", "mp")), lax.psum(split, "dp")

    def results(self, shapes, small, total, split):
        grads = [(*self.attn[l], *self.ffn[l]) for l in range(shapes[0][0])]
        matrices = tuple(jnp.stack(parts).astype(jnp.float32) for parts in zip(*grads))
        parts = [jnp.concatenate([total[2:6], total[:2]])]
        parts += [total[6 * l : 6 * l + 6] for l in range(1, len(grads))]
        pick = lambda i, j: jnp.stack([jnp.stack([p[i], p[j]]) for p in parts])
        n = small[0][1] * small[0][2]
        split = split[:, :n].reshape(small[0]), split[:, n:]
        return (*matrices, *split, pick(4, 0), pick(5, 1), pick(2, 3))


def shards(
    inputs,
    out_grad,
    project_weight,
    dense_weight,
    up_weight,
    down_weight,
    project_bias,
    up_bias,
    norm_gain,
    norm_bias,
    output_bias,
):
    tensor_size = lax.axis_size("mp")
    tensor_rank = lax.axis_index("mp")
    row_count, model_width = inputs.shape
    total_rows = row_count * tensor_size
    inner_width = project_weight.shape[3]
    heads_here = N_HEADS // tensor_size
    layer_count = project_weight.shape[0]
    slopes = 2.0 ** (
        -8.0
        * (tensor_rank * heads_here + lax.iota(jnp.int32, heads_here) + 1).astype(jnp.float32)
        / N_HEADS
    )
    fast = tensor_size == 8 and lax.axis_size("dp") == 4 and row_count == 256
    ops = (Fast if fast else Plain)(total_rows, model_width)
    none = jnp.zeros((inner_width,), jnp.float32)
    shifts = [
        jnp.concatenate([project_bias[l, 0], none, project_bias[l, 1]]) for l in range(layer_count)
    ]
    weights = (project_weight, dense_weight, up_weight, down_weight)
    ops.start(inputs, norm_gain[0, 0], norm_bias[0, 0], shifts[0], out_grad, weights)
    stream = inputs
    last = layer_count - 1
    stored = []
    for l in range(layer_count):
        normed_all, project = ops.project(l, shifts[l])
        context, log_norms = ops.attend(l, project, slopes)
        middle, normed2_all, active, slope = ops.attn_out(
            l,
            stream,
            context,
            output_bias[l, 0],
            norm_gain[l, 1],
            norm_bias[l, 1],
            up_bias[l],
        )
        stored.append(
            (stream, normed_all, project, log_norms, context, middle, normed2_all, active, slope)
        )
        if l < last:
            stream = ops.ffn_out(
                l, middle, active, output_bias[l, 1], norm_gain[l + 1, 0], norm_bias[l + 1, 0]
            )
    outputs, *step = ops.last_out(last, middle, active, slope, output_bias[last, 1])
    grad = out_grad
    down_bias_grad = jnp.sum(grad.astype(jnp.float32), axis=0)
    sums = [None] * layer_count
    split = [None] * layer_count
    for l in reversed(range(layer_count)):
        stream, normed_all, project, log_norms, context, middle, normed2_all, active, _ = stored[l]
        grad_down, grad_hidden, up_bias_part = step
        grad, second, grad_branch, grad_context = ops.ffn_back(
            l, grad, middle, norm_gain[l, 1], grad_hidden, active, normed2_all, grad_down
        )
        grad_project, project_bias_part = ops.attend_back(
            l, project, grad_context, context, log_norms, slopes
        )
        sums[l] = [second[0], second[1], second[2], down_bias_grad]
        split[l] = jnp.concatenate([project_bias_part.reshape(-1), up_bias_part.reshape(-1)])
        args = (grad, stream, norm_gain[l, 0], grad_project, context, grad_branch, normed_all)
        if l:
            grad, first, step = ops.attn_back(l, *args, stored[l - 1][-1])
            sums[l] += [first[0], first[1]]
            down_bias_grad = first[2]
    rows = sums[0] + [x for parts in sums[1:] for x in parts]
    grad, total, split = ops.first_attn_back(*args, rows, jnp.stack(split))
    shapes = [x.shape for x in weights]
    small = [x.shape for x in (project_bias, up_bias, norm_gain)]
    return outputs, grad, *ops.results(shapes, small, total, split)


def solution(mesh):
    rows = P(("dp", "mp"), None)
    specs = (P(None, "dp", None, "mp"), P(None, "mp", "dp"), P(None, "dp", "mp"), P(None, "mp", "dp"))
    biases = (P(None, None, "mp"), P(None, "mp"), P(), P(), P())
    return jax.shard_map(
        shards,
        mesh=mesh,
        in_specs=(rows, rows, *specs, *biases),
        out_specs=(rows, rows, *specs, *biases),
        check_vma=False,
    )
```

```python
import functools

import jax
import jax.numpy as jnp
from jax import lax
from jax.experimental import pallas as pl
from jax.experimental.pallas import tpu as pltpu
from jax.sharding import PartitionSpec as P

N_HEADS = 16
BLOCK = 256
HEAD = 128
LOG2E = 1.4426950408889634
MESH = pl.DeviceIdType.MESH
NT_DIMS = (((1,), (1,)), ((), ()))
norm_eps = 1e-05


def nt(a, b):
    return lax.dot_general(a, b, NT_DIMS, preferred_element_type=jnp.float32)


def nn(a, b):
    return jnp.dot(a, b, preferred_element_type=jnp.float32)


def layer_norm(values, scale_row, shift_row):
    centre = jnp.mean(values, axis=-1, keepdims=True)
    centred = values - centre
    spread = jnp.mean(centred * centred, axis=-1, keepdims=True)
    return centred * lax.rsqrt(spread + norm_eps) * scale_row + shift_row


def peers():
    me = lax.axis_index("mp")
    core = me % 2
    bx = (me // 2) % 2
    by = me // 4
    return me, core, bx, by, me + 1 - 2 * core, me + 2 - 4 * bx, me + 4 - 8 * by


def owner(rel, core, bx, by):
    c = core if rel % 2 == 0 else 1 - core
    x = bx if (rel // 2) % 2 == 0 else 1 - bx
    y = by if rel // 4 == 0 else 1 - by
    return y * 4 + x * 2 + c


def z_peers():
    z = lax.axis_index("dp")
    z1 = z + 1 - 2 * (z % 2)
    return z, z1, (z + 2) % 4, (z1 + 2) % 4


def enter(partner, xn, yn, z=False):
    barrier = pltpu.get_barrier_semaphore()
    for n in (partner, xn, yn):
        pl.semaphore_signal(barrier, inc=1, device_id={"mp": n}, device_id_type=MESH)
    if z:
        _, z1, z2, _ = z_peers()
        for n in (z1, z2):
            pl.semaphore_signal(barrier, inc=1, device_id={"dp": n}, device_id_type=MESH)
    pl.semaphore_wait(barrier, 5 if z else 3)


ZR = 128


class ZSum:
    ahead = 3

    def __init__(self, plan, srcs, out, scratch):
        self.plan, self.srcs, self.out = plan, srcs, out[0]
        self.recv, self.own, self.send_sem, self.recv_sem, self.loc = scratch
        self.z, self.z1, self.z2, self.z3 = z_peers()
        self.sent, self.begun = [], False
        self.events = [functools.partial(self.event, c) for c in range(len(plan))]

    def block(self, c, z):
        i, row = self.plan[c]
        return self.srcs[i].at[z, pl.ds(row, ZR), :]

    def remote(self, src, kind, c, target):
        return pltpu.make_async_remote_copy(
            src_ref=src,
            dst_ref=self.recv.at[kind, c],
            send_sem=self.send_sem.at[kind, c],
            recv_sem=self.recv_sem.at[kind, c],
            device_id={"dp": target},
            device_id_type=MESH,
        )

    def push(self, *args):
        c = self.remote(*args)
        c.start()
        self.sent.append(c)

    def here(self, kind, c):
        return pltpu.make_async_copy(
            self.block(c, self.z2 if kind else self.z), self.own.at[kind, c], self.loc.at[kind, c]
        )

    def arrive(self, kind, c):
        self.remote(self.own.at[0, c], kind, c, self.z1).wait_recv()

    def start(self):
        self.begun = True
        for c in range(min(self.ahead, len(self.plan))):
            self.push(self.block(c, self.z3), 1, c, self.z1)
        for c in range(len(self.plan)):
            self.here(1, c).start()
            self.here(0, c).start()

    def event(self, c):
        if c + self.ahead < len(self.plan):
            n = c + self.ahead
            self.push(self.block(n, self.z3), 1, n, self.z1)
        self.arrive(1, c)
        self.here(1, c).wait()

        @pl.loop(0, ZR // 16)
        def _(i):
            rows = pl.ds(pl.multiple_of(i * 16, 16), 16)
            self.own[1, c, rows, :] = (
                self.own[1, c, rows, :].astype(jnp.float32)
                + self.recv[1, c, rows, :].astype(jnp.float32)
            ).astype(jnp.bfloat16)

        self.push(self.own.at[1, c], 2, c, self.z2)
        self.push(self.block(c, self.z1), 0, c, self.z1)

    def tick(self, n=1):
        n = min(n, len(self.events)) if self.begun else 0
        for _ in range(n):
            self.events.pop(0)()
        return n > 0

    def finish(self):
        self.tick(len(self.events))
        for c in range(len(self.plan)):
            self.here(0, c).wait()
            self.arrive(0, c)
            self.arrive(2, c)

            @pl.loop(0, ZR // 16)
            def _(i):
                rows = pl.ds(pl.multiple_of(i * 16, 16), 16)
                to = pl.ds(pl.multiple_of(c * ZR + i * 16, 16), 16)
                self.out[to, :] = (
                    self.own[0, c, rows, :].astype(jnp.float32)
                    + self.recv[0, c, rows, :].astype(jnp.float32)
                    + self.recv[2, c, rows, :].astype(jnp.float32)
                ).astype(jnp.bfloat16)

        for c in self.sent:
            c.wait_send()


class ZGather:
    ahead = 4

    def __init__(self, plan, srcs, outs, scratch):
        self.plan, self.srcs, self.outs = plan, srcs, outs
        self.send_sem, self.recv_sem, self.loc = scratch
        self.z, self.z1, self.z2, self.z3 = z_peers()
        self.sent = []
        self.passed, self.settled = 0, 0

    def place(self, c, z):
        i, row, size, _ = self.plan[c]
        return self.outs[i].at[z, pl.ds(row, size), :]

    def own(self, c):
        i, row, size, layer = self.plan[c]
        return self.srcs[i].at[layer, pl.ds(row, size), :]

    def remote(self, src, z, kind, c, target):
        return pltpu.make_async_remote_copy(
            src_ref=src,
            dst_ref=self.place(c, z),
            send_sem=self.send_sem.at[kind, c],
            recv_sem=self.recv_sem.at[kind, c],
            device_id={"dp": target},
            device_id_type=MESH,
        )

    def push(self, *args):
        c = self.remote(*args)
        c.start()
        self.sent.append(c)

    def here(self, c):
        return pltpu.make_async_copy(self.own(c), self.place(c, self.z), self.loc.at[c])

    def start(self):
        for c in range(len(self.plan)):
            if c < self.ahead:
                self.send_own(c)
            self.here(c).start()

    def send_own(self, c):
        self.push(self.own(c), self.z, 0, c, self.z2)
        self.push(self.own(c), self.z, 1, c, self.z1)

    def event(self, c):
        if c + self.ahead < len(self.plan):
            self.send_own(c + self.ahead)
        self.remote(self.own(c), self.z2, 0, c, self.z2).wait_recv()
        self.push(self.place(c, self.z2), self.z2, 2, c, self.z1)

    def tick(self, n=1):
        n = min(n, len(self.plan) - self.passed)
        for _ in range(n):
            self.event(self.passed)
            self.passed += 1
        return n > 0

    def settle(self, n):
        self.tick(n - self.passed)
        for c in range(self.settled, n):
            self.remote(self.own(c), self.z1, 1, c, self.z1).wait_recv()
            self.remote(self.own(c), self.z3, 2, c, self.z1).wait_recv()
            self.here(c).wait()
        self.settled = n

    def finish(self):
        self.settle(len(self.plan))
        for c in self.sent:
            c.wait_send()


class NoZ:
    ahead = 0

    def start(self):
        pass

    def tick(self, n=1):
        return False

    def finish(self):
        pass


class ZCall:
    plan, arrays, out_shapes, out_space, scratch = (), (), (), pltpu.VMEM, ()

    def make(self, refs):
        return NoZ()

    def done(self, results):
        pass

    def aliases(self, first_in, first_out):
        return {}

    def counts(self):
        return len(self.arrays), len(self.out_shapes), len(self.scratch)

    def in_specs(self):
        return [pl.BlockSpec(memory_space=pl.ANY)] * len(self.arrays)

    def out_specs(self):
        return (pl.BlockSpec(memory_space=self.out_space),) * len(self.out_shapes)


def sum_scratch(n, w):
    return (
        pltpu.VMEM((3, n, ZR, w), jnp.bfloat16),
        pltpu.VMEM((2, n, ZR, w), jnp.bfloat16),
        pltpu.SemaphoreType.DMA((3, n)),
        pltpu.SemaphoreType.DMA((3, n)),
        pltpu.SemaphoreType.DMA((2, n)),
    )


class SumCall(ZCall):
    def __init__(self, backlog, limit):
        self.plan, self.arrays, self.pieces = [], [], []
        while limit and backlog.queue:
            entry = backlog.queue[0]
            key, array, row = entry
            if not any(a is array for a in self.arrays):
                self.arrays.append(array)
            i = [a is array for a in self.arrays].index(True)
            self.pieces.append((key, row))
            self.plan.append((i, row))
            limit -= 1
            entry[2] += ZR
            if entry[2] == array.shape[1]:
                backlog.queue.pop(0)
        self.backlog = backlog
        n = len(self.plan)
        if n:
            w = self.arrays[0].shape[2]
            self.out_shapes = (jax.ShapeDtypeStruct((n * ZR, w), jnp.bfloat16),)
            self.scratch = sum_scratch(n, w)

    def make(self, refs):
        i, o, _ = self.counts()
        return ZSum(self.plan, refs[:i], refs[i : i + o], refs[i + o :]) if self.plan else NoZ()

    def done(self, results):
        for n, (key, row) in enumerate(self.pieces):
            self.backlog.sums.append((key, row, results[0], n * ZR))


class Backlog:
    def __init__(self):
        self.queue, self.sums = [], []

    def add(self, key, array, summed=None):
        done = 0 if summed is None else summed.shape[0]
        self.sums += [(key, row, summed, row) for row in range(0, done, ZR)]
        self.queue.append([key, array, done])

    def take(self, limit):
        return SumCall(self, limit)


class GatherCall(ZCall):
    out_space = pl.ANY

    def __init__(self, queue, limit):
        self.queue, self.keys, self.plan = queue, [], []
        shards, begun, shapes = [], [], []
        while limit and queue.entries:
            entry = queue.entries[0]
            key, shard, row, size, layer = entry
            if key not in self.keys:
                self.keys.append(key)
                shards.append(shard)
                shapes.append(jax.ShapeDtypeStruct((4, *shard.shape[1:]), shard.dtype))
                if key in queue.arrays:
                    begun.append((len(self.keys) - 1, queue.arrays[key]))
            self.plan.append((self.keys.index(key), row, size, layer))
            limit -= 1
            entry[2] += size
            if entry[2] == shard.shape[1]:
                queue.entries.pop(0)
        self.arrays = shards + [x for _, x in begun]
        self.begun = [i for i, _ in begun]
        self.out_shapes = tuple(shapes)
        n = len(self.plan)
        self.scratch = (
            pltpu.SemaphoreType.DMA((3, n)),
            pltpu.SemaphoreType.DMA((3, n)),
            pltpu.SemaphoreType.DMA((n,)),
        )

    def aliases(self, first_in, first_out):
        n = len(self.keys)
        return {first_in + n + j: first_out + i for j, i in enumerate(self.begun)}

    def make(self, refs):
        i, o, _ = self.counts()
        return ZGather(self.plan, refs[:i], refs[i : i + o], refs[i + o :])

    def done(self, results):
        for key, array in zip(self.keys, results):
            self.queue.arrays[key] = array


class GatherQueue:
    def __init__(self):
        self.entries, self.arrays = [], {}

    def add(self, key, shard, layer, size):
        self.entries.append([key, shard, 0, size, layer])

    def take(self, limit):
        return GatherCall(self, limit) if limit and self.entries else NO_Z


NO_Z = ZCall()


def cost(flops):
    return pl.CostEstimate(flops=flops, bytes_accessed=1 << 16, transcendentals=0)


def split_refs(refs, *counts):
    parts = []
    for n in counts:
        parts.append(refs[:n])
        refs = refs[n:]
    return parts


def bias_tile(slope, first_key, first_query, keys, queries):
    kp = first_key + lax.broadcasted_iota(jnp.int32, (keys, queries), 0)
    qp = first_query + lax.broadcasted_iota(jnp.int32, (keys, queries), 1)
    return (jnp.abs(qp - kp).astype(jnp.float32)) * (-slope * LOG2E)

def scores_t(q, k, slope, i, B):
    L = (i+1)*B
    factor = q.shape[1] ** (-0.5) * LOG2E
    st = nt(k, q) * factor
    key = lax.broadcasted_iota(jnp.int32, (L, 1), 0)
    if i > 0:
        m = i * B
        kp = lax.broadcasted_iota(jnp.int32, (m, 1), 0).astype(jnp.float32)
        qp = (m + lax.broadcasted_iota(jnp.int32, (1, B), 1)).astype(jnp.float32)
        head = st[:m] - (qp - kp) * (slope * LOG2E)
        tail = st[m:] + bias_tile(slope, 0, 0, B, B)
        return head, tail
    return None, st + bias_tile(slope, 0, 0, B, B)

def enter_z(zc):
    if zc.plan:
        _, z1, z2, _ = z_peers()
        barrier = pltpu.get_barrier_semaphore()
        for n in (z1, z2):
            pl.semaphore_signal(barrier, inc=1, device_id={"dp": n}, device_id_type=MESH)
        pl.semaphore_wait(barrier, 2)


def attend_fwd_kernel(zc, slope_ref, p_ref, *refs):
    zi, zo, zs = zc.counts()
    z_in, (ctx_ref, lse_ref), z_out, (vt_ref,), z_scratch = split_refs(refs, zi, 2, zo, 1, zs)
    z = zc.make(z_in + z_out + z_scratch)
    enter_z(zc)
    z.start()
    B = BLOCK
    T, W = p_ref.shape
    H = W // (3 * HEAD)
    for h in range(H):
        q, k, v = (pl.ds((part * H + h) * HEAD, HEAD) for part in range(3))
        slope = slope_ref[h]
        vt_ref[...] = p_ref[:, v].T
        for i in range(T // B):
            L = (i + 1) * B
            head, tail = scores_t(p_ref[i * B : L, q], p_ref[:L, k], slope, i, B)
            top = jnp.max(tail, axis=0, keepdims=True)
            if head is not None:
                top = jnp.maximum(top, jnp.max(head, axis=0, keepdims=True))
            pt = jnp.exp2(tail - top)
            den = jnp.sum(pt, axis=0, keepdims=True)
            ct = nn(vt_ref[:, i * B : L], pt.astype(jnp.bfloat16))
            if head is not None:
                ph = jnp.exp2(head - top)
                den = den + jnp.sum(ph, axis=0, keepdims=True)
                ct = ct + nn(vt_ref[:, : i * B], ph.astype(jnp.bfloat16))
            ctx_ref[i * B : L, pl.ds(h * HEAD, HEAD)] = (ct / den).T.astype(ctx_ref.dtype)
            lse_ref[h, i : i + 1, :] = top + jnp.log2(den)
            if i % 4 == 3:
                z.tick()
    z.finish()


def attend_bwd_kernel(zc, slope_ref, p_ref, g_ref, c_ref, lse_ref, *refs):
    zi, zo, zs = zc.counts()
    z_in, (out_ref, sums_ref), z_out, (kt_ref, dk_ref, dv_ref), z_scratch = split_refs(
        refs, zi, 2, zo, 3, zs
    )
    z = zc.make(z_in + z_out + z_scratch)
    enter_z(zc)
    z.start()
    B = BLOCK
    T, W = p_ref.shape
    H = W // (3 * HEAD)
    n = T // B
    factor = HEAD ** (-0.5)
    ones = jnp.ones((8, HEAD), jnp.float32)
    for h in range(H):
        qc, kc, vc = (pl.ds((part * H + h) * HEAD, HEAD) for part in range(3))
        cols = pl.ds(h * HEAD, HEAD)
        slope = slope_ref[h]
        kt_ref[...] = p_ref[:, kc].T
        qsum = jnp.zeros((1, HEAD), jnp.float32)
        for i in reversed(range(n)):
            L = (i + 1) * B
            q = p_ref[i * B : L, qc]
            g = g_ref[i * B : L, cols]
            head, tail = scores_t(q, p_ref[:L, kc], slope, i, B)
            prod = g.astype(jnp.float32) * c_ref[i * B : L, cols].astype(jnp.float32)
            inner = lax.dot_general(
                ones,
                prod,
                NT_DIMS,
                preferred_element_type=jnp.float32,
                precision=lax.Precision.HIGHEST,
            )[:1]
            lse = lse_ref[h, i : i + 1, :]
            dpt = nt(p_ref[:L, vc], g)
            dqt = None
            for part, lo, hi in ((head, 0, i * B), (tail, i * B, L)):
                if part is None:
                    continue
                pt = jnp.exp2(part - lse)
                ds = (pt * (dpt[lo:hi] - inner)).astype(jnp.bfloat16)
                pt = pt.astype(jnp.bfloat16)
                dk = nn(ds, q)
                dv = nn(pt, g)
                if i == n - 1:
                    dk_ref[lo:hi, :] = dk
                    dv_ref[lo:hi, :] = dv
                else:
                    dk_ref[lo:hi, :] += dk
                    dv_ref[lo:hi, :] += dv
                t = nn(kt_ref[:, lo:hi], ds)
                dqt = t if dqt is None else dqt + t
            dq = (dqt * factor).T.astype(jnp.bfloat16)
            out_ref[0, i * B : L, cols] = dq
            qsum += jnp.sum(dq.astype(jnp.float32), axis=0, keepdims=True)
            if i % 4 == 3:
                z.tick()
        out_ref[1, :, cols] = (dk_ref[...] * factor).astype(jnp.bfloat16)
        dv = dv_ref[...].astype(jnp.bfloat16)
        out_ref[2, :, cols] = dv
        sums_ref[0:1, cols] = qsum
        sums_ref[1:2, cols] = jnp.sum(dv.astype(jnp.float32), axis=0, keepdims=True)
    z.finish()


def attend_call(kernel, cid, name, slopes, arrays, outs, scratch, z):
    vmem = pl.BlockSpec(memory_space=pltpu.VMEM)
    out = pl.pallas_call(
        functools.partial(kernel, z),
        out_shape=(*outs, *z.out_shapes),
        in_specs=[pl.BlockSpec(memory_space=pltpu.SMEM)] + [vmem] * len(arrays) + z.in_specs(),
        out_specs=(vmem,) * len(outs) + z.out_specs(),
        scratch_shapes=[*scratch, *z.scratch],
        compiler_params=pltpu.CompilerParams(
            collective_id=cid if z.plan else None,
            has_side_effects=bool(z.plan),
            vmem_limit_bytes=60 << 20,
        ),
        input_output_aliases=z.aliases(1 + len(arrays), len(outs)),
        cost_estimate=cost(1 << 20),
        name=name,
    )(slopes, *arrays, *z.arrays)
    z.done(out[len(outs) :])
    return out[: len(outs)]


def attend_fwd(cid, project, slopes, z):
    T, W = project.shape
    H = W // (3 * HEAD)
    outs = (
        jax.ShapeDtypeStruct((T, H * HEAD), jnp.bfloat16),
        jax.ShapeDtypeStruct((H, T // BLOCK, BLOCK), jnp.float32),
    )
    scratch = (pltpu.VMEM((HEAD, T), jnp.bfloat16),)
    return attend_call(attend_fwd_kernel, cid, "attend_fwd", slopes, (project,), outs, scratch, z)


def attend_bwd(cid, project, grad_context, context, lse, slopes, z):
    T, W = project.shape
    H = W // (3 * HEAD)
    outs = (
        jax.ShapeDtypeStruct((3, T, H * HEAD), jnp.bfloat16),
        jax.ShapeDtypeStruct((2, H * HEAD), jnp.float32),
    )
    scratch = (
        pltpu.VMEM((HEAD, T), jnp.bfloat16),
        pltpu.VMEM((T, HEAD), jnp.float32),
        pltpu.VMEM((T, HEAD), jnp.float32),
    )
    arrays = (project, grad_context, context, lse)
    return attend_call(attend_bwd_kernel, cid, "attend_bwd", slopes, arrays, outs, scratch, z)


class Links:
    def __init__(self, z):
        self.me, self.core, self.bx, self.by, self.partner, self.xn, self.yn = peers()
        self.z, self.late = z, NoZ()
        self.more, self.made = False, ()
        self.sent, self.kept = [], []

    def owner(self, rel):
        return owner(rel, self.core, self.bx, self.by)

    def tick(self, n=1):
        for _ in range(n):
            if not self.z.tick() and not self.late.tick():
                break

    def finish(self):
        self.z.finish()
        self.late.finish()
        for c in self.sent:
            c.wait_send()
        for c in self.kept:
            c.wait()


class Fetched:
    def __init__(self, src, ref, sem):
        self.ref, self.copy, self.here = ref, pltpu.make_async_copy(src, ref, sem), False

    def wait(self):
        if not self.here:
            self.copy.wait()
        self.here = True


def need(operands):
    for x in operands:
        if isinstance(x, Fetched):
            x.wait()
    return refs_of(operands)


def refs_of(operands):
    return tuple(x.ref if isinstance(x, Fetched) else x for x in operands)


def fill(steps, n):
    for _ in range(min(n, len(steps))):
        steps.pop(0)()


class Gather:
    late = 0

    def __init__(
        self, R, D, x, ins, outs, body, more=(), more_out=(), scratch=(), filler=None, C=4
    ):
        self.R, self.D, self.C, self.given = R, D, C, x is not None
        self.body, self.filler = body, filler
        self.counts = (len(ins), len(more), len(outs), len(more_out))
        self.ins = [(x, True)] * self.given + [(a, True) for a in ins] + list(more)
        low = jnp.bfloat16
        self.outs = [(jax.ShapeDtypeStruct((8 * R, D), low), False)]
        self.outs += [(o, True) for o in outs] + list(more_out)
        self.scratch = [
            pltpu.VMEM((C, 8, R // C, D), low),
            pltpu.SemaphoreType.DMA((7, C)),
            pltpu.SemaphoreType.DMA((8, C)),
            pltpu.SemaphoreType.DMA((C, 8)),
            *scratch,
        ]

    def run(self, links, x_ref, ins, outs, scratch):
        n_in, n_more, n_out, n_more_out = self.counts
        if self.given:
            (x_ref,), ins = need(ins[:1]), ins[1:]
        ins, more = split_refs(ins, n_in, n_more)
        (full_ref,), outs, more_out = split_refs(outs, 1, n_out, n_more_out)
        buf, send, recv, loc = scratch[:4]
        steps = []
        if self.filler:
            steps = self.filler(refs_of(ins), refs_of(more), more_out, scratch[4:])
            steps = [functools.partial(need, more)] + steps
        R, D, C, body = self.R, self.D, self.C, self.body
        rc = R // C
        partner, xn, yn, core = links.partner, links.xn, links.yn, links.core

        def copy(src, rel, k, target, sidx):
            return pltpu.make_async_remote_copy(
                src_ref=src,
                dst_ref=buf.at[k, rel],
                send_sem=send.at[sidx, k],
                recv_sem=recv.at[rel, k],
                device_id={"mp": target},
                device_id_type=MESH,
            )

        def push(src, rel, k, target, sidx):
            c = copy(src, rel, k, target, sidx)
            c.start()
            links.sent.append(c)

        def arrive(rel, k):
            copy(buf.at[k, 0], rel, k, partner, 0).wait_recv()

        def keep(src, start, size, k, rel):
            c = pltpu.make_async_copy(src, full_ref.at[pl.ds(start, size), :], loc.at[k, rel])
            c.start()
            links.kept.append(c)

        def place(rel, k):
            return pl.multiple_of(links.owner(rel) * R + k * rc, rc)

        def run(k, lo, hi):
            starts = [place(rel, k) for rel in range(lo, hi)]
            for rel, start in zip(range(lo, hi), starts):
                keep(buf.at[k, rel], start, rc, k, rel)
            body(
                False,
                lambda: buf[k, lo:hi].reshape((hi - lo) * rc, D),
                [pl.ds(start, rc) for start in starts],
                ins,
                outs,
            )

        for k in range(C):
            own = x_ref.at[pl.ds(k * rc, rc), :]
            push(own, 2, k, xn, 1)
            push(own, 4, k, yn, 2)
            push(own, 1, k, partner, 0)
        start = pl.multiple_of(links.me * R, R)
        keep(x_ref, start, R, 0, 0)
        ins = need(ins)
        body(True, lambda: x_ref[...], [pl.ds(start, R)], ins, outs)
        links.tick()
        fill(steps, 2)
        across = jnp.where(core == 0, xn, yn)
        for k in range(C + 2):
            if k < C:
                arrive(2, k)
                arrive(4, k)
                push(buf.at[k, 4 - 2 * core], 6, k, across, 3)
                push(buf.at[k, 2], 3, k, partner, 4)
                push(buf.at[k, 4], 5, k, partner, 5)
            if k == 0:
                starts = [place(1, j) for j in range(C)]
                for j in range(C):
                    arrive(1, j)
                    keep(buf.at[j, 1], starts[j], rc, j, 1)
                body(
                    False,
                    lambda: buf[:, 1].reshape(R, D),
                    [pl.ds(start, rc) for start in starts],
                    ins,
                    outs,
                )
            if 1 <= k <= C:
                arrive(3, k - 1)
                arrive(5, k - 1)
                run(k - 1, 2, 6)
                arrive(6, k - 1)
                push(buf.at[k - 1, 6], 7, k - 1, partner, 6)
            if k >= 2:
                arrive(7, k - 2)
                run(k - 2, 6, 8)
            links.tick()
            fill(steps, 1)
        fill(steps, len(steps))


class Scatter:
    def __init__(
        self,
        T,
        D,
        ins,
        body,
        epilogue,
        more=(),
        more_out=(),
        scratch=(),
        filler=None,
        late=0,
        C=4,
    ):
        R = T // 8
        self.R, self.D, self.C = R, D, C
        self.body, self.epilogue, self.filler, self.late = body, epilogue, filler, late
        self.n_scratch = len(scratch)
        if late:
            w = more_out[0][0].shape[2]
            more_out = [*more_out, (jax.ShapeDtypeStruct((late * ZR, w), jnp.bfloat16), True)]
            scratch = [*scratch, *sum_scratch(late, w)]
        self.counts = (len(ins), len(epilogue.ins), len(more)), (len(epilogue.outs), len(more_out))
        self.ins = [(a, True) for a in ins] + [(a, True) for a in epilogue.ins] + list(more)
        self.outs = [(o, True) for o in epilogue.outs] + list(more_out)
        self.scratch = [
            pltpu.VMEM((8, R, D), jnp.bfloat16),
            pltpu.VMEM((7, R, D), jnp.bfloat16),
            pltpu.SemaphoreType.DMA((7, C)),
            pltpu.SemaphoreType.DMA((7, C)),
            *epilogue.scratch,
            *scratch,
        ]

    def run(self, links, _, ins, outs, scratch):
        ins, end_ins, more = split_refs(ins, *self.counts[0])
        end_outs, more_out = split_refs(outs, *self.counts[1])
        (pbuf, rbuf, send, recv), end_scratch, scratch, late_scratch = split_refs(
            scratch, 4, len(self.epilogue.scratch), self.n_scratch, 5 if self.late else 0
        )
        steps = []
        if self.late:
            plan = [(0, ZR * c) for c in range(self.late)]
            links.late = ZSum(plan, more_out[:1], more_out[-1:], late_scratch)
            more_out = more_out[:-1]
        if self.filler:
            steps = self.filler(refs_of(ins), refs_of(more), more_out, scratch)
            steps = [functools.partial(need, more)] + steps + [links.late.start]
        ins = need(ins)
        R, D, C = self.R, self.D, self.C
        rc = R // C
        core, bx, by, partner = links.core, links.bx, links.by, links.partner
        dn = jnp.where(core == 0, links.yn, links.xn)
        fn = jnp.where(core == 0, links.xn, links.yn)

        def copy(src, slot, k, target):
            rows = pl.ds(k * rc, rc)
            return pltpu.make_async_remote_copy(
                src_ref=src.at[rows, :],
                dst_ref=rbuf.at[slot, rows, :],
                send_sem=send.at[slot, k],
                recv_sem=recv.at[slot, k],
                device_id={"mp": target},
                device_id_type=MESH,
            )

        def push(slot, to, target, k):
            c = copy(pbuf.at[slot], to, k, target)
            c.start()
            links.sent.append(c)

        def arrive(slot, k):
            copy(pbuf.at[0], slot, k, partner).wait_recv()

        def dest_rank(which, c):
            if which == 0:
                return (1 - by) * 4 + (1 - bx) * 2 + c
            if which == 3:
                return by * 4 + bx * 2 + c
            flip_y = (1 - c) if which == 1 else c
            y = by + flip_y * (1 - 2 * by)
            x = bx + (1 - flip_y) * (1 - 2 * bx)
            return y * 4 + x * 2 + c

        def compute(which, c, slot, part=0, parts=1):
            n = R // parts
            rows = pl.ds(pl.multiple_of(dest_rank(which, c) * R + part * n, n), n)
            self.body(rows, ins, pbuf.at[slot, pl.ds(part * n, n), :])

        def theirs(which, part=0, parts=1):
            compute(which, 1 - core, which, part, parts)
            for k in range(part * C // parts, (part + 1) * C // parts):
                push(which, which, partner, k)

        def add(slot, rslot, k):
            @pl.loop(0, rc // 16)
            def _(i):
                rows = pl.ds(pl.multiple_of(k * rc + i * 16, 16), 16)
                pbuf[slot, rows, :] = (
                    pbuf[slot, rows, :].astype(jnp.float32)
                    + rbuf[rslot, rows, :].astype(jnp.float32)
                ).astype(pbuf.dtype)

        def join(which, part=0, parts=1):
            for k in range(part * C // parts, (part + 1) * C // parts):
                arrive(which, k)
                add(4 + which, which, k)
                if which < 2:
                    push(4 + which, 4 + which, dn, k)

        theirs(0, 0, 2)
        theirs(0, 1, 2)
        compute(0, core, 4, 0, 2)
        compute(0, core, 4, 1, 2)
        join(0, 0, 2)
        theirs(1)
        join(0, 1, 2)
        compute(1, core, 5)
        theirs(2)
        join(1)
        compute(2, core, 6)
        theirs(3)
        join(2)
        compute(3, core, 7)
        join(3)
        weights = isinstance(links.z, ZGather)
        links.tick(0 if weights else 2 if links.more else 3)
        share = -(-len(steps) // C) if self.late else 2
        for k in range(C):
            arrive(4, k)
            add(6, 4, k)
            push(6, 6, fn, k)
            links.tick(k // 2 if weights else 1 if links.more else 2)
            fill(steps, share)
        fill(steps, len(steps))
        end_ins = need(end_ins)
        self.epilogue.begin(end_outs, end_scratch)
        for k in range(C):
            arrive(5, k)
            arrive(6, k)

            @pl.loop(0, rc // 16)
            def _(i):
                rows = pl.ds(pl.multiple_of(k * rc + i * 16, 16), 16)
                total = (
                    pbuf[7, rows, :].astype(jnp.float32)
                    + rbuf[5, rows, :].astype(jnp.float32)
                    + rbuf[6, rows, :].astype(jnp.float32)
                )
                self.epilogue.rows(rows, total, end_ins, end_outs, end_scratch)

        links.made = end_outs
        return self.epilogue.end(end_outs, end_scratch)


class AddNorm:
    def __init__(self, stream, bias, gain, shift, keep):
        self.ins = (stream, bias[None], gain[None], shift[None])
        self.keep = keep
        low = jax.ShapeDtypeStruct(stream.shape, jnp.bfloat16)
        self.outs = (jax.ShapeDtypeStruct(stream.shape, jnp.float32),) + (low,) * keep
        self.scratch = () if keep else (pltpu.VMEM(stream.shape, jnp.bfloat16),)

    def begin(self, outs, scratch):
        pass

    def rows(self, rows, total, ins, outs, scratch):
        stream, bias, gain, shift = ins
        value = stream[rows, :].astype(jnp.float32) + total + bias[...]
        outs[0][rows, :] = value
        low = outs[1] if self.keep else scratch[0]
        low[rows, :] = layer_norm(value, gain[...], shift[...]).astype(low.dtype)

    def end(self, outs, scratch):
        return None if self.keep else scratch[0]


class AddOnly:
    scratch = ()

    def __init__(self, stream, bias):
        self.ins = (stream, bias[None])
        self.outs = (jax.ShapeDtypeStruct(stream.shape, jnp.bfloat16),)

    def begin(self, outs, scratch):
        pass

    def rows(self, rows, total, ins, outs, scratch):
        outs[0][rows, :] = (ins[0][rows, :] + total + ins[1][...]).astype(jnp.bfloat16)

    def end(self, outs, scratch):
        return None


class NormBack:
    def __init__(self, grad, values, gain):
        R, D = values.shape
        self.ins = (grad, values, gain[None])
        self.outs = (
            jax.ShapeDtypeStruct((R, D), jnp.float32),
            jax.ShapeDtypeStruct((3, D), jnp.float32),
        )
        self.scratch = (pltpu.VMEM((R, D), jnp.bfloat16), pltpu.VMEM((3, 8, D), jnp.float32))

    def begin(self, outs, scratch):
        scratch[1][...] = jnp.zeros_like(scratch[1])

    def rows(self, rows, total, ins, outs, scratch):
        grad, values, gain = ins
        v = values[rows, :].astype(jnp.float32)
        centred = v - jnp.mean(v, axis=-1, keepdims=True)
        scale = lax.rsqrt(jnp.mean(centred * centred, axis=-1, keepdims=True) + norm_eps)
        unit = centred * scale
        inner = total * gain[...]
        mean = jnp.mean(inner, axis=-1, keepdims=True)
        along = jnp.mean(inner * unit, axis=-1, keepdims=True)
        new = grad[rows, :].astype(jnp.float32) + scale * (inner - mean - unit * along)
        outs[0][rows, :] = new
        scratch[0][rows, :] = new.astype(jnp.bfloat16)
        for i, x in enumerate((total * unit, total, new)):
            scratch[1][i] += x[:8] + x[8:]

    def end(self, outs, scratch):
        outs[1][...] = jnp.sum(scratch[1][...], axis=1)
        return scratch[0]


def shared_ins(phases):
    places = []
    flat = []
    for p in phases:
        mine = []
        for x, inside in p.ins:
            at = [i for i, (y, where) in enumerate(flat) if y is x and where == inside]
            if not at:
                flat.append((x, inside))
            mine.append(at[0] if at else len(flat) - 1)
        places.append(mine)
    return flat, places


def shared_scratch(phases):
    flat, places = [], []
    for p in phases:
        mine = []
        for x in p.scratch:
            common = any(x is y for y in STREAM_SCRATCH)
            at = [i for i, y in enumerate(flat) if y is x] if common else []
            if not at:
                flat.append(x)
            mine.append(at[0] if at else len(flat) - 1)
        places.append(mine)
    return flat, places


def chain_kernel(phases, zc, inside, in_places, n_scratch, scratch_places, *refs):
    zi, zo, zs = zc.counts()
    n_fetch = sum(inside)
    ins, z_in, outs, z_out, scratch, z_scratch, held, sems = split_refs(
        refs,
        len(inside),
        zi,
        sum(len(p.outs) for p in phases),
        zo,
        n_scratch,
        zs,
        n_fetch,
        1,
    )
    operands, n = [], 0
    for ref, fetch in zip(ins, inside):
        operands.append(Fetched(ref, held[n], sems[0].at[n]) if fetch else ref)
        n += fetch
    for x in operands:
        if isinstance(x, Fetched):
            x.copy.start()
    z = zc.make(z_in + z_out + z_scratch)
    if isinstance(phases[0], Scatter):
        z.ahead = max(z.ahead, 6)
    links = Links(z)
    enter(links.partner, links.xn, links.yn, bool(zc.plan) or any(p.late for p in phases))
    z.start()
    rows = None
    for p, here, there in zip(phases, in_places, scratch_places):
        links.more = p is not phases[-1]
        made, outs = outs[: len(p.outs)], outs[len(p.outs) :]
        mine, room = tuple(operands[i] for i in here), tuple(scratch[i] for i in there)
        rows = p.run(links, rows, mine, made, room)
    links.finish()
    need(operands)


def chain_call(name, cid, phases, z=NO_Z):
    vmem = pl.BlockSpec(memory_space=pltpu.VMEM)
    anywhere = pl.BlockSpec(memory_space=pl.ANY)
    spec = lambda inside: vmem if inside else anywhere
    ins, in_places = shared_ins(phases)
    scratch, scratch_places = shared_scratch(phases)
    outs = [x for p in phases for x in p.outs]
    out = pl.pallas_call(
        functools.partial(
            chain_kernel,
            phases,
            z,
            [i for _, i in ins],
            in_places,
            len(scratch),
            scratch_places,
        ),
        out_shape=(*(shape for shape, _ in outs), *z.out_shapes),
        in_specs=[anywhere] * len(ins) + z.in_specs(),
        out_specs=tuple(spec(i) for _, i in outs) + z.out_specs(),
        scratch_shapes=[
            *scratch,
            *z.scratch,
            *(pltpu.VMEM(x.shape, x.dtype) for x, i in ins if i),
            pltpu.SemaphoreType.DMA((max(1, sum(i for _, i in ins)),)),
        ],
        compiler_params=pltpu.CompilerParams(
            collective_id=cid, has_side_effects=True, vmem_limit_bytes=62 << 20
        ),
        input_output_aliases=z.aliases(len(ins), len(outs)),
        cost_estimate=cost(1 << 20),
        name=name,
    )(*(x for x, _ in ins), *z.arrays)
    z.done(out[len(outs) :])
    return split_refs(out, *(len(p.outs) for p in phases))


def gather_only_kernel(C, n, n_after, zc, *refs):
    zi, zo, zs = zc.counts()
    xs, _, z_in, fulls, z_out, (send, recv, loc), z_scratch = split_refs(
        refs, n, n_after, zi, n, zo, 3, zs
    )
    R, D = xs[0].shape
    rc = R // C
    me, core, bx, by, partner, xn, yn = peers()
    z = zc.make(z_in + z_out + z_scratch)
    enter(partner, xn, yn, bool(zc.plan))
    sent = []

    def copy(src, a, k, target, rel, sidx, whose):
        rows = pl.ds(pl.multiple_of(whose * R + k * rc, rc), rc)
        return pltpu.make_async_remote_copy(
            src_ref=fulls[a].at[rows, :] if src is None else src,
            dst_ref=fulls[a].at[rows, :],
            send_sem=send.at[a, sidx, k],
            recv_sem=recv.at[a, rel, k],
            device_id={"mp": target},
            device_id_type=MESH,
        )

    def push(*args):
        c = copy(*args)
        c.start()
        sent.append(c)

    def arrive(a, k, rel):
        copy(None, a, k, partner, rel, 0, owner(rel, core, bx, by)).wait_recv()

    kept = []
    for a in range(n):
        for k in range(C):
            own = xs[a].at[pl.ds(k * rc, rc), :]
            push(own, a, k, xn, 2, 1, me)
            push(own, a, k, yn, 4, 2, me)
            push(own, a, k, partner, 1, 0, me)
        c = pltpu.make_async_copy(
            xs[a], fulls[a].at[pl.ds(pl.multiple_of(me * R, R), R), :], loc.at[a]
        )
        c.start()
        kept.append(c)
    z.start()
    across = jnp.where(core == 0, xn, yn)
    x_core = owner(2, core, bx, by)
    y_core = owner(4, core, bx, by)
    through = jnp.where(core == 0, y_core, x_core)
    steps = [(a, k) for a in range(n) for k in range(C)]
    for i in range(len(steps) + 1):
        if i < len(steps):
            a, k = steps[i]
            arrive(a, k, 2)
            arrive(a, k, 4)
            push(None, a, k, across, 6, 3, through)
            push(None, a, k, partner, 3, 4, x_core)
            push(None, a, k, partner, 5, 5, y_core)
        if i >= 1:
            a, k = steps[i - 1]
            arrive(a, k, 6)
            push(None, a, k, partner, 7, 6, owner(6, core, bx, by))
        z.tick(-(-len(zc.plan) // (len(steps) + 1)))
    for a, k in steps:
        for rel in (1, 3, 5, 7):
            arrive(a, k, rel)
    z.finish()
    for c in sent:
        c.wait_send()
    for c in kept:
        c.wait()


def gather_only(cid, xs, after=(), z=NO_Z, C=4):
    R, D = xs[0].shape
    n = len(xs)
    anywhere = pl.BlockSpec(memory_space=pl.ANY)
    out = pl.pallas_call(
        functools.partial(gather_only_kernel, C, n, len(after), z),
        out_shape=tuple(jax.ShapeDtypeStruct((8 * R, D), x.dtype) for x in xs) + tuple(z.out_shapes),
        in_specs=[anywhere] * (n + len(after)) + z.in_specs(),
        out_specs=(anywhere,) * n + z.out_specs(),
        scratch_shapes=[
            pltpu.SemaphoreType.DMA((n, 7, C)),
            pltpu.SemaphoreType.DMA((n, 8, C)),
            pltpu.SemaphoreType.DMA((n,)),
            *z.scratch,
        ],
        compiler_params=pltpu.CompilerParams(collective_id=cid, has_side_effects=True),
        input_output_aliases=z.aliases(n + len(after), n),
        cost_estimate=cost(1 << 20),
        name="gather_rows",
    )(*xs, *after, *z.arrays)
    z.done(out[n:])
    return out[:n]


def tiles(n, step, f):
    step = min(step, n)

    @pl.loop(0, n // step)
    def _(j):
        f(pl.ds(pl.multiple_of(j * step, step), step))


def put(ref, pieces, cols, value):
    at = 0
    for rows in pieces:
        ref[rows, cols] = value[at : at + rows.size]
        at += rows.size


def take(ref, pieces, cols):
    parts = [ref[rows, cols] for rows in pieces]
    return parts[0] if len(parts) == 1 else jnp.concatenate(parts, axis=0)


def project_body(first, lhs, pieces, ins, outs):
    w, shift = ins

    def f(cols):
        put(outs[0], pieces, cols, (nn(lhs(), w[:, cols]) + shift[:, cols]).astype(jnp.bfloat16))

    tiles(w.shape[1], 256, f)


def gelu_both(v):
    t = jnp.tanh(0.7978845608028654 * (v + 0.044715 * v * v * v))
    d = 0.5 * (1.0 + t) + 0.5 * v * (1.0 - t * t) * (
        0.7978845608028654 * (1.0 + 3 * 0.044715 * v * v)
    )
    return (0.5 * v * (1.0 + t)).astype(jnp.bfloat16), d.astype(jnp.bfloat16)


def up_body(first, lhs, pieces, ins, outs):
    w, shift = ins

    def f(cols):
        active, slope = gelu_both(nn(lhs(), w[:, cols]) + shift[:, cols])
        put(outs[0], pieces, cols, active)
        put(outs[1], pieces, cols, slope)

    tiles(w.shape[1], 256, f)


def wide_nt(src, w, cols):
    Z, _, d = w.shape
    total = None
    for z in range(Z):
        t = nt(src[:, z * d : (z + 1) * d], w[z, cols, :])
        total = t if total is None else total + t
    return total


def down_back_body(first, lhs, pieces, ins, outs):
    w, slope = ins

    def f(cols):
        g = wide_nt(lhs(), w, cols) * take(slope, pieces, cols).astype(jnp.float32)
        g = g.astype(jnp.bfloat16)
        put(outs[0], pieces, cols, g)
        sums = jnp.sum(g.astype(jnp.float32), axis=0, keepdims=True)
        if first:
            outs[1][:, cols] = sums
        else:
            outs[1][:, cols] += sums

    tiles(w.shape[1], 256, f)


def dense_back_body(first, lhs, pieces, ins, outs):
    (w,) = ins

    def f(cols):
        put(outs[0], pieces, cols, wide_nt(lhs(), w, cols).astype(jnp.bfloat16))

    tiles(w.shape[1], 256, f)


def row_split_body(rows, ins, out):
    a, w = ins
    Z, _, d = w.shape
    for z in range(Z):
        out[:, z * d : (z + 1) * d] = nn(a[rows, :], w[z]).astype(out.dtype)


def up_back_body(rows, ins, out):
    a, w = ins

    def f(cols):
        out[:, cols] = nt(a[rows, :], w[cols, :]).astype(out.dtype)

    tiles(w.shape[0], 512, f)


def project_back_body(rows, ins, out):
    a, w = ins
    S, _, width = a.shape

    def f(cols):
        total = None
        for s in range(S):
            t = nt(a[s, rows, :], w[cols, s * width : (s + 1) * width])
            total = t if total is None else total + t
        out[:, cols] = total.astype(out.dtype)

    tiles(w.shape[0], 512, f)


class Stream:
    def __init__(self, chunks, buf, sems, stage, out_sems):
        self.chunks, self.buf, self.sems = chunks, buf, sems
        self.stage, self.out_sems = stage, out_sems
        self.turn, self.flying = 0, [[], []]

    def fetch(self, i):
        src, j = self.chunks[i]
        w = self.buf.shape[2]
        return pltpu.make_async_copy(
            src.at[:, pl.ds(j * w, w)], self.buf.at[i % 2], self.sems.at[i % 2]
        )

    def get(self, i):
        self.fetch(i).wait()
        if i + 1 < len(self.chunks):
            self.fetch(i + 1).start()
        return self.buf.at[i % 2]

    def result(self, make, targets):
        slot = self.turn % 2
        self.turn += 1
        for c in self.flying[slot]:
            c.wait()
        make(self.stage.at[slot])
        self.flying[slot] = []
        for n, (lo, width, dest) in enumerate(targets):
            c = pltpu.make_async_copy(
                self.stage.at[slot, :, pl.ds(lo, width)], dest, self.out_sems.at[slot, n]
            )
            c.start()
            self.flying[slot].append(c)

    def drain(self):
        for slot in range(2):
            for c in self.flying[slot]:
                c.wait()
            self.flying[slot] = []


STREAM_SCRATCH = (
    pltpu.VMEM((2, 2048, 256), jnp.bfloat16),
    pltpu.SemaphoreType.DMA((2,)),
    pltpu.VMEM((2, 256, 1024), jnp.bfloat16),
    pltpu.SemaphoreType.DMA((2, 4)),
    pltpu.VMEM((256, 2048), jnp.bfloat16),
)


def tile_product(turned, right, lo, half):
    def make(tile):
        def f(cols):
            at = pl.ds(pl.multiple_of(lo + cols.start, 256), cols.size)
            tile[:, cols] = nn(turned[...], right[:, at]).astype(tile.dtype)

        tiles(half, 256, f)

    return make


def down_steps(stream, out, turned, held, held_copy, chunk, n, w):
    half = stream.stage.shape[2]
    D = held.shape[1]
    d = out.shape[2]
    steps = []

    def step(j, h):
        if h == 0:
            turned[...] = chunk(j).T
        if j == 0 and h == 0 and held_copy is not None:
            held_copy.wait()
        targets = [
            (b * d, d, out.at[h * (half // d) + b, pl.ds(j * w, w), :]) for b in range(half // d)
        ]
        stream.result(tile_product(turned, held, h * half, half), targets)

    for j in range(n):
        for h in range(D // half):
            steps.append(functools.partial(step, j, h))
    return steps


def up_steps(stream, out, turned, hidden, first, D, w):
    F = hidden.shape[1]
    d = out.shape[2]

    def step(j):
        turned[...] = stream.get(first + j)[...].T
        z, r = (j * w) // d, (j * w) % d
        targets = [(b * d, d, out.at[z, pl.ds(b * d + r, w), :]) for b in range(F // d)]
        stream.result(tile_product(turned, hidden, 0, F), targets)

    return [functools.partial(step, j) for j in range(D // w)]


def down_filler(ins, more, more_out, scratch):
    active, grad = more
    (down_out,) = more_out
    buf, sems, stage, out_sems, turned, held, held_sem = scratch
    T, F = active.shape
    D = grad.shape[1]
    w = buf.shape[2]
    n = F // w
    stream = Stream([(active, j) for j in range(n)], buf, sems, stage, out_sems)
    held_copy = pltpu.make_async_copy(grad, held, held_sem)
    stream.fetch(0).start()
    held_copy.start()
    steps = down_steps(
        stream, down_out, turned, held, held_copy, lambda j: stream.get(j)[...], n, w
    )
    return steps + [stream.drain]


def up_filler(ins, more, more_out, scratch):
    hidden, normed = more
    buf, sems, stage, out_sems, turned = scratch
    D = normed.shape[1]
    w = buf.shape[2]
    stream = Stream([(normed, j) for j in range(D // w)], buf, sems, stage, out_sems)
    stream.fetch(0).start()
    return up_steps(stream, more_out[0], turned, hidden, 0, D, w) + [stream.drain]


def last_filler(ins, more, more_out, scratch):
    active, w_down = ins
    slope, grad = more
    hidden_out, sum_out, down_out = more_out
    stage, out_sems, turned, held, held_sem = scratch
    T, F = active.shape
    w = turned.shape[0]
    stream = Stream([], None, None, stage, out_sems)
    held_copy = pltpu.make_async_copy(grad, held, held_sem)
    held_copy.start()

    def back(i):
        if i == 0:
            held_copy.wait()
        rows = pl.ds(i * BLOCK, BLOCK)
        down_back_body(
            i == 0, lambda: held[rows, :], [rows], (w_down, slope), (hidden_out, sum_out)
        )

    steps = [functools.partial(back, i) for i in range(T // BLOCK)]
    steps += down_steps(
        stream, down_out, turned, held, None, lambda j: active[:, j * w : (j + 1) * w], F // w, w
    )
    return steps + [stream.drain]


def attn_filler(ins, more, more_out, scratch):
    parts = ins[0]
    context, grad, normed = more
    (out,) = more_out
    buf, sems, stage, out_sems, turned, ctx_t = scratch
    S, T, width = parts.shape
    D = grad.shape[1]
    Z = out.shape[0]
    d = D // Z
    w = buf.shape[2]
    n = D // w
    stream = Stream(
        [(context, 0)] + [(grad, j) for j in range(n)] + [(normed, j) for j in range(n)],
        buf,
        sems,
        stage,
        out_sems,
    )
    stream.fetch(0).start()
    steps = []

    def dense(j):
        def step():
            if j == 0:
                ctx_t[...] = stream.get(0)[...].T
            right = stream.get(1 + j)

            def make(tile):
                tile[:, :w] = nn(ctx_t[...], right[...]).astype(tile.dtype)

            z, r = (j * w) // d, (j * w) % d
            stream.result(make, [(0, w, out.at[z, pl.ds(0, width), pl.ds(r, w)])])

        return step

    def project(j):
        def step():
            turned[...] = stream.get(1 + n + j)[...].T

            def make(tile):
                for s in range(S):
                    tile[:, s * width : (s + 1) * width] = nn(turned[...], parts[s]).astype(
                        tile.dtype
                    )

            z, r = (j * w) // d, (j * w) % d
            side = pl.ds(r // w * width, width)
            stream.result(
                make,
                [(s * width, width, out.at[z, pl.ds(width + s * w, w), side]) for s in range(S)],
            )

        return step

    for j in range(n):
        steps.append(dense(j))
    for j in range(n):
        steps.append(project(j))
    steps.append(stream.drain)
    return steps


class Finish:
    late = 0

    def __init__(self, v, u):
        self.ins = [(v, True), (u, True)]
        self.outs = [
            (jax.ShapeDtypeStruct(v.shape, v.dtype), True),
            (jax.ShapeDtypeStruct(u.shape, u.dtype), True),
        ]
        self.scratch = [
            pltpu.VMEM((6, *v.shape), v.dtype),
            pltpu.VMEM((6, *u.shape), u.dtype),
            pltpu.VMEM((5, *v.shape), v.dtype),
            pltpu.VMEM((5, *u.shape), u.dtype),
            pltpu.SemaphoreType.DMA((2, 5)),
            pltpu.SemaphoreType.DMA((2, 5)),
        ]

    def run(self, links, _, ins, outs, scratch):
        v_ref, u_ref = need(ins)
        v_out, u_out = outs
        vs, us, v_in, u_in, send, recv = scratch
        _, z1, z2, _ = z_peers()
        hops = [({"mp": n}, False) for n in (links.partner, links.xn, links.yn)]
        hops += [({"dp": z1}, True), ({"dp": z2}, True)]
        vs[0] = v_ref[...]
        vs[0, 0:2, :] = links.made[1][0:2, :]
        us[3] = u_ref[...]
        for i, (target, both) in enumerate(hops):
            copies = []
            for n, (src, dst) in enumerate(((vs, v_in), (us, u_in))[: 2 if both else 1]):
                c = pltpu.make_async_remote_copy(
                    src_ref=src.at[i],
                    dst_ref=dst.at[i],
                    send_sem=send.at[n, i],
                    recv_sem=recv.at[n, i],
                    device_id=target,
                    device_id_type=MESH,
                )
                c.start()
                copies.append(c)
            links.tick(2)
            for c in copies:
                c.wait()
            vs[i + 1] = vs[i] + v_in[i]
            if both:
                us[i + 1] = us[i] + u_in[i]
        v_out[...] = vs[5]
        u_out[...] = us[5]


def place_kernel(moves, n_src, *refs):
    (v, u), srcs, outs, small, (low, wide, in_sem, out_sem) = split_refs(refs, 2, n_src, 4, 5, 4)
    gain, shift, bias, of_project, of_up = small
    for l in range(gain.shape[0]):
        at = 6 * l
        order = (0, 2, 1, 3, 4, 5) if l == 0 else (at + 4, at, at + 5, at + 1, at + 2, at + 3)
        for i, ref in enumerate((gain, shift, bias)):
            for j in range(2):
                r = order[2 * i + j]
                ref[l, j : j + 1, :] = v[r : r + 1, :]
        width = of_project.shape[2]
        for j in range(2):
            of_project[l, j : j + 1, :] = u[l : l + 1, j * width : (j + 1) * width]
        of_up[l : l + 1, :] = u[l : l + 1, 2 * width :]
    depth = low.shape[0]

    def fetch(i):
        s, row, _ = moves[i]
        return pltpu.make_async_copy(
            srcs[s].at[pl.ds(row, ZR), :], low.at[i % depth], in_sem.at[i % depth]
        )

    def store(i):
        _, _, targets = moves[i]
        copies = []
        for n, (o, index, lo, width) in enumerate(targets):
            copies.append(
                pltpu.make_async_copy(
                    wide.at[i % depth, :, pl.ds(lo, width)],
                    outs[o].at[index],
                    out_sem.at[i % depth, n],
                )
            )
        return copies

    for i in range(min(depth, len(moves))):
        fetch(i).start()
    for i in range(len(moves)):
        fetch(i).wait()
        if i >= depth:
            for c in store(i - depth):
                c.wait()
        wide[i % depth] = low[i % depth].astype(jnp.float32)
        for c in store(i):
            c.start()
        if i + depth < len(moves):
            fetch(i + depth).start()
    for i in range(max(0, len(moves) - depth), len(moves)):
        for c in store(i):
            c.wait()


def place_call(sums, out_shapes, targets_of, v, u, small):
    vmem = pl.BlockSpec(memory_space=pltpu.VMEM)
    arrays, moves = [], []
    for key, row, array, at in sums:
        if not any(a is array for a in arrays):
            arrays.append(array)
        i = [a is array for a in arrays].index(True)
        moves.append((i, at, targets_of(key, row)))
    w = arrays[0].shape[1]
    depth = 12
    anywhere = pl.BlockSpec(memory_space=pl.ANY)
    return pl.pallas_call(
        functools.partial(place_kernel, moves, len(arrays)),
        out_shape=tuple(out_shapes) + tuple(small),
        in_specs=[vmem] * 2 + [anywhere] * len(arrays),
        out_specs=(anywhere,) * len(out_shapes) + (vmem,) * len(small),
        scratch_shapes=[
            pltpu.VMEM((depth, ZR, w), jnp.bfloat16),
            pltpu.VMEM((depth, ZR, w), jnp.float32),
            pltpu.SemaphoreType.DMA((depth,)),
            pltpu.SemaphoreType.DMA((depth, 2)),
        ],
        compiler_params=pltpu.CompilerParams(vmem_limit_bytes=62 << 20),
        cost_estimate=cost(1 << 20),
        name="place",
    )(v, u, *arrays)


def first_kernel(C, zc, n_project, *refs):
    zi, zo, zs = zc.counts()
    ins, z_in, outs, z_out, scratch, z_scratch = split_refs(refs, 6, zi, 6, zo, 14, zs)
    x_ref, gain_ref, bias_ref, shift_ref, up_ref, down_ref = ins
    full_ref, project_ref, up_out, down_out = *outs[:2], outs[2:4], outs[4:6]
    x_low, w_here, w_sem, wide, low, wide_sem, low_sem, *mine = scratch
    buf, send, recv, loc, wide2, low2, total_ref = mine
    R, D = x_ref.shape
    rc = R // C
    me, core, bx, by, partner, xn, yn = peers()
    z = zc.make(z_in + z_out + z_scratch)

    pieces = []
    both = ((up_ref, up_out, wide, low, 0), (down_ref, down_out, wide2, low2, 1))
    for l in range(2):
        for ref, out, w, n, stage in both:
            size = w.shape[1]
            pieces += [
                (ref.at[l, pl.ds(r, size), :], out[l].at[pl.ds(r, size), :], w, n, stage)
                for r in range(0, ref.shape[1], size)
            ]

    def read(i):
        src, _, w, _, stage = pieces[i]
        return pltpu.make_async_copy(src, w.at[i % 2], wide_sem.at[stage, i % 2])

    def write(i):
        _, dst, _, n, stage = pieces[i]
        return pltpu.make_async_copy(n.at[i % 2], dst, low_sem.at[stage, i % 2])

    def cast(i):
        _, _, w, n, _ = pieces[i]
        read(i).wait()
        if i >= 2:
            write(i - 2).wait()
        n[i % 2] = w[i % 2].astype(n.dtype)
        write(i).start()
        if i + 2 < len(pieces):
            read(i + 2).start()

    for i in range(2):
        read(i).start()
    z.ahead = n_project
    enter(partner, xn, yn, True)
    z.start()

    @pl.loop(0, R // 16)
    def _(i):
        rows = pl.ds(pl.multiple_of(i * 16, 16), 16)
        v = x_ref[rows, :].astype(jnp.float32)
        x_low[rows, :] = layer_norm(v, gain_ref[...], bias_ref[...]).astype(x_low.dtype)

    sent = []

    def copy(src, rel, k, target, sidx):
        return pltpu.make_async_remote_copy(
            src_ref=src,
            dst_ref=buf.at[k, rel],
            send_sem=send.at[sidx, k],
            recv_sem=recv.at[rel, k],
            device_id={"mp": target},
            device_id_type=MESH,
        )

    def push(src, rel, k, target, sidx):
        c = copy(src, rel, k, target, sidx)
        c.start()
        sent.append(c)

    def arrive(rel, k):
        copy(buf.at[k, 0], rel, k, partner, 0).wait_recv()

    for k in range(C):
        own = x_low.at[pl.ds(k * rc, rc), :]
        push(own, 2, k, xn, 1)
        push(own, 4, k, yn, 2)
        push(own, 1, k, partner, 0)
    kept = [
        pltpu.make_async_copy(
            x_low, full_ref.at[pl.ds(pl.multiple_of(me * R, R), R), :], loc.at[0, 0]
        )
    ]
    kept[0].start()
    starts = [pl.multiple_of(owner(rel, core, bx, by) * R, R) for rel in range(8)]
    across = jnp.where(core == 0, xn, yn)
    for k in range(C + 1):
        if k < C:
            arrive(2, k)
            arrive(4, k)
            push(buf.at[k, 4 - 2 * core], 6, k, across, 3)
            push(buf.at[k, 2], 3, k, partner, 4)
            push(buf.at[k, 4], 5, k, partner, 5)
        if k >= 1:
            arrive(6, k - 1)
            push(buf.at[k - 1, 6], 7, k - 1, partner, 6)
        for i in range(2 * k, min(2 * k + 2, len(pieces))):
            cast(i)
        z.tick((0, 0, 3, 2, 1)[k])
    for k in range(C):
        for rel in range(1, 8):
            if rel in (1, 3, 5, 7):
                arrive(rel, k)
            start = pl.multiple_of(starts[rel] + k * rc, rc)
            c = pltpu.make_async_copy(
                buf.at[k, rel], full_ref.at[pl.ds(start, rc), :], loc.at[k, rel]
            )
            c.start()
            kept.append(c)
    for i in range(2 * C + 2, len(pieces)):
        cast(i)
    for i in range(len(pieces) - 2, len(pieces)):
        write(i).wait()
    z.tick(n_project)
    Z, per, _ = w_here.shape
    parts = w_sem.shape[0]
    size = per // parts
    for p in range(parts):
        z.settle((p + 1) * n_project // parts)
        here = pl.ds(p * size, size)
        weights = pltpu.make_async_copy(z_out[0].at[:, here, :], w_here.at[:, here, :], w_sem.at[p])
        weights.start()
        weights.wait()
        for rel in range(8):
            rows = pl.ds(starts[rel], R)

            def f(cols, rel=rel, rows=rows):
                lhs = []
                for i in range(Z):
                    depth = pl.ds(i * per + p * size, size)
                    x = x_low[:, depth] if rel == 0 else buf[:, rel, :, depth].reshape(R, size)
                    lhs.append(x)
                w = w_here[:, here, cols].reshape(Z * size, cols.size)
                term = nn(jnp.concatenate(lhs, axis=1), w)
                if p > 0:
                    term = term + total_ref[rows, cols]
                if p < parts - 1:
                    total_ref[rows, cols] = term
                else:
                    project_ref[rows, cols] = (term + shift_ref[:, cols]).astype(jnp.bfloat16)

            tiles(project_ref.shape[1], 256, f)
            z.tick()
    z.finish()
    for c in sent:
        c.wait_send()
    for c in kept:
        c.wait()


def first_call(cid, x, gain, bias, shift, up, down, z, n_project, C=4):
    R, D = x.shape
    N = shift.shape[0]
    w = z.arrays[0]
    vmem = pl.BlockSpec(memory_space=pltpu.VMEM)
    anywhere = pl.BlockSpec(memory_space=pl.ANY)
    low = jnp.bfloat16
    out = pl.pallas_call(
        functools.partial(first_kernel, C, z, n_project),
        out_shape=(
            jax.ShapeDtypeStruct((8 * R, D), low),
            jax.ShapeDtypeStruct((8 * R, N), low),
            *[jax.ShapeDtypeStruct(up.shape[1:], low)] * 2,
            *[jax.ShapeDtypeStruct(down.shape[1:], low)] * 2,
            *z.out_shapes,
        ),
        in_specs=[vmem] * 4 + [anywhere] * 2 + z.in_specs(),
        out_specs=(anywhere, vmem) + (anywhere,) * 4 + z.out_specs(),
        scratch_shapes=[
            pltpu.VMEM((R, D), low),
            pltpu.VMEM((4, *w.shape[1:]), low),
            pltpu.SemaphoreType.DMA((2,)),
            pltpu.VMEM((2, 256, up.shape[2]), jnp.float32),
            pltpu.VMEM((2, 256, up.shape[2]), low),
            pltpu.SemaphoreType.DMA((2, 2)),
            pltpu.SemaphoreType.DMA((2, 2)),
            pltpu.VMEM((C, 8, R // C, D), low),
            pltpu.SemaphoreType.DMA((7, C)),
            pltpu.SemaphoreType.DMA((8, C)),
            pltpu.SemaphoreType.DMA((C, 8)),
            pltpu.VMEM((2, 512, down.shape[2]), jnp.float32),
            pltpu.VMEM((2, 512, down.shape[2]), low),
            pltpu.VMEM((8 * R, N), jnp.float32),
            *z.scratch,
        ],
        compiler_params=pltpu.CompilerParams(
            collective_id=cid, has_side_effects=True, vmem_limit_bytes=60 << 20
        ),
        cost_estimate=cost(1 << 20),
        name="first",
    )(x, gain[None], bias[None], shift[None], up, down, *z.arrays)
    z.done(out[6:])
    return out[:6]


def gather_sum(part):
    return lax.psum_scatter(
        part.astype(jnp.bfloat16), "mp", scatter_dimension=0, tiled=True
    ).astype(jnp.float32)


def gather_all(x):
    return lax.all_gather(x, "mp", axis=0, tiled=True)


def side_by_side(w):
    return jnp.concatenate([w[z] for z in range(w.shape[0])], axis=1)


def reduce_dp(part):
    return lax.psum_scatter(part.astype(jnp.bfloat16), "dp", scatter_dimension=0)


class Fast:
    def __init__(self, T, D):
        self.T, self.D = T, D
        self.backlog = Backlog()
        self.rows = None

    def start(self, x, gain, bias, shift, out_grad, weights):
        project, dense, up, down = weights
        low = jnp.bfloat16
        project = project.reshape(*project.shape[:2], -1).astype(low)
        dense = dense.astype(low)
        self.weights = queue = GatherQueue()
        queue.add(("project", 0), project, 0, 64)
        n_project = project.shape[1] // 64
        rows, out, up0, up1, down0, down1 = first_call(
            0, x, gain, bias, shift, up, down, queue.take(n_project), n_project
        )
        self.first = rows, out
        for key, shard in (
            (("up", 0), up0),
            (("down", 0), down0),
            (("project", 1), project[1]),
            (("up", 1), up1),
        ):
            queue.arrays[key] = lax.all_gather(shard, "dp", axis=0)
        queue.add(("dense", 0), dense, 0, 128)
        (self.grad_rows,) = gather_only(8, (out_grad,), z=queue.take(2))
        queue.add(("dense", 1), dense, 1, 128)
        queue.add(("down", 1), down1[None], 0, 128)

    def weight(self, name, l):
        w = self.weights.arrays[name, l]
        return w.reshape(-1, w.shape[2]) if name in ("project", "up") else w

    def shape(self, width, dtype=jnp.bfloat16):
        return jax.ShapeDtypeStruct((self.T, width), dtype)

    def packed(self, rows):
        return jax.ShapeDtypeStruct((4, rows, self.D // 4), jnp.bfloat16), False

    def scatter(self, ins, body, epilogue, **more):
        return Scatter(self.T, self.D, ins, body, epilogue, **more)

    def gather(self, x, ins, outs, body, **more):
        return Gather(self.T // 8, self.D, x, ins, outs, body, **more)

    def project(self, l, shift):
        if l == 0:
            return self.first
        w = self.weight("project", l)
        phase = self.gather(self.rows, (w, shift[None]), (self.shape(w.shape[1]),), project_body)
        return chain_call("gather_project", 10 * l, [phase], self.weights.take(2))[0]

    def attend(self, l, project, slopes):
        return attend_fwd(20 + l, project, slopes, NO_Z)

    def attn_out(self, l, stream, context, bias, gain, shift, up_shift):
        phase = self.scatter(
            (context, self.weight("dense", l)), row_split_body, AddNorm(stream, bias, gain, shift, True)
        )
        z = self.weights.take(2 * l)
        ((middle, rows),) = chain_call("dense_scatter", 10 * l + 1, [phase], z)
        w = self.weight("up", l)
        shape = self.shape(w.shape[1])
        phase = self.gather(rows, (w, up_shift[None]), (shape, shape), up_body)
        z = self.weights.take(6 * l)
        return middle, *chain_call("gather_up", 10 * l + 2, [phase], z)[0]

    def ffn_out(self, l, middle, active, bias, gain, shift):
        phase = self.scatter(
            (active, self.weight("down", l)),
            row_split_body,
            AddNorm(middle, bias, gain, shift, True),
            more=((self.grad_rows, False),),
        )
        ((stream, self.rows),) = chain_call("down_scatter", 10 * l + 3, [phase])
        return stream

    def last_out(self, l, middle, active, slope, bias):
        T, F = active.shape
        grad = self.grad_rows
        phase = self.scatter(
            (active, self.weight("down", l)),
            row_split_body,
            AddOnly(middle, bias),
            more=((slope, True), (grad, False)),
            more_out=(
                (self.shape(F), True),
                (jax.ShapeDtypeStruct((1, F), jnp.float32), True),
                self.packed(F),
            ),
            scratch=(*STREAM_SCRATCH[2:], pltpu.VMEM((T, self.D), jnp.bfloat16), pltpu.SemaphoreType.DMA),
            filler=last_filler,
        )
        ((rows, grad_hidden, sums, packed),) = chain_call("last_scatter", 10 * l + 3, [phase])
        self.backlog.add(("down", l), packed)
        return rows, grad, grad_hidden, sums

    def ffn_back(self, l, grad, middle, gain, grad_hidden, active, normed, grad_down):
        T, F = active.shape
        epilogue = NormBack(grad, middle, gain)
        ins = (grad_hidden, self.weight("up", l))
        up = dict(
            more=((grad_hidden, True), (normed, False)),
            more_out=(self.packed(F),),
            scratch=STREAM_SCRATCH,
            filler=up_filler,
        )
        down = dict(
            more=((active, False), (grad_down, False)),
            more_out=(self.packed(F),),
            scratch=STREAM_SCRATCH
            + (pltpu.VMEM((T, self.D), jnp.bfloat16), pltpu.SemaphoreType.DMA),
            filler=down_filler,
        )
        beside = dict(up, late=1) if l else dict(down, late=6)
        first = self.scatter(ins, up_back_body, epilogue, **beside)
        w = self.weight("dense", l)
        beside = {} if l else up
        second = self.gather(None, (w,), (self.shape(w.shape[1]),), dense_back_body, **beside)
        z = self.backlog.take(8 if l else 5)
        one, two = chain_call("ffn_back", 10 * l + 5, [first, second], z)
        self.backlog.add(("up" if l else "down", l), one[2], one[3])
        if not l:
            self.backlog.add(("up", l), two[2])
        return one[0], one[1], two[0], two[1]

    def attend_back(self, l, project, grad_context, context, log_norms, slopes):
        z = self.backlog.take(0 if l else 2)
        return attend_bwd(22 + l, project, grad_context, context, log_norms, slopes, z)

    def project_back(self, grad, stream, gain, grad_project, l, context, grad_branch, normed, late):
        S, T, width = grad_project.shape
        return self.scatter(
            (grad_project, self.weight("project", l)),
            project_back_body,
            NormBack(grad, stream, gain),
            more=((context, False), (grad_branch, False), (normed, False)),
            more_out=(self.packed((S + 1) * width),),
            scratch=STREAM_SCRATCH + (pltpu.VMEM((width, T), jnp.bfloat16),),
            filler=attn_filler,
            late=late,
        )

    def attn_back(self, l, grad, stream, gain, grad_project, context, grad_branch, normed, slope):
        first = self.project_back(
            grad, stream, gain, grad_project, l, context, grad_branch, normed, 3
        )
        F = slope.shape[1]
        w = self.weight("down", l - 1)
        second = self.gather(
            None,
            (w, slope),
            (self.shape(F), jax.ShapeDtypeStruct((1, F), jnp.float32)),
            down_back_body,
        )
        one, two = chain_call("attn_back", 10 * l + 7, [first, second], self.backlog.take(7))
        self.backlog.add(("attn", l), one[2], one[3])
        return one[0], one[1], two

    def first_attn_back(
        self, grad, stream, gain, grad_project, context, grad_branch, normed, rows, split
    ):
        chunks = 4 * grad_project.shape[2] // ZR
        first = self.project_back(
            grad, stream, gain, grad_project, 0, context, grad_branch, normed, chunks
        )
        v = jnp.concatenate([jnp.zeros((2, self.D), jnp.float32), jnp.stack(rows)])
        u = jnp.pad(split, ((0, -split.shape[0] % 8), (0, 0)))
        second = Finish(jnp.pad(v, ((0, -v.shape[0] % 8), (0, 0))), u)
        one, two = chain_call("first_attn_back", 7, [first, second], self.backlog.take(1000))
        self.backlog.add(("attn", 0), one[2], one[3])
        return one[0], two[0], two[1]

    def results(self, shapes, small, v, u):
        layers, d, parts, width = shapes[0]
        group = self.D // lax.axis_size("dp")

        def targets(key, row):
            kind, l = key
            if kind == "down":
                return [(3, (l, pl.ds(row, ZR)), 0, group)]
            if kind == "up":
                b, r = divmod(row, group)
                return [(2, (l, pl.ds(r, ZR), pl.ds(b * group, group)), 0, group)]
            if row < width:
                return [(1, (l, pl.ds(row, ZR)), 0, group)]
            s, r = divmod(row - width, width)
            return [(0, (l, s, pl.ds(h * width + r, ZR)), h * width, width) for h in range(2)]

        shapes = [(layers, parts, d, width), *shapes[1:]]
        shape = lambda x: jax.ShapeDtypeStruct(x, jnp.float32)
        out = place_call(
            self.backlog.sums,
            [shape(x) for x in shapes],
            targets,
            v,
            u,
            [shape(x) for x in (small[2], small[2], small[2], small[0], small[1])],
        )
        out = (*out[:4], out[7], out[8], *out[4:7])
        return (out[0].transpose(0, 2, 1, 3), *out[1:])


class Plain:
    def __init__(self, T, D):
        self.T, self.D = T, D
        self.ffn, self.attn = {}, {}

    def start(self, x, gain, bias, shift, out_grad, weights):
        self.rows = layer_norm(x.astype(jnp.float32), gain, bias).astype(jnp.bfloat16)
        self.out_grad = out_grad
        low = jnp.bfloat16
        self.weights = []
        for l in range(weights[0].shape[0]):
            project, dense, up, down = (x[l].astype(low) for x in weights)
            project = project.reshape(project.shape[0], -1)
            self.weights.append(
                (
                    lax.all_gather(project, "dp", axis=0, tiled=True),
                    lax.all_gather(dense, "dp", axis=0),
                    lax.all_gather(up, "dp", axis=0, tiled=True),
                    lax.all_gather(down, "dp", axis=0),
                )
            )

    def project(self, l, shift):
        full = gather_all(self.rows)
        return full, (nn(full, self.weights[l][0]) + shift).astype(jnp.bfloat16)

    def attend(self, l, project, slopes):
        return attend_fwd(0, project, slopes, NO_Z)

    def attn_out(self, l, stream, context, bias, gain, shift, up_shift):
        middle = stream + gather_sum(nn(context, side_by_side(self.weights[l][1]))) + bias
        full = gather_all(layer_norm(middle, gain, shift).astype(jnp.bfloat16))
        return middle, full, *gelu_both(nn(full, self.weights[l][2]) + up_shift)

    def ffn_out(self, l, middle, active, bias, gain, shift):
        stream = middle + gather_sum(nn(active, side_by_side(self.weights[l][3]))) + bias
        self.rows = layer_norm(stream, gain, shift).astype(jnp.bfloat16)
        return stream

    def down_back(self, l, grad, slope):
        full = gather_all(grad)
        g = (nt(full, side_by_side(self.weights[l][3])) * slope.astype(jnp.float32)).astype(
            jnp.bfloat16
        )
        return full, g, jnp.sum(g.astype(jnp.float32), axis=0, keepdims=True)

    def last_out(self, l, middle, active, slope, bias):
        rows = middle + gather_sum(nn(active, side_by_side(self.weights[l][3]))) + bias
        return rows.astype(jnp.bfloat16), *self.down_back(l, self.out_grad, slope)

    def norm_back(self, grad, values, gain, total):
        back = jax.vjp(layer_norm, values.astype(jnp.float32), gain, gain)[1]
        step, gain_sum, shift_sum = back(total)
        grad = grad + step
        return grad, jnp.stack([gain_sum, shift_sum, jnp.sum(grad, axis=0)])

    def ffn_back(self, l, grad, middle, gain, grad_hidden, active, normed, grad_down):
        Z = lax.axis_size("dp")
        F = grad_hidden.shape[1]
        d = self.D // Z
        up = jnp.einsum("td,tf->df", normed, grad_hidden, preferred_element_type=jnp.float32)
        down = jnp.einsum(
            "tf,tzd->zfd", active, grad_down.reshape(-1, Z, d), preferred_element_type=jnp.float32
        )
        self.ffn[l] = reduce_dp(up.reshape(Z, d, F)), reduce_dp(down)
        total = gather_sum(nt(grad_hidden, self.weights[l][2]))
        grad, sums = self.norm_back(grad, middle, gain, total)
        full = gather_all(grad.astype(jnp.bfloat16))
        return grad, sums, full, nt(full, side_by_side(self.weights[l][1])).astype(jnp.bfloat16)

    def attend_back(self, l, project, grad_context, context, log_norms, slopes):
        return attend_bwd(0, project, grad_context, context, log_norms, slopes, NO_Z)

    def project_back(self, l, grad, stream, gain, grad_project, context, grad_branch, normed):
        S, T, width = grad_project.shape
        w = self.weights[l][0]
        Z = lax.axis_size("dp")
        d = self.D // Z
        dense = jnp.einsum(
            "ti,tzd->zid", context, grad_branch.reshape(T, Z, d), preferred_element_type=jnp.float32
        )
        project = jnp.einsum(
            "td,sti->dsi", normed, grad_project, preferred_element_type=jnp.float32
        )
        self.attn[l] = reduce_dp(project.reshape(Z, d, S, width)), reduce_dp(dense)
        part = sum(nt(grad_project[s], w[:, s * width : (s + 1) * width]) for s in range(S))
        return self.norm_back(grad, stream, gain, gather_sum(part))

    def attn_back(self, l, grad, stream, gain, grad_project, context, grad_branch, normed, slope):
        grad, sums = self.project_back(
            l, grad, stream, gain, grad_project, context, grad_branch, normed
        )
        return grad, sums, self.down_back(l - 1, grad.astype(jnp.bfloat16), slope)

    def first_attn_back(
        self, grad, stream, gain, grad_project, context, grad_branch, normed, rows, split
    ):
        grad, sums = self.project_back(
            0, grad, stream, gain, grad_project, context, grad_branch, normed
        )
        rows = jnp.concatenate([sums[:2], jnp.stack(rows)])
        return grad, lax.psum(rows, ("dp", "mp")), lax.psum(split, "dp")

    def results(self, shapes, small, total, split):
        grads = [(*self.attn[l], *self.ffn[l]) for l in range(shapes[0][0])]
        matrices = tuple(jnp.stack(parts).astype(jnp.float32) for parts in zip(*grads))
        parts = [jnp.concatenate([total[2:6], total[:2]])]
        parts += [total[6 * l : 6 * l + 6] for l in range(1, len(grads))]
        pick = lambda i, j: jnp.stack([jnp.stack([p[i], p[j]]) for p in parts])
        n = small[0][1] * small[0][2]
        split = split[:, :n].reshape(small[0]), split[:, n:]
        return (*matrices, *split, pick(4, 0), pick(5, 1), pick(2, 3))


def shards(
    inputs,
    out_grad,
    project_weight,
    dense_weight,
    up_weight,
    down_weight,
    project_bias,
    up_bias,
    norm_gain,
    norm_bias,
    output_bias,
):
    tensor_size = lax.axis_size("mp")
    tensor_rank = lax.axis_index("mp")
    row_count, model_width = inputs.shape
    total_rows = row_count * tensor_size
    inner_width = project_weight.shape[3]
    heads_here = N_HEADS // tensor_size
    layer_count = project_weight.shape[0]
    slopes = 2.0 ** (
        -8.0
        * (tensor_rank * heads_here + lax.iota(jnp.int32, heads_here) + 1).astype(jnp.float32)
        / N_HEADS
    )
    fast = tensor_size == 8 and lax.axis_size("dp") == 4 and row_count == 256
    ops = (Fast if fast else Plain)(total_rows, model_width)
    none = jnp.zeros((inner_width,), jnp.float32)
    shifts = [
        jnp.concatenate([project_bias[l, 0], none, project_bias[l, 1]]) for l in range(layer_count)
    ]
    weights = (project_weight, dense_weight, up_weight, down_weight)
    ops.start(inputs, norm_gain[0, 0], norm_bias[0, 0], shifts[0], out_grad, weights)
    stream = inputs
    last = layer_count - 1
    stored = []
    for l in range(layer_count):
        normed_all, project = ops.project(l, shifts[l])
        context, log_norms = ops.attend(l, project, slopes)
        middle, normed2_all, active, slope = ops.attn_out(
            l,
            stream,
            context,
            output_bias[l, 0],
            norm_gain[l, 1],
            norm_bias[l, 1],
            up_bias[l],
        )
        stored.append(
            (stream, normed_all, project, log_norms, context, middle, normed2_all, active, slope)
        )
        if l < last:
            stream = ops.ffn_out(
                l, middle, active, output_bias[l, 1], norm_gain[l + 1, 0], norm_bias[l + 1, 0]
            )
    outputs, *step = ops.last_out(last, middle, active, slope, output_bias[last, 1])
    grad = out_grad
    down_bias_grad = jnp.sum(grad.astype(jnp.float32), axis=0)
    sums = [None] * layer_count
    split = [None] * layer_count
    for l in reversed(range(layer_count)):
        stream, normed_all, project, log_norms, context, middle, normed2_all, active, _ = stored[l]
        grad_down, grad_hidden, up_bias_part = step
        grad, second, grad_branch, grad_context = ops.ffn_back(
            l, grad, middle, norm_gain[l, 1], grad_hidden, active, normed2_all, grad_down
        )
        grad_project, project_bias_part = ops.attend_back(
            l, project, grad_context, context, log_norms, slopes
        )
        sums[l] = [second[0], second[1], second[2], down_bias_grad]
        split[l] = jnp.concatenate([project_bias_part.reshape(-1), up_bias_part.reshape(-1)])
        args = (grad, stream, norm_gain[l, 0], grad_project, context, grad_branch, normed_all)
        if l:
            grad, first, step = ops.attn_back(l, *args, stored[l - 1][-1])
            sums[l] += [first[0], first[1]]
            down_bias_grad = first[2]
    rows = sums[0] + [x for parts in sums[1:] for x in parts]
    grad, total, split = ops.first_attn_back(*args, rows, jnp.stack(split))
    shapes = [x.shape for x in weights]
    small = [x.shape for x in (project_bias, up_bias, norm_gain)]
    return outputs, grad, *ops.results(shapes, small, total, split)


def solution(mesh):
    rows = P(("dp", "mp"), None)
    specs = (P(None, "dp", None, "mp"), P(None, "mp", "dp"), P(None, "dp", "mp"), P(None, "mp", "dp"))
    biases = (P(None, None, "mp"), P(None, "mp"), P(), P(), P())
    return jax.shard_map(
        shards,
        mesh=mesh,
        in_specs=(rows, rows, *specs, *biases),
        out_specs=(rows, rows, *specs, *biases),
        check_vma=False,
    )
```
